32 devices in a mesh: dp: 4 (over y, core), blk: 8 (over z, x).
Axes of the slice: x: 2, y: 2, z: 4, core: 2. Of those that a mesh axis runs over, the one named last changes fastest.
Arguments:
- features: bfloat16 [4, 2, 32, 64, 512], P('dp', None, 'blk'), may hold values from -24 to 24
- bounds: int32 [4, 2, 2], P('dp'), may hold values from 1 to 31, as said below
- out_grad: bfloat16 [4, 2, 32, 64, 512], P('dp', None, 'blk'), may hold values from -6 to 6
- norm1_gain: bfloat16 [512], P('blk'), may hold values from 0.5 to 1.5
- norm1_shift: bfloat16 [512], P('blk'), may hold values from -2.5 to 2.5
- conv1_weight: bfloat16 [4608, 512], P('blk', 'dp'), may hold values from -0.09375 to 0.09375
- norm2_gain: bfloat16 [512], P('blk'), may hold values from 0.5 to 1.5
- norm2_shift: bfloat16 [512], P('blk'), may hold values from -2.5 to 2.5
- conv2_weight: bfloat16 [4608, 512], P('blk', 'dp'), may hold values from -0.09375 to 0.09375
- norm3_gain: bfloat16 [512], P('blk'), may hold values from 0.5 to 1.5
- norm3_shift: bfloat16 [512], P('blk'), may hold values from -2.5 to 2.5
- query_weight: bfloat16 [512, 512], P('blk', 'dp'), may hold values from -0.25 to 0.25
- key_weight: bfloat16 [512, 512], P('blk', 'dp'), may hold values from -0.25 to 0.25
- value_weight: bfloat16 [512, 512], P('blk', 'dp'), may hold values from -0.25 to 0.25
- output_weight: bfloat16 [512, 512], P('blk', 'dp'), may hold values from -1.5 to 1.5
Outputs:
- activations: float32 [4, 2, 32, 64, 512], P('dp', None, 'blk')
- input_grad: float32 [4, 2, 32, 64, 512], P('dp', None, 'blk')
- norm1_gain_grad: float32 [512], P('blk')
- norm1_shift_grad: float32 [512], P('blk')
- conv1_grad: float32 [4608, 512], P('blk', 'dp')
- norm2_gain_grad: float32 [512], P('blk')
- norm2_shift_grad: float32 [512], P('blk')
- conv2_grad: float32 [4608, 512], P('blk', 'dp')
- norm3_gain_grad: float32 [512], P('blk')
- norm3_shift_grad: float32 [512], P('blk')
- query_grad: float32 [512, 512], P('blk', 'dp')
- key_grad: float32 [512, 512], P('blk', 'dp')
- value_grad: float32 [512, 512], P('blk', 'dp')
- output_grad: float32 [512, 512], P('blk', 'dp')
The draws below stay inside these ranges and needn't reach their ends.
Inputs may be any that keep to these rules, and one draw needn't show every extreme that they name: In each micro-batch of each data group canvas 0 holds rows [0, bounds[0]), canvas 1 row [bounds[0], bounds[1]), canvas 2 rows [bounds[1], 32); bounds[0] and 32 - bounds[1] each lie in 1 to 3.
All inputs are finite; a program needn't handle non-finite values.
Results may differ from the reference program's by a relative error of at most 0.015.
Values may be sent and summed in bfloat16 or wider, within the bound.
A program may use at most 384 MiB of HBM per device.

```python
import math
import jax
import jax.numpy as jnp
from jax import lax

C = 512
GROUPS = 32
W = 64
ROW_DEV = 4
MICRO = 2
CANVASES = 3
DATA_GROUPS = 4
ROWS = 32


def draw_bounds(key, part):
    count = DATA_GROUPS * MICRO
    order_head = jax.random.permutation(jax.random.fold_in(key, 11), count)
    order_tail = jax.random.permutation(jax.random.fold_in(key, 12), count)
    head_rows = 1 + order_head % (ROW_DEV - 1)
    tail_rows = 1 + order_tail % (ROW_DEV - 1)
    paired = jnp.stack([head_rows, ROWS - tail_rows], axis=-1)
    return paired.reshape(DATA_GROUPS, MICRO, 2).astype(jnp.int32)


def draw_features(key, part):
    shape = (DATA_GROUPS, MICRO, ROWS, W, C)
    position = jnp.arange(ROWS, dtype=jnp.float32) / float(max(ROWS - 1, 1))
    trend = 0.3 * jnp.exp(position * jnp.log(3.0))
    rough = jnp.exp(jax.random.uniform(jax.random.fold_in(key, 21), (DATA_GROUPS, MICRO, ROWS)) * jnp.log(10.0 / 3.0))
    channel_scale = jnp.exp(jax.random.uniform(jax.random.fold_in(key, 22), (C,), minval=jnp.log(0.32), maxval=jnp.log(3.2)))
    scales = (trend * rough)[..., None, None] * channel_scale
    base = jax.random.normal(jax.random.fold_in(key, 23), shape)
    return jnp.clip(base * scales, -24.0, 24.0).astype(jnp.bfloat16)


def spiked(values, own_key, source, target, shards_of, factor):
    owner, partner = [(jnp.arange(values.shape[dim]) // (values.shape[dim] // shards_of)).reshape([-1 if axis == dim else 1 for axis in range(values.ndim)]) for dim in (source, target)]
    chosen = jax.random.permutation(own_key, shards_of)[partner]
    strong = (owner == chosen) | (owner == (partner + shards_of // 2) % shards_of)
    return jnp.where(strong, factor * values, values)


def levels(key, dims, shards, least, largest):
    def one(dim, parts):
        draws = jax.random.uniform(jax.random.fold_in(jax.random.fold_in(key, 6), dim), (parts,), jnp.float32, least / len(shards), largest / len(shards))
        return jnp.repeat(jnp.exp(draws), dims[dim] // parts).reshape((-1,) + (1,) * (len(dims) - dim - 1))

    factor_of = one(*shards[0])
    for cut in shards[1:]:
        factor_of = factor_of * one(*cut)
    return factor_of


def noise(rng, extent, scale, most, pieces=(), kind=jnp.bfloat16):
    loudness = levels(rng, extent, pieces, -0.22, 0.18) if pieces else 1.0
    values = jax.random.normal(rng, extent, jnp.float32) * scale * loudness
    return jnp.minimum(jnp.maximum(values, -most), most).astype(kind)


def noise_with(stream_key, dims, spread, limit, shards, heavy, kind=jnp.bfloat16):
    drawn = spread * jax.random.normal(stream_key, dims, jnp.float32)
    if shards:
        drawn = drawn * levels(stream_key, dims, shards, -0.22, 0.18)
    return jnp.clip(spiked(drawn, jax.random.fold_in(stream_key, 3), *heavy), -limit, limit).astype(kind)


def setup_inputs(seed: int = 0) -> dict:
    splits = jax.random.split(jax.random.key(seed), 16)
    return {
        "features": draw_features(jax.random.fold_in(splits[15], 71), 0),
        "bounds": draw_bounds(jax.random.fold_in(splits[15], 71), 0),
        "out_grad": noise_with(splits[2], (DATA_GROUPS, MICRO, ROWS, W, C), 1.0, 6.0, ((0, 4), (2, 8)), (2, 4, 8, 2.0)),
        "norm1_gain": jnp.clip(1.0 + 0.1 * jax.random.normal(splits[3], (C,), jnp.float32), 0.5, 1.5).astype(jnp.bfloat16),
        "norm1_shift": noise(splits[4], (C,), 0.3, 2.5, ((0, 8),)),
        "conv1_weight": noise(splits[5], (9 * C, C), (9 * C) ** -0.5, 0.09375, ((0, 8), (1, 4))),
        "norm2_gain": jnp.clip(1.0 + 0.1 * jax.random.normal(splits[6], (C,), jnp.float32), 0.5, 1.5).astype(jnp.bfloat16),
        "norm2_shift": noise(splits[7], (C,), 0.3, 2.5, ((0, 8),)),
        "conv2_weight": noise(splits[8], (9 * C, C), (9 * C) ** -0.5, 0.09375, ((0, 8), (1, 4))),
        "norm3_gain": jnp.clip(1.0 + 0.1 * jax.random.normal(splits[9], (C,), jnp.float32), 0.5, 1.5).astype(jnp.bfloat16),
        "norm3_shift": noise(splits[10], (C,), 0.3, 2.5, ((0, 8),)),
        "query_weight": noise(splits[11], (C, C), C ** -0.5, 0.25, ((0, 8), (1, 4))),
        "key_weight": noise(splits[12], (C, C), C ** -0.5, 0.25, ((0, 8), (1, 4))),
        "value_weight": noise(splits[13], (C, C), C ** -0.5, 0.25, ((0, 8), (1, 4))),
        "output_weight": noise(splits[14], (C, C), (max(1, C // ROWS)) ** -0.5, 1.5, ((0, 8), (1, 4))),
    }


@jax.custom_vjp
def low(v):
    return lax.optimization_barrier(v.astype(jnp.bfloat16)).astype(jnp.float32)

@jax.custom_vjp
def low_back(v):
    return v

def low_keep(v):
    return (low(v), None)

def low_pass(kept, grad):
    return (grad,)

def back_keep(v):
    return (v, None)

def back_low(kept, grad):
    return (low(grad),)
low.defvjp(low_keep, low_pass)
low_back.defvjp(back_keep, back_low)
EPSILON = 1e-06
HIGHEST = lax.Precision.HIGHEST
NEGATIVE = -1e+30

def canvas_index(global_rows, first_row, second_row):
    return (global_rows >= first_row).astype(jnp.int32) + (global_rows >= second_row).astype(jnp.int32)

def swish(argument):
    return argument * jax.nn.sigmoid(argument)

def group_norm(inputs, seg_rows, counts, norm_gain, norm_shift):
    row_count, width, channels = inputs.shape
    grouped = inputs.reshape(row_count, width, GROUPS, channels // GROUPS)
    result = jnp.zeros_like(grouped)
    for canvas in range(CANVASES):
        inside = (seg_rows == canvas)[:, None, None, None]
        totals = lax.optimization_barrier(jnp.sum(jnp.where(inside, grouped, 0.0), axis=(0, 1, 3)))
        square = lax.optimization_barrier(jnp.sum(jnp.where(inside, grouped * grouped, 0.0), axis=(0, 1, 3)))
        average = totals / counts[canvas]
        inverse = lax.rsqrt(square / counts[canvas] - average * average + EPSILON)
        normal = (grouped - average[None, None, :, None]) * inverse[None, None, :, None]
        result = jnp.where(inside, normal, result)
    return result.reshape(row_count, width, channels) * norm_gain + norm_shift

def convolve(activation, seg_rows, kernel):
    row_count, width, channels = activation.shape
    padded = jnp.pad(activation, ((1, 1), (1, 1), (0, 0)))
    seg_pad = jnp.pad(seg_rows, (1, 1), constant_values=-1)
    columns = []
    for step_row in (-1, 0, 1):
        allowed = (seg_pad[1 + step_row:1 + step_row + row_count] == seg_rows).astype(jnp.float32)[:, None, None]
        for step_col in (-1, 0, 1):
            columns.append(padded[1 + step_row:1 + step_row + row_count, 1 + step_col:1 + step_col + width, :] * allowed)
    stacked = jnp.concatenate(columns, axis=-1).reshape(row_count * width, 9 * channels)
    return jnp.dot(stacked, kernel, precision=HIGHEST).reshape(row_count, width, channels)

def attend(normed, token_seg, query_matrix, key_matrix, value_matrix):
    scale = C ** (-0.5)
    queries = low_back(low(jnp.dot(normed, query_matrix, precision=HIGHEST)))
    keys_all = low_back(low(jnp.dot(normed, key_matrix, precision=HIGHEST)))
    values_all = low_back(low(jnp.dot(normed, value_matrix, precision=HIGHEST)))
    token_total = queries.shape[0]
    block = math.gcd(token_total, 512)

    def one_block(inputs):
        query_block, seg_block = inputs
        scores = low_back(jnp.dot(query_block, keys_all.T, precision=HIGHEST) * scale)
        shared = seg_block[:, None] == token_seg[None, :]
        masked = jnp.where(shared, scores, NEGATIVE)
        maximum = lax.optimization_barrier(jnp.max(masked, axis=1, keepdims=True))
        weights = jnp.where(shared, jnp.exp(masked - maximum), 0.0)
        probs = weights / lax.optimization_barrier(jnp.sum(weights, axis=1, keepdims=True))
        return jnp.dot(low(probs), values_all, precision=HIGHEST)
    result = lax.map(jax.checkpoint(one_block), (queries.reshape(-1, block, C), token_seg.reshape(-1, block)))
    return result.reshape(token_total, C)

def block_forward(inputs, seg_rows, counts, weights):
    gain_one, shift_one, conv_one, gain_two, shift_two, conv_two, gain_three, shift_three, query_matrix, key_matrix, value_matrix, output_matrix = weights
    act_one = low(swish(group_norm(inputs, seg_rows, counts, gain_one, shift_one)))
    hidden_one = low_back(convolve(act_one, seg_rows, conv_one))
    act_two = low(swish(group_norm(hidden_one, seg_rows, counts, gain_two, shift_two)))
    hidden_two = low_back(convolve(act_two, seg_rows, conv_two))
    residual = inputs + hidden_two
    normed = low(group_norm(residual, seg_rows, counts, gain_three, shift_three)).reshape(-1, C)
    token_seg = jnp.repeat(seg_rows, W)
    heads = low_back(low(attend(normed, token_seg, query_matrix, key_matrix, value_matrix)))
    return residual + jnp.dot(heads, output_matrix, precision=HIGHEST).reshape(residual.shape)

def reference(features, bounds, out_grad, norm1_gain, norm1_shift, conv1_weight, norm2_gain, norm2_shift, conv2_weight, norm3_gain, norm3_shift, query_weight, key_weight, value_weight, output_weight):
    params = tuple((item.astype(jnp.float32) for item in (norm1_gain, norm1_shift, conv1_weight, norm2_gain, norm2_shift, conv2_weight, norm3_gain, norm3_shift, query_weight, key_weight, value_weight, output_weight)))
    row_index = jnp.arange(ROWS, dtype=jnp.int32)
    flat_inputs = features.reshape(DATA_GROUPS * MICRO, ROWS, W, C)
    flat_bounds = bounds.reshape(DATA_GROUPS * MICRO, 2)
    flat_grads = out_grad.reshape(DATA_GROUPS * MICRO, ROWS, W, C)

    def one_group(running, item):
        inputs, bound_pair, upstream = item
        seg_rows = canvas_index(row_index, bound_pair[0], bound_pair[1])
        counts = jnp.stack([bound_pair[0], bound_pair[1] - bound_pair[0], ROWS - bound_pair[1]]).astype(jnp.float32) * float(W * (C // GROUPS))

        def forward(values_in, *weights):
            return block_forward(values_in, seg_rows, counts, weights)
        output, pullback = jax.vjp(forward, inputs.astype(jnp.float32), *params)
        gradients = pullback(upstream.astype(jnp.float32))
        updated = tuple((acc + new for acc, new in zip(running, gradients[1:])))
        return (updated, (output, gradients[0]))
    initial = tuple((jnp.zeros_like(item) for item in params))
    sums, (outputs, input_grads) = lax.scan(one_group, initial, (flat_inputs, flat_bounds, flat_grads))
    activations = outputs.reshape(features.shape)
    input_grad = input_grads.reshape(features.shape)
    return (activations, input_grad, sums[0], sums[1], sums[2], sums[3], sums[4], sums[5], sums[6], sums[7], sums[8], sums[9], sums[10], sums[11])
```

```python
import functools

import jax
import jax.numpy as jnp
from jax import lax
from jax.experimental import pallas as pl
from jax.experimental.pallas import tpu as pltpu
from jax.sharding import PartitionSpec as P

GROUPS = 32
CANVASES = 3


EPSILON = 1e-06
HIGHEST = lax.Precision.HIGHEST
NEGATIVE = -1e30
MESH = pl.DeviceIdType.MESH


class Place:
    def __init__(self):
        self.d = lax.axis_index("dp")
        self.b = lax.axis_index("blk")
        self.y, self.c = self.d // 2, self.d % 2
        self.z, self.x = self.b // 2, self.b % 2
        self.up = {"dp": self.d, "blk": self.b + 2}
        self.down = {"dp": self.d, "blk": self.b - 2}
        self.xn = {"dp": self.d, "blk": self.z * 2 + 1 - self.x}
        self.yn = {"dp": (1 - self.y) * 2 + self.c, "blk": self.b}
        self.cn = {"dp": self.y * 2 + 1 - self.c, "blk": self.b}


def enter(here, nz):
    barrier = pltpu.get_barrier_semaphore()
    for device in (here.xn, here.yn, here.cn):
        pl.semaphore_signal(barrier, inc=1, device_id=device, device_id_type=MESH)

    @pl.when(here.z < nz - 1)
    def _():
        pl.semaphore_signal(barrier, inc=1, device_id=here.up, device_id_type=MESH)

    @pl.when(here.z > 0)
    def _():
        pl.semaphore_signal(barrier, inc=1, device_id=here.down, device_id_type=MESH)

    lines = (here.z < nz - 1).astype(jnp.int32) + (here.z > 0).astype(jnp.int32)
    pl.semaphore_wait(barrier, 3 + lines)


def remote(src, dst, send, recv, device):
    return pltpu.make_async_remote_copy(
        src_ref=src, dst_ref=dst, send_sem=send, recv_sem=recv, device_id=device, device_id_type=MESH
    )


def steps_of(z, nz):
    visits = [(z, None)]
    for k in range(1, nz):
        visits.append((z - k, z >= k))
        visits.append((z + k, z + k < nz))
    return visits


def guarded(valid, body):
    if valid is None:
        body()
    else:
        pl.when(valid)(body)


class Gather:
    SEMS = 40

    def __init__(self, here, nz, at, sems):
        self.here, self.nz, self.at, self.sems = here, nz, at, sems
        self.visits = steps_of(here.z, nz)

    def sem(self, kind, z, way):
        base = {"z": 0, "x": 4, "y": 8, "da": 12, "db": 16, "co": 20, "cx": 24, "cy": 28, "cd": 32, "zd": 36}[kind]
        return self.sems.at[way, base + z]

    def cp(self, kind, z, src, device, skind=None):
        return remote(src, src, self.sem(skind or kind, z, 0), self.sem(kind, z, 1), device)

    def own(self, z):
        return self.at(z, self.here.x, self.here.d, None)

    def colx(self, z, half=None):
        return self.at(z, 1 - self.here.x, self.here.d, half)

    def coly(self, z, half=None):
        return self.at(z, self.here.x, (1 - self.here.y) * 2 + self.here.c, half)

    def cold(self, z, half=None):
        return self.at(z, 1 - self.here.x, (1 - self.here.y) * 2 + self.here.c, half)

    def have(self, j):
        z, valid = self.visits[j]
        here = self.here

        def body():
            src = self.own(z)
            if j > 0:
                self.cp("z", z, src, here.up).wait_recv()
            if j == 0 or j % 2 == 1:

                @pl.when(here.z < self.nz - 1)
                def _():
                    self.cp("z", z, src, here.up).start()

            if j == 0 or j % 2 == 0:

                @pl.when(here.z > 0)
                def _():
                    self.cp("z", z, src, here.down, "zd").start()

            self.cp("x", z, src, here.xn).start()
            self.cp("y", z, src, here.yn).start()
            self.cp("co", z, src, here.cn).start()

        guarded(valid, body)

    def cross(self, j):
        z, valid = self.visits[j]
        here = self.here

        def body():
            self.cp("x", z, self.colx(z), here.xn).wait_recv()
            self.cp("da", z, self.colx(z, 0), here.yn).start()
            self.cp("cx", z, self.colx(z), here.cn).start()
            self.cp("y", z, self.coly(z), here.yn).wait_recv()
            self.cp("db", z, self.coly(z, 1), here.xn).start()
            self.cp("cy", z, self.coly(z), here.cn).start()

        guarded(valid, body)

    def diagonal(self, j):
        z, valid = self.visits[j]
        here = self.here

        def body():
            self.cp("da", z, self.cold(z, 0), here.yn).wait_recv()
            self.cp("db", z, self.cold(z, 1), here.xn).wait_recv()
            self.cp("cd", z, self.cold(z), here.cn).start()

        guarded(valid, body)

    def arrive(self):
        here = self.here
        near, far = here.y * 2 + 1 - here.c, (1 - here.y) * 2 + 1 - here.c
        for z in range(self.nz):
            for kind, x, d in (("co", here.x, near), ("cx", 1 - here.x, near), ("cy", here.x, far), ("cd", 1 - here.x, far)):
                self.cp(kind, z, self.at(z, x, d, None), here.cn).wait_recv()

    def finish(self):
        here = self.here
        for j, (z, valid) in enumerate(self.visits):

            def body():
                src = self.own(z)
                if j == 0 or j % 2 == 1:

                    @pl.when(here.z < self.nz - 1)
                    def _():
                        self.cp("z", z, src, here.up).wait_send()

                if j == 0 or j % 2 == 0:

                    @pl.when(here.z > 0)
                    def _():
                        self.cp("z", z, src, here.down, "zd").wait_send()

                self.cp("x", z, src, here.xn).wait_send()
                self.cp("y", z, src, here.yn).wait_send()
                self.cp("da", z, self.colx(z, 0), here.yn).wait_send()
                self.cp("db", z, self.coly(z, 1), here.xn).wait_send()
                for kind in ("co", "cx", "cy", "cd"):
                    self.cp(kind, z, src, here.cn).wait_send()

            guarded(valid, body)

    def program(self):
        todo = [lambda: self.have(0)]
        pairs = [(0,)] + [(2 * k - 1, 2 * k) for k in range(1, self.nz)]
        for k in range(1, self.nz + 2):
            if k < self.nz:
                todo += [lambda j=j: self.have(j) for j in pairs[k]]
            if k - 1 < self.nz:
                todo += [lambda j=j: self.cross(j) for j in pairs[k - 1]]
            if 0 <= k - 2 < self.nz:
                todo += [lambda j=j: self.diagonal(j) for j in pairs[k - 2]]
        return todo


class Scatter:
    SEMS = 44

    def __init__(self, here, nz, at, part, sems, bufs):
        self.here, self.nz, self.at, self.part, self.sems = here, nz, at, part, sems
        self.core, self.acc, self.half, self.side, self.line = bufs
        visits = steps_of(here.z, nz)
        self.visits = visits[::-1]

    def sem(self, kind, z, way):
        base = {"c0": 0, "c1": 4, "c2": 8, "c3": 12, "da": 16, "db": 20, "x": 24, "y": 28, "l": 32, "ld": 36}[kind]
        return self.sems.at[way, base + z]

    def cp(self, kind, z, src, dst, device, skind=None):
        return remote(src, dst, self.sem(skind or kind, z, 0), self.sem(kind, z, 1), device)

    def places(self, z, c):
        here = self.here
        y, x = here.y, here.x
        return [(z, x, y * 2 + c), (z, 1 - x, y * 2 + c), (z, x, (1 - y) * 2 + c), (z, 1 - x, (1 - y) * 2 + c)]

    def core_cp(self, z, k):
        return self.cp("c%d" % k, z, self.at(*self.places(z, 1 - self.here.c)[k]), self.core.at[k, z], self.here.cn)

    def begin(self, j):
        z, valid = self.visits[j]

        def body():
            for k in (3, 1, 2, 0):
                self.core_cp(z, k).start()

        guarded(valid, body)

    def halves(self, z):
        return (
            self.cp("da", z, self.part(self.acc.at[3, z], 0), self.half.at[0, z], self.here.xn),
            self.cp("db", z, self.part(self.acc.at[3, z], 1), self.half.at[1, z], self.here.yn),
        )

    def sides(self, z):
        return (
            self.cp("x", z, self.acc.at[1, z], self.side.at[0, z], self.here.xn),
            self.cp("y", z, self.acc.at[2, z], self.side.at[1, z], self.here.yn),
        )

    def pair(self, z, k):
        self.core_cp(z, k).wait_recv()
        mine = self.at(*self.places(z, self.here.c)[k])[...].astype(jnp.float32)
        return mine + self.core[k, z].astype(jnp.float32)

    def corner(self, j):
        z, valid = self.visits[j]

        def body():
            self.acc[3, z] = self.pair(z, 3).astype(jnp.bfloat16)
            for copy in self.halves(z):
                copy.start()

        guarded(valid, body)

    def edges(self, j):
        z, valid = self.visits[j]

        def body():
            from_x, from_y = self.halves(z)
            for k, copy, h in ((1, from_y, 1), (2, from_x, 0)):
                total = self.pair(z, k)
                copy.wait_recv()
                self.acc[k, z] = total.astype(jnp.bfloat16)
                place = self.part(self.acc.at[k, z], h)
                place[...] = (place[...].astype(jnp.float32) + self.half[h, z].astype(jnp.float32)).astype(jnp.bfloat16)
                self.sides(z)[k - 1].start()

        guarded(valid, body)

    def line_cp(self, z, upward):
        here = self.here
        if upward:
            return self.cp("l", z, self.acc.at[0, z], self.line.at[0, z], here.up)
        return self.cp("ld", z, self.acc.at[0, z], self.line.at[1, z], here.down)

    def column(self, j, out=None):
        z, valid = self.visits[j]
        here, nz = self.here, self.nz
        last = j == len(self.visits) - 1

        def body():
            total = self.pair(z, 0)
            for copy, k in zip(self.sides(z), (0, 1)):
                copy.wait_recv()
                total = total + self.side[k, z].astype(jnp.float32)
            if last:
                out[...] = total

                @pl.when(here.z > 0)
                def _():
                    self.line_cp(z, True).wait_recv()
                    out[...] += self.line[0, z].astype(jnp.float32)

                @pl.when(here.z < nz - 1)
                def _():
                    self.line_cp(z, False).wait_recv()
                    out[...] += self.line[1, z].astype(jnp.float32)
            else:
                upward = j % 2 == 0
                self.acc[0, z] = total.astype(jnp.bfloat16)

                @pl.when((here.z > 0) if upward else (here.z < nz - 1))
                def _():
                    self.line_cp(z, upward).wait_recv()
                    k = 0 if upward else 1
                    self.acc[0, z] = (self.acc[0, z].astype(jnp.float32) + self.line[k, z].astype(jnp.float32)).astype(jnp.bfloat16)

                self.line_cp(z, upward).start()

        guarded(valid, body)

    def finish(self):
        for j, (z, valid) in enumerate(self.visits):
            last = j == len(self.visits) - 1

            def body():
                for k in range(4):
                    self.core_cp(z, k).wait_send()
                for copy in self.halves(z) + self.sides(z):
                    copy.wait_send()
                if not last:
                    self.line_cp(z, j % 2 == 0).wait_send()

            guarded(valid, body)

    def program(self, out):
        pairs = [[2 * k, 2 * k + 1] for k in range(self.nz - 1)] + [[2 * (self.nz - 1)]]
        todo = []
        for k in range(self.nz + 3):
            if k < self.nz:
                todo += [lambda j=j: self.begin(j) for j in pairs[k]]
            if 0 <= k - 1 < self.nz:
                todo += [lambda j=j: self.corner(j) for j in pairs[k - 1]]
            if 0 <= k - 2 < self.nz:
                todo += [lambda j=j: self.edges(j) for j in pairs[k - 2]]
            if 0 <= k - 3 < self.nz:
                todo += [lambda j=j: self.column(j, out) for j in pairs[k - 3]]
        return todo

def weight_places(ref, rows):
    def at(z, x, d, half=None):
        base, count = (z * 2 + x) * rows, rows
        if half is not None:
            base, count = base + half * (rows // 2), rows // 2
        return ref.at[pl.ds(pl.multiple_of(base, 16), count), pl.ds(pl.multiple_of(d * 128, 128), 128)]

    return at


def gather_kernel(nz, rows, *refs):
    count = len(rows)
    shards, wholes, (sems, local) = refs[:count], refs[count : 2 * count], refs[2 * count :]
    here = Place()
    enter(here, nz)
    gathers = []
    for k in range(count):
        at = weight_places(wholes[k], rows[k])
        gathers.append(Gather(here, nz, at, sems.at[k]))
        own = pltpu.make_async_copy(shards[k], at(here.z, here.x, here.d), local.at[k])
        own.start()
    for k in range(count):
        pltpu.make_async_copy(shards[k], gathers[k].own(here.z), local.at[k]).wait()
        for step in gathers[k].program():
            step()
    for gather in gathers:
        gather.arrive()
        gather.finish()


def gather_all(shards, nz):
    rows = [item.shape[0] for item in shards]
    return pl.pallas_call(
        functools.partial(gather_kernel, nz, rows),
        out_shape=[jax.ShapeDtypeStruct((r * nz * 2, 512), jnp.bfloat16) for r in rows],
        in_specs=[pl.BlockSpec(memory_space=pltpu.VMEM)] * len(rows),
        out_specs=[pl.BlockSpec(memory_space=pltpu.VMEM)] * len(rows),
        scratch_shapes=[
            pltpu.SemaphoreType.DMA((len(rows), 2, Gather.SEMS)),
            pltpu.SemaphoreType.DMA((len(rows),)),
        ],
        compiler_params=pltpu.CompilerParams(collective_id=0, has_side_effects=True, vmem_limit_bytes=56 << 20),
    )(*shards)


def scatter_kernel(nz, rows, *refs):
    count = len(rows)
    wholes, outs = refs[:count], refs[count : 2 * count]
    bufs, sems = refs[2 * count : -1], refs[-1]
    here = Place()
    enter(here, nz)
    scatters = []
    for k in range(count):
        at = weight_places(wholes[k], rows[k])
        half = rows[k] // 2

        def part(ref, h, half=half):
            return ref.at[pl.ds(h * half, half)]

        scatters.append(Scatter(here, nz, at, part, sems.at[k], bufs[5 * k : 5 * k + 5]))
    for k in range(count):
        for step in scatters[k].program(outs[k]):
            step()
    for scatter in scatters:
        scatter.finish()


def scatter_all(wholes, nz):
    rows = [item.shape[0] // (nz * 2) for item in wholes]
    scratch = []
    for r in rows:
        for shape in ((4, nz, r, 128), (4, nz, r, 128), (2, nz, r // 2, 128), (2, nz, r, 128), (2, nz, r, 128)):
            scratch.append(pltpu.VMEM(shape, jnp.bfloat16))
    return pl.pallas_call(
        functools.partial(scatter_kernel, nz, rows),
        out_shape=[jax.ShapeDtypeStruct((r, 128), jnp.float32) for r in rows],
        in_specs=[pl.BlockSpec(memory_space=pltpu.VMEM)] * len(rows),
        out_specs=[pl.BlockSpec(memory_space=pltpu.VMEM)] * len(rows),
        scratch_shapes=scratch + [pltpu.SemaphoreType.DMA((len(rows), 2, Scatter.SEMS))],
        compiler_params=pltpu.CompilerParams(collective_id=1, has_side_effects=True, vmem_limit_bytes=60 << 20),
    )(*wholes)


def extended(shard, sides, width):
    for axis, dim in sides:
        devices, length = (lax.axis_size(axis), shard.shape[dim])
        up = [(i, (i + 1) % devices) for i in range(devices - 1)]
        down = [(j, i) for i, j in up]
        last = lax.slice_in_dim(shard, length - width, length, axis=dim)
        initial = lax.slice_in_dim(shard, 0, width, axis=dim)
        before = lax.ppermute(last, axis, up)
        after = lax.ppermute(initial, axis, down)
        shard = jnp.concatenate([before, shard, after], axis=dim)
    return shard


def canvas_index(global_rows, first_row, second_row):
    return (global_rows >= first_row).astype(jnp.int32) + (global_rows >= second_row).astype(
        jnp.int32
    )


def swish(argument):
    return argument * jax.nn.sigmoid(argument)


def swish_slope(argument):
    sigmoid_value = jax.nn.sigmoid(argument)
    return sigmoid_value * (1.0 + argument * (1.0 - sigmoid_value))


def group_sums(member, grouped):
    return jnp.einsum("rk,rwgc->kg", member, grouped, precision=HIGHEST)


def spread_rows(member, lookup):
    return jnp.dot(member, lookup, precision=HIGHEST)


def norm_forward(inputs, member, counts, norm_gain, norm_shift):
    row_count, width, channels = inputs.shape
    grouped = inputs.reshape(row_count, width, GROUPS, channels // GROUPS)
    totals, square = lax.psum(
        (group_sums(member, grouped), group_sums(member, grouped * grouped)), "blk"
    )
    average = totals / counts[:, None]
    inverse = lax.rsqrt(square / counts[:, None] - average * average + EPSILON)
    average_rows = spread_rows(member, average)
    scale_rows = spread_rows(member, inverse)
    normal = (grouped - average_rows[:, None, :, None]) * scale_rows[:, None, :, None]
    normal = normal.reshape(row_count, width, channels)
    return (normal * norm_gain + norm_shift, normal, scale_rows)


def norm_backward(incoming, normal, scale_rows, member, counts, norm_gain):
    row_count, width, channels = incoming.shape
    gain_grad = jnp.sum(incoming * normal, axis=(0, 1))
    shift_grad = jnp.sum(incoming, axis=(0, 1))
    scaled = (incoming * norm_gain).reshape(row_count, width, GROUPS, channels // GROUPS)
    grouped_normal = normal.reshape(row_count, width, GROUPS, channels // GROUPS)
    first_sum, second_sum = lax.psum(
        (group_sums(member, scaled), group_sums(member, scaled * grouped_normal)), "blk"
    )
    first_rows = spread_rows(member, first_sum / counts[:, None])
    second_rows = spread_rows(member, second_sum / counts[:, None])
    result = scale_rows[:, None, :, None] * (
        scaled - first_rows[:, None, :, None] - grouped_normal * second_rows[:, None, :, None]
    )
    return (result.reshape(row_count, width, channels), gain_grad, shift_grad)


def gather_taps(padded, seg_pad, seg_rows, direction):
    row_count = seg_rows.shape[0]
    width = padded.shape[1]
    widened = jnp.pad(padded, ((0, 0), (1, 1), (0, 0)))
    pieces = []
    for step_row in (-1, 0, 1):
        low_row = 1 + direction * step_row
        allowed = (seg_pad[low_row : low_row + row_count] == seg_rows).astype(padded.dtype)[
            :, None, None
        ]
        for step_col in (-1, 0, 1):
            low_col = 1 + direction * step_col
            pieces.append(
                widened[low_row : low_row + row_count, low_col : low_col + width, :] * allowed
            )
    return jnp.stack(pieces, axis=2)


def conv_apply(activation, seg_pad, seg_rows, weight_matrix):
    row_count, width, channels = activation.shape
    padded = extended(activation, (("blk", 0),), 1)
    stacked = gather_taps(padded, seg_pad, seg_rows, 1).reshape(row_count * width, 9 * channels)
    result = jnp.dot(stacked, weight_matrix, preferred_element_type=jnp.float32)
    return (result.reshape(row_count, width, channels), stacked)


def conv_reverse(gradient, stacked, seg_pad, seg_rows, weight_matrix):
    row_count, width, channels = gradient.shape
    flattened = gradient.reshape(row_count * width, channels)
    weight_grad = lax.dot_general(
        stacked, flattened, (((0,), (0,)), ((), ())), preferred_element_type=jnp.float32
    )
    padded = extended(gradient, (("blk", 0),), 1)
    mirrored = gather_taps(padded, seg_pad, seg_rows, -1).reshape(row_count * width, 9, channels)
    kernel = weight_matrix.reshape(9, channels, channels)
    result = lax.dot_general(
        mirrored, kernel, (((1, 2), (0, 2)), ((), ())), preferred_element_type=jnp.float32
    )
    return (result.reshape(row_count, width, channels), weight_grad)


def attention_forward(
    queries, keys_local, values_local, token_seg, first_row, second_row, width, scale
):
    token_count, channels = queries.shape

    def absorb(running, portion, offset):
        key_block, value_block = portion
        maximum, totals, accumulated = running
        key_seg = canvas_index(
            jnp.arange(key_block.shape[0], dtype=jnp.int32) // width, first_row, second_row
        )
        shared = token_seg[:, None] == key_seg[None, :]
        scores = (
            lax.dot_general(
                queries, key_block, (((1,), (1,)), ((), ())), preferred_element_type=jnp.float32
            )
            * scale
        )
        masked = jnp.where(shared, scores, NEGATIVE)
        new_maximum = jnp.maximum(maximum, jnp.max(masked, axis=1))
        weights = jnp.where(shared, jnp.exp(masked - new_maximum[:, None]), 0.0)
        totals = jnp.sum(weights, axis=1)
        accumulated = jnp.dot(
            weights.astype(jnp.bfloat16), value_block, preferred_element_type=jnp.float32
        )
        return (new_maximum, totals, accumulated)

    initial = (
        jnp.full((token_count,), NEGATIVE, jnp.float32),
        jnp.zeros((token_count,), jnp.float32),
        jnp.zeros((token_count, channels), jnp.float32),
    )
    maximum, totals, accumulated = absorb(
        initial,
        (
            lax.all_gather(keys_local, "blk", axis=0, tiled=True),
            lax.all_gather(values_local, "blk", axis=0, tiled=True),
        ),
        jnp.int32(0),
    )
    return (accumulated / totals[:, None], maximum + jnp.log(totals))


def attention_query_grad(
    queries,
    heads_grad,
    log_total,
    correction,
    keys_local,
    values_local,
    token_seg,
    first_row,
    second_row,
    width,
    scale,
):

    def absorb(running, portion, offset):
        key_block, value_block = portion
        key_seg = canvas_index(
            jnp.arange(key_block.shape[0], dtype=jnp.int32) // width, first_row, second_row
        )
        shared = token_seg[:, None] == key_seg[None, :]
        scores = (
            lax.dot_general(
                queries, key_block, (((1,), (1,)), ((), ())), preferred_element_type=jnp.float32
            )
            * scale
        )
        weights = jnp.where(
            shared, jnp.exp(jnp.where(shared, scores, NEGATIVE) - log_total[:, None]), 0.0
        )
        slopes = lax.dot_general(
            heads_grad, value_block, (((1,), (1,)), ((), ())), preferred_element_type=jnp.float32
        )
        score_grad = (weights * (slopes - correction[:, None])).astype(jnp.bfloat16)
        return jnp.dot(score_grad, key_block, preferred_element_type=jnp.float32) * scale

    return absorb(
        jnp.zeros(queries.shape, jnp.float32),
        (
            lax.all_gather(keys_local, "blk", axis=0, tiled=True),
            lax.all_gather(values_local, "blk", axis=0, tiled=True),
        ),
        jnp.int32(0),
    )


def attention_key_grad(
    queries,
    heads_grad,
    log_total,
    correction,
    keys_local,
    values_local,
    token_seg,
    first_row,
    second_row,
    width,
    scale,
):

    def absorb(running, portion, offset):
        query_part, upstream_part, total_part, correct_part = portion
        query_seg = canvas_index(
            jnp.arange(query_part.shape[0], dtype=jnp.int32) // width, first_row, second_row
        )
        query_low = query_part.astype(jnp.bfloat16)
        upstream_low = upstream_part.astype(jnp.bfloat16)
        shared = query_seg[:, None] == token_seg[None, :]
        scores = (
            lax.dot_general(
                query_low, keys_local, (((1,), (1,)), ((), ())), preferred_element_type=jnp.float32
            )
            * scale
        )
        weights = jnp.where(
            shared, jnp.exp(jnp.where(shared, scores, NEGATIVE) - total_part[:, None]), 0.0
        )
        value_acc = lax.dot_general(
            weights.astype(jnp.bfloat16),
            upstream_low,
            (((0,), (0,)), ((), ())),
            preferred_element_type=jnp.float32,
        )
        slopes = lax.dot_general(
            upstream_low, values_local, (((1,), (1,)), ((), ())), preferred_element_type=jnp.float32
        )
        score_grad = (weights * (slopes - correct_part[:, None])).astype(jnp.bfloat16)
        key_acc = (
            lax.dot_general(
                score_grad, query_low, (((0,), (0,)), ((), ())), preferred_element_type=jnp.float32
            )
            * scale
        )
        return (key_acc, value_acc)

    empty = jnp.zeros(keys_local.shape, jnp.float32)
    return absorb(
        (empty, empty),
        (
            lax.all_gather(queries.astype(jnp.float32), "blk", axis=0, tiled=True),
            lax.all_gather(heads_grad.astype(jnp.float32), "blk", axis=0, tiled=True),
            lax.all_gather(log_total, "blk", axis=0, tiled=True),
            lax.all_gather(correction, "blk", axis=0, tiled=True),
        ),
        jnp.int32(0),
    )


def collect(
    conv1_weight,
    conv2_weight,
    query_weight,
    key_weight,
    value_weight,
    output_weight,
    norm1_gain,
    norm1_shift,
    norm2_gain,
    norm2_shift,
    norm3_gain,
    norm3_shift,
):
    row_parts = (
        lax.all_gather(conv1_weight, "blk", axis=0, tiled=True),
        lax.all_gather(conv2_weight, "blk", axis=0, tiled=True),
        lax.all_gather(query_weight, "blk", axis=0, tiled=True),
        lax.all_gather(key_weight, "blk", axis=0, tiled=True),
        lax.all_gather(value_weight, "blk", axis=0, tiled=True),
        lax.all_gather(output_weight, "blk", axis=0, tiled=True),
        lax.all_gather(norm1_gain, "blk", axis=0, tiled=True),
        lax.all_gather(norm1_shift, "blk", axis=0, tiled=True),
        lax.all_gather(norm2_gain, "blk", axis=0, tiled=True),
        lax.all_gather(norm2_shift, "blk", axis=0, tiled=True),
        lax.all_gather(norm3_gain, "blk", axis=0, tiled=True),
        lax.all_gather(norm3_shift, "blk", axis=0, tiled=True),
    )
    full_parts = (
        lax.all_gather(row_parts[0], "dp", axis=1, tiled=True),
        lax.all_gather(row_parts[1], "dp", axis=1, tiled=True),
        lax.all_gather(row_parts[2], "dp", axis=1, tiled=True),
        lax.all_gather(row_parts[3], "dp", axis=1, tiled=True),
        lax.all_gather(row_parts[4], "dp", axis=1, tiled=True),
        lax.all_gather(row_parts[5], "dp", axis=1, tiled=True),
    )
    return (tuple(full_parts), tuple(row_parts[6:]))


def reduce_all(gradients):
    row_sums = (
        lax.psum_scatter(gradients[0], "blk", scatter_dimension=0, tiled=True),
        lax.psum_scatter(gradients[1], "blk", scatter_dimension=0, tiled=True),
        lax.psum_scatter(gradients[2], "blk", scatter_dimension=0, tiled=True),
        lax.psum_scatter(gradients[3], "blk", scatter_dimension=0, tiled=True),
        lax.psum_scatter(gradients[4], "blk", scatter_dimension=0, tiled=True),
        lax.psum_scatter(gradients[5], "blk", scatter_dimension=0, tiled=True),
        lax.psum_scatter(gradients[6], "blk", scatter_dimension=0, tiled=True),
        lax.psum_scatter(gradients[7], "blk", scatter_dimension=0, tiled=True),
        lax.psum_scatter(gradients[8], "blk", scatter_dimension=0, tiled=True),
        lax.psum_scatter(gradients[9], "blk", scatter_dimension=0, tiled=True),
        lax.psum_scatter(gradients[10], "blk", scatter_dimension=0, tiled=True),
        lax.psum_scatter(gradients[11], "blk", scatter_dimension=0, tiled=True),
    )
    matrix_sums = (
        lax.psum_scatter(row_sums[0], "dp", scatter_dimension=1, tiled=True),
        lax.psum_scatter(row_sums[1], "dp", scatter_dimension=1, tiled=True),
        lax.psum_scatter(row_sums[2], "dp", scatter_dimension=1, tiled=True),
        lax.psum_scatter(row_sums[3], "dp", scatter_dimension=1, tiled=True),
        lax.psum_scatter(row_sums[4], "dp", scatter_dimension=1, tiled=True),
        lax.psum_scatter(row_sums[5], "dp", scatter_dimension=1, tiled=True),
    )
    norm_sums = lax.psum(
        (row_sums[6], row_sums[7], row_sums[8], row_sums[9], row_sums[10], row_sums[11]), "dp"
    )
    return tuple(matrix_sums) + tuple(norm_sums)


def one_batch(inputs_low, bound_pair, upstream_low, matrices, norm_params, position, blocks):
    row_count, width, channels = inputs_low.shape
    token_count = row_count * width
    total_rows = row_count * blocks
    scale = channels ** (-0.5)
    first_row = bound_pair[0]
    second_row = bound_pair[1]
    local_rows = position * row_count + jnp.arange(row_count, dtype=jnp.int32)
    padded_rows = position * row_count - 1 + jnp.arange(row_count + 2, dtype=jnp.int32)
    seg_rows = canvas_index(local_rows, first_row, second_row)
    seg_pad = canvas_index(padded_rows, first_row, second_row)
    member = (seg_rows[:, None] == jnp.arange(CANVASES, dtype=jnp.int32)[None, :]).astype(
        jnp.float32
    )
    counts = jnp.stack([first_row, second_row - first_row, total_rows - second_row]).astype(
        jnp.float32
    ) * float(width * (channels // GROUPS))
    gains = [item.astype(jnp.float32) for item in norm_params]
    inputs = inputs_low.astype(jnp.float32)
    norm_one, normal_one, scale_one = norm_forward(inputs, member, counts, gains[0], gains[1])
    act_one = swish(norm_one).astype(jnp.bfloat16)
    hidden_one, stacked_one = conv_apply(act_one, seg_pad, seg_rows, matrices[0])
    norm_two, normal_two, scale_two = norm_forward(hidden_one, member, counts, gains[2], gains[3])
    act_two = swish(norm_two).astype(jnp.bfloat16)
    hidden_two, stacked_two = conv_apply(act_two, seg_pad, seg_rows, matrices[1])
    residual = inputs + hidden_two
    norm_three, normal_three, scale_three = norm_forward(
        residual, member, counts, gains[4], gains[5]
    )
    normed = norm_three.astype(jnp.bfloat16).reshape(token_count, channels)
    queries = jnp.dot(normed, matrices[2], preferred_element_type=jnp.float32).astype(jnp.bfloat16)
    keys_local = jnp.dot(normed, matrices[3], preferred_element_type=jnp.float32).astype(
        jnp.bfloat16
    )
    values_local = jnp.dot(normed, matrices[4], preferred_element_type=jnp.float32).astype(
        jnp.bfloat16
    )
    token_seg = jnp.repeat(seg_rows, width)
    attended, log_total = attention_forward(
        queries, keys_local, values_local, token_seg, first_row, second_row, width, scale
    )
    heads = attended.astype(jnp.bfloat16)
    activation = residual + jnp.dot(heads, matrices[5], preferred_element_type=jnp.float32).reshape(
        row_count, width, channels
    )
    upstream = upstream_low.reshape(token_count, channels)
    output_weight_grad = lax.dot_general(
        heads, upstream, (((0,), (0,)), ((), ())), preferred_element_type=jnp.float32
    )
    heads_grad = lax.dot_general(
        upstream, matrices[5], (((1,), (1,)), ((), ())), preferred_element_type=jnp.float32
    ).astype(jnp.bfloat16)
    correction = jnp.sum(heads_grad.astype(jnp.float32) * attended, axis=1)
    query_sum = attention_query_grad(
        queries,
        heads_grad,
        log_total,
        correction,
        keys_local,
        values_local,
        token_seg,
        first_row,
        second_row,
        width,
        scale,
    )
    key_sum, value_sum = attention_key_grad(
        queries,
        heads_grad,
        log_total,
        correction,
        keys_local,
        values_local,
        token_seg,
        first_row,
        second_row,
        width,
        scale,
    )
    query_low = query_sum.astype(jnp.bfloat16)
    key_low = key_sum.astype(jnp.bfloat16)
    value_low = value_sum.astype(jnp.bfloat16)
    contract_rows = (((0,), (0,)), ((), ()))
    contract_cols = (((1,), (1,)), ((), ()))
    query_weight_grad = lax.dot_general(
        normed, query_low, contract_rows, preferred_element_type=jnp.float32
    )
    key_weight_grad = lax.dot_general(
        normed, key_low, contract_rows, preferred_element_type=jnp.float32
    )
    value_weight_grad = lax.dot_general(
        normed, value_low, contract_rows, preferred_element_type=jnp.float32
    )
    normed_grad = (
        lax.dot_general(query_low, matrices[2], contract_cols, preferred_element_type=jnp.float32)
        + lax.dot_general(key_low, matrices[3], contract_cols, preferred_element_type=jnp.float32)
        + lax.dot_general(value_low, matrices[4], contract_cols, preferred_element_type=jnp.float32)
    )
    back_three, gain_three_grad, shift_three_grad = norm_backward(
        normed_grad.reshape(row_count, width, channels),
        normal_three,
        scale_three,
        member,
        counts,
        gains[4],
    )
    residual_grad = upstream_low.astype(jnp.float32) + back_three
    act_two_grad, conv_two_grad = conv_reverse(
        residual_grad.astype(jnp.bfloat16), stacked_two, seg_pad, seg_rows, matrices[1]
    )
    back_two, gain_two_grad, shift_two_grad = norm_backward(
        act_two_grad * swish_slope(norm_two), normal_two, scale_two, member, counts, gains[2]
    )
    act_one_grad, conv_one_grad = conv_reverse(
        back_two.astype(jnp.bfloat16), stacked_one, seg_pad, seg_rows, matrices[0]
    )
    back_one, gain_one_grad, shift_one_grad = norm_backward(
        act_one_grad * swish_slope(norm_one), normal_one, scale_one, member, counts, gains[0]
    )
    input_grad = residual_grad + back_one
    local_grads = (
        conv_one_grad,
        conv_two_grad,
        query_weight_grad,
        key_weight_grad,
        value_weight_grad,
        output_weight_grad,
        gain_one_grad,
        shift_one_grad,
        gain_two_grad,
        shift_two_grad,
        gain_three_grad,
        shift_three_grad,
    )
    return (activation, input_grad, local_grads)


def by_block(whole, nz):
    split = whole.reshape(nz * 2, 4, -1, 512)
    return [split[:, k].reshape(-1, 512) for k in range(4)]


def fast_collect(conv1_weight, conv2_weight, query_weight, key_weight, value_weight, output_weight, *norms):
    nz = lax.axis_size("blk") // 2
    stacked = jnp.concatenate([query_weight, key_weight, value_weight, output_weight])
    w1, w2, wa = gather_all((conv1_weight, conv2_weight, stacked), nz)
    rows = tuple(lax.all_gather(item, "blk", axis=0, tiled=True) for item in norms)
    return (w1, w2, *by_block(wa, nz)), rows


def fast_reduce(gradients):
    nz = lax.axis_size("blk") // 2
    low_grads = [item.astype(jnp.bfloat16) for item in gradients[:6]]
    attn = jnp.stack([item.reshape(nz * 2, -1, 512) for item in low_grads[2:]], axis=1).reshape(-1, 512)
    g2, ga, g1 = scatter_all((low_grads[1], attn, low_grads[0]), nz)
    ga = ga.reshape(4, -1, 128)
    norms = tuple(lax.psum_scatter(item, "blk", scatter_dimension=0, tiled=True) for item in gradients[6:])
    return (g1, g2, ga[0], ga[1], ga[2], ga[3]) + tuple(lax.psum(norms, "dp"))


def shards(
    features,
    bounds,
    out_grad,
    norm1_gain,
    norm1_shift,
    conv1_weight,
    norm2_gain,
    norm2_shift,
    conv2_weight,
    norm3_gain,
    norm3_shift,
    query_weight,
    key_weight,
    value_weight,
    output_weight,
):
    blocks = lax.axis_size("blk")
    position = lax.axis_index("blk")
    micro_count = features.shape[1]
    local_sums = None
    outputs = []
    input_grads = []
    near = lax.axis_size("dp") == 4 and blocks == 8
    matrices, norm_params = (fast_collect if near else collect)(
        conv1_weight,
        conv2_weight,
        query_weight,
        key_weight,
        value_weight,
        output_weight,
        norm1_gain,
        norm1_shift,
        norm2_gain,
        norm2_shift,
        norm3_gain,
        norm3_shift,
    )
    for micro_index in range(micro_count):
        activation, input_grad, local_grads = one_batch(
            features[0, micro_index],
            bounds[0, micro_index],
            out_grad[0, micro_index],
            matrices,
            norm_params,
            position,
            blocks,
        )
        outputs.append(activation)
        input_grads.append(input_grad)
        local_sums = (
            local_grads
            if local_sums is None
            else tuple((acc + new for acc, new in zip(local_sums, local_grads)))
        )
    shard_sums = (fast_reduce if near else reduce_all)(local_sums)
    activations = jnp.stack(outputs)[None]
    input_grad_all = jnp.stack(input_grads)[None]
    return (
        activations,
        input_grad_all,
        shard_sums[6],
        shard_sums[7],
        shard_sums[0],
        shard_sums[8],
        shard_sums[9],
        shard_sums[1],
        shard_sums[10],
        shard_sums[11],
        shard_sums[2],
        shard_sums[3],
        shard_sums[4],
        shard_sums[5],
    )


def solution(mesh):
    in_specs = (
        P("dp", None, "blk", None, None),
        P("dp", None, None),
        P("dp", None, "blk", None, None),
        P("blk"),
        P("blk"),
        P("blk", "dp"),
        P("blk"),
        P("blk"),
        P("blk", "dp"),
        P("blk"),
        P("blk"),
        P("blk", "dp"),
        P("blk", "dp"),
        P("blk", "dp"),
        P("blk", "dp"),
    )
    out_specs = (
        P("dp", None, "blk", None, None),
        P("dp", None, "blk", None, None),
        P("blk"),
        P("blk"),
        P("blk", "dp"),
        P("blk"),
        P("blk"),
        P("blk", "dp"),
        P("blk"),
        P("blk"),
        P("blk", "dp"),
        P("blk", "dp"),
        P("blk", "dp"),
        P("blk", "dp"),
    )
    return jax.shard_map(shards, mesh=mesh, in_specs=in_specs, out_specs=out_specs, check_vma=False)
```

```python
import functools

import jax
import jax.numpy as jnp
from jax import lax
from jax.experimental import pallas as pl
from jax.experimental.pallas import tpu as pltpu
from jax.sharding import PartitionSpec as P

GROUPS = 32
CANVASES = 3


EPSILON = 1e-06
HIGHEST = lax.Precision.HIGHEST
NEGATIVE = -1e30
MESH = pl.DeviceIdType.MESH


class Place:
    def __init__(self):
        self.d = lax.axis_index("dp")
        self.b = lax.axis_index("blk")
        self.y, self.c = self.d // 2, self.d % 2
        self.z, self.x = self.b // 2, self.b % 2
        self.up = {"dp": self.d, "blk": self.b + 2}
        self.down = {"dp": self.d, "blk": self.b - 2}
        self.xn = {"dp": self.d, "blk": self.z * 2 + 1 - self.x}
        self.yn = {"dp": (1 - self.y) * 2 + self.c, "blk": self.b}
        self.cn = {"dp": self.y * 2 + 1 - self.c, "blk": self.b}


def enter(here, nz):
    barrier = pltpu.get_barrier_semaphore()
    for device in (here.xn, here.yn, here.cn):
        pl.semaphore_signal(barrier, inc=1, device_id=device, device_id_type=MESH)

    @pl.when(here.z < nz - 1)
    def _():
        pl.semaphore_signal(barrier, inc=1, device_id=here.up, device_id_type=MESH)

    @pl.when(here.z > 0)
    def _():
        pl.semaphore_signal(barrier, inc=1, device_id=here.down, device_id_type=MESH)

    lines = (here.z < nz - 1).astype(jnp.int32) + (here.z > 0).astype(jnp.int32)
    pl.semaphore_wait(barrier, 3 + lines)


def remote(src, dst, send, recv, device):
    return pltpu.make_async_remote_copy(
        src_ref=src, dst_ref=dst, send_sem=send, recv_sem=recv, device_id=device, device_id_type=MESH
    )


def steps_of(z, nz):
    visits = [(z, None)]
    for k in range(1, nz):
        visits.append((z - k, z >= k))
        visits.append((z + k, z + k < nz))
    return visits


def guarded(valid, body):
    if valid is None:
        body()
    else:
        pl.when(valid)(body)


class Gather:
    SEMS = 40

    def __init__(self, here, nz, at, sems):
        self.here, self.nz, self.at, self.sems = here, nz, at, sems
        self.visits = steps_of(here.z, nz)

    def sem(self, kind, z, way):
        base = {"z": 0, "x": 4, "y": 8, "da": 12, "db": 16, "co": 20, "cx": 24, "cy": 28, "cd": 32, "zd": 36}[kind]
        return self.sems.at[way, base + z]

    def cp(self, kind, z, src, device, skind=None):
        return remote(src, src, self.sem(skind or kind, z, 0), self.sem(kind, z, 1), device)

    def own(self, z):
        return self.at(z, self.here.x, self.here.d, None)

    def colx(self, z, half=None):
        return self.at(z, 1 - self.here.x, self.here.d, half)

    def coly(self, z, half=None):
        return self.at(z, self.here.x, (1 - self.here.y) * 2 + self.here.c, half)

    def cold(self, z, half=None):
        return self.at(z, 1 - self.here.x, (1 - self.here.y) * 2 + self.here.c, half)

    def have(self, j):
        z, valid = self.visits[j]
        here = self.here

        def body():
            src = self.own(z)
            if j > 0:
                self.cp("z", z, src, here.up).wait_recv()
            if j == 0 or j % 2 == 1:

                @pl.when(here.z < self.nz - 1)
                def _():
                    self.cp("z", z, src, here.up).start()

            if j == 0 or j % 2 == 0:

                @pl.when(here.z > 0)
                def _():
                    self.cp("z", z, src, here.down, "zd").start()

            self.cp("x", z, src, here.xn).start()
            self.cp("y", z, src, here.yn).start()
            self.cp("co", z, src, here.cn).start()

        guarded(valid, body)

    def cross(self, j):
        z, valid = self.visits[j]
        here = self.here

        def body():
            self.cp("x", z, self.colx(z), here.xn).wait_recv()
            self.cp("da", z, self.colx(z, 0), here.yn).start()
            self.cp("cx", z, self.colx(z), here.cn).start()
            self.cp("y", z, self.coly(z), here.yn).wait_recv()
            self.cp("db", z, self.coly(z, 1), here.xn).start()
            self.cp("cy", z, self.coly(z), here.cn).start()

        guarded(valid, body)

    def diagonal(self, j):
        z, valid = self.visits[j]
        here = self.here

        def body():
            self.cp("da", z, self.cold(z, 0), here.yn).wait_recv()
            self.cp("db", z, self.cold(z, 1), here.xn).wait_recv()
            self.cp("cd", z, self.cold(z), here.cn).start()

        guarded(valid, body)

    def arrive(self):
        here = self.here
        near, far = here.y * 2 + 1 - here.c, (1 - here.y) * 2 + 1 - here.c
        for z in range(self.nz):
            for kind, x, d in (("co", here.x, near), ("cx", 1 - here.x, near), ("cy", here.x, far), ("cd", 1 - here.x, far)):
                self.cp(kind, z, self.at(z, x, d, None), here.cn).wait_recv()

    def finish(self):
        here = self.here
        for j, (z, valid) in enumerate(self.visits):

            def body():
                src = self.own(z)
                if j == 0 or j % 2 == 1:

                    @pl.when(here.z < self.nz - 1)
                    def _():
                        self.cp("z", z, src, here.up).wait_send()

                if j == 0 or j % 2 == 0:

                    @pl.when(here.z > 0)
                    def _():
                        self.cp("z", z, src, here.down, "zd").wait_send()

                self.cp("x", z, src, here.xn).wait_send()
                self.cp("y", z, src, here.yn).wait_send()
                self.cp("da", z, self.colx(z, 0), here.yn).wait_send()
                self.cp("db", z, self.coly(z, 1), here.xn).wait_send()
                for kind in ("co", "cx", "cy", "cd"):
                    self.cp(kind, z, src, here.cn).wait_send()

            guarded(valid, body)

    def program(self):
        todo = [lambda: self.have(0)]
        pairs = [(0,)] + [(2 * k - 1, 2 * k) for k in range(1, self.nz)]
        for k in range(1, self.nz + 2):
            if k < self.nz:
                todo += [lambda j=j: self.have(j) for j in pairs[k]]
            if k - 1 < self.nz:
                todo += [lambda j=j: self.cross(j) for j in pairs[k - 1]]
            if 0 <= k - 2 < self.nz:
                todo += [lambda j=j: self.diagonal(j) for j in pairs[k - 2]]
        return todo


class Scatter:
    SEMS = 44

    def __init__(self, here, nz, at, part, sems, bufs):
        self.here, self.nz, self.at, self.part, self.sems = here, nz, at, part, sems
        self.core, self.acc, self.half, self.side, self.line = bufs
        visits = steps_of(here.z, nz)
        self.visits = visits[::-1]

    def sem(self, kind, z, way):
        base = {"c0": 0, "c1": 4, "c2": 8, "c3": 12, "da": 16, "db": 20, "x": 24, "y": 28, "l": 32, "ld": 36}[kind]
        return self.sems.at[way, base + z]

    def cp(self, kind, z, src, dst, device, skind=None):
        return remote(src, dst, self.sem(skind or kind, z, 0), self.sem(kind, z, 1), device)

    def places(self, z, c):
        here = self.here
        y, x = here.y, here.x
        return [(z, x, y * 2 + c), (z, 1 - x, y * 2 + c), (z, x, (1 - y) * 2 + c), (z, 1 - x, (1 - y) * 2 + c)]

    def core_cp(self, z, k):
        return self.cp("c%d" % k, z, self.at(*self.places(z, 1 - self.here.c)[k]), self.core.at[k, z], self.here.cn)

    def begin(self, j):
        z, valid = self.visits[j]

        def body():
            for k in (3, 1, 2, 0):
                self.core_cp(z, k).start()

        guarded(valid, body)

    def halves(self, z):
        return (
            self.cp("da", z, self.part(self.acc.at[3, z], 0), self.half.at[0, z], self.here.xn),
            self.cp("db", z, self.part(self.acc.at[3, z], 1), self.half.at[1, z], self.here.yn),
        )

    def sides(self, z):
        return (
            self.cp("x", z, self.acc.at[1, z], self.side.at[0, z], self.here.xn),
            self.cp("y", z, self.acc.at[2, z], self.side.at[1, z], self.here.yn),
        )

    def pair(self, z, k):
        self.core_cp(z, k).wait_recv()
        mine = self.at(*self.places(z, self.here.c)[k])[...].astype(jnp.float32)
        return mine + self.core[k, z].astype(jnp.float32)

    def corner(self, j):
        z, valid = self.visits[j]

        def body():
            self.acc[3, z] = self.pair(z, 3).astype(jnp.bfloat16)
            for copy in self.halves(z):
                copy.start()

        guarded(valid, body)

    def edges(self, j):
        z, valid = self.visits[j]

        def body():
            from_x, from_y = self.halves(z)
            for k, copy, h in ((1, from_y, 1), (2, from_x, 0)):
                total = self.pair(z, k)
                copy.wait_recv()
                self.acc[k, z] = total.astype(jnp.bfloat16)
                place = self.part(self.acc.at[k, z], h)
                place[...] = (place[...].astype(jnp.float32) + self.half[h, z].astype(jnp.float32)).astype(jnp.bfloat16)
                self.sides(z)[k - 1].start()

        guarded(valid, body)

    def line_cp(self, z, upward):
        here = self.here
        if upward:
            return self.cp("l", z, self.acc.at[0, z], self.line.at[0, z], here.up)
        return self.cp("ld", z, self.acc.at[0, z], self.line.at[1, z], here.down)

    def column(self, j, out=None):
        z, valid = self.visits[j]
        here, nz = self.here, self.nz
        last = j == len(self.visits) - 1

        def body():
            total = self.pair(z, 0)
            for copy, k in zip(self.sides(z), (0, 1)):
                copy.wait_recv()
                total = total + self.side[k, z].astype(jnp.float32)
            if last:
                out[...] = total

                @pl.when(here.z > 0)
                def _():
                    self.line_cp(z, True).wait_recv()
                    out[...] += self.line[0, z].astype(jnp.float32)

                @pl.when(here.z < nz - 1)
                def _():
                    self.line_cp(z, False).wait_recv()
                    out[...] += self.line[1, z].astype(jnp.float32)
            else:
                upward = j % 2 == 0
                self.acc[0, z] = total.astype(jnp.bfloat16)

                @pl.when((here.z > 0) if upward else (here.z < nz - 1))
                def _():
                    self.line_cp(z, upward).wait_recv()
                    k = 0 if upward else 1
                    self.acc[0, z] = (self.acc[0, z].astype(jnp.float32) + self.line[k, z].astype(jnp.float32)).astype(jnp.bfloat16)

                self.line_cp(z, upward).start()

        guarded(valid, body)

    def finish(self):
        for j, (z, valid) in enumerate(self.visits):
            last = j == len(self.visits) - 1

            def body():
                for k in range(4):
                    self.core_cp(z, k).wait_send()
                for copy in self.halves(z) + self.sides(z):
                    copy.wait_send()
                if not last:
                    self.line_cp(z, j % 2 == 0).wait_send()

            guarded(valid, body)

    def program(self, out):
        pairs = [[2 * k, 2 * k + 1] for k in range(self.nz - 1)] + [[2 * (self.nz - 1)]]
        todo = []
        for k in range(self.nz + 3):
            if k < self.nz:
                todo += [lambda j=j: self.begin(j) for j in pairs[k]]
            if 0 <= k - 1 < self.nz:
                todo += [lambda j=j: self.corner(j) for j in pairs[k - 1]]
            if 0 <= k - 2 < self.nz:
                todo += [lambda j=j: self.edges(j) for j in pairs[k - 2]]
            if 0 <= k - 3 < self.nz:
                todo += [lambda j=j: self.column(j, out) for j in pairs[k - 3]]
        return todo

def weight_places(ref, rows):
    def at(z, x, d, half=None):
        base, count = (z * 2 + x) * rows, rows
        if half is not None:
            base, count = base + half * (rows // 2), rows // 2
        return ref.at[pl.ds(pl.multiple_of(base, 16), count), pl.ds(pl.multiple_of(d * 128, 128), 128)]

    return at


BF = jnp.bfloat16
F32 = jnp.float32
ROW = 8
PARAMS = 16


def both(a, b):
    return jnp.logical_and(a, b)


def cols(a, b):
    return lax.dot_general(a, b, (((1,), (1,)), ((), ())), preferred_element_type=F32)


def mm(a, b):
    return jnp.dot(a, b, preferred_element_type=F32)


class Unit(Place):
    def __init__(self):
        super().__init__()
        self.q = self.x * 2 + self.c
        self.mu = self.z % 2
        self.alone = both(both(self.c == self.z % 2, self.x == self.z // 2), self.c == self.z // 2)

    def peer(self, q):
        return {"dp": self.y * 2 + q % 2, "blk": self.z * 2 + q // 2}

    def worker(self, m):
        return {"dp": self.y * 2 + self.z % 2, "blk": (2 * self.c + m) * 2 + self.z // 2}

    def keeper(self, h):
        return {"dp": self.y * 2 + self.z // 2, "blk": self.q * 2 + h}

    def line(self, k):
        return {"dp": self.d, "blk": ((self.z + k) % 4) * 2 + self.x}

    def enter(self, shares, lines):
        barrier = pltpu.get_barrier_semaphore()

        def greet(device):
            pl.semaphore_signal(barrier, inc=1, device_id=device, device_id_type=MESH)

        for k in (1, 2, 3):
            greet(self.peer((self.q + k) % 4))
        count = 3
        if lines:
            greet(self.yn)
            for k in (1, 2, 3):
                greet(self.line(k))
            count += 4
        if shares:
            for m in (0, 1):
                pl.when(jnp.logical_not(both(self.alone, self.c == m)))(lambda m=m: greet(self.worker(m)))
            for h in (0, 1):
                pl.when(jnp.logical_not(both(self.alone, self.x == h)))(lambda h=h: greet(self.keeper(h)))
            count = count + 4 - 2 * self.alone.astype(jnp.int32)
        pl.semaphore_wait(barrier, count)


class Share:
    def __init__(self, u, sems, local):
        self.u, self.sems, self.local = u, sems, local

    def send(self, src, dst):
        u = self.u
        for m in (0, 1):
            mine = both(u.alone, u.c == m)
            place = dst.at[pl.ds(4 * u.x, 4)]
            pl.when(mine)(lambda: pltpu.make_async_copy(src.at[m], place, self.local).start())
            pl.when(jnp.logical_not(mine))(
                lambda: remote(src.at[m], place, self.sems.at[0, m], self.sems.at[1, u.x], u.worker(m)).start()
            )

    def wait(self, src, dst):
        u = self.u
        for h in (0, 1):
            mine = both(u.alone, u.x == h)
            place = dst.at[pl.ds(4 * h, 4)]
            pl.when(mine)(lambda: pltpu.make_async_copy(src.at[0], place, self.local).wait())
            pl.when(jnp.logical_not(mine))(
                lambda: remote(place, place, self.sems.at[0, 0], self.sems.at[1, h], u.keeper(h)).wait_recv()
            )

    def sent(self, src, dst):
        u = self.u
        for m in (0, 1):
            place = dst.at[pl.ds(4 * u.x, 4)]
            pl.when(jnp.logical_not(both(u.alone, u.c == m)))(
                lambda: remote(src.at[m], place, self.sems.at[0, m], self.sems.at[1, u.x], u.worker(m)).wait_send()
            )

    def back(self, src, dst):
        u = self.u
        for h in (0, 1):
            mine = both(u.alone, u.x == h)
            piece = src.at[pl.ds(4 * h, 4)]
            pl.when(mine)(lambda: pltpu.make_async_copy(piece, dst.at[u.mu], self.local).start())
            pl.when(jnp.logical_not(mine))(
                lambda: remote(piece, dst.at[u.mu], self.sems.at[0, h], self.sems.at[1, u.mu], u.keeper(h)).start()
            )

    def back_wait(self, src, dst):
        u = self.u
        for m in (0, 1):
            mine = both(u.alone, u.c == m)
            pl.when(mine)(lambda: pltpu.make_async_copy(src.at[pl.ds(0, 4)], dst.at[m], self.local).wait())
            pl.when(jnp.logical_not(mine))(
                lambda: remote(dst.at[m], dst.at[m], self.sems.at[0, 0], self.sems.at[1, m], u.worker(m)).wait_recv()
            )
        for h in (0, 1):
            pl.when(jnp.logical_not(both(u.alone, u.x == h)))(
                lambda: remote(
                    src.at[pl.ds(4 * h, 4)], dst.at[u.mu], self.sems.at[0, h], self.sems.at[1, u.mu], u.keeper(h)
                ).wait_send()
            )


class Swap:
    def __init__(self, u, buf, sems):
        self.u, self.buf, self.sems = u, buf, sems

    def cps(self):
        u = self.u
        out = []
        for k in (1, 2, 3):
            out.append((self.buf.at[u.q], self.sems.at[0, k], self.sems.at[1, u.q], u.peer((u.q + k) % 4)))
        return out

    def send(self):
        for ref, s, r, dev in self.cps():
            remote(ref, ref, s, r, dev).start()

    def wait(self):
        u = self.u
        for k in (1, 2, 3):
            p = (u.q + k) % 4
            remote(self.buf.at[p], self.buf.at[p], self.sems.at[0, k], self.sems.at[1, p], u.peer(p)).wait_recv()

    def sent(self):
        for ref, s, r, dev in self.cps():
            remote(ref, ref, s, r, dev).wait_send()

    def total(self):
        return self.buf[0] + self.buf[1] + self.buf[2] + self.buf[3]


class Spread:
    def __init__(self, u, buf, sems, parts):
        self.u, self.buf, self.sems, self.parts = u, buf, sems, parts

    def cp(self, kind, p, part):
        u = self.u
        ref = self.buf.at[p, part]
        device = u.xn if kind == 1 else u.cn
        return remote(ref, ref, self.sems.at[0, kind, part], self.sems.at[1, kind, part], device)

    def send(self, part):
        self.cp(1, self.u.q, part).start()
        self.cp(0, self.u.q, part).start()

    def across(self):
        return (1 - self.u.x) * 2 + self.u.c

    def relay(self, part):
        copy = self.cp(1, self.across(), part)
        copy.wait_recv()
        self.cp(2, self.across(), part).start()

    def wait(self, part):
        u = self.u
        self.cp(0, u.x * 2 + 1 - u.c, part).wait_recv()
        self.cp(2, (1 - u.x) * 2 + 1 - u.c, part).wait_recv()

    def sent(self, part):
        self.cp(1, self.u.q, part).wait_send()
        self.cp(0, self.u.q, part).wait_send()
        self.cp(2, self.across(), part).wait_send()


class Halo:
    def __init__(self, u, buf, sems):
        self.u, self.buf, self.sems = u, buf, sems

    def cp(self, downward):
        u, buf = self.u, self.buf
        if downward:
            return remote(buf.at[1], buf.at[ROW + 1], self.sems.at[0, 0], self.sems.at[1, 0], u.peer(jnp.maximum(u.q - 1, 0)))
        return remote(buf.at[ROW], buf.at[0], self.sems.at[0, 1], self.sems.at[1, 1], u.peer(jnp.minimum(u.q + 1, 3)))

    def send(self):
        u, buf = self.u, self.buf
        pl.when(u.q > 0)(lambda: self.cp(True).start())
        pl.when(u.q < 3)(lambda: self.cp(False).start())

        @pl.when(u.q == 0)
        def _():
            buf[0] = jnp.zeros(buf.shape[1:], buf.dtype)

        @pl.when(u.q == 3)
        def _():
            buf[ROW + 1] = jnp.zeros(buf.shape[1:], buf.dtype)

    def wait(self):
        u = self.u
        pl.when(u.q > 0)(lambda: self.cp(False).wait_recv())
        pl.when(u.q < 3)(lambda: self.cp(True).wait_recv())

    def sent(self):
        u = self.u
        pl.when(u.q > 0)(lambda: self.cp(True).wait_send())
        pl.when(u.q < 3)(lambda: self.cp(False).wait_send())


def canvas_of(rows, limits):
    return (rows >= limits[0:1]).astype(F32) + (rows >= limits[1:2]).astype(F32)


def row_numbers(u, offset, shape):
    return (ROW * u.q + offset + lax.broadcasted_iota(jnp.int32, shape, 0)).astype(F32)


def counts_of(limits, total_rows):
    each = 64.0 * 16.0
    return (limits[0:1] * each, (limits[1:2] - limits[0:1]) * each, (total_rows - limits[1:2]) * each)


def group_total(sums):
    width = sums.shape[1]
    lane = lax.broadcasted_iota(jnp.int32, sums.shape, 1)
    for step in (1, 2, 4, 8):
        after = pltpu.roll(sums, width - step, 1)
        before = pltpu.roll(sums, step, 1)
        sums = sums + jnp.where((lane // step) % 2 == 0, after, before)
    return sums


def canvas_sums(first, second, seg):
    out = []
    for rows in (first, second):
        for k in range(CANVASES):
            out.append(jnp.sum(jnp.where(seg == float(k), rows, 0.0), axis=0, keepdims=True))
    out.append(jnp.zeros((2, first.shape[1]), F32))
    return jnp.concatenate(out, axis=0)


def by_row(values, seg):
    return jnp.where(seg == 0.0, values[0], jnp.where(seg == 1.0, values[1], values[2]))


def moments(total, counts, seg):
    grouped = group_total(total)
    averages, inverses = [], []
    for k in range(CANVASES):
        average = grouped[k : k + 1] / counts[k]
        averages.append(average)
        inverses.append(lax.rsqrt(grouped[3 + k : 4 + k] / counts[k] - average * average + EPSILON))
    return by_row(averages, seg), by_row(inverses, seg)


def sigmoid(argument):
    return 0.5 * jnp.tanh(0.5 * argument) + 0.5


def each_row(body):
    lax.fori_loop(0, ROW, lambda r, carry: (body(r), carry)[1], 0)


def row_of(ref, r):
    return ref[pl.ds(r, 1), :]


def tap_masks(u, limits, masks):
    shape = (ROW, limits.shape[1])
    rows = row_numbers(u, 0, shape)
    seg = canvas_of(rows, limits)
    masks[0] = both(canvas_of(rows - 1.0, limits) == seg, rows >= 1.0).astype(F32)
    masks[1] = both(canvas_of(rows + 1.0, limits) == seg, rows < 4.0 * ROW - 1.0).astype(F32)
    return seg


def shifted(line):
    position = lax.broadcasted_iota(jnp.int32, line.shape, 0)
    width = line.shape[0]
    before = jnp.where(position == 0, 0.0, pltpu.roll(line, 1, 0))
    after = jnp.where(position == width - 1, 0.0, pltpu.roll(line, width - 1, 0))
    return before, line, after


def taps_inner(buf, masks, taps):
    def body(s):
        lines = shifted(buf[s + 1].astype(F32))
        for k in range(3):
            taps[3 + k, s] = lines[k].astype(BF)

        @pl.when(s < ROW - 1)
        def _():
            mask = masks[0, pl.ds(s + 1, 1), :]
            for k in range(3):
                taps[k, s + 1] = (lines[k] * mask).astype(BF)

        @pl.when(s > 0)
        def _():
            mask = masks[1, pl.ds(s - 1, 1), :]
            for k in range(3):
                taps[6 + k, s - 1] = (lines[k] * mask).astype(BF)

    each_row(body)


def taps_outer(buf, masks, taps):
    for k, line in enumerate(shifted(buf[0].astype(F32))):
        taps[k, 0] = (line * masks[0, 0:1, :]).astype(BF)
    for k, line in enumerate(shifted(buf[ROW + 1].astype(F32))):
        taps[6 + k, ROW - 1] = (line * masks[1, ROW - 1 : ROW, :]).astype(BF)


def conv_tile(taps, weight, m, flip):
    total = None
    for tap in range(9):
        left = taps[8 - tap if flip else tap, pl.ds(pl.multiple_of(m * 4, 4), 4)].reshape(256, -1)
        right = weight[tap * 512 : (tap + 1) * 512, :]
        term = cols(left, right) if flip else mm(left, right)
        total = term if total is None else total + term
    return total.reshape(4, 64, -1)


def conv_all(taps, weight, out, flip, between=None):
    for m in range(2):
        out[4 * m : 4 * m + 4] = conv_tile(taps, weight, m, flip)
        if between is not None:
            between()


def conv_weight_grad(act_t, taps, out, first, last):
    def body(tap, carry):
        piece = mm(act_t[...], taps[8 - tap].reshape(512, -1))
        out[pl.ds(pl.multiple_of(tap * 512, 512), 512), :] = piece.astype(BF)
        return carry

    lax.fori_loop(first, last, body, 0)


class Steps:
    def __init__(self, *programs):
        self.todo = [step for program in programs for step in program]

    def run(self, count=None):
        count = len(self.todo) if count is None else count
        now, self.todo = self.todo[:count], self.todo[count:]
        for step in now:
            step()


def attn_places(ref):
    def at(z, x, d, half=None):
        place = ref.at[z * 2 + x]
        lanes = pl.ds(pl.multiple_of(d * 128, 128), 128)
        if half is None:
            return place.at[:, lanes]
        return place.at[pl.ds(half * 128, 128), lanes]

    return at


def param_places(ref):
    def at(z, x, d, half=None):
        place = ref.at[z * 2 + x]
        lanes = pl.ds(pl.multiple_of(d * 128, 128), 128)
        if half is None:
            return place.at[:, lanes]
        return place.at[pl.ds(half * 8, 8), lanes]

    return at


def forward_kernel(
    feat, grad, bounds, par, s1, s2, sa,
    w1_out, w2_out, wa_out, small_out, nall_out, oall_out, resid_out, hidden_out, x_out,
    w1, w2, wa, pb, bb, xin, oall, nall, taps, a1, a2, masks, hidden, resid, small, rows_a, rows_b, swaps,
    gsems, local, share_sems, bound_sems, swap_sems, spread_sems, halo_sems, out_sems,
):
    u = Unit()
    u.enter(True, True)
    groups = []
    for k, at in enumerate((weight_places(w1, 576), weight_places(w2, 576), attn_places(wa), param_places(pb))):
        groups.append(Gather(u, 4, at, gsems.at[k]))
    g1, g2, ga, gp = groups
    own = [pltpu.make_async_copy(src, group.own(u.z), local.at[k]) for k, (src, group) in enumerate(zip((s1, s2, sa, par), groups))]
    for copy in own:
        copy.start()
    keep = pltpu.make_async_copy(bounds, bb.at[u.c], local.at[4])
    keep.start()
    share_x, share_o = Share(u, share_sems.at[0], local.at[5]), Share(u, share_sems.at[1], local.at[6])
    share_x.send(feat, xin)
    bound_cp = remote(bounds, bb.at[u.c], bound_sems.at[0], bound_sems.at[1], u.cn)
    bound_cp.start()
    for copy in own:
        copy.wait()
    lead, follow = gp.program(), g1.program()
    early = []
    for k in range(len(follow)):
        early += [follow[k], lead[k]]
    early = Steps(early)
    early.run(12)
    keep.wait()
    remote(bounds, bb.at[1 - u.c], bound_sems.at[0], bound_sems.at[1], u.cn).wait_recv()
    limits = jnp.where(u.mu == 0, bb[u.z // 2, 0:2, :], bb[u.z // 2, 2:4, :])
    seg = tap_masks(u, limits, masks)
    counts = counts_of(limits, 4.0 * ROW)
    early.run(8)

    share_x.wait(feat, xin)
    share_o.send(grad, oall.at[u.z])
    swap = [Swap(u, swaps.at[k], swap_sems.at[k]) for k in range(3)]
    halo = [Halo(u, buf, halo_sems.at[k]) for k, buf in enumerate((a1, a2))]

    def sums_of(value):
        def body(r):
            line = value(r)
            rows_a[pl.ds(r, 1), :] = jnp.sum(line, axis=0, keepdims=True)
            rows_b[pl.ds(r, 1), :] = jnp.sum(line * line, axis=0, keepdims=True)

        each_row(body)

    def norm_send(k, value):
        sums_of(value)
        swap[k].buf[u.q] = canvas_sums(rows_a[...], rows_b[...], seg)
        swap[k].send()

    def norm_stats(k):
        swap[k].wait()
        average, inverse = moments(swap[k].total(), counts, seg)
        small[2 * k] = average
        small[2 * k + 1] = inverse

    def normal(k, value, r):
        line = (value(r) - small[2 * k, pl.ds(r, 1), :]) * small[2 * k + 1, pl.ds(r, 1), :]
        return line * small[6, 2 * k : 2 * k + 1, :] + small[6, 2 * k + 1 : 2 * k + 2, :]

    def feature(r):
        return xin[r].astype(F32)

    norm_send(0, feature)
    early.run()
    gp.arrive()
    total = pb[0, 0:8, :]
    for b in range(1, 8):
        total = total + pb[b, 0:8, :]
    small[6] = total
    small[7] = jnp.concatenate([limits, jnp.zeros((6, limits.shape[1]), F32)], axis=0)
    norm_stats(0)

    def activate(k, value, buf):
        def body(r):
            line = normal(k, value, r)
            buf[r + 1] = (line * sigmoid(line)).astype(BF)

        each_row(body)

    later = Steps(g2.program(), ga.program())
    later.run(1)
    activate(0, feature, a1)
    halo[0].send()
    taps_inner(a1, masks, taps)
    halo[0].wait()
    taps_outer(a1, masks, taps)
    share_o.wait(grad, oall.at[u.q])
    later.run(2)
    g1.arrive()
    spread_o = Spread(u, oall_parts(oall), spread_sems.at[0], 2)
    spread_n = Spread(u, oall_parts(nall), spread_sems.at[1], 2)
    for part in range(2):
        spread_o.send(part)

    copies = [pltpu.make_async_copy(w1, w1_out, out_sems.at[0])]
    copies[-1].start()
    conv_all(taps, w1, hidden, False, lambda: later.run(2))

    def middle(r):
        return hidden[r]

    norm_send(1, middle)
    later.run(6)
    copies.append(pltpu.make_async_copy(hidden, hidden_out, out_sems.at[1]))
    copies[-1].start()
    norm_stats(1)
    activate(1, middle, a2)
    halo[1].send()
    taps_inner(a2, masks, taps)
    halo[1].wait()
    taps_outer(a2, masks, taps)
    later.run(len(later.todo) - 14)
    for part in range(2):
        spread_o.relay(part)
    g2.arrive()

    copies.append(pltpu.make_async_copy(w2, w2_out, out_sems.at[2]))
    copies[-1].start()
    for m in range(2):
        piece = conv_tile(taps, w2, m, False)
        resid[4 * m : 4 * m + 4] = piece + xin[4 * m : 4 * m + 4].astype(F32)
        later.run(2)

    def last(r):
        return resid[r]

    norm_send(2, last)
    later.run(4)
    copies.append(pltpu.make_async_copy(resid, resid_out, out_sems.at[3]))
    copies.append(pltpu.make_async_copy(xin, x_out, out_sems.at[4]))
    for copy in copies[-2:]:
        copy.start()
    norm_stats(2)

    def normed_row(r):
        nall[u.q, r] = normal(2, last, r).astype(BF)

    for part in range(2):
        lax.fori_loop(4 * part, 4 * part + 4, lambda r, carry: (normed_row(r), carry)[1], 0)
        spread_n.send(part)
    later.run()
    ga.arrive()
    copies.append(pltpu.make_async_copy(wa, wa_out, out_sems.at[5]))
    copies.append(pltpu.make_async_copy(small, small_out, out_sems.at[6]))
    for copy in copies[-2:]:
        copy.start()
    for part in range(2):
        spread_n.relay(part)
    for part in range(2):
        spread_o.wait(part)
        spread_n.wait(part)
    copies.append(pltpu.make_async_copy(oall, oall_out, out_sems.at[7]))
    copies.append(pltpu.make_async_copy(nall, nall_out, out_sems.at[8]))
    for copy in copies[-2:]:
        copy.start()
    for group in groups:
        group.finish()
    bound_cp.wait_send()
    share_x.sent(feat, xin)
    share_o.sent(grad, oall.at[u.z])
    for item in swap + halo:
        item.sent()
    for item in (spread_o, spread_n):
        for part in range(2):
            item.sent(part)
    for copy in copies:
        copy.wait()


class oall_parts:
    def __init__(self, ref):
        self.ref = ref

    @property
    def at(self):
        return self

    def __getitem__(self, index):
        member, part = index
        return self.ref.at[member, pl.ds(part * (ROW // 2), ROW // 2)]


ANY = pl.BlockSpec(memory_space=pl.ANY)
VM = pl.BlockSpec(memory_space=pltpu.VMEM)


def forward_call(features, out_grad, limits, params, s1, s2, sa):
    full = lambda shape, kind: jax.ShapeDtypeStruct(shape, kind)
    dma = pltpu.SemaphoreType.DMA
    rows = (ROW, 64, 512)
    return pl.pallas_call(
        forward_kernel,
        out_shape=[
            full((4608, 512), BF), full((4608, 512), BF), full((8, 256, 512), BF), full((8, 8, 512), F32),
            full((4, *rows), BF), full((4, *rows), BF), full(rows, F32), full(rows, F32), full(rows, BF),
        ],
        in_specs=[VM] * 7,
        out_specs=[ANY] * 9,
        scratch_shapes=[
            pltpu.VMEM((4608, 512), BF), pltpu.VMEM((4608, 512), BF), pltpu.VMEM((8, 256, 512), BF),
            pltpu.VMEM((8, PARAMS, 512), F32), pltpu.VMEM((2, 8, 512), F32), pltpu.VMEM(rows, BF),
            pltpu.VMEM((4, *rows), BF), pltpu.VMEM((4, *rows), BF), pltpu.VMEM((9, *rows), BF),
            pltpu.VMEM((ROW + 2, 64, 512), BF), pltpu.VMEM((ROW + 2, 64, 512), BF), pltpu.VMEM((2, ROW, 512), F32),
            pltpu.VMEM(rows, F32), pltpu.VMEM(rows, F32), pltpu.VMEM((8, 8, 512), F32),
            pltpu.VMEM((ROW, 512), F32), pltpu.VMEM((ROW, 512), F32), pltpu.VMEM((3, 4, 8, 512), F32),
            dma((4, 2, Gather.SEMS)), dma((7,)), dma((2, 2, 2)), dma((2,)), dma((3, 2, 4)), dma((2, 2, 3, 2)),
            dma((2, 2, 2)), dma((9,)),
        ],
        compiler_params=pltpu.CompilerParams(collective_id=2, has_side_effects=True, vmem_limit_bytes=58 << 20),
    )(features, out_grad, limits, params, s1, s2, sa)


def unit_inputs(features, bounds, out_grad, norms, conv1, conv2, attn):
    d, b = lax.axis_index("dp"), lax.axis_index("blk")
    limits = jnp.broadcast_to(bounds.reshape(-1).astype(F32)[:, None], (4, 512))
    limits = jnp.concatenate([limits, jnp.zeros((4, 512), F32)])
    rows = jnp.stack([item.astype(F32) for item in norms])
    mine = jnp.where(d == b // 2, rows, 0.0)
    params = jnp.concatenate([jnp.where(b % 2 == 0, mine, 0.0), jnp.where(b % 2 == 1, mine, 0.0)], axis=1)
    params = jnp.concatenate([params, jnp.zeros((PARAMS - 6, 128), F32)])
    return (features[0], out_grad[0], limits, params, conv1, conv2, jnp.concatenate(attn))


def forward_all(
    features, bounds, out_grad, norm1_gain, norm1_shift, conv1_weight, norm2_gain, norm2_shift, conv2_weight,
    norm3_gain, norm3_shift, query_weight, key_weight, value_weight, output_weight,
):
    norms = (norm1_gain, norm1_shift, norm2_gain, norm2_shift, norm3_gain, norm3_shift)
    attn = (query_weight, key_weight, value_weight, output_weight)
    return forward_call(*unit_inputs(features, bounds, out_grad, norms, conv1_weight, conv2_weight, attn))


def attention_kernel(
    nall, oall, wa, resid, small,
    act_out, ga_out, gn_out,
    qall, kall, vall, doall, scores, slopes, heads, gq, gk, gv, lcol, dcol, ld, dk, dv,
    sems,
):
    u = Unit()
    u.enter(False, False)
    swap = Swap(u, ld, sems)
    scale = 512.0 ** (-0.5)
    limits = small[7]
    low, high = limits[0:1, 0:1], limits[1:2, 0:1]

    def matrix(k):
        return wa[:, pl.ds(k * 64, 64), :].reshape(512, 512)

    def project(i, carry):
        tokens, upstream = nall[i], oall[i]
        qall[i] = mm(tokens, matrix(0)).astype(BF)
        kall[i] = mm(tokens, matrix(1)).astype(BF)
        vall[i] = mm(tokens, matrix(2)).astype(BF)
        doall[i] = cols(upstream, matrix(3)).astype(BF)
        return carry

    lax.fori_loop(0, 4, project, 0)

    def canvas(rows):
        return (rows >= low).astype(F32) + (rows >= high).astype(F32)

    def seg_col(q, offset, count):
        token = offset + lax.broadcasted_iota(jnp.int32, (count, 1), 0)
        return canvas((ROW * q + token // 64).astype(F32))

    def seg_row(q):
        token = lax.broadcasted_iota(jnp.int32, (1, 512), 1)
        return canvas((ROW * q + token // 64).astype(F32))

    def queries(j, carry):
        block = pl.ds(pl.multiple_of(j * 256, 256), 256)
        query, upstream = qall[u.q, block], doall[u.q, block]
        seg = seg_col(u.q, j * 256, 256)
        most = jnp.full((256, 1), NEGATIVE, F32)
        for i in range(4):
            part = jnp.where(seg == seg_row(i), cols(query, kall[i]) * scale, NEGATIVE)
            scores[i] = part
            most = jnp.maximum(most, jnp.max(part, axis=1, keepdims=True))
        total = jnp.zeros((256, 1), F32)
        for i in range(4):
            part = jnp.exp(scores[i] - most)
            total = total + jnp.sum(part, axis=1, keepdims=True)
            scores[i] = part
        inverse = 1.0 / total
        found = jnp.zeros((256, 512), F32)
        correction = jnp.zeros((256, 1), F32)
        for i in range(4):
            part = scores[i] * inverse
            scores[i] = part
            found = found + mm(part.astype(BF), vall[i])
            slope = cols(upstream, vall[i])
            slopes[i] = slope
            correction = correction + jnp.sum(part * slope, axis=1, keepdims=True)
        heads[block, :] = found.astype(BF)
        back = jnp.zeros((256, 512), F32)
        for i in range(4):
            back = back + mm((scores[i] * (slopes[i] - correction)).astype(BF), kall[i])
        gq[block, :] = (back * scale).astype(BF)
        lcol[block, :] = jnp.broadcast_to(most + jnp.log(total), (256, 128))
        dcol[block, :] = jnp.broadcast_to(correction, (256, 128))
        return carry

    lax.fori_loop(0, 2, queries, 0)
    ld[u.q] = jnp.concatenate([lcol[...].T[0:1], dcol[...].T[0:1], jnp.zeros((6, 512), F32)], axis=0)
    swap.send()
    low_heads = heads[...]
    act_out[...] = (resid[...] + mm(low_heads, matrix(3)).reshape(ROW, 64, 512)).astype(BF)
    ga_out[:, 192:256, :] = mm(low_heads.T, oall[u.q]).astype(BF).reshape(8, 64, 512)
    dk[...] = jnp.zeros_like(dk)
    dv[...] = jnp.zeros_like(dv)
    swap.wait()

    def keys(step, carry):
        i, j = step // 2, step % 2
        block = pl.ds(pl.multiple_of(j * 256, 256), 256)
        key, value = kall[u.q, block], vall[u.q, block]
        query, upstream = qall[i], doall[i]
        shared = seg_col(u.q, j * 256, 256) == seg_row(i)
        part = jnp.where(shared, cols(key, query) * scale, NEGATIVE)
        part = jnp.where(shared, jnp.exp(part - ld[i, 0:1, :]), 0.0)
        dv[block, :] += mm(part.astype(BF), upstream)
        slope = cols(value, upstream) - ld[i, 1:2, :]
        dk[block, :] += mm((part * slope).astype(BF), query)
        return carry

    lax.fori_loop(0, 8, keys, 0)
    gk[...] = (dk[...] * scale).astype(BF)
    gv[...] = dv[...].astype(BF)
    tokens = nall[u.q].T
    total = None
    for k, part in enumerate((gq, gk, gv)):
        ga_out[:, k * 64 : (k + 1) * 64, :] = mm(tokens, part[...]).astype(BF).reshape(8, 64, 512)
        term = cols(part[...], matrix(k))
        total = term if total is None else total + term
    gn_out[...] = total.reshape(ROW, 64, 512)
    swap.sent()


def attention_call(nall, oall, wa, resid, small):
    rows = (ROW, 64, 512)
    full = lambda shape, kind: jax.ShapeDtypeStruct(shape, kind)
    square = (512, 512)
    return pl.pallas_call(
        attention_kernel,
        out_shape=[full(rows, BF), full((8, 256, 512), BF), full(rows, F32)],
        in_specs=[VM] * 5,
        out_specs=[VM] * 3,
        scratch_shapes=[pltpu.VMEM((4, *square), BF)] * 4
        + [pltpu.VMEM((4, 256, 512), F32)] * 2
        + [pltpu.VMEM(square, BF)] * 4
        + [pltpu.VMEM((512, 128), F32)] * 2
        + [pltpu.VMEM((4, 8, 512), F32)]
        + [pltpu.VMEM(square, F32)] * 2
        + [pltpu.SemaphoreType.DMA((2, 4))],
        compiler_params=pltpu.CompilerParams(collective_id=3, has_side_effects=True, vmem_limit_bytes=58 << 20),
    )(nall.reshape(4, *square), oall.reshape(4, *square), wa, resid, small)


def backward_kernel(
    act, ga, gn, resid, hidden, xin, small,
    w1_in, w2_in, oall_in,
    act_back, grad_back, g1_out, g2_out, ga_out, norm_out,
    w1, w2, og, taps, a1, a2, act_t1, act_t2, masks, big, gres, grad_low, wg1, wg2, rows_a, rows_b, swaps,
    psum_y, psum_z, mine,
    c1, c2, c3, c4, c5, d1, d2, d3, d4, d5, e1, e2, e3, e4, e5,
    ssems, local, share_sems, swap_sems, halo_sems, py_sems, pz_sems,
):
    u = Unit()
    u.enter(True, True)
    mine[...] = jnp.zeros_like(mine)
    loads = [
        pltpu.make_async_copy(oall_in.at[u.q], og, local.at[0]),
        pltpu.make_async_copy(w2_in, w2, local.at[1]),
        pltpu.make_async_copy(w1_in, w1, local.at[2]),
    ]
    for copy in loads:
        copy.start()
    share_a, share_g = Share(u, share_sems.at[0], local.at[3]), Share(u, share_sems.at[1], local.at[4])

    def part_of(half):
        return lambda ref, h: ref.at[pl.ds(h * half, half)]

    sum_a = Scatter(u, 4, attn_places(ga), part_of(128), ssems.at[0], (c1, c2, c3, c4, c5))
    sum_2 = Scatter(u, 4, weight_places(wg2, 576), part_of(288), ssems.at[1], (d1, d2, d3, d4, d5))
    sum_1 = Scatter(u, 4, weight_places(wg1, 576), part_of(288), ssems.at[2], (e1, e2, e3, e4, e5))
    steps = Steps(sum_a.program(ga_out))
    steps.run(2)
    share_a.back(act, act_back)

    limits = small[7]
    seg = tap_masks(u, limits, masks)
    counts = counts_of(limits, 4.0 * ROW)
    swap = [Swap(u, swaps.at[k], swap_sems.at[k]) for k in range(3)]
    halo = [Halo(u, buf, halo_sems.at[k]) for k, buf in enumerate((a1, a2))]

    def xhat(k, value, r):
        return (value(r) - small[2 * k, pl.ds(r, 1), :]) * small[2 * k + 1, pl.ds(r, 1), :]

    def param(j):
        return small[6, j : j + 1, :]

    def send_sums(k, value, incoming):
        def body(r):
            line = incoming(r)
            rows_a[pl.ds(r, 1), :] = jnp.sum(line, axis=0, keepdims=True)
            rows_b[pl.ds(r, 1), :] = jnp.sum(line * xhat(k, value, r), axis=0, keepdims=True)

        each_row(body)
        swap[k].buf[u.q] = canvas_sums(rows_a[...], rows_b[...], seg)
        swap[k].send()

    def take_sums(k):
        swap[k].wait()
        total = swap[k].total()
        mine[2 * k : 2 * k + 1, :] = jnp.sum(total[3:6], axis=0, keepdims=True)
        mine[2 * k + 1 : 2 * k + 2, :] = jnp.sum(total[0:3], axis=0, keepdims=True)
        grouped = group_total(total * param(2 * k))
        rows_a[...] = by_row([grouped[j : j + 1] / counts[j] for j in range(3)], seg)
        rows_b[...] = by_row([grouped[3 + j : 4 + j] / counts[j] for j in range(3)], seg)

    def back(k, value, incoming, r):
        line = incoming(r) * param(2 * k) - row_of(rows_a, r) - xhat(k, value, r) * row_of(rows_b, r)
        return line * small[2 * k + 1, pl.ds(r, 1), :]

    def third(r):
        return resid[r]

    def second(r):
        return hidden[r]

    def first(r):
        return xin[r].astype(F32)

    def swish_of(k, value, out):
        def body(r):
            line = xhat(k, value, r) * param(2 * k) + param(2 * k + 1)
            out[r] = (line * sigmoid(line)).astype(BF)

        each_row(body)

    def slope_of(k, value, r):
        line = xhat(k, value, r) * param(2 * k) + param(2 * k + 1)
        part = sigmoid(line)
        return part * (1.0 + line * (1.0 - part))

    send_sums(2, third, lambda r: gn[r])
    swish_of(1, second, grad_low)
    act_t2[...] = grad_low[...].reshape(512, 512).T
    steps.run(4)
    take_sums(2)
    loads[0].wait()

    def resid_grad(r):
        line = og[r].astype(F32) + back(2, third, lambda s: gn[s], r)
        gres[r] = line
        a2[r + 1] = line.astype(BF)

    each_row(resid_grad)
    halo[1].send()
    taps_inner(a2, masks, taps)
    halo[1].wait()
    taps_outer(a2, masks, taps)

    loads[1].wait()
    conv_weight_grad(act_t2, taps, wg2, 0, 9)
    steps = Steps(steps.todo, sum_2.program(g2_out))
    steps.run(6)
    for m in range(2):
        big[4 * m : 4 * m + 4] = conv_tile(taps, w2, m, True)
        steps.run(3)

    def scaled(k, value):
        def body(r):
            big[r] = big[r] * slope_of(k, value, r)

        each_row(body)

    scaled(1, second)
    send_sums(1, second, lambda r: big[r])
    swish_of(0, first, grad_low)
    act_t1[...] = grad_low[...].reshape(512, 512).T
    steps.run(3)
    take_sums(1)

    def hidden_grad(r):
        a1[r + 1] = back(1, second, lambda s: big[s], r).astype(BF)

    each_row(hidden_grad)
    halo[0].send()
    taps_inner(a1, masks, taps)
    halo[0].wait()
    taps_outer(a1, masks, taps)
    steps.run(4)

    loads[2].wait()
    conv_weight_grad(act_t1, taps, wg1, 0, 9)
    steps = Steps(steps.todo, sum_1.program(g1_out))
    steps.run(12)
    for m in range(2):
        big[4 * m : 4 * m + 4] = conv_tile(taps, w1, m, True)
        steps.run(4)
    scaled(0, first)
    send_sums(0, first, lambda r: big[r])
    steps.run(2)
    take_sums(0)

    def input_grad(r):
        grad_low[r] = (gres[r] + back(0, first, lambda s: big[s], r)).astype(BF)

    each_row(input_grad)
    share_g.back(grad_low, grad_back)

    py = remote(mine, psum_y, py_sems.at[0], py_sems.at[1], u.yn)
    py.start()
    steps.run(4)
    py.wait()
    psum_z[u.z] = mine[...] + psum_y[...]
    pz = []
    for k in (1, 2, 3):
        pz.append(remote(psum_z.at[u.z], psum_z.at[u.z], pz_sems.at[0, k], pz_sems.at[1, u.z], u.line(k)))
        pz[-1].start()
    steps.run()
    for k in (1, 2, 3):
        other = (u.z + k) % 4
        remote(psum_z.at[other], psum_z.at[other], pz_sems.at[0, k], pz_sems.at[1, other], u.line(k)).wait_recv()
    norm_out[...] = psum_z[0] + psum_z[1] + psum_z[2] + psum_z[3]
    for copy in pz:
        copy.wait_send()
    share_a.back_wait(act, act_back)
    share_g.back_wait(grad_low, grad_back)
    for item in (sum_a, sum_2, sum_1):
        item.finish()
    for item in swap + halo:
        item.sent()


def backward_call(act, ga, gn, resid, hidden, xin, small, w1, w2, oall):
    full = lambda shape, kind: jax.ShapeDtypeStruct(shape, kind)
    dma = pltpu.SemaphoreType.DMA
    rows = (ROW, 64, 512)
    padded = (ROW + 2, 64, 512)
    sums = []
    for r in (256, 576, 576):
        for shape in ((4, 4, r, 128), (4, 4, r, 128), (2, 4, r // 2, 128), (2, 4, r, 128), (2, 4, r, 128)):
            sums.append(pltpu.VMEM(shape, BF))
    return pl.pallas_call(
        backward_kernel,
        out_shape=[
            full((2, 4, 64, 512), BF), full((2, 4, 64, 512), BF), full((576, 128), F32), full((576, 128), F32),
            full((256, 128), F32), full((8, 512), F32),
        ],
        in_specs=[VM] * 7 + [ANY] * 3,
        out_specs=[VM] * 6,
        scratch_shapes=[
            pltpu.VMEM((4608, 512), BF), pltpu.VMEM((4608, 512), BF), pltpu.VMEM(rows, BF), pltpu.VMEM((9, *rows), BF),
            pltpu.VMEM(padded, BF), pltpu.VMEM(padded, BF), pltpu.VMEM((512, 512), BF), pltpu.VMEM((512, 512), BF),
            pltpu.VMEM((2, ROW, 512), F32), pltpu.VMEM(rows, F32), pltpu.VMEM(rows, F32), pltpu.VMEM(rows, BF),
            pltpu.VMEM((4608, 512), BF), pltpu.VMEM((4608, 512), BF), pltpu.VMEM((ROW, 512), F32),
            pltpu.VMEM((ROW, 512), F32), pltpu.VMEM((3, 4, 8, 512), F32), pltpu.VMEM((8, 512), F32),
            pltpu.VMEM((4, 8, 512), F32), pltpu.VMEM((8, 512), F32), *sums,
            dma((3, 2, Scatter.SEMS)), dma((5,)), dma((2, 2, 2)), dma((3, 2, 4)), dma((2, 2, 2)), dma((2,)), dma((2, 4)),
        ],
        compiler_params=pltpu.CompilerParams(collective_id=4, has_side_effects=True, vmem_limit_bytes=62 << 20),
    )(act, ga, gn, resid, hidden, xin, small, w1, w2, oall)


def unit_shards(*args):
    w1, w2, wa, small, nall, oall, resid, hidden, xin = forward_all(*args)
    act, ga, gn = attention_call(nall, oall, wa, resid, small)
    act_back, grad_back, g1, g2, ga, norms = backward_call(act, ga, gn, resid, hidden, xin, small, w1, w2, oall)
    norms = lax.dynamic_slice_in_dim(norms, lax.axis_index("blk") * 64, 64, axis=1)
    ga = ga.reshape(4, 64, 128)
    return (
        act_back.astype(F32)[None], grad_back.astype(F32)[None], norms[0], norms[1], g1, norms[2], norms[3], g2,
        norms[4], norms[5], ga[0], ga[1], ga[2], ga[3],
    )


def extended(shard, sides, width):
    for axis, dim in sides:
        devices, length = (lax.axis_size(axis), shard.shape[dim])
        up = [(i, (i + 1) % devices) for i in range(devices - 1)]
        down = [(j, i) for i, j in up]
        last = lax.slice_in_dim(shard, length - width, length, axis=dim)
        initial = lax.slice_in_dim(shard, 0, width, axis=dim)
        before = lax.ppermute(last, axis, up)
        after = lax.ppermute(initial, axis, down)
        shard = jnp.concatenate([before, shard, after], axis=dim)
    return shard


def canvas_index(global_rows, first_row, second_row):
    return (global_rows >= first_row).astype(jnp.int32) + (global_rows >= second_row).astype(
        jnp.int32
    )


def swish(argument):
    return argument * jax.nn.sigmoid(argument)


def swish_slope(argument):
    sigmoid_value = jax.nn.sigmoid(argument)
    return sigmoid_value * (1.0 + argument * (1.0 - sigmoid_value))


def group_sums(member, grouped):
    return jnp.einsum("rk,rwgc->kg", member, grouped, precision=HIGHEST)


def spread_rows(member, lookup):
    return jnp.dot(member, lookup, precision=HIGHEST)


def norm_forward(inputs, member, counts, norm_gain, norm_shift):
    row_count, width, channels = inputs.shape
    grouped = inputs.reshape(row_count, width, GROUPS, channels // GROUPS)
    totals, square = lax.psum(
        (group_sums(member, grouped), group_sums(member, grouped * grouped)), "blk"
    )
    average = totals / counts[:, None]
    inverse = lax.rsqrt(square / counts[:, None] - average * average + EPSILON)
    average_rows = spread_rows(member, average)
    scale_rows = spread_rows(member, inverse)
    normal = (grouped - average_rows[:, None, :, None]) * scale_rows[:, None, :, None]
    normal = normal.reshape(row_count, width, channels)
    return (normal * norm_gain + norm_shift, normal, scale_rows)


def norm_backward(incoming, normal, scale_rows, member, counts, norm_gain):
    row_count, width, channels = incoming.shape
    gain_grad = jnp.sum(incoming * normal, axis=(0, 1))
    shift_grad = jnp.sum(incoming, axis=(0, 1))
    scaled = (incoming * norm_gain).reshape(row_count, width, GROUPS, channels // GROUPS)
    grouped_normal = normal.reshape(row_count, width, GROUPS, channels // GROUPS)
    first_sum, second_sum = lax.psum(
        (group_sums(member, scaled), group_sums(member, scaled * grouped_normal)), "blk"
    )
    first_rows = spread_rows(member, first_sum / counts[:, None])
    second_rows = spread_rows(member, second_sum / counts[:, None])
    result = scale_rows[:, None, :, None] * (
        scaled - first_rows[:, None, :, None] - grouped_normal * second_rows[:, None, :, None]
    )
    return (result.reshape(row_count, width, channels), gain_grad, shift_grad)


def gather_taps(padded, seg_pad, seg_rows, direction):
    row_count = seg_rows.shape[0]
    width = padded.shape[1]
    widened = jnp.pad(padded, ((0, 0), (1, 1), (0, 0)))
    pieces = []
    for step_row in (-1, 0, 1):
        low_row = 1 + direction * step_row
        allowed = (seg_pad[low_row : low_row + row_count] == seg_rows).astype(padded.dtype)[
            :, None, None
        ]
        for step_col in (-1, 0, 1):
            low_col = 1 + direction * step_col
            pieces.append(
                widened[low_row : low_row + row_count, low_col : low_col + width, :] * allowed
            )
    return jnp.stack(pieces, axis=2)


def conv_apply(activation, seg_pad, seg_rows, weight_matrix):
    row_count, width, channels = activation.shape
    padded = extended(activation, (("blk", 0),), 1)
    stacked = gather_taps(padded, seg_pad, seg_rows, 1).reshape(row_count * width, 9 * channels)
    result = jnp.dot(stacked, weight_matrix, preferred_element_type=jnp.float32)
    return (result.reshape(row_count, width, channels), stacked)


def conv_reverse(gradient, stacked, seg_pad, seg_rows, weight_matrix):
    row_count, width, channels = gradient.shape
    flattened = gradient.reshape(row_count * width, channels)
    weight_grad = lax.dot_general(
        stacked, flattened, (((0,), (0,)), ((), ())), preferred_element_type=jnp.float32
    )
    padded = extended(gradient, (("blk", 0),), 1)
    mirrored = gather_taps(padded, seg_pad, seg_rows, -1).reshape(row_count * width, 9, channels)
    kernel = weight_matrix.reshape(9, channels, channels)
    result = lax.dot_general(
        mirrored, kernel, (((1, 2), (0, 2)), ((), ())), preferred_element_type=jnp.float32
    )
    return (result.reshape(row_count, width, channels), weight_grad)


def attention_forward(
    queries, keys_local, values_local, token_seg, first_row, second_row, width, scale
):
    token_count, channels = queries.shape

    def absorb(running, portion, offset):
        key_block, value_block = portion
        maximum, totals, accumulated = running
        key_seg = canvas_index(
            jnp.arange(key_block.shape[0], dtype=jnp.int32) // width, first_row, second_row
        )
        shared = token_seg[:, None] == key_seg[None, :]
        scores = (
            lax.dot_general(
                queries, key_block, (((1,), (1,)), ((), ())), preferred_element_type=jnp.float32
            )
            * scale
        )
        masked = jnp.where(shared, scores, NEGATIVE)
        new_maximum = jnp.maximum(maximum, jnp.max(masked, axis=1))
        weights = jnp.where(shared, jnp.exp(masked - new_maximum[:, None]), 0.0)
        totals = jnp.sum(weights, axis=1)
        accumulated = jnp.dot(
            weights.astype(jnp.bfloat16), value_block, preferred_element_type=jnp.float32
        )
        return (new_maximum, totals, accumulated)

    initial = (
        jnp.full((token_count,), NEGATIVE, jnp.float32),
        jnp.zeros((token_count,), jnp.float32),
        jnp.zeros((token_count, channels), jnp.float32),
    )
    maximum, totals, accumulated = absorb(
        initial,
        (
            lax.all_gather(keys_local, "blk", axis=0, tiled=True),
            lax.all_gather(values_local, "blk", axis=0, tiled=True),
        ),
        jnp.int32(0),
    )
    return (accumulated / totals[:, None], maximum + jnp.log(totals))


def attention_query_grad(
    queries,
    heads_grad,
    log_total,
    correction,
    keys_local,
    values_local,
    token_seg,
    first_row,
    second_row,
    width,
    scale,
):

    def absorb(running, portion, offset):
        key_block, value_block = portion
        key_seg = canvas_index(
            jnp.arange(key_block.shape[0], dtype=jnp.int32) // width, first_row, second_row
        )
        shared = token_seg[:, None] == key_seg[None, :]
        scores = (
            lax.dot_general(
                queries, key_block, (((1,), (1,)), ((), ())), preferred_element_type=jnp.float32
            )
            * scale
        )
        weights = jnp.where(
            shared, jnp.exp(jnp.where(shared, scores, NEGATIVE) - log_total[:, None]), 0.0
        )
        slopes = lax.dot_general(
            heads_grad, value_block, (((1,), (1,)), ((), ())), preferred_element_type=jnp.float32
        )
        score_grad = (weights * (slopes - correction[:, None])).astype(jnp.bfloat16)
        return jnp.dot(score_grad, key_block, preferred_element_type=jnp.float32) * scale

    return absorb(
        jnp.zeros(queries.shape, jnp.float32),
        (
            lax.all_gather(keys_local, "blk", axis=0, tiled=True),
            lax.all_gather(values_local, "blk", axis=0, tiled=True),
        ),
        jnp.int32(0),
    )


def attention_key_grad(
    queries,
    heads_grad,
    log_total,
    correction,
    keys_local,
    values_local,
    token_seg,
    first_row,
    second_row,
    width,
    scale,
):

    def absorb(running, portion, offset):
        query_part, upstream_part, total_part, correct_part = portion
        query_seg = canvas_index(
            jnp.arange(query_part.shape[0], dtype=jnp.int32) // width, first_row, second_row
        )
        query_low = query_part.astype(jnp.bfloat16)
        upstream_low = upstream_part.astype(jnp.bfloat16)
        shared = query_seg[:, None] == token_seg[None, :]
        scores = (
            lax.dot_general(
                query_low, keys_local, (((1,), (1,)), ((), ())), preferred_element_type=jnp.float32
            )
            * scale
        )
        weights = jnp.where(
            shared, jnp.exp(jnp.where(shared, scores, NEGATIVE) - total_part[:, None]), 0.0
        )
        value_acc = lax.dot_general(
            weights.astype(jnp.bfloat16),
            upstream_low,
            (((0,), (0,)), ((), ())),
            preferred_element_type=jnp.float32,
        )
        slopes = lax.dot_general(
            upstream_low, values_local, (((1,), (1,)), ((), ())), preferred_element_type=jnp.float32
        )
        score_grad = (weights * (slopes - correct_part[:, None])).astype(jnp.bfloat16)
        key_acc = (
            lax.dot_general(
                score_grad, query_low, (((0,), (0,)), ((), ())), preferred_element_type=jnp.float32
            )
            * scale
        )
        return (key_acc, value_acc)

    empty = jnp.zeros(keys_local.shape, jnp.float32)
    return absorb(
        (empty, empty),
        (
            lax.all_gather(queries.astype(jnp.float32), "blk", axis=0, tiled=True),
            lax.all_gather(heads_grad.astype(jnp.float32), "blk", axis=0, tiled=True),
            lax.all_gather(log_total, "blk", axis=0, tiled=True),
            lax.all_gather(correction, "blk", axis=0, tiled=True),
        ),
        jnp.int32(0),
    )


def collect(
    conv1_weight,
    conv2_weight,
    query_weight,
    key_weight,
    value_weight,
    output_weight,
    norm1_gain,
    norm1_shift,
    norm2_gain,
    norm2_shift,
    norm3_gain,
    norm3_shift,
):
    row_parts = (
        lax.all_gather(conv1_weight, "blk", axis=0, tiled=True),
        lax.all_gather(conv2_weight, "blk", axis=0, tiled=True),
        lax.all_gather(query_weight, "blk", axis=0, tiled=True),
        lax.all_gather(key_weight, "blk", axis=0, tiled=True),
        lax.all_gather(value_weight, "blk", axis=0, tiled=True),
        lax.all_gather(output_weight, "blk", axis=0, tiled=True),
        lax.all_gather(norm1_gain, "blk", axis=0, tiled=True),
        lax.all_gather(norm1_shift, "blk", axis=0, tiled=True),
        lax.all_gather(norm2_gain, "blk", axis=0, tiled=True),
        lax.all_gather(norm2_shift, "blk", axis=0, tiled=True),
        lax.all_gather(norm3_gain, "blk", axis=0, tiled=True),
        lax.all_gather(norm3_shift, "blk", axis=0, tiled=True),
    )
    full_parts = (
        lax.all_gather(row_parts[0], "dp", axis=1, tiled=True),
        lax.all_gather(row_parts[1], "dp", axis=1, tiled=True),
        lax.all_gather(row_parts[2], "dp", axis=1, tiled=True),
        lax.all_gather(row_parts[3], "dp", axis=1, tiled=True),
        lax.all_gather(row_parts[4], "dp", axis=1, tiled=True),
        lax.all_gather(row_parts[5], "dp", axis=1, tiled=True),
    )
    return (tuple(full_parts), tuple(row_parts[6:]))


def reduce_all(gradients):
    row_sums = (
        lax.psum_scatter(gradients[0], "blk", scatter_dimension=0, tiled=True),
        lax.psum_scatter(gradients[1], "blk", scatter_dimension=0, tiled=True),
        lax.psum_scatter(gradients[2], "blk", scatter_dimension=0, tiled=True),
        lax.psum_scatter(gradients[3], "blk", scatter_dimension=0, tiled=True),
        lax.psum_scatter(gradients[4], "blk", scatter_dimension=0, tiled=True),
        lax.psum_scatter(gradients[5], "blk", scatter_dimension=0, tiled=True),
        lax.psum_scatter(gradients[6], "blk", scatter_dimension=0, tiled=True),
        lax.psum_scatter(gradients[7], "blk", scatter_dimension=0, tiled=True),
        lax.psum_scatter(gradients[8], "blk", scatter_dimension=0, tiled=True),
        lax.psum_scatter(gradients[9], "blk", scatter_dimension=0, tiled=True),
        lax.psum_scatter(gradients[10], "blk", scatter_dimension=0, tiled=True),
        lax.psum_scatter(gradients[11], "blk", scatter_dimension=0, tiled=True),
    )
    matrix_sums = (
        lax.psum_scatter(row_sums[0], "dp", scatter_dimension=1, tiled=True),
        lax.psum_scatter(row_sums[1], "dp", scatter_dimension=1, tiled=True),
        lax.psum_scatter(row_sums[2], "dp", scatter_dimension=1, tiled=True),
        lax.psum_scatter(row_sums[3], "dp", scatter_dimension=1, tiled=True),
        lax.psum_scatter(row_sums[4], "dp", scatter_dimension=1, tiled=True),
        lax.psum_scatter(row_sums[5], "dp", scatter_dimension=1, tiled=True),
    )
    norm_sums = lax.psum(
        (row_sums[6], row_sums[7], row_sums[8], row_sums[9], row_sums[10], row_sums[11]), "dp"
    )
    return tuple(matrix_sums) + tuple(norm_sums)


def one_batch(inputs_low, bound_pair, upstream_low, matrices, norm_params, position, blocks):
    row_count, width, channels = inputs_low.shape
    token_count = row_count * width
    total_rows = row_count * blocks
    scale = channels ** (-0.5)
    first_row = bound_pair[0]
    second_row = bound_pair[1]
    local_rows = position * row_count + jnp.arange(row_count, dtype=jnp.int32)
    padded_rows = position * row_count - 1 + jnp.arange(row_count + 2, dtype=jnp.int32)
    seg_rows = canvas_index(local_rows, first_row, second_row)
    seg_pad = canvas_index(padded_rows, first_row, second_row)
    member = (seg_rows[:, None] == jnp.arange(CANVASES, dtype=jnp.int32)[None, :]).astype(
        jnp.float32
    )
    counts = jnp.stack([first_row, second_row - first_row, total_rows - second_row]).astype(
        jnp.float32
    ) * float(width * (channels // GROUPS))
    gains = [item.astype(jnp.float32) for item in norm_params]
    inputs = inputs_low.astype(jnp.float32)
    norm_one, normal_one, scale_one = norm_forward(inputs, member, counts, gains[0], gains[1])
    act_one = swish(norm_one).astype(jnp.bfloat16)
    hidden_one, stacked_one = conv_apply(act_one, seg_pad, seg_rows, matrices[0])
    norm_two, normal_two, scale_two = norm_forward(hidden_one, member, counts, gains[2], gains[3])
    act_two = swish(norm_two).astype(jnp.bfloat16)
    hidden_two, stacked_two = conv_apply(act_two, seg_pad, seg_rows, matrices[1])
    residual = inputs + hidden_two
    norm_three, normal_three, scale_three = norm_forward(
        residual, member, counts, gains[4], gains[5]
    )
    normed = norm_three.astype(jnp.bfloat16).reshape(token_count, channels)
    queries = jnp.dot(normed, matrices[2], preferred_element_type=jnp.float32).astype(jnp.bfloat16)
    keys_local = jnp.dot(normed, matrices[3], preferred_element_type=jnp.float32).astype(
        jnp.bfloat16
    )
    values_local = jnp.dot(normed, matrices[4], preferred_element_type=jnp.float32).astype(
        jnp.bfloat16
    )
    token_seg = jnp.repeat(seg_rows, width)
    attended, log_total = attention_forward(
        queries, keys_local, values_local, token_seg, first_row, second_row, width, scale
    )
    heads = attended.astype(jnp.bfloat16)
    activation = residual + jnp.dot(heads, matrices[5], preferred_element_type=jnp.float32).reshape(
        row_count, width, channels
    )
    upstream = upstream_low.reshape(token_count, channels)
    output_weight_grad = lax.dot_general(
        heads, upstream, (((0,), (0,)), ((), ())), preferred_element_type=jnp.float32
    )
    heads_grad = lax.dot_general(
        upstream, matrices[5], (((1,), (1,)), ((), ())), preferred_element_type=jnp.float32
    ).astype(jnp.bfloat16)
    correction = jnp.sum(heads_grad.astype(jnp.float32) * attended, axis=1)
    query_sum = attention_query_grad(
        queries,
        heads_grad,
        log_total,
        correction,
        keys_local,
        values_local,
        token_seg,
        first_row,
        second_row,
        width,
        scale,
    )
    key_sum, value_sum = attention_key_grad(
        queries,
        heads_grad,
        log_total,
        correction,
        keys_local,
        values_local,
        token_seg,
        first_row,
        second_row,
        width,
        scale,
    )
    query_low = query_sum.astype(jnp.bfloat16)
    key_low = key_sum.astype(jnp.bfloat16)
    value_low = value_sum.astype(jnp.bfloat16)
    contract_rows = (((0,), (0,)), ((), ()))
    contract_cols = (((1,), (1,)), ((), ()))
    query_weight_grad = lax.dot_general(
        normed, query_low, contract_rows, preferred_element_type=jnp.float32
    )
    key_weight_grad = lax.dot_general(
        normed, key_low, contract_rows, preferred_element_type=jnp.float32
    )
    value_weight_grad = lax.dot_general(
        normed, value_low, contract_rows, preferred_element_type=jnp.float32
    )
    normed_grad = (
        lax.dot_general(query_low, matrices[2], contract_cols, preferred_element_type=jnp.float32)
        + lax.dot_general(key_low, matrices[3], contract_cols, preferred_element_type=jnp.float32)
        + lax.dot_general(value_low, matrices[4], contract_cols, preferred_element_type=jnp.float32)
    )
    back_three, gain_three_grad, shift_three_grad = norm_backward(
        normed_grad.reshape(row_count, width, channels),
        normal_three,
        scale_three,
        member,
        counts,
        gains[4],
    )
    residual_grad = upstream_low.astype(jnp.float32) + back_three
    act_two_grad, conv_two_grad = conv_reverse(
        residual_grad.astype(jnp.bfloat16), stacked_two, seg_pad, seg_rows, matrices[1]
    )
    back_two, gain_two_grad, shift_two_grad = norm_backward(
        act_two_grad * swish_slope(norm_two), normal_two, scale_two, member, counts, gains[2]
    )
    act_one_grad, conv_one_grad = conv_reverse(
        back_two.astype(jnp.bfloat16), stacked_one, seg_pad, seg_rows, matrices[0]
    )
    back_one, gain_one_grad, shift_one_grad = norm_backward(
        act_one_grad * swish_slope(norm_one), normal_one, scale_one, member, counts, gains[0]
    )
    input_grad = residual_grad + back_one
    local_grads = (
        conv_one_grad,
        conv_two_grad,
        query_weight_grad,
        key_weight_grad,
        value_weight_grad,
        output_weight_grad,
        gain_one_grad,
        shift_one_grad,
        gain_two_grad,
        shift_two_grad,
        gain_three_grad,
        shift_three_grad,
    )
    return (activation, input_grad, local_grads)


def shards(
    features,
    bounds,
    out_grad,
    norm1_gain,
    norm1_shift,
    conv1_weight,
    norm2_gain,
    norm2_shift,
    conv2_weight,
    norm3_gain,
    norm3_shift,
    query_weight,
    key_weight,
    value_weight,
    output_weight,
):
    blocks = lax.axis_size("blk")
    position = lax.axis_index("blk")
    micro_count = features.shape[1]
    shard_sums = None
    outputs = []
    input_grads = []
    for micro_index in range(micro_count):
        matrices, norm_params = collect(
            conv1_weight,
            conv2_weight,
            query_weight,
            key_weight,
            value_weight,
            output_weight,
            norm1_gain,
            norm1_shift,
            norm2_gain,
            norm2_shift,
            norm3_gain,
            norm3_shift,
        )
        activation, input_grad, local_grads = one_batch(
            features[0, micro_index],
            bounds[0, micro_index],
            out_grad[0, micro_index],
            matrices,
            norm_params,
            position,
            blocks,
        )
        outputs.append(activation)
        input_grads.append(input_grad)
        reduced = reduce_all(local_grads)
        shard_sums = (
            reduced
            if shard_sums is None
            else tuple((acc + new for acc, new in zip(shard_sums, reduced)))
        )
    activations = jnp.stack(outputs)[None]
    input_grad_all = jnp.stack(input_grads)[None]
    return (
        activations,
        input_grad_all,
        shard_sums[6],
        shard_sums[7],
        shard_sums[0],
        shard_sums[8],
        shard_sums[9],
        shard_sums[1],
        shard_sums[10],
        shard_sums[11],
        shard_sums[2],
        shard_sums[3],
        shard_sums[4],
        shard_sums[5],
    )


def solution(mesh):
    in_specs = (
        P("dp", None, "blk", None, None),
        P("dp", None, None),
        P("dp", None, "blk", None, None),
        P("blk"),
        P("blk"),
        P("blk", "dp"),
        P("blk"),
        P("blk"),
        P("blk", "dp"),
        P("blk"),
        P("blk"),
        P("blk", "dp"),
        P("blk", "dp"),
        P("blk", "dp"),
        P("blk", "dp"),
    )
    out_specs = (
        P("dp", None, "blk", None, None),
        P("dp", None, "blk", None, None),
        P("blk"),
        P("blk"),
        P("blk", "dp"),
        P("blk"),
        P("blk"),
        P("blk", "dp"),
        P("blk"),
        P("blk"),
        P("blk", "dp"),
        P("blk", "dp"),
        P("blk", "dp"),
        P("blk", "dp"),
    )
    near = mesh.shape["dp"] == 4 and mesh.shape["blk"] == 8
    return jax.shard_map(unit_shards if near else shards, mesh=mesh, in_specs=in_specs, out_specs=out_specs, check_vma=False)
```

```python
import functools
import types

import jax
import jax.numpy as jnp
from jax import lax
from jax.experimental import pallas as pl
from jax.experimental.pallas import tpu as pltpu
from jax.sharding import PartitionSpec as P

GROUPS = 32
CANVASES = 3


EPSILON = 1e-06
HIGHEST = lax.Precision.HIGHEST
NEGATIVE = -1e30
MESH = pl.DeviceIdType.MESH
def in_order(s):
    s.ow(), s.gpl0(), s.g1l0(), s.gpo0(), s.gao0(), s.g2o0(), s.g2l0(), s.gpl1()
    s.gpo1(), s.gal0(), s.g1l1(), s.g1o1(), s.gpl2(), s.g2l1(), s.g1o0(), s.gpo2()
    s.gpy1(), s.gpx1(), s.g1l2(), s.gpl3(), s.g2o1(), s.gpo3(), s.g1o2(), s.gpx0()
    s.gpx3(), s.gpy0(), s.g1l3(), s.g1o3(), s.xs(), s.g2l2(), s.gpy2(), s.g1x1()
    s.gal1(), s.g1x2(), s.gpx2(), s.gpy3(), s.bw(), s.g2x0(), s.g1x3(), s.g1y0()
    s.g2l3(), s.g1y2(), s.g1y1(), s.gal2(), s.g1y3(), s.g2o3(), s.g1x0(), s.n1a()
    s.gao1(), s.gpd2(), s.os(), s.gpd0(), s.g2o2(), s.gpd1(), s.gpd3(), s.n1b()
    s.gal3(), s.n1c(), s.gao2(), s.g1d0(), s.g1d1(), s.g1d3(), s.n1d(), s.g2y3()
    s.g1d2(), s.g2y0(), s.g2x3(), s.g1a(), s.g2y1(), s.gao3(), s.n1e(), s.c10()
    s.c11(), s.n2a(), s.g2x2(), s.g2y2(), s.gay1(), s.gax3(), s.gay2(), s.g2x1()
    s.gay3(), s.g2d3(), s.gay0(), s.n2b(), s.n2c(), s.ob(), s.g2d2(), s.n2d()
    s.gax1(), s.n2e(), s.g2d0(), s.g2d1(), s.g2a(), s.c20(), s.gax2(), s.gad1()
    s.c21(), s.n3a(), s.gad2(), s.gax0(), s.n3b(), s.n3c(), s.t2(), s.gad3()
    s.or0(), s.or1(), s.gad0(), s.gaa(), s.po1(), s.pj1(), s.pj0(), s.po0()
    s.po2(), s.nr0(), s.po3(), s.nr1(), s.pj2(), s.pj3(), s.qf(), s.qb()
    s.hw(), s.gz(), s.hd(), s.ks(), s.an(), s.b3a(), s.aw(), s.rab3()
    s.rab0(), s.t1(), s.rab1(), s.rab2(), s.rac3(), s.b3b(), s.rac1(), s.b3c()
    s.rac2(), s.rac0(), s.b3d(), s.d20(), s.w20(), s.d21(), s.b2a(), s.r2b0()
    s.w21(), s.r2b1(), s.w22(), s.r2b3(), s.rae2(), s.b2b(), s.r2b2(), s.rae1()
    s.r2c2(), s.b2c(), s.raf2(), s.r2c3(), s.r2c0(), s.b2d(), s.d10(), s.d11()
    s.b1a(), s.rae3(), s.r2e2(), s.w10(), s.r2e3(), s.raf1(), s.rae0(), s.b1m()
    s.r2c1(), s.b1b(), s.raf3(), s.r2e0(), s.w11(), s.r1b0(), s.r2f2(), s.ps()
    s.w12(), s.r1b3(), s.r1b1(), s.r1b2(), s.r1c3(), s.r2f3(), s.r1e3(), s.r1c2()
    s.raf0(), s.r1f3(), s.r2e1(), s.r1e2(), s.py(), s.r2f0(), s.r1c1(), s.r2f1()
    s.r1e1(), s.r1c0(), s.rat(), s.r1f2(), s.r1f1(), s.pz(), s.r1e0(), s.r2t()
    s.r1f0(), s.r1t()


DIRECT = (False, False, False, False)
LIMIT = 60 << 20
SPLIT, SPLIT_A = 432, 192
CUT, CUT_A = 112, 48


class Place:
    def __init__(self):
        self.d = lax.axis_index("dp")
        self.b = lax.axis_index("blk")
        self.y, self.c = self.d // 2, self.d % 2
        self.z, self.x = self.b // 2, self.b % 2
        self.up = {"dp": self.d, "blk": self.b + 2}
        self.down = {"dp": self.d, "blk": self.b - 2}
        self.xn = {"dp": self.d, "blk": self.z * 2 + 1 - self.x}
        self.yn = {"dp": (1 - self.y) * 2 + self.c, "blk": self.b}
        self.cn = {"dp": self.y * 2 + 1 - self.c, "blk": self.b}


def remote(src, dst, send, recv, device):
    return pltpu.make_async_remote_copy(
        src_ref=src, dst_ref=dst, send_sem=send, recv_sem=recv, device_id=device, device_id_type=MESH
    )


def steps_of(z, nz):
    visits = [(z, None)]
    for k in range(1, nz):
        visits.append((z - k, z >= k))
        visits.append((z + k, z + k < nz))
    return visits


def guarded(valid, body):
    if valid is None:
        body()
    else:
        pl.when(valid)(body)


class Gather:
    SEMS = 40

    def __init__(self, here, nz, at, sems, direct):
        self.here, self.nz, self.at, self.sems, self.direct = here, nz, at, sems, direct
        self.visits = steps_of(here.z, nz)

    def sem(self, kind, z, way):
        base = {"z": 0, "x": 4, "y": 8, "da": 12, "db": 16, "co": 20, "cx": 24, "cy": 28, "cd": 32, "zd": 36}[kind]
        return self.sems.at[way, base + z]

    def cp(self, kind, z, src, device, skind=None):
        return remote(src, src, self.sem(skind or kind, z, 0), self.sem(kind, z, 1), device)

    def own(self, z):
        return self.at(z, self.here.x, self.here.d, None)

    def colx(self, z, half=None):
        return self.at(z, 1 - self.here.x, self.here.d, half)

    def coly(self, z, half=None):
        return self.at(z, self.here.x, (1 - self.here.y) * 2 + self.here.c, half)

    def cold(self, z, half=None):
        return self.at(z, 1 - self.here.x, (1 - self.here.y) * 2 + self.here.c, half)

    def line_cp(self, k):
        here = self.here
        z = (here.z + k) % self.nz
        device = {"dp": here.d, "blk": z * 2 + here.x}
        return remote(self.own(here.z), self.own(here.z), self.sem("z", z, 0), self.sem("z", here.z, 1), device)

    def line(self, j):
        z, valid = self.visits[j]
        here = self.here
        if j == 0 and self.direct:
            for k in range(1, self.nz):
                self.line_cp(k).start()
            return

        def body():
            src = self.own(z)
            if j > 0:
                self.cp("z", z, src, here.up).wait_recv()
            if self.direct:
                return
            if j == 0 or j % 2 == 1:

                @pl.when(here.z < self.nz - 1)
                def _():
                    self.cp("z", z, src, here.up).start()

            if j == 0 or j % 2 == 0:

                @pl.when(here.z > 0)
                def _():
                    self.cp("z", z, src, here.down, "zd").start()

        guarded(valid, body)

    def out(self, j):
        z, valid = self.visits[j]
        here = self.here

        def body():
            src = self.own(z)
            self.cp("x", z, src, here.xn).start()
            self.cp("y", z, src, here.yn).start()
            self.cp("co", z, src, here.cn).start()

        guarded(valid, body)

    def have(self, j):
        self.line(j)
        self.out(j)

    def from_x(self, j):
        z, valid = self.visits[j]

        def body():
            self.cp("x", z, self.colx(z), self.here.xn).wait_recv()
            self.cp("da", z, self.colx(z, 0), self.here.yn).start()
            self.cp("cx", z, self.colx(z), self.here.cn).start()

        guarded(valid, body)

    def from_y(self, j):
        z, valid = self.visits[j]

        def body():
            self.cp("y", z, self.coly(z), self.here.yn).wait_recv()
            self.cp("db", z, self.coly(z, 1), self.here.xn).start()
            self.cp("cy", z, self.coly(z), self.here.cn).start()

        guarded(valid, body)

    def cross(self, j):
        self.from_x(j)
        self.from_y(j)

    def diagonal(self, j):
        z, valid = self.visits[j]
        here = self.here

        def body():
            self.cp("da", z, self.cold(z, 0), here.yn).wait_recv()
            self.cp("db", z, self.cold(z, 1), here.xn).wait_recv()
            self.cp("cd", z, self.cold(z), here.cn).start()

        guarded(valid, body)

    def arrive(self):
        here = self.here
        near, far = here.y * 2 + 1 - here.c, (1 - here.y) * 2 + 1 - here.c
        for z in range(self.nz):
            for kind, x, d in (("co", here.x, near), ("cx", 1 - here.x, near), ("cy", here.x, far), ("cd", 1 - here.x, far)):
                self.cp(kind, z, self.at(z, x, d, None), here.cn).wait_recv()

    def finish(self):
        here = self.here
        if self.direct:
            for k in range(1, self.nz):
                self.line_cp(k).wait_send()
        for j, (z, valid) in enumerate(self.visits):

            def body():
                src = self.own(z)
                if not self.direct and (j == 0 or j % 2 == 1):

                    @pl.when(here.z < self.nz - 1)
                    def _():
                        self.cp("z", z, src, here.up).wait_send()

                if not self.direct and (j == 0 or j % 2 == 0):

                    @pl.when(here.z > 0)
                    def _():
                        self.cp("z", z, src, here.down, "zd").wait_send()

                self.cp("x", z, src, here.xn).wait_send()
                self.cp("y", z, src, here.yn).wait_send()
                self.cp("da", z, self.colx(z, 0), here.yn).wait_send()
                self.cp("db", z, self.coly(z, 1), here.xn).wait_send()
                for kind in ("co", "cx", "cy", "cd"):
                    self.cp(kind, z, src, here.cn).wait_send()

            guarded(valid, body)

    def table(self, name):
        kinds = {"l": self.line, "o": self.out, "x": self.from_x, "y": self.from_y, "d": self.diagonal}
        found = {name + "a": self.arrive}
        for kind, step in kinds.items():
            for k in range(self.nz):
                js = (0,) if k == 0 else (2 * k - 1, 2 * k)
                found["%s%s%d" % (name, kind, k)] = lambda js=js, step=step: [step(j) for j in js]
        return found


class Scatter:
    SEMS = 48

    def __init__(self, here, nz, at, core_at, part, sems, bufs):
        self.here, self.nz, self.at, self.core_at, self.part, self.sems = here, nz, at, core_at, part, sems
        self.half, self.side, self.last = bufs
        self.visits = steps_of(here.z, nz)[::-1]

    def sem(self, kind, z, way):
        base = ("c0", "c1", "c2", "c3", "da", "db", "xa", "xb", "ya", "yb", "l").index(kind) * 4
        return self.sems.at[way, base + z]

    def cp(self, kind, z, src, dst, device):
        return remote(src, dst, self.sem(kind, z, 0), self.sem(kind, z, 1), device)

    def places(self, z, c):
        here = self.here
        y, x = here.y, here.x
        return [(z, x, y * 2 + c), (z, 1 - x, y * 2 + c), (z, x, (1 - y) * 2 + c), (z, 1 - x, (1 - y) * 2 + c)]

    def mine(self, z, k):
        return self.at(*self.places(z, self.here.c)[k])

    def core_cp(self, z, k):
        place = self.places(z, 1 - self.here.c)[k]
        return self.cp("c%d" % k, z, self.at(*place), self.core_at(k, *place), self.here.cn)

    def core_in(self, z, k):
        place = self.core_at(k, *self.places(z, self.here.c)[k])
        self.cp("c%d" % k, z, place, place, self.here.cn).wait_recv()
        return place[...]

    def begin(self, z):
        for k in (3, 1, 2, 0):
            self.core_cp(z, k).start()

    def half_cp(self, z, h):
        return self.cp(("da", "db")[h], z, self.part(self.mine(z, 3), h), self.half[h].at[z], (self.here.xn, self.here.yn)[h])

    def side_cp(self, z, side, h):
        return self.cp(
            "xy"[side] + "ab"[h], z, self.part(self.mine(z, 1 + side), h), self.part(self.side.at[side, z], h),
            (self.here.xn, self.here.yn)[side],
        )

    def corner(self, j):
        z, valid = self.visits[j]

        def body():
            for k in (3, 1, 2):
                place = self.mine(z, k)
                place[...] = place[...] + self.core_in(z, k)
                if k == 3:
                    self.half_cp(z, 0).start()
                    self.half_cp(z, 1).start()
                else:
                    self.side_cp(z, k - 1, k - 1).start()

        guarded(valid, body)

    def edges(self, j):
        z, valid = self.visits[j]

        def body():
            for side, h in ((0, 1), (1, 0)):
                self.half_cp(z, h).wait_recv()
                place = self.part(self.mine(z, 1 + side), h)
                place[...] = place[...] + self.half[h][z]
                self.side_cp(z, side, h).start()

        guarded(valid, body)

    def column(self, j, out):
        z, valid = self.visits[j]
        here = self.here

        def body():
            place = self.mine(z, 0)
            total = place[...].astype(jnp.float32) + self.core_in(z, 0).astype(jnp.float32)
            for side in (0, 1):
                for h in (0, 1):
                    self.side_cp(z, side, h).wait_recv()
                total = total + self.side[side, z].astype(jnp.float32)
            if j == len(self.visits) - 1:
                out[...] = total
            else:
                place[...] = total.astype(jnp.bfloat16)
                self.last_cp(z).start()

        guarded(valid, body)

    def last_cp(self, z):
        here = self.here
        device = {"dp": here.d, "blk": z * 2 + here.x}
        return remote(self.mine(z, 0), self.last.at[here.z], self.sem("l", z, 0), self.sem("l", here.z, 1), device)

    def total(self, out):
        here = self.here
        for k in range(1, self.nz):
            z = (here.z + k) % self.nz
            remote(self.last.at[z], self.last.at[z], self.sem("l", z, 0), self.sem("l", z, 1), here.up).wait_recv()
            out[...] += self.last[z].astype(jnp.float32)

    def finish(self):
        for j, (z, valid) in enumerate(self.visits):

            def body():
                for k in range(4):
                    self.core_cp(z, k).wait_send()
                for h in (0, 1):
                    self.half_cp(z, h).wait_send()
                    for side in (0, 1):
                        self.side_cp(z, side, h).wait_send()
                if j < len(self.visits) - 1:
                    self.last_cp(z).wait_send()

            guarded(valid, body)

    def table(self, name, out):
        kinds = {"c": self.corner, "e": self.edges, "f": lambda j: self.column(j, out)}
        top = 2 * (self.nz - 1)
        found = {name + "t": lambda: self.total(out)}
        for z in range(self.nz):
            found["%sb%d" % (name, z)] = functools.partial(self.begin, z)
        for kind, step in kinds.items():
            for k in range(self.nz):
                js = (top,) if k == 0 else (top - 2 * k, top - 2 * k + 1)
                found["%s%s%d" % (name, kind, k)] = lambda js=js, step=step: [step(j) for j in js]
        return found


def part_of(ref, half, split, rows):
    return ref.at[pl.ds(0, split)] if half == 0 else ref.at[pl.ds(split, rows - split)]


def weight_places(ref, rows, split=0):
    def at(z, x, d, half=None):
        base, count = (z * 2 + x) * rows, rows
        if half is not None:
            base, count = base + half * split, rows - split if half else split
        return ref.at[pl.ds(pl.multiple_of(base, 16), count), pl.ds(pl.multiple_of(d * 128, 128), 128)]

    return at


BF = jnp.bfloat16
F32 = jnp.float32
ROW = 8
PARAMS = 16


def both(a, b):
    return jnp.logical_and(a, b)


def cols(a, b):
    return lax.dot_general(a, b, (((1,), (1,)), ((), ())), preferred_element_type=F32)


def mm(a, b):
    return jnp.dot(a, b, preferred_element_type=F32)


class Unit(Place):
    def __init__(self):
        super().__init__()
        self.q = jnp.where(self.c == 0, self.x, 3 - self.x)
        self.mu = self.z % 2
        self.alone = self.z == self.q

    def member(self, q, z):
        return {"dp": self.y * 2 + q // 2, "blk": z * 2 + jnp.where(q < 2, q, 3 - q)}

    def peer(self, q):
        return self.member(q, self.z)

    def worker(self, m):
        return self.member(self.z, 2 * self.c + m)

    def keeper(self, h):
        return {"dp": self.y * 2 + self.z // 2, "blk": self.q * 2 + h}

    def column_worker(self, m):
        return {"dp": self.y * 2 + self.z // 2, "blk": (2 * self.c + m) * 2 + self.x}

    def column_keeper(self, k):
        return {"dp": self.y * 2 + self.z // 2, "blk": (2 * self.c + k) * 2 + self.x}

    def line(self, k):
        return {"dp": self.d, "blk": ((self.z + k) % 4) * 2 + self.x}

    def enter(self, shares, lines):
        barrier = pltpu.get_barrier_semaphore()

        def greet(device):
            pl.semaphore_signal(barrier, inc=1, device_id=device, device_id_type=MESH)

        for k in (1, 2, 3):
            greet(self.peer((self.q + k) % 4))
        count = 3
        if lines:
            greet(self.yn)
            for k in (1, 2, 3):
                greet(self.line(k))
            count += 4
        if shares:
            for m in (0, 1):
                pl.when(jnp.logical_not(both(self.alone, self.mu == m)))(lambda m=m: greet(self.worker(m)))
            for h in (0, 1):
                pl.when(jnp.logical_not(both(self.alone, self.x == h)))(lambda h=h: greet(self.keeper(h)))
            near = self.c == self.z // 2
            for k in (0, 1):
                pl.when(jnp.logical_not(both(near, self.mu == k)))(lambda k=k: greet(self.column_worker(k)))
            count = count + 6 - 2 * self.alone.astype(jnp.int32) - near.astype(jnp.int32)
        pl.semaphore_wait(barrier, count)


class Share:
    def __init__(self, u, sems, local):
        self.u, self.sems, self.local = u, sems, local

    def send(self, src, dst):
        u = self.u
        for m in (0, 1):
            mine = both(u.alone, u.mu == m)
            place = dst.at[pl.ds(4 * u.x, 4)]
            pl.when(mine)(lambda: pltpu.make_async_copy(src.at[m], place, self.local).start())
            pl.when(jnp.logical_not(mine))(
                lambda: remote(src.at[m], place, self.sems.at[0, m], self.sems.at[1, u.x], u.worker(m)).start()
            )

    def wait(self, src, dst):
        u = self.u
        for h in (0, 1):
            mine = both(u.alone, u.x == h)
            place = dst.at[pl.ds(4 * h, 4)]
            pl.when(mine)(lambda: pltpu.make_async_copy(src.at[0], place, self.local).wait())
            pl.when(jnp.logical_not(mine))(
                lambda: remote(place, place, self.sems.at[0, 0], self.sems.at[1, h], u.keeper(h)).wait_recv()
            )

    def sent(self, src, dst):
        u = self.u
        for m in (0, 1):
            place = dst.at[pl.ds(4 * u.x, 4)]
            pl.when(jnp.logical_not(both(u.alone, u.mu == m)))(
                lambda: remote(src.at[m], place, self.sems.at[0, m], self.sems.at[1, u.x], u.worker(m)).wait_send()
            )

    def back(self, src, dst):
        u = self.u
        for h in (0, 1):
            mine = both(u.alone, u.x == h)
            piece = src.at[pl.ds(4 * h, 4)]
            pl.when(mine)(lambda: pltpu.make_async_copy(piece, dst.at[u.mu], self.local).start())
            pl.when(jnp.logical_not(mine))(
                lambda: remote(piece, dst.at[u.mu], self.sems.at[0, h], self.sems.at[1, u.mu], u.keeper(h)).start()
            )

    def back_wait(self, src, dst):
        u = self.u
        for m in (0, 1):
            mine = both(u.alone, u.mu == m)
            pl.when(mine)(lambda: pltpu.make_async_copy(src.at[pl.ds(0, 4)], dst.at[m], self.local).wait())
            pl.when(jnp.logical_not(mine))(
                lambda: remote(dst.at[m], dst.at[m], self.sems.at[0, 0], self.sems.at[1, m], u.worker(m)).wait_recv()
            )
        for h in (0, 1):
            pl.when(jnp.logical_not(both(u.alone, u.x == h)))(
                lambda: remote(
                    src.at[pl.ds(4 * h, 4)], dst.at[u.mu], self.sems.at[0, h], self.sems.at[1, u.mu], u.keeper(h)
                ).wait_send()
            )


class ColumnShare:
    def __init__(self, u, buf, sems, local):
        self.u, self.buf, self.sems, self.local = u, buf, sems, local
        self.alone = u.c == u.z // 2

    def place(self, z):
        return self.buf.at[z, pl.ds(4 * self.u.x, 4)]

    def cp(self, src, m):
        u = self.u
        return remote(src.at[m], self.place(u.z), self.sems.at[0, m], self.sems.at[1, u.mu], u.column_worker(m))

    def send(self, src):
        u = self.u
        for m in (0, 1):
            mine = both(self.alone, u.mu == m)
            pl.when(mine)(lambda: pltpu.make_async_copy(src.at[m], self.place(u.z), self.local).start())
            pl.when(jnp.logical_not(mine))(lambda: self.cp(src, m).start())

    def wait(self, src):
        u = self.u
        for k in (0, 1):
            mine = both(self.alone, u.mu == k)
            place = self.place(2 * u.c + k)
            pl.when(mine)(lambda: pltpu.make_async_copy(src.at[0], place, self.local).wait())
            pl.when(jnp.logical_not(mine))(
                lambda: remote(place, place, self.sems.at[0, 0], self.sems.at[1, k], u.column_keeper(k)).wait_recv()
            )

    def sent(self, src):
        u = self.u
        for m in (0, 1):
            pl.when(jnp.logical_not(both(self.alone, u.mu == m)))(lambda: self.cp(src, m).wait_send())


class Swap:
    def __init__(self, u, buf, sems):
        self.u, self.buf, self.sems = u, buf, sems

    def cps(self):
        u = self.u
        out = []
        for k in (1, 2, 3):
            out.append((self.buf.at[u.q], self.sems.at[0, k], self.sems.at[1, u.q], u.peer((u.q + k) % 4)))
        return out

    def send(self):
        for ref, s, r, dev in self.cps():
            remote(ref, ref, s, r, dev).start()

    def wait(self):
        u = self.u
        for k in (1, 2, 3):
            p = (u.q + k) % 4
            remote(self.buf.at[p], self.buf.at[p], self.sems.at[0, k], self.sems.at[1, p], u.peer(p)).wait_recv()

    def sent(self):
        for ref, s, r, dev in self.cps():
            remote(ref, ref, s, r, dev).wait_send()

    def total(self):
        return self.buf[0] + self.buf[1] + self.buf[2] + self.buf[3]


class Spread:
    def __init__(self, u, buf, sems, parts):
        self.u, self.buf, self.sems, self.parts = u, buf, sems, parts

    def cp(self, kind, p, part):
        u = self.u
        ref = self.buf.at[p, part]
        device = u.xn if kind == 1 else u.cn
        return remote(ref, ref, self.sems.at[0, kind, part], self.sems.at[1, kind, part], device)

    def send(self, part):
        self.cp(1, self.u.q, part).start()
        self.cp(0, self.u.q, part).start()

    def across(self):
        q = self.u.q
        return q + 1 - 2 * (q % 2)

    def relay(self, part):
        copy = self.cp(1, self.across(), part)
        copy.wait_recv()
        self.cp(2, self.across(), part).start()

    def near(self, part):
        self.cp(0, 3 - self.u.q, part).wait_recv()

    def far(self, part):
        self.cp(2, 3 - self.across(), part).wait_recv()

    def sent(self, part):
        self.cp(1, self.u.q, part).wait_send()
        self.cp(0, self.u.q, part).wait_send()
        self.cp(2, self.across(), part).wait_send()


class Halo:
    def __init__(self, u, buf, sems):
        self.u, self.buf, self.sems = u, buf, sems

    def cp(self, downward):
        u, buf = self.u, self.buf
        if downward:
            return remote(buf.at[1], buf.at[ROW + 1], self.sems.at[0, 0], self.sems.at[1, 0], u.peer(jnp.maximum(u.q - 1, 0)))
        return remote(buf.at[ROW], buf.at[0], self.sems.at[0, 1], self.sems.at[1, 1], u.peer(jnp.minimum(u.q + 1, 3)))

    def send(self):
        u, buf = self.u, self.buf
        pl.when(u.q > 0)(lambda: self.cp(True).start())
        pl.when(u.q < 3)(lambda: self.cp(False).start())

        @pl.when(u.q == 0)
        def _():
            buf[0] = jnp.zeros(buf.shape[1:], buf.dtype)

        @pl.when(u.q == 3)
        def _():
            buf[ROW + 1] = jnp.zeros(buf.shape[1:], buf.dtype)

    def wait(self):
        u = self.u
        pl.when(u.q > 0)(lambda: self.cp(False).wait_recv())
        pl.when(u.q < 3)(lambda: self.cp(True).wait_recv())

    def sent(self):
        u = self.u
        pl.when(u.q > 0)(lambda: self.cp(True).wait_send())
        pl.when(u.q < 3)(lambda: self.cp(False).wait_send())


def canvas_of(rows, limits):
    return (rows >= limits[0:1]).astype(F32) + (rows >= limits[1:2]).astype(F32)


def row_numbers(u, offset, shape):
    return (ROW * u.q + offset + lax.broadcasted_iota(jnp.int32, shape, 0)).astype(F32)


def counts_of(limits, total_rows):
    each = 64.0 * 16.0
    return (limits[0:1] * each, (limits[1:2] - limits[0:1]) * each, (total_rows - limits[1:2]) * each)


def group_total(sums):
    width = sums.shape[1]
    lane = lax.broadcasted_iota(jnp.int32, sums.shape, 1)
    for step in (1, 2, 4, 8):
        after = pltpu.roll(sums, width - step, 1)
        before = pltpu.roll(sums, step, 1)
        sums = sums + jnp.where((lane // step) % 2 == 0, after, before)
    return sums


def canvas_sums(first, second, seg):
    out = []
    for rows in (first, second):
        for k in range(CANVASES):
            out.append(jnp.sum(jnp.where(seg == float(k), rows, 0.0), axis=0, keepdims=True))
    out.append(jnp.zeros((2, first.shape[1]), F32))
    return jnp.concatenate(out, axis=0)


def by_row(values, seg):
    return jnp.where(seg == 0.0, values[0], jnp.where(seg == 1.0, values[1], values[2]))


def moments(total, counts, seg):
    grouped = group_total(total)
    averages, inverses = [], []
    for k in range(CANVASES):
        average = grouped[k : k + 1] / counts[k]
        averages.append(average)
        inverses.append(lax.rsqrt(grouped[3 + k : 4 + k] / counts[k] - average * average + EPSILON))
    return by_row(averages, seg), by_row(inverses, seg)


def sigmoid(argument):
    return 0.5 * jnp.tanh(0.5 * argument) + 0.5


def each_row(body):
    lax.fori_loop(0, ROW, lambda r, carry: (body(r), carry)[1], 0)


def row_of(ref, r):
    return ref[pl.ds(r, 1), :]


def tap_masks(u, limits, masks):
    shape = (ROW, limits.shape[1])
    rows = row_numbers(u, 0, shape)
    seg = canvas_of(rows, limits)
    masks[0] = both(canvas_of(rows - 1.0, limits) == seg, rows >= 1.0).astype(F32)
    masks[1] = both(canvas_of(rows + 1.0, limits) == seg, rows < 4.0 * ROW - 1.0).astype(F32)
    return seg


def shifted(line):
    position = lax.broadcasted_iota(jnp.int32, line.shape, 0)
    width = line.shape[0]
    before = jnp.where(position == 0, 0.0, pltpu.roll(line, 1, 0))
    after = jnp.where(position == width - 1, 0.0, pltpu.roll(line, width - 1, 0))
    return before, line, after


def taps_inner(buf, masks, taps):
    def body(s):
        lines = shifted(buf[s + 1].astype(F32))
        for k in range(3):
            taps[3 + k, s] = lines[k].astype(BF)

        @pl.when(s < ROW - 1)
        def _():
            mask = masks[0, pl.ds(s + 1, 1), :]
            for k in range(3):
                taps[k, s + 1] = (lines[k] * mask).astype(BF)

        @pl.when(s > 0)
        def _():
            mask = masks[1, pl.ds(s - 1, 1), :]
            for k in range(3):
                taps[6 + k, s - 1] = (lines[k] * mask).astype(BF)

    each_row(body)


def taps_outer(buf, masks, taps):
    for k, line in enumerate(shifted(buf[0].astype(F32))):
        taps[k, 0] = (line * masks[0, 0:1, :]).astype(BF)
    for k, line in enumerate(shifted(buf[ROW + 1].astype(F32))):
        taps[6 + k, ROW - 1] = (line * masks[1, ROW - 1 : ROW, :]).astype(BF)


def conv_tile(taps, weight, m, flip):
    total = None
    for tap in range(9):
        left = taps[8 - tap if flip else tap, pl.ds(pl.multiple_of(m * 4, 4), 4)].reshape(256, -1)
        right = weight[tap * 512 : (tap + 1) * 512, :]
        term = cols(left, right) if flip else mm(left, right)
        total = term if total is None else total + term
    return total.reshape(4, 64, -1)


def conv_weight_grad(act_t, taps, out, first, last):
    def body(tap, carry):
        piece = mm(act_t[...], taps[8 - tap].reshape(512, -1))
        out[pl.ds(pl.multiple_of(tap * 512, 512), 512), :] = piece.astype(BF)
        return carry

    lax.fori_loop(first, last, body, 0)


def attn_places(ref, split=0):
    def at(z, x, d, half=None):
        place = ref.at[z * 2 + x]
        lanes = pl.ds(pl.multiple_of(d * 128, 128), 128)
        if half is None:
            return place.at[:, lanes]
        return place.at[pl.ds(half * split, 256 - split if half else split), lanes]

    return at


def param_places(ref):
    def at(z, x, d, half=None):
        place = ref.at[z * 2 + x]
        lanes = pl.ds(pl.multiple_of(d * 128, 128), 128)
        if half is None:
            return place.at[:, lanes]
        return place.at[pl.ds(half * 8, 8), lanes]

    return at


class Halves:
    def __init__(self, ref):
        self.ref = ref

    @property
    def at(self):
        return self

    def __getitem__(self, index):
        member, part = index
        return self.ref.at[member, pl.ds(part * (ROW // 2), ROW // 2)]


ANY = pl.BlockSpec(memory_space=pl.ANY)
VM = pl.BlockSpec(memory_space=pltpu.VMEM)


class Blocks:
    def __init__(self, ref):
        self.ref = ref

    @property
    def at(self):
        return self

    def __getitem__(self, index):
        member, part = index
        x = jnp.where(member < 2, member, 3 - member)
        return self.ref.at[2 * (member // 2) + part, pl.ds(4 * x, 4)]


def unit_inputs(features, bounds, out_grad, norms, conv1, conv2, attn):
    d, b = lax.axis_index("dp"), lax.axis_index("blk")
    limits = jnp.broadcast_to(bounds.reshape(-1).astype(F32)[:, None], (4, 512))
    limits = jnp.concatenate([limits, jnp.zeros((4, 512), F32)])
    rows = jnp.stack([item.astype(F32) for item in norms])
    mine = jnp.where(d == b // 2, rows, 0.0)
    params = jnp.concatenate([jnp.where(b % 2 == 0, mine, 0.0), jnp.where(b % 2 == 1, mine, 0.0)], axis=1)
    params = jnp.concatenate([params, jnp.zeros((PARAMS - 6, 128), F32)])
    return (features[0], out_grad[0], limits, params, conv1, conv2, jnp.concatenate(attn))


def whole_kernel(
    feat, grad, bounds, par, s1, s2, sa,
    act_back, grad_back, g1_out, g2_out, ga_out, norm_out,
    w1, w2, wa, pb, bb, xin, oall, nall, taps, a1, a2, masks, hidden, resid, small, rows_a, rows_b, swaps, lds,
    wg1, wg2, scores, gk, gv, lcol, dcol, big, gres, low, act, act_t1, act_t2, ga, mine, psum_y, psum_z,
    core_a, core_2, half_a, rest_a, side_a, last_a, half_2, rest_2, side_2, last_2, half_1, rest_1, side_1, last_1,
    gsems, ssems, local, share_sems, bound_sems, swap_sems, spread_sems, halo_sems, py_sems, pz_sems,
):
    u = Unit()
    u.enter(True, True)
    mine[...] = jnp.zeros_like(mine)
    table = {}
    ats = (weight_places(w1, 576, SPLIT), weight_places(w2, 576, SPLIT), attn_places(wa, SPLIT_A), param_places(pb))
    groups = [Gather(u, 4, at, gsems.at[k], DIRECT[k]) for k, at in enumerate(ats)]
    for name, group in zip(("g1", "g2", "ga", "gp"), groups):
        table.update(group.table(name))
    sources = (s1, s2, sa, par)
    own = [pltpu.make_async_copy(src, group.own(u.z), local.at[k]) for k, (src, group) in enumerate(zip(sources, groups))]
    for copy in own:
        copy.start()
    keep = pltpu.make_async_copy(bounds, bb.at[u.c], local.at[4])
    keep.start()
    share_x, share_a, share_g = [Share(u, share_sems.at[k], local.at[5 + k]) for k in range(3)]
    share_o = ColumnShare(u, oall, share_sems.at[3], local.at[8])
    swap = [Swap(u, swaps.at[k], swap_sems.at[k]) for k in range(6)] + [Swap(u, lds, swap_sems.at[6])]
    halo = [Halo(u, (a1, a2)[k % 2], halo_sems.at[k]) for k in range(4)]
    spread_o = Spread(u, Blocks(oall), spread_sems.at[0], 2)
    spread_n = Spread(u, Halves(nall), spread_sems.at[1], 2)

    w2_at = weight_places(w2, 576)
    part_a = lambda ref, h: part_of(ref, h, CUT_A, 256)
    part_w = lambda ref, h: part_of(ref, h, CUT, 576)
    sum_a = Scatter(
        u, 4, attn_places(ga), lambda k, z, x, d: core_a.at[k, z], part_a, ssems.at[0], ((half_a, rest_a), side_a, last_a)
    )
    sum_2 = Scatter(
        u, 4, weight_places(wg2, 576), lambda k, z, x, d: core_2.at[k, z], part_w, ssems.at[1], ((half_2, rest_2), side_2, last_2)
    )
    sum_1 = Scatter(
        u, 4, weight_places(wg1, 576), lambda k, z, x, d: w2_at(z, x, d), part_w, ssems.at[2], ((half_1, rest_1), side_1, last_1)
    )
    for name, total, out in (("ra", sum_a, ga_out), ("r2", sum_2, g2_out), ("r1", sum_1, g1_out)):
        table.update(total.table(name, out))
    bound_cp = remote(bounds, bb.at[u.c], bound_sems.at[0], bound_sems.at[1], u.cn)
    state = {}

    def step(function):
        table[function.__name__] = function
        return function


    @step
    def xs():
        share_x.send(feat, xin)
        bound_cp.start()

    @step
    def os():
        share_o.send(grad)

    @step
    def ow():
        for copy in own:
            copy.wait()

    @step
    def bw():
        keep.wait()
        remote(bounds, bb.at[1 - u.c], bound_sems.at[0], bound_sems.at[1], u.cn).wait_recv()
        limits = jnp.where(u.mu == 0, bb[u.z // 2, 0:2, :], bb[u.z // 2, 2:4, :])
        small[7] = jnp.concatenate([limits, jnp.zeros((6, limits.shape[1]), F32)], axis=0)
        state["seg"] = tap_masks(u, limits, masks)
        state["counts"] = counts_of(limits, 4.0 * ROW)

    def first(r):
        return xin[r].astype(F32)

    def second(r):
        return hidden[r]

    def third(r):
        return resid[r]

    values = (first, second, third)

    def norm_sums(k):
        def body(r):
            line = values[k](r)
            rows_a[pl.ds(r, 1), :] = jnp.sum(line, axis=0, keepdims=True)
            rows_b[pl.ds(r, 1), :] = jnp.sum(line * line, axis=0, keepdims=True)

        each_row(body)
        swap[k].buf[u.q] = canvas_sums(rows_a[...], rows_b[...], state["seg"])
        swap[k].send()

    def norm_stats(k):
        swap[k].wait()
        average, inverse = moments(swap[k].total(), state["counts"], state["seg"])
        small[2 * k] = average
        small[2 * k + 1] = inverse

    def param(j):
        return small[6, j : j + 1, :]

    def xhat(k, r):
        return (values[k](r) - small[2 * k, pl.ds(r, 1), :]) * small[2 * k + 1, pl.ds(r, 1), :]

    def normal(k, r):
        return xhat(k, r) * param(2 * k) + param(2 * k + 1)

    def activate(k, buf):
        def body(r):
            line = normal(k, r)
            buf[r + 1] = (line * sigmoid(line)).astype(BF)

        each_row(body)

    @step
    def n1a():
        share_x.wait(feat, xin)
        norm_sums(0)

    @step
    def n1b():
        groups[3].arrive()
        total = pb[0, 0:8, :]
        for b in range(1, 8):
            total = total + pb[b, 0:8, :]
        small[6] = total
        norm_stats(0)

    def conv_steps(name, k, buf):
        def c():
            activate(k, buf)
            halo[k].send()

        def d():
            taps_inner(buf, masks, taps)

        def e():
            halo[k].wait()
            taps_outer(buf, masks, taps)
            halo[k].sent()

        table[name + "c"], table[name + "d"], table[name + "e"] = c, d, e

    conv_steps("n1", 0, a1)
    conv_steps("n2", 1, a2)

    @step
    def t1():
        act_t1[...] = a1[1 : ROW + 1].reshape(512, 512).T

    @step
    def t2():
        act_t2[...] = a2[1 : ROW + 1].reshape(512, 512).T

    def first_conv(m):
        hidden[4 * m : 4 * m + 4] = conv_tile(taps, w1, m, False)

    def second_conv(m):
        resid[4 * m : 4 * m + 4] = conv_tile(taps, w2, m, False) + xin[4 * m : 4 * m + 4].astype(F32)

    for m in (0, 1):
        table["c1%d" % m] = functools.partial(first_conv, m)
        table["c2%d" % m] = functools.partial(second_conv, m)
    table["n2a"], table["n2b"] = functools.partial(norm_sums, 1), functools.partial(norm_stats, 1)
    table["n3a"], table["n3b"] = functools.partial(norm_sums, 2), functools.partial(norm_stats, 2)

    @step
    def n3c():
        def row(r):
            nall[u.q, r] = normal(2, r).astype(BF)

        for part in range(2):
            lax.fori_loop(4 * part, 4 * part + 4, lambda r, carry: (row(r), carry)[1], 0)
            spread_n.send(part)

    @step
    def ob():
        share_o.wait(grad)
        for part in range(2):
            spread_o.send(part)

    for part in (0, 1):
        table["or%d" % part] = functools.partial(spread_o.relay, part)
        table["nr%d" % part] = functools.partial(spread_n.relay, part)

    scale = 512.0 ** (-0.5)

    def slot(ref, i):
        return ref.at[pl.ds(pl.multiple_of(i * 512, 512), 512)]

    def query_of(i):
        return slot(wg1, i)

    def key_of(i):
        return slot(wg1, 4 + i)

    def value_of(i):
        return slot(wg2, i)

    def upstream_of(i):
        return slot(wg2, 4 + i)

    heads, gq = slot(wg1, 8), slot(wg2, 8)

    def matrix(k):
        return wa[:, pl.ds(k * 64, 64), :].reshape(512, 512)

    across = u.q + 1 - 2 * (u.q % 2)
    members = (u.q, 3 - u.q, across, 3 - across)

    def project(k):
        if k in (1, 3):
            for part in range(2):
                (spread_n.near if k == 1 else spread_n.far)(part)
        tokens = nall[members[k]].reshape(512, 512)
        query_of(members[k])[...] = mm(tokens, matrix(0)).astype(BF)
        key_of(members[k])[...] = mm(tokens, matrix(1)).astype(BF)
        value_of(members[k])[...] = mm(tokens, matrix(2)).astype(BF)

    def project_up(k):
        if k == 1:
            for part in range(2):
                spread_o.near(part)
                spread_o.far(part)
        upstream = oall[members[k]].reshape(512, 512)
        upstream_of(members[k])[...] = cols(upstream, matrix(3)).astype(BF)

    for k in range(4):
        table["pj%d" % k] = functools.partial(project, k)
        table["po%d" % k] = functools.partial(project_up, k)

    def canvas(rows):
        return (rows >= small[7, 0:1, 0:1]).astype(F32) + (rows >= small[7, 1:2, 0:1]).astype(F32)

    def seg_col(q, offset, count):
        token = offset + lax.broadcasted_iota(jnp.int32, (count, 1), 0)
        return canvas((ROW * q + token // 64).astype(F32))

    def seg_row(q):
        token = lax.broadcasted_iota(jnp.int32, (1, 512), 1)
        return canvas((ROW * q + token // 64).astype(F32))

    def kept(j, i):
        return taps.at[i, pl.ds(pl.multiple_of(j * 4, 4), 4)]

    def queries(j, carry):
        block = pl.ds(pl.multiple_of(j * 256, 256), 256)
        query = query_of(u.q)[block]
        seg = seg_col(u.q, j * 256, 256)
        most = jnp.full((256, 1), NEGATIVE, F32)
        for i in range(4):
            part = jnp.where(seg == seg_row(i), cols(query, key_of(i)[...]) * scale, NEGATIVE)
            scores[i] = part
            most = jnp.maximum(most, jnp.max(part, axis=1, keepdims=True))
        total = jnp.zeros((256, 1), F32)
        for i in range(4):
            part = jnp.exp(scores[i] - most)
            total = total + jnp.sum(part, axis=1, keepdims=True)
            scores[i] = part
        inverse = 1.0 / total
        found = jnp.zeros((256, 512), F32)
        for i in range(4):
            part = (scores[i] * inverse).astype(BF)
            kept(j, i)[...] = part.reshape(4, 64, 512)
            found = found + mm(part, value_of(i)[...])
        heads[block, :] = found.astype(BF)
        lcol[block, :] = jnp.broadcast_to(most + jnp.log(total), (256, 128))
        return carry

    @step
    def qf():
        lax.fori_loop(0, 2, queries, 0)

    def queries_back(j, carry):
        block = pl.ds(pl.multiple_of(j * 256, 256), 256)
        upstream = upstream_of(u.q)[block]
        correction = jnp.zeros((256, 1), F32)
        for i in range(4):
            slope = cols(upstream, value_of(i)[...])
            scores[i] = slope
            part = kept(j, i)[...].reshape(256, 512).astype(F32)
            correction = correction + jnp.sum(part * slope, axis=1, keepdims=True)
        back = jnp.zeros((256, 512), F32)
        for i in range(4):
            part = kept(j, i)[...].reshape(256, 512).astype(F32)
            back = back + mm((part * (scores[i] - correction)).astype(BF), key_of(i)[...])
        gq[block, :] = (back * scale).astype(BF)
        dcol[block, :] = jnp.broadcast_to(correction, (256, 128))
        return carry

    @step
    def qb():
        lax.fori_loop(0, 2, queries_back, 0)
        lds[u.q] = jnp.concatenate([lcol[...].T[0:1], dcol[...].T[0:1], jnp.zeros((6, 512), F32)], axis=0)
        swap[6].send()

    @step
    def gz():
        for group in groups:
            group.finish()

    @step
    def hd():
        act[...] = (resid[...] + mm(heads[...], matrix(3)).reshape(ROW, 64, 512)).astype(BF)
        share_a.back(act, act_back)

    @step
    def hw():
        ga[:, 192:256, :] = mm(heads[...].T, oall[u.q].reshape(512, 512)).astype(BF).reshape(8, 64, 512)

    def keys(index, carry):
        i, j = index // 2, index % 2
        block = pl.ds(pl.multiple_of(j * 256, 256), 256)
        key, value = key_of(u.q)[block], value_of(u.q)[block]
        query, upstream = query_of(i)[...], upstream_of(i)[...]
        shared = seg_col(u.q, j * 256, 256) == seg_row(i)
        part = jnp.where(shared, cols(key, query) * scale, NEGATIVE)
        part = jnp.where(shared, jnp.exp(part - lds[i, 0:1, :]), 0.0)
        rows = pl.ds(pl.multiple_of(j * 4, 4), 4)
        gres[rows] += mm(part.astype(BF), upstream).reshape(4, 64, 512)
        slope = cols(value, upstream) - lds[i, 1:2, :]
        big[rows] += mm((part * slope).astype(BF), query).reshape(4, 64, 512)
        return carry

    @step
    def ks():
        big[...] = jnp.zeros_like(big)
        gres[...] = jnp.zeros_like(gres)
        swap[6].wait()
        lax.fori_loop(0, 8, keys, 0)
        gk[...] = (big[...] * scale).astype(BF).reshape(512, 512)
        gv[...] = gres[...].astype(BF).reshape(512, 512)

    @step
    def aw():
        tokens = nall[u.q].reshape(512, 512).T
        for k, part in enumerate((gq, gk, gv)):
            ga[:, k * 64 : (k + 1) * 64, :] = mm(tokens, part[...]).astype(BF).reshape(8, 64, 512)

    @step
    def an():
        total = None
        for k, part in enumerate((gq, gk, gv)):
            term = cols(part[...], matrix(k))
            total = term if total is None else total + term
        big[...] = total.reshape(ROW, 64, 512)


    def back_sums(k, slope):
        def body(r):
            line = big[r]
            if slope:
                value = normal(k, r)
                part = sigmoid(value)
                line = line * (part * (1.0 + value * (1.0 - part)))
                big[r] = line
            rows_a[pl.ds(r, 1), :] = jnp.sum(line, axis=0, keepdims=True)
            rows_b[pl.ds(r, 1), :] = jnp.sum(line * xhat(k, r), axis=0, keepdims=True)

        each_row(body)
        swap[3 + k].buf[u.q] = canvas_sums(rows_a[...], rows_b[...], state["seg"])
        swap[3 + k].send()

    def back_means(k):
        swap[3 + k].wait()
        total = swap[3 + k].total()
        mine[2 * k : 2 * k + 1, :] = jnp.sum(total[3:6], axis=0, keepdims=True)
        mine[2 * k + 1 : 2 * k + 2, :] = jnp.sum(total[0:3], axis=0, keepdims=True)
        grouped = group_total(total * param(2 * k))
        counts, seg = state["counts"], state["seg"]
        rows_a[...] = by_row([grouped[j : j + 1] / counts[j] for j in range(3)], seg)
        rows_b[...] = by_row([grouped[3 + j : 4 + j] / counts[j] for j in range(3)], seg)

    def back(k, r):
        line = big[r] * param(2 * k) - row_of(rows_a, r) - xhat(k, r) * row_of(rows_b, r)
        return line * small[2 * k + 1, pl.ds(r, 1), :]

    @step
    def b3a():
        back_sums(2, False)

    @step
    def b3b():
        back_means(2)

        def row(r):
            line = oall[u.q, r].astype(F32) + back(2, r)
            gres[r] = line
            a2[r + 1] = line.astype(BF)

        each_row(row)
        halo[3].send()

    @step
    def b2a():
        back_sums(1, True)

    @step
    def b2b():
        back_means(1)

        def row(r):
            a1[r + 1] = back(1, r).astype(BF)

        each_row(row)
        halo[2].send()

    @step
    def b1a():
        back_sums(0, True)

    @step
    def b1m():
        back_means(0)

    @step
    def b1b():
        def row(r):
            low[r] = (gres[r] + back(0, r)).astype(BF)

        each_row(row)
        share_g.back(low, grad_back)

    @step
    def ps():
        remote(mine, psum_y, py_sems.at[0], py_sems.at[1], u.yn).start()

    def back_taps(name, k, buf):
        def c():
            taps_inner(buf, masks, taps)

        def d():
            halo[k].wait()
            taps_outer(buf, masks, taps)
            halo[k].sent()

        table[name + "c"], table[name + "d"] = c, d

    back_taps("b3", 3, a2)
    back_taps("b2", 2, a1)

    def tile_back(weight, m):
        big[4 * m : 4 * m + 4] = conv_tile(taps, weight, m, True)

    for m in (0, 1):
        table["d2%d" % m] = functools.partial(tile_back, w2, m)
        table["d1%d" % m] = functools.partial(tile_back, w1, m)
    for k in range(3):
        table["w2%d" % k] = functools.partial(conv_weight_grad, act_t2, taps, wg2, 3 * k, 3 * k + 3)
        table["w1%d" % k] = functools.partial(conv_weight_grad, act_t1, taps, wg1, 3 * k, 3 * k + 3)

    def line_cp(k):
        return remote(psum_z.at[u.z], psum_z.at[u.z], pz_sems.at[0, k], pz_sems.at[1, u.z], u.line(k))

    @step
    def py():
        remote(mine, psum_y, py_sems.at[0], py_sems.at[1], u.yn).wait()
        psum_z[u.z] = mine[...] + psum_y[...]
        for k in (1, 2, 3):
            line_cp(k).start()

    @step
    def pz():
        for k in (1, 2, 3):
            other = (u.z + k) % 4
            remote(psum_z.at[other], psum_z.at[other], pz_sems.at[0, k], pz_sems.at[1, other], u.line(k)).wait_recv()
        norm_out[...] = psum_z[0] + psum_z[1] + psum_z[2] + psum_z[3]

    in_order(types.SimpleNamespace(**table))

    share_a.back_wait(act, act_back)
    share_g.back_wait(low, grad_back)
    for total in (sum_a, sum_2, sum_1):
        total.finish()
    bound_cp.wait_send()
    share_x.sent(feat, xin)
    share_o.sent(grad)
    for item in swap:
        item.sent()
    for item in (spread_o, spread_n):
        for part in range(2):
            item.sent(part)
    for k in (1, 2, 3):
        line_cp(k).wait_send()


def whole_call(features, out_grad, limits, params, s1, s2, sa):
    full = lambda shape, kind: jax.ShapeDtypeStruct(shape, kind)
    dma = pltpu.SemaphoreType.DMA
    rows, padded, square, weight = (ROW, 64, 512), (ROW + 2, 64, 512), (512, 512), (4608, 512)
    low = lambda *shape: pltpu.VMEM(shape, BF)
    wide = lambda *shape: pltpu.VMEM(shape, F32)
    sums = []
    for r, cut in ((256, CUT_A), (576, CUT), (576, CUT)):
        sums += [low(4, cut, 128), low(4, r - cut, 128), low(2, 4, r, 128), low(4, r, 128)]
    return pl.pallas_call(
        whole_kernel,
        out_shape=[
            full((2, 4, 64, 512), BF), full((2, 4, 64, 512), BF), full((576, 128), F32), full((576, 128), F32),
            full((256, 128), F32), full((8, 512), F32),
        ],
        in_specs=[ANY] * 7,
        out_specs=[VM] * 6,
        scratch_shapes=[
            low(*weight), low(*weight), low(8, 256, 512), wide(8, PARAMS, 512), wide(2, 8, 512), low(*rows),
            low(4, *rows), low(4, *rows), low(9, *rows), low(*padded), low(*padded), wide(2, ROW, 512),
            wide(*rows), wide(*rows), wide(8, 8, 512), wide(ROW, 512), wide(ROW, 512), wide(6, 4, 8, 512), wide(4, 8, 512),
            low(*weight), low(*weight), wide(4, 256, 512), low(*square), low(*square),
            wide(512, 128), wide(512, 128), wide(*rows), wide(*rows), low(*rows), low(*rows), low(*square), low(*square),
            low(8, 256, 512), wide(8, 512), wide(8, 512), wide(4, 8, 512),
            low(4, 4, 256, 128), low(4, 4, 576, 128), *sums,
            dma((4, 2, Gather.SEMS)), dma((3, 2, Scatter.SEMS)), dma((9,)), dma((4, 2, 2)), dma((2,)), dma((7, 2, 4)),
            dma((2, 2, 3, 2)), dma((4, 2, 2)), dma((2,)), dma((2, 4)),
        ],
        compiler_params=pltpu.CompilerParams(collective_id=0, has_side_effects=True, vmem_limit_bytes=LIMIT),
    )(features, out_grad, limits, params, s1, s2, sa)


def unit_shards(
    features, bounds, out_grad, norm1_gain, norm1_shift, conv1_weight, norm2_gain, norm2_shift, conv2_weight,
    norm3_gain, norm3_shift, query_weight, key_weight, value_weight, output_weight,
):
    norms = (norm1_gain, norm1_shift, norm2_gain, norm2_shift, norm3_gain, norm3_shift)
    attn = (query_weight, key_weight, value_weight, output_weight)
    act_back, grad_back, g1, g2, ga, norms = whole_call(
        *unit_inputs(features, bounds, out_grad, norms, conv1_weight, conv2_weight, attn)
    )
    norms = lax.dynamic_slice_in_dim(norms, lax.axis_index("blk") * 64, 64, axis=1)
    ga = ga.reshape(4, 64, 128)
    return (
        act_back.astype(F32)[None], grad_back.astype(F32)[None], norms[0], norms[1], g1, norms[2], norms[3], g2,
        norms[4], norms[5], ga[0], ga[1], ga[2], ga[3],
    )


def extended(shard, sides, width):
    for axis, dim in sides:
        devices, length = (lax.axis_size(axis), shard.shape[dim])
        up = [(i, (i + 1) % devices) for i in range(devices - 1)]
        down = [(j, i) for i, j in up]
        last = lax.slice_in_dim(shard, length - width, length, axis=dim)
        initial = lax.slice_in_dim(shard, 0, width, axis=dim)
        before = lax.ppermute(last, axis, up)
        after = lax.ppermute(initial, axis, down)
        shard = jnp.concatenate([before, shard, after], axis=dim)
    return shard


def canvas_index(global_rows, first_row, second_row):
    return (global_rows >= first_row).astype(jnp.int32) + (global_rows >= second_row).astype(
        jnp.int32
    )


def swish(argument):
    return argument * jax.nn.sigmoid(argument)


def swish_slope(argument):
    sigmoid_value = jax.nn.sigmoid(argument)
    return sigmoid_value * (1.0 + argument * (1.0 - sigmoid_value))


def group_sums(member, grouped):
    return jnp.einsum("rk,rwgc->kg", member, grouped, precision=HIGHEST)


def spread_rows(member, lookup):
    return jnp.dot(member, lookup, precision=HIGHEST)


def norm_forward(inputs, member, counts, norm_gain, norm_shift):
    row_count, width, channels = inputs.shape
    grouped = inputs.reshape(row_count, width, GROUPS, channels // GROUPS)
    totals, square = lax.psum(
        (group_sums(member, grouped), group_sums(member, grouped * grouped)), "blk"
    )
    average = totals / counts[:, None]
    inverse = lax.rsqrt(square / counts[:, None] - average * average + EPSILON)
    average_rows = spread_rows(member, average)
    scale_rows = spread_rows(member, inverse)
    normal = (grouped - average_rows[:, None, :, None]) * scale_rows[:, None, :, None]
    normal = normal.reshape(row_count, width, channels)
    return (normal * norm_gain + norm_shift, normal, scale_rows)


def norm_backward(incoming, normal, scale_rows, member, counts, norm_gain):
    row_count, width, channels = incoming.shape
    gain_grad = jnp.sum(incoming * normal, axis=(0, 1))
    shift_grad = jnp.sum(incoming, axis=(0, 1))
    scaled = (incoming * norm_gain).reshape(row_count, width, GROUPS, channels // GROUPS)
    grouped_normal = normal.reshape(row_count, width, GROUPS, channels // GROUPS)
    first_sum, second_sum = lax.psum(
        (group_sums(member, scaled), group_sums(member, scaled * grouped_normal)), "blk"
    )
    first_rows = spread_rows(member, first_sum / counts[:, None])
    second_rows = spread_rows(member, second_sum / counts[:, None])
    result = scale_rows[:, None, :, None] * (
        scaled - first_rows[:, None, :, None] - grouped_normal * second_rows[:, None, :, None]
    )
    return (result.reshape(row_count, width, channels), gain_grad, shift_grad)


def gather_taps(padded, seg_pad, seg_rows, direction):
    row_count = seg_rows.shape[0]
    width = padded.shape[1]
    widened = jnp.pad(padded, ((0, 0), (1, 1), (0, 0)))
    pieces = []
    for step_row in (-1, 0, 1):
        low_row = 1 + direction * step_row
        allowed = (seg_pad[low_row : low_row + row_count] == seg_rows).astype(padded.dtype)[
            :, None, None
        ]
        for step_col in (-1, 0, 1):
            low_col = 1 + direction * step_col
            pieces.append(
                widened[low_row : low_row + row_count, low_col : low_col + width, :] * allowed
            )
    return jnp.stack(pieces, axis=2)


def conv_apply(activation, seg_pad, seg_rows, weight_matrix):
    row_count, width, channels = activation.shape
    padded = extended(activation, (("blk", 0),), 1)
    stacked = gather_taps(padded, seg_pad, seg_rows, 1).reshape(row_count * width, 9 * channels)
    result = jnp.dot(stacked, weight_matrix, preferred_element_type=jnp.float32)
    return (result.reshape(row_count, width, channels), stacked)


def conv_reverse(gradient, stacked, seg_pad, seg_rows, weight_matrix):
    row_count, width, channels = gradient.shape
    flattened = gradient.reshape(row_count * width, channels)
    weight_grad = lax.dot_general(
        stacked, flattened, (((0,), (0,)), ((), ())), preferred_element_type=jnp.float32
    )
    padded = extended(gradient, (("blk", 0),), 1)
    mirrored = gather_taps(padded, seg_pad, seg_rows, -1).reshape(row_count * width, 9, channels)
    kernel = weight_matrix.reshape(9, channels, channels)
    result = lax.dot_general(
        mirrored, kernel, (((1, 2), (0, 2)), ((), ())), preferred_element_type=jnp.float32
    )
    return (result.reshape(row_count, width, channels), weight_grad)


def attention_forward(
    queries, keys_local, values_local, token_seg, first_row, second_row, width, scale
):
    token_count, channels = queries.shape

    def absorb(running, portion, offset):
        key_block, value_block = portion
        maximum, totals, accumulated = running
        key_seg = canvas_index(
            jnp.arange(key_block.shape[0], dtype=jnp.int32) // width, first_row, second_row
        )
        shared = token_seg[:, None] == key_seg[None, :]
        scores = (
            lax.dot_general(
                queries, key_block, (((1,), (1,)), ((), ())), preferred_element_type=jnp.float32
            )
            * scale
        )
        masked = jnp.where(shared, scores, NEGATIVE)
        new_maximum = jnp.maximum(maximum, jnp.max(masked, axis=1))
        weights = jnp.where(shared, jnp.exp(masked - new_maximum[:, None]), 0.0)
        totals = jnp.sum(weights, axis=1)
        accumulated = jnp.dot(
            weights.astype(jnp.bfloat16), value_block, preferred_element_type=jnp.float32
        )
        return (new_maximum, totals, accumulated)

    initial = (
        jnp.full((token_count,), NEGATIVE, jnp.float32),
        jnp.zeros((token_count,), jnp.float32),
        jnp.zeros((token_count, channels), jnp.float32),
    )
    maximum, totals, accumulated = absorb(
        initial,
        (
            lax.all_gather(keys_local, "blk", axis=0, tiled=True),
            lax.all_gather(values_local, "blk", axis=0, tiled=True),
        ),
        jnp.int32(0),
    )
    return (accumulated / totals[:, None], maximum + jnp.log(totals))


def attention_query_grad(
    queries,
    heads_grad,
    log_total,
    correction,
    keys_local,
    values_local,
    token_seg,
    first_row,
    second_row,
    width,
    scale,
):

    def absorb(running, portion, offset):
        key_block, value_block = portion
        key_seg = canvas_index(
            jnp.arange(key_block.shape[0], dtype=jnp.int32) // width, first_row, second_row
        )
        shared = token_seg[:, None] == key_seg[None, :]
        scores = (
            lax.dot_general(
                queries, key_block, (((1,), (1,)), ((), ())), preferred_element_type=jnp.float32
            )
            * scale
        )
        weights = jnp.where(
            shared, jnp.exp(jnp.where(shared, scores, NEGATIVE) - log_total[:, None]), 0.0
        )
        slopes = lax.dot_general(
            heads_grad, value_block, (((1,), (1,)), ((), ())), preferred_element_type=jnp.float32
        )
        score_grad = (weights * (slopes - correction[:, None])).astype(jnp.bfloat16)
        return jnp.dot(score_grad, key_block, preferred_element_type=jnp.float32) * scale

    return absorb(
        jnp.zeros(queries.shape, jnp.float32),
        (
            lax.all_gather(keys_local, "blk", axis=0, tiled=True),
            lax.all_gather(values_local, "blk", axis=0, tiled=True),
        ),
        jnp.int32(0),
    )


def attention_key_grad(
    queries,
    heads_grad,
    log_total,
    correction,
    keys_local,
    values_local,
    token_seg,
    first_row,
    second_row,
    width,
    scale,
):

    def absorb(running, portion, offset):
        query_part, upstream_part, total_part, correct_part = portion
        query_seg = canvas_index(
            jnp.arange(query_part.shape[0], dtype=jnp.int32) // width, first_row, second_row
        )
        query_low = query_part.astype(jnp.bfloat16)
        upstream_low = upstream_part.astype(jnp.bfloat16)
        shared = query_seg[:, None] == token_seg[None, :]
        scores = (
            lax.dot_general(
                query_low, keys_local, (((1,), (1,)), ((), ())), preferred_element_type=jnp.float32
            )
            * scale
        )
        weights = jnp.where(
            shared, jnp.exp(jnp.where(shared, scores, NEGATIVE) - total_part[:, None]), 0.0
        )
        value_acc = lax.dot_general(
            weights.astype(jnp.bfloat16),
            upstream_low,
            (((0,), (0,)), ((), ())),
            preferred_element_type=jnp.float32,
        )
        slopes = lax.dot_general(
            upstream_low, values_local, (((1,), (1,)), ((), ())), preferred_element_type=jnp.float32
        )
        score_grad = (weights * (slopes - correct_part[:, None])).astype(jnp.bfloat16)
        key_acc = (
            lax.dot_general(
                score_grad, query_low, (((0,), (0,)), ((), ())), preferred_element_type=jnp.float32
            )
            * scale
        )
        return (key_acc, value_acc)

    empty = jnp.zeros(keys_local.shape, jnp.float32)
    return absorb(
        (empty, empty),
        (
            lax.all_gather(queries.astype(jnp.float32), "blk", axis=0, tiled=True),
            lax.all_gather(heads_grad.astype(jnp.float32), "blk", axis=0, tiled=True),
            lax.all_gather(log_total, "blk", axis=0, tiled=True),
            lax.all_gather(correction, "blk", axis=0, tiled=True),
        ),
        jnp.int32(0),
    )


def collect(
    conv1_weight,
    conv2_weight,
    query_weight,
    key_weight,
    value_weight,
    output_weight,
    norm1_gain,
    norm1_shift,
    norm2_gain,
    norm2_shift,
    norm3_gain,
    norm3_shift,
):
    row_parts = (
        lax.all_gather(conv1_weight, "blk", axis=0, tiled=True),
        lax.all_gather(conv2_weight, "blk", axis=0, tiled=True),
        lax.all_gather(query_weight, "blk", axis=0, tiled=True),
        lax.all_gather(key_weight, "blk", axis=0, tiled=True),
        lax.all_gather(value_weight, "blk", axis=0, tiled=True),
        lax.all_gather(output_weight, "blk", axis=0, tiled=True),
        lax.all_gather(norm1_gain, "blk", axis=0, tiled=True),
        lax.all_gather(norm1_shift, "blk", axis=0, tiled=True),
        lax.all_gather(norm2_gain, "blk", axis=0, tiled=True),
        lax.all_gather(norm2_shift, "blk", axis=0, tiled=True),
        lax.all_gather(norm3_gain, "blk", axis=0, tiled=True),
        lax.all_gather(norm3_shift, "blk", axis=0, tiled=True),
    )
    full_parts = (
        lax.all_gather(row_parts[0], "dp", axis=1, tiled=True),
        lax.all_gather(row_parts[1], "dp", axis=1, tiled=True),
        lax.all_gather(row_parts[2], "dp", axis=1, tiled=True),
        lax.all_gather(row_parts[3], "dp", axis=1, tiled=True),
        lax.all_gather(row_parts[4], "dp", axis=1, tiled=True),
        lax.all_gather(row_parts[5], "dp", axis=1, tiled=True),
    )
    return (tuple(full_parts), tuple(row_parts[6:]))


def reduce_all(gradients):
    row_sums = (
        lax.psum_scatter(gradients[0], "blk", scatter_dimension=0, tiled=True),
        lax.psum_scatter(gradients[1], "blk", scatter_dimension=0, tiled=True),
        lax.psum_scatter(gradients[2], "blk", scatter_dimension=0, tiled=True),
        lax.psum_scatter(gradients[3], "blk", scatter_dimension=0, tiled=True),
        lax.psum_scatter(gradients[4], "blk", scatter_dimension=0, tiled=True),
        lax.psum_scatter(gradients[5], "blk", scatter_dimension=0, tiled=True),
        lax.psum_scatter(gradients[6], "blk", scatter_dimension=0, tiled=True),
        lax.psum_scatter(gradients[7], "blk", scatter_dimension=0, tiled=True),
        lax.psum_scatter(gradients[8], "blk", scatter_dimension=0, tiled=True),
        lax.psum_scatter(gradients[9], "blk", scatter_dimension=0, tiled=True),
        lax.psum_scatter(gradients[10], "blk", scatter_dimension=0, tiled=True),
        lax.psum_scatter(gradients[11], "blk", scatter_dimension=0, tiled=True),
    )
    matrix_sums = (
        lax.psum_scatter(row_sums[0], "dp", scatter_dimension=1, tiled=True),
        lax.psum_scatter(row_sums[1], "dp", scatter_dimension=1, tiled=True),
        lax.psum_scatter(row_sums[2], "dp", scatter_dimension=1, tiled=True),
        lax.psum_scatter(row_sums[3], "dp", scatter_dimension=1, tiled=True),
        lax.psum_scatter(row_sums[4], "dp", scatter_dimension=1, tiled=True),
        lax.psum_scatter(row_sums[5], "dp", scatter_dimension=1, tiled=True),
    )
    norm_sums = lax.psum(
        (row_sums[6], row_sums[7], row_sums[8], row_sums[9], row_sums[10], row_sums[11]), "dp"
    )
    return tuple(matrix_sums) + tuple(norm_sums)


def one_batch(inputs_low, bound_pair, upstream_low, matrices, norm_params, position, blocks):
    row_count, width, channels = inputs_low.shape
    token_count = row_count * width
    total_rows = row_count * blocks
    scale = channels ** (-0.5)
    first_row = bound_pair[0]
    second_row = bound_pair[1]
    local_rows = position * row_count + jnp.arange(row_count, dtype=jnp.int32)
    padded_rows = position * row_count - 1 + jnp.arange(row_count + 2, dtype=jnp.int32)
    seg_rows = canvas_index(local_rows, first_row, second_row)
    seg_pad = canvas_index(padded_rows, first_row, second_row)
    member = (seg_rows[:, None] == jnp.arange(CANVASES, dtype=jnp.int32)[None, :]).astype(
        jnp.float32
    )
    counts = jnp.stack([first_row, second_row - first_row, total_rows - second_row]).astype(
        jnp.float32
    ) * float(width * (channels // GROUPS))
    gains = [item.astype(jnp.float32) for item in norm_params]
    inputs = inputs_low.astype(jnp.float32)
    norm_one, normal_one, scale_one = norm_forward(inputs, member, counts, gains[0], gains[1])
    act_one = swish(norm_one).astype(jnp.bfloat16)
    hidden_one, stacked_one = conv_apply(act_one, seg_pad, seg_rows, matrices[0])
    norm_two, normal_two, scale_two = norm_forward(hidden_one, member, counts, gains[2], gains[3])
    act_two = swish(norm_two).astype(jnp.bfloat16)
    hidden_two, stacked_two = conv_apply(act_two, seg_pad, seg_rows, matrices[1])
    residual = inputs + hidden_two
    norm_three, normal_three, scale_three = norm_forward(
        residual, member, counts, gains[4], gains[5]
    )
    normed = norm_three.astype(jnp.bfloat16).reshape(token_count, channels)
    queries = jnp.dot(normed, matrices[2], preferred_element_type=jnp.float32).astype(jnp.bfloat16)
    keys_local = jnp.dot(normed, matrices[3], preferred_element_type=jnp.float32).astype(
        jnp.bfloat16
    )
    values_local = jnp.dot(normed, matrices[4], preferred_element_type=jnp.float32).astype(
        jnp.bfloat16
    )
    token_seg = jnp.repeat(seg_rows, width)
    attended, log_total = attention_forward(
        queries, keys_local, values_local, token_seg, first_row, second_row, width, scale
    )
    heads = attended.astype(jnp.bfloat16)
    activation = residual + jnp.dot(heads, matrices[5], preferred_element_type=jnp.float32).reshape(
        row_count, width, channels
    )
    upstream = upstream_low.reshape(token_count, channels)
    output_weight_grad = lax.dot_general(
        heads, upstream, (((0,), (0,)), ((), ())), preferred_element_type=jnp.float32
    )
    heads_grad = lax.dot_general(
        upstream, matrices[5], (((1,), (1,)), ((), ())), preferred_element_type=jnp.float32
    ).astype(jnp.bfloat16)
    correction = jnp.sum(heads_grad.astype(jnp.float32) * attended, axis=1)
    query_sum = attention_query_grad(
        queries,
        heads_grad,
        log_total,
        correction,
        keys_local,
        values_local,
        token_seg,
        first_row,
        second_row,
        width,
        scale,
    )
    key_sum, value_sum = attention_key_grad(
        queries,
        heads_grad,
        log_total,
        correction,
        keys_local,
        values_local,
        token_seg,
        first_row,
        second_row,
        width,
        scale,
    )
    query_low = query_sum.astype(jnp.bfloat16)
    key_low = key_sum.astype(jnp.bfloat16)
    value_low = value_sum.astype(jnp.bfloat16)
    contract_rows = (((0,), (0,)), ((), ()))
    contract_cols = (((1,), (1,)), ((), ()))
    query_weight_grad = lax.dot_general(
        normed, query_low, contract_rows, preferred_element_type=jnp.float32
    )
    key_weight_grad = lax.dot_general(
        normed, key_low, contract_rows, preferred_element_type=jnp.float32
    )
    value_weight_grad = lax.dot_general(
        normed, value_low, contract_rows, preferred_element_type=jnp.float32
    )
    normed_grad = (
        lax.dot_general(query_low, matrices[2], contract_cols, preferred_element_type=jnp.float32)
        + lax.dot_general(key_low, matrices[3], contract_cols, preferred_element_type=jnp.float32)
        + lax.dot_general(value_low, matrices[4], contract_cols, preferred_element_type=jnp.float32)
    )
    back_three, gain_three_grad, shift_three_grad = norm_backward(
        normed_grad.reshape(row_count, width, channels),
        normal_three,
        scale_three,
        member,
        counts,
        gains[4],
    )
    residual_grad = upstream_low.astype(jnp.float32) + back_three
    act_two_grad, conv_two_grad = conv_reverse(
        residual_grad.astype(jnp.bfloat16), stacked_two, seg_pad, seg_rows, matrices[1]
    )
    back_two, gain_two_grad, shift_two_grad = norm_backward(
        act_two_grad * swish_slope(norm_two), normal_two, scale_two, member, counts, gains[2]
    )
    act_one_grad, conv_one_grad = conv_reverse(
        back_two.astype(jnp.bfloat16), stacked_one, seg_pad, seg_rows, matrices[0]
    )
    back_one, gain_one_grad, shift_one_grad = norm_backward(
        act_one_grad * swish_slope(norm_one), normal_one, scale_one, member, counts, gains[0]
    )
    input_grad = residual_grad + back_one
    local_grads = (
        conv_one_grad,
        conv_two_grad,
        query_weight_grad,
        key_weight_grad,
        value_weight_grad,
        output_weight_grad,
        gain_one_grad,
        shift_one_grad,
        gain_two_grad,
        shift_two_grad,
        gain_three_grad,
        shift_three_grad,
    )
    return (activation, input_grad, local_grads)


def shards(
    features,
    bounds,
    out_grad,
    norm1_gain,
    norm1_shift,
    conv1_weight,
    norm2_gain,
    norm2_shift,
    conv2_weight,
    norm3_gain,
    norm3_shift,
    query_weight,
    key_weight,
    value_weight,
    output_weight,
):
    blocks = lax.axis_size("blk")
    position = lax.axis_index("blk")
    micro_count = features.shape[1]
    shard_sums = None
    outputs = []
    input_grads = []
    for micro_index in range(micro_count):
        matrices, norm_params = collect(
            conv1_weight,
            conv2_weight,
            query_weight,
            key_weight,
            value_weight,
            output_weight,
            norm1_gain,
            norm1_shift,
            norm2_gain,
            norm2_shift,
            norm3_gain,
            norm3_shift,
        )
        activation, input_grad, local_grads = one_batch(
            features[0, micro_index],
            bounds[0, micro_index],
            out_grad[0, micro_index],
            matrices,
            norm_params,
            position,
            blocks,
        )
        outputs.append(activation)
        input_grads.append(input_grad)
        reduced = reduce_all(local_grads)
        shard_sums = (
            reduced
            if shard_sums is None
            else tuple((acc + new for acc, new in zip(shard_sums, reduced)))
        )
    activations = jnp.stack(outputs)[None]
    input_grad_all = jnp.stack(input_grads)[None]
    return (
        activations,
        input_grad_all,
        shard_sums[6],
        shard_sums[7],
        shard_sums[0],
        shard_sums[8],
        shard_sums[9],
        shard_sums[1],
        shard_sums[10],
        shard_sums[11],
        shard_sums[2],
        shard_sums[3],
        shard_sums[4],
        shard_sums[5],
    )


def solution(mesh):
    in_specs = (
        P("dp", None, "blk", None, None),
        P("dp", None, None),
        P("dp", None, "blk", None, None),
        P("blk"),
        P("blk"),
        P("blk", "dp"),
        P("blk"),
        P("blk"),
        P("blk", "dp"),
        P("blk"),
        P("blk"),
        P("blk", "dp"),
        P("blk", "dp"),
        P("blk", "dp"),
        P("blk", "dp"),
    )
    out_specs = (
        P("dp", None, "blk", None, None),
        P("dp", None, "blk", None, None),
        P("blk"),
        P("blk"),
        P("blk", "dp"),
        P("blk"),
        P("blk"),
        P("blk", "dp"),
        P("blk"),
        P("blk"),
        P("blk", "dp"),
        P("blk", "dp"),
        P("blk", "dp"),
        P("blk", "dp"),
    )
    near = mesh.shape["dp"] == 4 and mesh.shape["blk"] == 8
    return jax.shard_map(unit_shards if near else shards, mesh=mesh, in_specs=in_specs, out_specs=out_specs, check_vma=False)
```

```python
import functools
import types

import jax
import jax.numpy as jnp
from jax import lax
from jax.experimental import pallas as pl
from jax.experimental.pallas import tpu as pltpu
from jax.sharding import PartitionSpec as P

GROUPS = 32
CANVASES = 3


EPSILON = 1e-06
HIGHEST = lax.Precision.HIGHEST
NEGATIVE = -1e30
MESH = pl.DeviceIdType.MESH
def in_order(s):
    s.ow(), s.gpl0(), s.g1l0(), s.gpo0(), s.gao0(), s.g2o0(), s.g2l0(), s.gpl1()
    s.gpo1(), s.gal0(), s.g1l1(), s.g1o1(), s.gpl2(), s.g2l1(), s.g1o0(), s.gpo2()
    s.gpy1(), s.gpx1(), s.g1l2(), s.gpl3(), s.g2o1(), s.gpo3(), s.g1o2(), s.gpx0()
    s.gpx3(), s.gpy0(), s.g1l3(), s.g1o3(), s.xs(), s.g2l2(), s.gpy2(), s.g1x1()
    s.gal1(), s.g1x2(), s.gpx2(), s.gpy3(), s.bw(), s.g2x0(), s.g1x3(), s.g1y0()
    s.g2l3(), s.g1y2(), s.g1y1(), s.gal2(), s.g1y3(), s.g2o3(), s.g1x0(), s.n1a()
    s.gao1(), s.gpd2(), s.os(), s.gpd0(), s.g2o2(), s.gpd1(), s.gpd3(), s.n1b()
    s.gal3(), s.n1c(), s.gao2(), s.g1d0(), s.g1d1(), s.g1d3(), s.n1d(), s.g2y3()
    s.g1d2(), s.g2y0(), s.g2x3(), s.g1a(), s.g2y1(), s.gao3(), s.n1e(), s.c10()
    s.c11(), s.n2a(), s.g2x2(), s.g2y2(), s.gay1(), s.gax3(), s.gay2(), s.g2x1()
    s.gay3(), s.g2d3(), s.gay0(), s.n2b(), s.n2c(), s.ob(), s.g2d2(), s.n2d()
    s.gax1(), s.n2e(), s.g2d0(), s.g2d1(), s.g2a(), s.c20(), s.gax2(), s.gad1()
    s.c21(), s.n3a(), s.gad2(), s.gax0(), s.n3b(), s.n3c(), s.t2(), s.gad3()
    s.or0(), s.or1(), s.gad0(), s.gaa(), s.po1(), s.pj1(), s.pj0(), s.po0()
    s.po2(), s.nr0(), s.po3(), s.nr1(), s.pj2(), s.pj3(), s.qf(), s.qb()
    s.hw(), s.gz(), s.hd(), s.ks(), s.an(), s.b3a(), s.aw(), s.rab3()
    s.rab0(), s.t1(), s.rab1(), s.rab2(), s.rac3(), s.b3b(), s.rac1(), s.b3c()
    s.rac2(), s.rac0(), s.b3d(), s.d20(), s.w20(), s.d21(), s.b2a(), s.r2b0()
    s.w21(), s.r2b1(), s.w22(), s.r2b3(), s.rae2(), s.b2b(), s.r2b2(), s.rae1()
    s.r2c2(), s.b2c(), s.raf2(), s.r2c3(), s.r2c0(), s.b2d(), s.d10(), s.d11()
    s.b1a(), s.rae3(), s.r2e2(), s.w10(), s.r2e3(), s.raf1(), s.rae0(), s.b1m()
    s.r2c1(), s.b1b(), s.raf3(), s.r2e0(), s.w11(), s.r1b0(), s.r2f2(), s.ps()
    s.w12(), s.r1b3(), s.r1b1(), s.r1b2(), s.r1c3(), s.r2f3(), s.r1e3(), s.r1c2()
    s.raf0(), s.r1f3(), s.r2e1(), s.r1e2(), s.py(), s.r2f0(), s.r1c1(), s.r2f1()
    s.r1e1(), s.r1c0(), s.rat(), s.r1f2(), s.r1f1(), s.pz(), s.r1e0(), s.r2t()
    s.r1f0(), s.r1t()


DIRECT = (False, False, False, False)
LIMIT = 60 << 20
SPLIT, SPLIT_A = 432, 192
CUT, CUT_A = 112, 48


class Place:
    def __init__(self):
        self.d = lax.axis_index("dp")
        self.b = lax.axis_index("blk")
        self.y, self.c = self.d // 2, self.d % 2
        self.z, self.x = self.b // 2, self.b % 2
        self.up = {"dp": self.d, "blk": self.b + 2}
        self.down = {"dp": self.d, "blk": self.b - 2}
        self.xn = {"dp": self.d, "blk": self.z * 2 + 1 - self.x}
        self.yn = {"dp": (1 - self.y) * 2 + self.c, "blk": self.b}
        self.cn = {"dp": self.y * 2 + 1 - self.c, "blk": self.b}


def remote(src, dst, send, recv, device):
    return pltpu.make_async_remote_copy(
        src_ref=src, dst_ref=dst, send_sem=send, recv_sem=recv, device_id=device, device_id_type=MESH
    )


def steps_of(z, nz):
    visits = [(z, None)]
    for k in range(1, nz):
        visits.append((z - k, z >= k))
        visits.append((z + k, z + k < nz))
    return visits


def guarded(valid, body):
    if valid is None:
        body()
    else:
        pl.when(valid)(body)


class Gather:
    SEMS = 27

    def __init__(self, here, nz, at, block, sems, direct):
        self.here, self.nz, self.at, self.block, self.sems, self.direct = here, nz, at, block, sems, direct
        self.visits = steps_of(here.z, nz)

    def ends(self, kind, z):
        if kind[0] == "c":
            return self.sems.at[26], self.sems.at[16]
        send = {"z": 17 + z, "zd": 21 + z}.get(kind, 25)
        recv = {"z": 0, "zd": 0, "x": 4, "y": 8, "da": 12, "db": 12}[kind] + z
        return self.sems.at[send], self.sems.at[recv]

    def cp(self, kind, z, src, device):
        return remote(src, src, *self.ends(kind, z), device)

    def own(self, z):
        return self.at(z, self.here.x, self.here.d, None)

    def colx(self, z, half=None):
        return self.at(z, 1 - self.here.x, self.here.d, half)

    def coly(self, z, half=None):
        return self.at(z, self.here.x, (1 - self.here.y) * 2 + self.here.c, half)

    def cold(self, z, half=None):
        return self.at(z, 1 - self.here.x, (1 - self.here.y) * 2 + self.here.c, half)

    def line_cp(self, k):
        here = self.here
        z = (here.z + k) % self.nz
        device = {"dp": here.d, "blk": z * 2 + here.x}
        return remote(self.own(here.z), self.own(here.z), self.sems.at[17 + z], self.sems.at[here.z], device)

    def line(self, j):
        z, valid = self.visits[j]
        here = self.here
        if j == 0 and self.direct:
            for k in range(1, self.nz):
                self.line_cp(k).start()
            return

        def body():
            src = self.own(z)
            if j > 0:
                self.cp("z", z, src, here.up).wait_recv()
            if self.direct:
                return
            if j == 0 or j % 2 == 1:

                @pl.when(here.z < self.nz - 1)
                def _():
                    self.cp("z", z, src, here.up).start()

            if j == 0 or j % 2 == 0:

                @pl.when(here.z > 0)
                def _():
                    self.cp("zd", z, src, here.down).start()

        guarded(valid, body)

    def out(self, j):
        z, valid = self.visits[j]
        here = self.here

        def body():
            src = self.own(z)
            self.cp("x", z, src, here.xn).start()
            self.cp("y", z, src, here.yn).start()
            self.cp("co", z, src, here.cn).start()

        guarded(valid, body)

    def have(self, j):
        self.line(j)
        self.out(j)

    def from_x(self, j):
        z, valid = self.visits[j]

        def body():
            self.cp("x", z, self.colx(z), self.here.xn).wait_recv()
            self.cp("da", z, self.colx(z, 0), self.here.yn).start()
            self.cp("cx", z, self.colx(z), self.here.cn).start()

        guarded(valid, body)

    def from_y(self, j):
        z, valid = self.visits[j]

        def body():
            self.cp("y", z, self.coly(z), self.here.yn).wait_recv()
            self.cp("db", z, self.coly(z, 1), self.here.xn).start()
            self.cp("cy", z, self.coly(z), self.here.cn).start()

        guarded(valid, body)

    def cross(self, j):
        self.from_x(j)
        self.from_y(j)

    def diagonal(self, j):
        z, valid = self.visits[j]
        here = self.here

        def body():
            self.cp("da", z, self.cold(z), here.yn).wait_recv()
            self.cp("cd", z, self.cold(z), here.cn).start()

        guarded(valid, body)

    def arrive(self):
        self.cp("co", 0, self.block(4 * self.nz), self.here.cn).wait_recv()

    def finish(self):
        here = self.here
        if self.direct:
            for k in range(1, self.nz):
                self.line_cp(k).wait_send()
        else:
            for j, (z, valid) in enumerate(self.visits):
                valid = True if valid is None else valid
                if j == 0 or j % 2 == 1:
                    going = jnp.logical_and(valid, here.z < self.nz - 1)
                    pl.when(going)(lambda: self.cp("z", z, self.own(z), here.up).wait_send())
                if j == 0 or j % 2 == 0:
                    going = jnp.logical_and(valid, here.z > 0)
                    pl.when(going)(lambda: self.cp("zd", z, self.own(z), here.down).wait_send())
        self.cp("x", 0, self.block(3 * self.nz), here.xn).wait_send()
        self.cp("co", 0, self.block(4 * self.nz), here.cn).wait_send()

    def table(self, name):
        kinds = {"l": self.line, "o": self.out, "x": self.from_x, "y": self.from_y, "d": self.diagonal}
        found = {name + "a": self.arrive}
        for kind, step in kinds.items():
            for k in range(self.nz):
                js = (0,) if k == 0 else (2 * k - 1, 2 * k)
                found["%s%s%d" % (name, kind, k)] = lambda js=js, step=step: [step(j) for j in js]
        return found


class Scatter:
    SEMS = 20

    def __init__(self, here, nz, at, core_at, part, block, sems, bufs):
        self.here, self.nz, self.at, self.core_at, self.part = here, nz, at, core_at, part
        self.block, self.sems = block, sems
        self.half, self.side, self.last = bufs
        self.visits = steps_of(here.z, nz)[::-1]

    def cp(self, send, recv, src, dst, device):
        return remote(src, dst, self.sems.at[17 + send], self.sems.at[recv], device)

    def places(self, z, c):
        here = self.here
        y, x = here.y, here.x
        return [(z, x, y * 2 + c), (z, 1 - x, y * 2 + c), (z, x, (1 - y) * 2 + c), (z, 1 - x, (1 - y) * 2 + c)]

    def mine(self, z, k):
        return self.at(*self.places(z, self.here.c)[k])

    def core_cp(self, z, k):
        place = self.places(z, 1 - self.here.c)[k]
        return self.cp(0, z, self.at(*place), self.core_at(k, *place), self.here.cn)

    def core_in(self, z, k):
        return self.core_at(k, *self.places(z, self.here.c)[k])[...]

    def begin(self, z):
        for k in (3, 1, 2, 0):
            self.core_cp(z, k).start()

    def half_cp(self, z, h):
        return self.cp(1, 4 + 4 * h + z, self.part(self.mine(z, 3), h), self.half[h].at[z], (self.here.xn, self.here.yn)[h])

    def side_cp(self, z, side, h):
        return self.cp(
            1, 12 + z, self.part(self.mine(z, 1 + side), h), self.part(self.side.at[side, z], h),
            (self.here.xn, self.here.yn)[side],
        )

    def corner(self, j):
        z, valid = self.visits[j]

        def body():
            self.cp(0, z, self.block(4), self.block(4), self.here.cn).wait_recv()
            for k in (3, 1, 2):
                place = self.mine(z, k)
                place[...] = place[...] + self.core_in(z, k)
                if k == 3:
                    self.half_cp(z, 0).start()
                    self.half_cp(z, 1).start()
                else:
                    self.side_cp(z, k - 1, k - 1).start()

        guarded(valid, body)

    def edges(self, j):
        z, valid = self.visits[j]

        def body():
            for side, h in ((0, 1), (1, 0)):
                self.half_cp(z, h).wait_recv()
                place = self.part(self.mine(z, 1 + side), h)
                place[...] = place[...] + self.half[h][z]
                self.side_cp(z, side, h).start()

        guarded(valid, body)

    def column(self, j, out):
        z, valid = self.visits[j]
        here = self.here

        def body():
            place = self.mine(z, 0)
            total = place[...].astype(jnp.float32) + self.core_in(z, 0).astype(jnp.float32)
            self.cp(1, 12 + z, self.side.at[:, z], self.side.at[:, z], here.xn).wait_recv()
            for side in (0, 1):
                total = total + self.side[side, z].astype(jnp.float32)
            if j == len(self.visits) - 1:
                out[...] = total
            else:
                place[...] = total.astype(jnp.bfloat16)
                self.last_cp(z).start()

        guarded(valid, body)

    def last_cp(self, z):
        here = self.here
        device = {"dp": here.d, "blk": z * 2 + here.x}
        return self.cp(2, 16, self.mine(z, 0), self.last.at[here.z], device)

    def others(self):
        others = self.last.at[pl.ds(0, self.nz - 1)]
        return self.cp(2, 16, others, others, self.here.up)

    def total(self, out):
        here = self.here
        self.others().wait_recv()
        for k in range(1, self.nz):
            out[...] += self.last[(here.z + k) % self.nz].astype(jnp.float32)

    def finish(self):
        here = self.here
        self.cp(0, 0, self.block(4 * self.nz), self.block(4 * self.nz), here.cn).wait_send()
        self.cp(1, 0, self.block(3 * self.nz), self.block(3 * self.nz), here.xn).wait_send()
        self.others().wait_send()

    def table(self, name, out):
        kinds = {"c": self.corner, "e": self.edges, "f": lambda j: self.column(j, out)}
        top = 2 * (self.nz - 1)
        found = {name + "t": lambda: self.total(out)}
        for z in range(self.nz):
            found["%sb%d" % (name, z)] = functools.partial(self.begin, z)
        for kind, step in kinds.items():
            for k in range(self.nz):
                js = (top,) if k == 0 else (top - 2 * k, top - 2 * k + 1)
                found["%s%s%d" % (name, kind, k)] = lambda js=js, step=step: [step(j) for j in js]
        return found


def part_of(ref, half, split, rows):
    return ref.at[pl.ds(0, split)] if half == 0 else ref.at[pl.ds(split, rows - split)]


def weight_block(ref):
    return lambda n: ref.at[pl.ds(0, n * 288), pl.ds(0, 256)]


def stacked_block(ref):
    return lambda n: ref.at[pl.ds(0, n // 2), :, pl.ds(0, 256)]


def weight_places(ref, rows, split=0):
    def at(z, x, d, half=None):
        base, count = (z * 2 + x) * rows, rows
        if half is not None:
            base, count = base + half * split, rows - split if half else split
        return ref.at[pl.ds(pl.multiple_of(base, 16), count), pl.ds(pl.multiple_of(d * 128, 128), 128)]

    return at


BF = jnp.bfloat16
F32 = jnp.float32
ROW = 8
PARAMS = 16


def both(a, b):
    return jnp.logical_and(a, b)


def cols(a, b):
    return lax.dot_general(a, b, (((1,), (1,)), ((), ())), preferred_element_type=F32)


def mm(a, b):
    return jnp.dot(a, b, preferred_element_type=F32)


class Unit(Place):
    def __init__(self):
        super().__init__()
        self.q = jnp.where(self.c == 0, self.x, 3 - self.x)
        self.mu = self.z % 2
        self.alone = self.z == self.q

    def member(self, q, z):
        return {"dp": self.y * 2 + q // 2, "blk": z * 2 + jnp.where(q < 2, q, 3 - q)}

    def peer(self, q):
        return self.member(q, self.z)

    def worker(self, m):
        return self.member(self.z, 2 * self.c + m)

    def keeper(self, h):
        return {"dp": self.y * 2 + self.z // 2, "blk": self.q * 2 + h}

    def column_worker(self, m):
        return {"dp": self.y * 2 + self.z // 2, "blk": (2 * self.c + m) * 2 + self.x}

    def column_keeper(self, k):
        return {"dp": self.y * 2 + self.z // 2, "blk": (2 * self.c + k) * 2 + self.x}

    def line(self, k):
        return {"dp": self.d, "blk": ((self.z + k) % 4) * 2 + self.x}

    def greet(self, shares, lines):
        barrier = pltpu.get_barrier_semaphore()

        def greet(device):
            pl.semaphore_signal(barrier, inc=1, device_id=device, device_id_type=MESH)

        for k in (1, 2, 3):
            greet(self.peer((self.q + k) % 4))
        count = 3
        if lines:
            greet(self.yn)
            for k in (1, 2, 3):
                greet(self.line(k))
            count += 4
        if shares:
            for m in (0, 1):
                pl.when(jnp.logical_not(both(self.alone, self.mu == m)))(lambda m=m: greet(self.worker(m)))
            for h in (0, 1):
                pl.when(jnp.logical_not(both(self.alone, self.x == h)))(lambda h=h: greet(self.keeper(h)))
            near = self.c == self.z // 2
            for k in (0, 1):
                pl.when(jnp.logical_not(both(near, self.mu == k)))(lambda k=k: greet(self.column_worker(k)))
            count = count + 6 - 2 * self.alone.astype(jnp.int32) - near.astype(jnp.int32)
        return count

    def enter(self, count):
        pl.semaphore_wait(pltpu.get_barrier_semaphore(), count)


class Share:
    def __init__(self, u, sems, local):
        self.u, self.sems, self.local = u, sems, local

    def send(self, src, dst):
        u = self.u
        for m in (0, 1):
            mine = both(u.alone, u.mu == m)
            place = dst.at[pl.ds(4 * u.x, 4)]
            pl.when(mine)(lambda: pltpu.make_async_copy(src.at[m], place, self.local).start())
            pl.when(jnp.logical_not(mine))(
                lambda: remote(src.at[m], place, self.sems.at[0, m], self.sems.at[1, u.x], u.worker(m)).start()
            )

    def wait(self, src, dst):
        u = self.u
        for h in (0, 1):
            mine = both(u.alone, u.x == h)
            place = dst.at[pl.ds(4 * h, 4)]
            pl.when(mine)(lambda: pltpu.make_async_copy(src.at[0], place, self.local).wait())
            pl.when(jnp.logical_not(mine))(
                lambda: remote(place, place, self.sems.at[0, 0], self.sems.at[1, h], u.keeper(h)).wait_recv()
            )

    def sent(self, src, dst):
        u = self.u
        for m in (0, 1):
            place = dst.at[pl.ds(4 * u.x, 4)]
            pl.when(jnp.logical_not(both(u.alone, u.mu == m)))(
                lambda: remote(src.at[m], place, self.sems.at[0, m], self.sems.at[1, u.x], u.worker(m)).wait_send()
            )

    def back(self, src, dst):
        u = self.u
        for h in (0, 1):
            mine = both(u.alone, u.x == h)
            piece = src.at[pl.ds(4 * h, 4)]
            pl.when(mine)(lambda: pltpu.make_async_copy(piece, dst.at[u.mu], self.local).start())
            pl.when(jnp.logical_not(mine))(
                lambda: remote(piece, dst.at[u.mu], self.sems.at[0, h], self.sems.at[1, u.mu], u.keeper(h)).start()
            )

    def back_wait(self, src, dst):
        u = self.u
        for m in (0, 1):
            mine = both(u.alone, u.mu == m)
            pl.when(mine)(lambda: pltpu.make_async_copy(src.at[pl.ds(0, 4)], dst.at[m], self.local).wait())
            pl.when(jnp.logical_not(mine))(
                lambda: remote(dst.at[m], dst.at[m], self.sems.at[0, 0], self.sems.at[1, m], u.worker(m)).wait_recv()
            )
        for h in (0, 1):
            pl.when(jnp.logical_not(both(u.alone, u.x == h)))(
                lambda: remote(
                    src.at[pl.ds(4 * h, 4)], dst.at[u.mu], self.sems.at[0, h], self.sems.at[1, u.mu], u.keeper(h)
                ).wait_send()
            )


class ColumnShare:
    def __init__(self, u, buf, sems, local):
        self.u, self.buf, self.sems, self.local = u, buf, sems, local
        self.alone = u.c == u.z // 2

    def place(self, z):
        return self.buf.at[z, pl.ds(4 * self.u.x, 4)]

    def cp(self, src, m):
        u = self.u
        return remote(src.at[m], self.place(u.z), self.sems.at[0, m], self.sems.at[1, u.mu], u.column_worker(m))

    def send(self, src):
        u = self.u
        for m in (0, 1):
            mine = both(self.alone, u.mu == m)
            pl.when(mine)(lambda: pltpu.make_async_copy(src.at[m], self.place(u.z), self.local).start())
            pl.when(jnp.logical_not(mine))(lambda: self.cp(src, m).start())

    def wait(self, src):
        u = self.u
        for k in (0, 1):
            mine = both(self.alone, u.mu == k)
            place = self.place(2 * u.c + k)
            pl.when(mine)(lambda: pltpu.make_async_copy(src.at[0], place, self.local).wait())
            pl.when(jnp.logical_not(mine))(
                lambda: remote(place, place, self.sems.at[0, 0], self.sems.at[1, k], u.column_keeper(k)).wait_recv()
            )

    def sent(self, src):
        u = self.u
        for m in (0, 1):
            pl.when(jnp.logical_not(both(self.alone, u.mu == m)))(lambda: self.cp(src, m).wait_send())


class Swap:
    def __init__(self, u, buf, sems):
        self.u, self.buf, self.sems = u, buf, sems

    def send(self):
        u = self.u
        block = self.buf.at[u.q]
        for k in (1, 2, 3):
            remote(block, block, self.sems.at[0], self.sems.at[1], u.peer((u.q + k) % 4)).start()

    def three(self):
        block = self.buf.at[pl.ds(0, 3)]
        return remote(block, block, self.sems.at[0], self.sems.at[1], self.u.cn)

    def wait(self):
        self.three().wait_recv()

    def sent(self):
        self.three().wait_send()

    def total(self):
        return self.buf[0] + self.buf[1] + self.buf[2] + self.buf[3]


class Spread:
    def __init__(self, u, buf, sems, parts):
        self.u, self.buf, self.sems, self.parts = u, buf, sems, parts

    def cp(self, kind, p, part):
        u = self.u
        ref = self.buf.at[p, part]
        device = u.xn if kind == 1 else u.cn
        return remote(ref, ref, self.sems.at[0, kind, part], self.sems.at[1, kind, part], device)

    def send(self, part):
        self.cp(1, self.u.q, part).start()
        self.cp(0, self.u.q, part).start()

    def across(self):
        q = self.u.q
        return q + 1 - 2 * (q % 2)

    def relay(self, part):
        copy = self.cp(1, self.across(), part)
        copy.wait_recv()
        self.cp(2, self.across(), part).start()

    def near(self, part):
        self.cp(0, 3 - self.u.q, part).wait_recv()

    def far(self, part):
        self.cp(2, 3 - self.across(), part).wait_recv()

    def sent(self, part):
        self.cp(1, self.u.q, part).wait_send()
        self.cp(0, self.u.q, part).wait_send()
        self.cp(2, self.across(), part).wait_send()


class Halo:
    def __init__(self, u, buf, sems):
        self.u, self.buf, self.sems = u, buf, sems

    def cp(self, downward):
        u, buf = self.u, self.buf
        if downward:
            return remote(buf.at[1], buf.at[ROW + 1], self.sems.at[0, 0], self.sems.at[1, 0], u.peer(jnp.maximum(u.q - 1, 0)))
        return remote(buf.at[ROW], buf.at[0], self.sems.at[0, 1], self.sems.at[1, 1], u.peer(jnp.minimum(u.q + 1, 3)))

    def send(self):
        u, buf = self.u, self.buf
        pl.when(u.q > 0)(lambda: self.cp(True).start())
        pl.when(u.q < 3)(lambda: self.cp(False).start())

        @pl.when(u.q == 0)
        def _():
            buf[0] = jnp.zeros(buf.shape[1:], buf.dtype)

        @pl.when(u.q == 3)
        def _():
            buf[ROW + 1] = jnp.zeros(buf.shape[1:], buf.dtype)

    def wait(self):
        u = self.u
        pl.when(u.q > 0)(lambda: self.cp(False).wait_recv())
        pl.when(u.q < 3)(lambda: self.cp(True).wait_recv())

    def sent(self):
        u = self.u
        pl.when(u.q > 0)(lambda: self.cp(True).wait_send())
        pl.when(u.q < 3)(lambda: self.cp(False).wait_send())


def canvas_of(rows, limits):
    return (rows >= limits[0:1]).astype(F32) + (rows >= limits[1:2]).astype(F32)


def row_numbers(u, offset, shape):
    return (ROW * u.q + offset + lax.broadcasted_iota(jnp.int32, shape, 0)).astype(F32)


def counts_of(limits, total_rows):
    each = 64.0 * 16.0
    return (limits[0:1] * each, (limits[1:2] - limits[0:1]) * each, (total_rows - limits[1:2]) * each)


def group_total(sums):
    width = sums.shape[1]
    lane = lax.broadcasted_iota(jnp.int32, sums.shape, 1)
    for step in (1, 2, 4, 8):
        after = pltpu.roll(sums, width - step, 1)
        before = pltpu.roll(sums, step, 1)
        sums = sums + jnp.where((lane // step) % 2 == 0, after, before)
    return sums


def canvas_sums(first, second, seg):
    out = []
    for rows in (first, second):
        for k in range(CANVASES):
            out.append(jnp.sum(jnp.where(seg == float(k), rows, 0.0), axis=0, keepdims=True))
    out.append(jnp.zeros((2, first.shape[1]), F32))
    return jnp.concatenate(out, axis=0)


def by_row(values, seg):
    return jnp.where(seg == 0.0, values[0], jnp.where(seg == 1.0, values[1], values[2]))


def moments(total, counts, seg):
    grouped = group_total(total)
    averages, inverses = [], []
    for k in range(CANVASES):
        average = grouped[k : k + 1] / counts[k]
        averages.append(average)
        inverses.append(lax.rsqrt(grouped[3 + k : 4 + k] / counts[k] - average * average + EPSILON))
    return by_row(averages, seg), by_row(inverses, seg)


def sigmoid(argument):
    return 0.5 * jnp.tanh(0.5 * argument) + 0.5


def each_row(body):
    lax.fori_loop(0, ROW, lambda r, carry: (body(r), carry)[1], 0)


def row_of(ref, r):
    return ref[pl.ds(r, 1), :]


def tap_masks(u, limits, masks):
    shape = (ROW, limits.shape[1])
    rows = row_numbers(u, 0, shape)
    seg = canvas_of(rows, limits)
    masks[0] = both(canvas_of(rows - 1.0, limits) == seg, rows >= 1.0).astype(F32)
    masks[1] = both(canvas_of(rows + 1.0, limits) == seg, rows < 4.0 * ROW - 1.0).astype(F32)
    return seg


def shifted(line):
    position = lax.broadcasted_iota(jnp.int32, line.shape, 0)
    width = line.shape[0]
    before = jnp.where(position == 0, 0.0, pltpu.roll(line, 1, 0))
    after = jnp.where(position == width - 1, 0.0, pltpu.roll(line, width - 1, 0))
    return before, line, after


def taps_inner(buf, masks, taps):
    def body(s):
        lines = shifted(buf[s + 1].astype(F32))
        for k in range(3):
            taps[3 + k, s] = lines[k].astype(BF)

        @pl.when(s < ROW - 1)
        def _():
            mask = masks[0, pl.ds(s + 1, 1), :]
            for k in range(3):
                taps[k, s + 1] = (lines[k] * mask).astype(BF)

        @pl.when(s > 0)
        def _():
            mask = masks[1, pl.ds(s - 1, 1), :]
            for k in range(3):
                taps[6 + k, s - 1] = (lines[k] * mask).astype(BF)

    each_row(body)


def taps_outer(buf, masks, taps):
    for k, line in enumerate(shifted(buf[0].astype(F32))):
        taps[k, 0] = (line * masks[0, 0:1, :]).astype(BF)
    for k, line in enumerate(shifted(buf[ROW + 1].astype(F32))):
        taps[6 + k, ROW - 1] = (line * masks[1, ROW - 1 : ROW, :]).astype(BF)


def conv_tile(taps, weight, m, flip):
    total = None
    for tap in range(9):
        left = taps[8 - tap if flip else tap, pl.ds(pl.multiple_of(m * 4, 4), 4)].reshape(256, -1)
        right = weight[tap * 512 : (tap + 1) * 512, :]
        term = cols(left, right) if flip else mm(left, right)
        total = term if total is None else total + term
    return total.reshape(4, 64, -1)


def conv_weight_grad(act_t, taps, out, first, last):
    def body(tap, carry):
        piece = mm(act_t[...], taps[8 - tap].reshape(512, -1))
        out[pl.ds(pl.multiple_of(tap * 512, 512), 512), :] = piece.astype(BF)
        return carry

    lax.fori_loop(first, last, body, 0)


def attn_places(ref, split=0):
    def at(z, x, d, half=None):
        place = ref.at[z * 2 + x]
        lanes = pl.ds(pl.multiple_of(d * 128, 128), 128)
        if half is None:
            return place.at[:, lanes]
        return place.at[pl.ds(half * split, 256 - split if half else split), lanes]

    return at


def param_places(ref):
    def at(z, x, d, half=None):
        place = ref.at[z * 2 + x]
        lanes = pl.ds(pl.multiple_of(d * 128, 128), 128)
        if half is None:
            return place.at[:, lanes]
        return place.at[pl.ds(half * 8, 8), lanes]

    return at


class Halves:
    def __init__(self, ref):
        self.ref = ref

    @property
    def at(self):
        return self

    def __getitem__(self, index):
        member, part = index
        return self.ref.at[member, pl.ds(part * (ROW // 2), ROW // 2)]


ANY = pl.BlockSpec(memory_space=pl.ANY)
VM = pl.BlockSpec(memory_space=pltpu.VMEM)


class Blocks:
    def __init__(self, ref):
        self.ref = ref

    @property
    def at(self):
        return self

    def __getitem__(self, index):
        member, part = index
        x = jnp.where(member < 2, member, 3 - member)
        return self.ref.at[2 * (member // 2) + part, pl.ds(4 * x, 4)]


def unit_inputs(bounds, norms):
    d, b = lax.axis_index("dp"), lax.axis_index("blk")
    rows = jnp.stack([item.astype(F32) for item in norms])
    lane = jnp.arange(128)[None] // 64
    params = jnp.where((d == b // 2) & (lane == b % 2), jnp.concatenate([rows, rows], axis=1), 0.0)
    limits = jnp.broadcast_to(bounds.reshape(-1).astype(F32)[:, None], (4, 128))
    blank = jnp.zeros((2, 128), F32)
    return jnp.concatenate([params, blank, limits, blank, blank])


def whole_kernel(
    feat, grad, par, s1, s2, sq, sk, sv, so,
    act_back, grad_back, weights_out, norm_out,
    w1, w2, wa, pb, bb, xin, oall, nall, taps, a1, a2, masks, hidden, resid, small, rows_a, rows_b, swaps, lds,
    wg1, wg2, scores, gk, gv, lcol, dcol, big, gres, low, act, act_t1, act_t2, ga, mine, psum_y, psum_z,
    core_a, core_2, half_a, rest_a, side_a, last_a, half_2, rest_2, side_2, last_2, half_1, rest_1, side_1, last_1,
    gsems, ssems, local, share_sems, bound_sems, swap_sems, spread_sems, halo_sems, py_sems, pz_sems,
):
    u = Unit()
    greeters = u.greet(True, True)
    mine[...] = jnp.zeros_like(mine)
    table = {}
    ats = (weight_places(w1, 576, SPLIT), weight_places(w2, 576, SPLIT), attn_places(wa, SPLIT_A), param_places(pb))
    blocks = (weight_block(w1), weight_block(w2), stacked_block(wa), stacked_block(pb))
    groups = [Gather(u, 4, ats[k], blocks[k], gsems.at[k], DIRECT[k]) for k in range(4)]
    for name, group in zip(("g1", "g2", "ga", "gp"), groups):
        table.update(group.table(name))
    own = [pltpu.make_async_copy(src, groups[k].own(u.z), local.at[k]) for k, src in ((0, s1), (1, s2), (3, par))]
    for k, src in enumerate((sq, sk, sv, so)):
        own.append(pltpu.make_async_copy(src, groups[2].own(u.z).at[pl.ds(64 * k, 64)], local.at[8 + k]))
    keep = pltpu.make_async_copy(par, bb.at[u.c], local.at[4])
    for copy in own + [keep]:
        copy.start()
    g1_out, g2_out = weights_out.at[pl.ds(0, 576)], weights_out.at[pl.ds(576, 576)]
    ga_out = weights_out.at[pl.ds(1152, 256)]
    share_x, share_a, share_g = [Share(u, share_sems.at[k], local.at[5 + k]) for k in range(3)]
    share_o = ColumnShare(u, oall, share_sems.at[3], local.at[2])
    swap = [Swap(u, swaps.at[k], swap_sems.at[k]) for k in range(6)] + [Swap(u, lds, swap_sems.at[6])]
    halo = [Halo(u, (a1, a2)[k % 2], halo_sems.at[k]) for k in range(4)]
    spread_o = Spread(u, Blocks(oall), spread_sems.at[0], 2)
    spread_n = Spread(u, Halves(nall), spread_sems.at[1], 2)

    w2_at = weight_places(w2, 576)
    part_a = lambda ref, h: part_of(ref, h, CUT_A, 256)
    part_w = lambda ref, h: part_of(ref, h, CUT, 576)
    sum_a = Scatter(
        u, 4, attn_places(ga), lambda k, z, x, d: core_a.at[k, z], part_a, stacked_block(ga), ssems.at[0], ((half_a, rest_a), side_a, last_a)
    )
    sum_2 = Scatter(
        u, 4, weight_places(wg2, 576), lambda k, z, x, d: core_2.at[k, z], part_w, weight_block(wg2), ssems.at[1], ((half_2, rest_2), side_2, last_2)
    )
    sum_1 = Scatter(
        u, 4, weight_places(wg1, 576), lambda k, z, x, d: w2_at(z, x, d), part_w, weight_block(wg1), ssems.at[2], ((half_1, rest_1), side_1, last_1)
    )
    for name, total, out in (("ra", sum_a, ga_out), ("r2", sum_2, g2_out), ("r1", sum_1, g1_out)):
        table.update(total.table(name, out))
    bound_cp = remote(par, bb.at[u.c], bound_sems.at[0], bound_sems.at[1], u.cn)
    state = {}

    def step(function):
        table[function.__name__] = function
        return function


    @step
    def xs():
        share_x.send(feat, xin)
        bound_cp.start()

    @step
    def os():
        share_o.send(grad)

    @step
    def ow():
        for copy in own:
            copy.wait()
        u.enter(greeters)

    @step
    def bw():
        keep.wait()
        remote(par, bb.at[1 - u.c], bound_sems.at[0], bound_sems.at[1], u.cn).wait_recv()
        limits = jnp.where(u.mu == 0, bb[u.z // 2, 8:10, :], bb[u.z // 2, 10:12, :])
        limits = jnp.concatenate([limits] * 4, axis=1)
        small[7] = jnp.concatenate([limits, jnp.zeros((6, limits.shape[1]), F32)], axis=0)
        state["seg"] = tap_masks(u, limits, masks)
        state["counts"] = counts_of(limits, 4.0 * ROW)

    def first(r):
        return xin[r].astype(F32)

    def second(r):
        return hidden[r]

    def third(r):
        return resid[r]

    values = (first, second, third)

    def norm_sums(k):
        def body(r):
            line = values[k](r)
            rows_a[pl.ds(r, 1), :] = jnp.sum(line, axis=0, keepdims=True)
            rows_b[pl.ds(r, 1), :] = jnp.sum(line * line, axis=0, keepdims=True)

        each_row(body)
        swap[k].buf[u.q] = canvas_sums(rows_a[...], rows_b[...], state["seg"])
        swap[k].send()

    def norm_stats(k):
        swap[k].wait()
        average, inverse = moments(swap[k].total(), state["counts"], state["seg"])
        small[2 * k] = average
        small[2 * k + 1] = inverse

    def param(j):
        return small[6, j : j + 1, :]

    def xhat(k, r):
        return (values[k](r) - small[2 * k, pl.ds(r, 1), :]) * small[2 * k + 1, pl.ds(r, 1), :]

    def normal(k, r):
        return xhat(k, r) * param(2 * k) + param(2 * k + 1)

    def activate(k, buf):
        def body(r):
            line = normal(k, r)
            buf[r + 1] = (line * sigmoid(line)).astype(BF)

        each_row(body)

    @step
    def n1a():
        share_x.wait(feat, xin)
        norm_sums(0)

    @step
    def n1b():
        groups[3].arrive()
        total = pb[0, 0:8, :]
        for b in range(1, 8):
            total = total + pb[b, 0:8, :]
        small[6] = total
        norm_stats(0)

    def conv_steps(name, k, buf):
        def c():
            activate(k, buf)
            halo[k].send()

        def d():
            taps_inner(buf, masks, taps)

        def e():
            halo[k].wait()
            taps_outer(buf, masks, taps)
            halo[k].sent()

        table[name + "c"], table[name + "d"], table[name + "e"] = c, d, e

    conv_steps("n1", 0, a1)
    conv_steps("n2", 1, a2)

    @step
    def t1():
        act_t1[...] = a1[1 : ROW + 1].reshape(512, 512).T

    @step
    def t2():
        act_t2[...] = a2[1 : ROW + 1].reshape(512, 512).T

    def first_conv(m):
        hidden[4 * m : 4 * m + 4] = conv_tile(taps, w1, m, False)

    def second_conv(m):
        resid[4 * m : 4 * m + 4] = conv_tile(taps, w2, m, False) + xin[4 * m : 4 * m + 4].astype(F32)

    for m in (0, 1):
        table["c1%d" % m] = functools.partial(first_conv, m)
        table["c2%d" % m] = functools.partial(second_conv, m)
    table["n2a"], table["n2b"] = functools.partial(norm_sums, 1), functools.partial(norm_stats, 1)
    table["n3a"], table["n3b"] = functools.partial(norm_sums, 2), functools.partial(norm_stats, 2)

    @step
    def n3c():
        def row(r):
            nall[u.q, r] = normal(2, r).astype(BF)

        for part in range(2):
            lax.fori_loop(4 * part, 4 * part + 4, lambda r, carry: (row(r), carry)[1], 0)
            spread_n.send(part)

    @step
    def ob():
        share_o.wait(grad)
        for part in range(2):
            spread_o.send(part)

    for part in (0, 1):
        table["or%d" % part] = functools.partial(spread_o.relay, part)
        table["nr%d" % part] = functools.partial(spread_n.relay, part)

    scale = 512.0 ** (-0.5)
    steep = scale * 1.4426950408889634

    def slot(ref, i):
        return ref.at[pl.ds(pl.multiple_of(i * 512, 512), 512)]

    def query_of(i):
        return slot(wg1, i)

    def key_of(i):
        return slot(wg1, 4 + i)

    def value_of(i):
        return slot(wg2, i)

    def upstream_of(i):
        return slot(wg2, 4 + i)

    heads, gq = slot(wg1, 8), slot(wg2, 8)

    def matrix(k):
        return wa[:, pl.ds(k * 64, 64), :].reshape(512, 512)

    across = u.q + 1 - 2 * (u.q % 2)
    members = (u.q, 3 - u.q, across, 3 - across)

    def project(k):
        if k in (1, 3):
            for part in range(2):
                (spread_n.near if k == 1 else spread_n.far)(part)
        tokens = nall[members[k]].reshape(512, 512)
        query_of(members[k])[...] = mm(tokens, matrix(0)).astype(BF)
        key_of(members[k])[...] = mm(tokens, matrix(1)).astype(BF)
        value_of(members[k])[...] = mm(tokens, matrix(2)).astype(BF)

    def project_up(k):
        if k == 1:
            for part in range(2):
                spread_o.near(part)
                spread_o.far(part)
        upstream = oall[members[k]].reshape(512, 512)
        upstream_of(members[k])[...] = cols(upstream, matrix(3)).astype(BF)

    for k in range(4):
        table["pj%d" % k] = functools.partial(project, k)
        table["po%d" % k] = functools.partial(project_up, k)

    def canvas(rows):
        return (rows >= small[7, 0:1, 0:1]).astype(F32) + (rows >= small[7, 1:2, 0:1]).astype(F32)

    def seg_col(q, offset, count):
        token = offset + lax.broadcasted_iota(jnp.int32, (count, 1), 0)
        return canvas((ROW * q + token // 64).astype(F32))

    def seg_row(q):
        token = lax.broadcasted_iota(jnp.int32, (1, 512), 1)
        return canvas((ROW * q + token // 64).astype(F32))

    def kept(j, i):
        return taps.at[i, pl.ds(pl.multiple_of(j * 4, 4), 4)]

    def queries(j, carry):
        block = pl.ds(pl.multiple_of(j * 256, 256), 256)
        query = query_of(u.q)[block]
        seg = seg_col(u.q, j * 256, 256)
        most = jnp.full((256, 1), NEGATIVE, F32)
        for i in range(4):
            part = jnp.where(seg == seg_row(i), cols(query, key_of(i)[...]) * steep, NEGATIVE)
            scores[i] = part
            most = jnp.maximum(most, jnp.max(part, axis=1, keepdims=True))
        total = jnp.zeros((256, 1), F32)
        for i in range(4):
            part = jnp.exp2(scores[i] - most)
            total = total + jnp.sum(part, axis=1, keepdims=True)
            scores[i] = part
        inverse = 1.0 / total
        found = jnp.zeros((256, 512), F32)
        for i in range(4):
            part = (scores[i] * inverse).astype(BF)
            kept(j, i)[...] = part.reshape(4, 64, 512)
            found = found + mm(part, value_of(i)[...])
        heads[block, :] = found.astype(BF)
        lcol[block, :] = jnp.broadcast_to(most + jnp.log2(total), (256, 128))
        return carry

    @step
    def qf():
        lax.fori_loop(0, 2, queries, 0)

    def queries_back(j, carry):
        block = pl.ds(pl.multiple_of(j * 256, 256), 256)
        upstream = upstream_of(u.q)[block]
        correction = jnp.zeros((256, 1), F32)
        for i in range(4):
            slope = cols(upstream, value_of(i)[...])
            scores[i] = slope
            part = kept(j, i)[...].reshape(256, 512).astype(F32)
            correction = correction + jnp.sum(part * slope, axis=1, keepdims=True)
        back = jnp.zeros((256, 512), F32)
        for i in range(4):
            part = kept(j, i)[...].reshape(256, 512).astype(F32)
            back = back + mm((part * (scores[i] - correction)).astype(BF), key_of(i)[...])
        gq[block, :] = (back * scale).astype(BF)
        dcol[block, :] = jnp.broadcast_to(correction, (256, 128))
        return carry

    @step
    def qb():
        lax.fori_loop(0, 2, queries_back, 0)
        lds[u.q] = jnp.concatenate([lcol[...].T[0:1], dcol[...].T[0:1], jnp.zeros((6, 512), F32)], axis=0)
        swap[6].send()

    @step
    def gz():
        for group in groups:
            group.finish()

    @step
    def hd():
        act[...] = (resid[...] + mm(heads[...], matrix(3)).reshape(ROW, 64, 512)).astype(BF)
        share_a.back(act, act_back)

    @step
    def hw():
        ga[:, 192:256, :] = mm(heads[...].T, oall[u.q].reshape(512, 512)).astype(BF).reshape(8, 64, 512)

    def keys(i, carry):
        query, upstream = query_of(i)[...], upstream_of(i)[...]
        for j in (0, 1):
            key, value = key_of(u.q)[256 * j : 256 * j + 256], value_of(u.q)[256 * j : 256 * j + 256]
            shared = seg_col(u.q, j * 256, 256) == seg_row(i)
            part = jnp.exp2(jnp.where(shared, cols(key, query) * steep, NEGATIVE) - lds[i, 0:1, :])
            slope = cols(value, upstream) - lds[i, 1:2, :]
            rows = pl.ds(4 * j, 4)
            gres[rows] += mm(part.astype(BF), upstream).reshape(4, 64, 512)
            big[rows] += mm((part * slope).astype(BF), query).reshape(4, 64, 512)
        return carry

    @step
    def ks():
        big[...] = jnp.zeros_like(big)
        gres[...] = jnp.zeros_like(gres)
        swap[6].wait()
        lax.fori_loop(0, 4, keys, 0)
        gk[...] = (big[...] * scale).astype(BF).reshape(512, 512)
        gv[...] = gres[...].astype(BF).reshape(512, 512)

    @step
    def aw():
        tokens = nall[u.q].reshape(512, 512).T
        for k, part in enumerate((gq, gk, gv)):
            ga[:, k * 64 : (k + 1) * 64, :] = mm(tokens, part[...]).astype(BF).reshape(8, 64, 512)

    @step
    def an():
        total = None
        for k, part in enumerate((gq, gk, gv)):
            term = cols(part[...], matrix(k))
            total = term if total is None else total + term
        big[...] = total.reshape(ROW, 64, 512)


    def back_sums(k, slope):
        def body(r):
            line = big[r]
            if slope:
                value = normal(k, r)
                part = sigmoid(value)
                line = line * (part * (1.0 + value * (1.0 - part)))
                big[r] = line
            rows_a[pl.ds(r, 1), :] = jnp.sum(line, axis=0, keepdims=True)
            rows_b[pl.ds(r, 1), :] = jnp.sum(line * xhat(k, r), axis=0, keepdims=True)

        each_row(body)
        swap[3 + k].buf[u.q] = canvas_sums(rows_a[...], rows_b[...], state["seg"])
        swap[3 + k].send()

    def back_means(k):
        swap[3 + k].wait()
        total = swap[3 + k].total()
        mine[2 * k : 2 * k + 1, :] = jnp.sum(total[3:6], axis=0, keepdims=True)
        mine[2 * k + 1 : 2 * k + 2, :] = jnp.sum(total[0:3], axis=0, keepdims=True)
        grouped = group_total(total * param(2 * k))
        counts, seg = state["counts"], state["seg"]
        rows_a[...] = by_row([grouped[j : j + 1] / counts[j] for j in range(3)], seg)
        rows_b[...] = by_row([grouped[3 + j : 4 + j] / counts[j] for j in range(3)], seg)

    def back(k, r):
        line = big[r] * param(2 * k) - row_of(rows_a, r) - xhat(k, r) * row_of(rows_b, r)
        return line * small[2 * k + 1, pl.ds(r, 1), :]

    @step
    def b3a():
        back_sums(2, False)

    @step
    def b3b():
        back_means(2)

        def row(r):
            line = oall[u.q, r].astype(F32) + back(2, r)
            gres[r] = line
            a2[r + 1] = line.astype(BF)

        each_row(row)
        halo[3].send()

    @step
    def b2a():
        back_sums(1, True)

    @step
    def b2b():
        back_means(1)

        def row(r):
            a1[r + 1] = back(1, r).astype(BF)

        each_row(row)
        halo[2].send()

    @step
    def b1a():
        back_sums(0, True)

    @step
    def b1m():
        back_means(0)

    @step
    def b1b():
        def row(r):
            low[r] = (gres[r] + back(0, r)).astype(BF)

        each_row(row)
        share_g.back(low, grad_back)

    @step
    def ps():
        remote(mine, psum_y, py_sems.at[0], py_sems.at[1], u.yn).start()

    def back_taps(name, k, buf):
        def c():
            taps_inner(buf, masks, taps)

        def d():
            halo[k].wait()
            taps_outer(buf, masks, taps)
            halo[k].sent()

        table[name + "c"], table[name + "d"] = c, d

    back_taps("b3", 3, a2)
    back_taps("b2", 2, a1)

    def tile_back(weight, m):
        big[4 * m : 4 * m + 4] = conv_tile(taps, weight, m, True)

    for m in (0, 1):
        table["d2%d" % m] = functools.partial(tile_back, w2, m)
        table["d1%d" % m] = functools.partial(tile_back, w1, m)
    for k in range(3):
        table["w2%d" % k] = functools.partial(conv_weight_grad, act_t2, taps, wg2, 3 * k, 3 * k + 3)
        table["w1%d" % k] = functools.partial(conv_weight_grad, act_t1, taps, wg1, 3 * k, 3 * k + 3)

    def line_cp(block, k):
        return remote(block, block, pz_sems.at[0], pz_sems.at[1], u.line(k))

    @step
    def py():
        remote(mine, psum_y, py_sems.at[0], py_sems.at[1], u.yn).wait()
        psum_z[u.z] = mine[...] + psum_y[...]
        for k in (1, 2, 3):
            line_cp(psum_z.at[u.z], k).start()

    @step
    def pz():
        line_cp(psum_z.at[pl.ds(0, 3)], 1).wait_recv()
        total = psum_z[0] + psum_z[1] + psum_z[2] + psum_z[3]
        norm_out[...] = pltpu.roll(total, lax.rem(512 - 64 * u.b, 512), 1)[:, 0:128]

    in_order(types.SimpleNamespace(**table))

    share_a.back_wait(act, act_back)
    share_g.back_wait(low, grad_back)
    for total in (sum_a, sum_2, sum_1):
        total.finish()
    bound_cp.wait_send()
    share_x.sent(feat, xin)
    share_o.sent(grad)
    for item in swap:
        item.sent()
    for item in (spread_o, spread_n):
        for part in range(2):
            item.sent(part)
    line_cp(psum_z.at[pl.ds(0, 3)], 1).wait_send()


def whole_call(features, out_grad, params, *shards):
    full = lambda shape, kind: jax.ShapeDtypeStruct(shape, kind)
    dma = pltpu.SemaphoreType.DMA
    rows, padded, square, weight = (ROW, 64, 512), (ROW + 2, 64, 512), (512, 512), (4608, 512)
    low = lambda *shape: pltpu.VMEM(shape, BF)
    wide = lambda *shape: pltpu.VMEM(shape, F32)
    sums = []
    for r, cut in ((256, CUT_A), (576, CUT), (576, CUT)):
        sums += [low(4, cut, 128), low(4, r - cut, 128), low(2, 4, r, 128), low(4, r, 128)]
    return pl.pallas_call(
        whole_kernel,
        out_shape=[
            full((2, 4, 64, 512), BF), full((2, 4, 64, 512), BF), full((1408, 128), F32),
            full((8, 128), F32),
        ],
        in_specs=[ANY] * 9,
        out_specs=[VM] * 4,
        scratch_shapes=[
            low(*weight), low(*weight), low(8, 256, 512), wide(8, PARAMS, 512), wide(2, PARAMS, 128), low(*rows),
            low(4, *rows), low(4, *rows), low(9, *rows), low(*padded), low(*padded), wide(2, ROW, 512),
            wide(*rows), wide(*rows), wide(8, 8, 512), wide(ROW, 512), wide(ROW, 512), wide(6, 4, 8, 512), wide(4, 8, 512),
            low(*weight), low(*weight), wide(4, 256, 512), low(*square), low(*square),
            wide(512, 128), wide(512, 128), wide(*rows), wide(*rows), low(*rows), low(*rows), low(*square), low(*square),
            low(8, 256, 512), wide(8, 512), wide(8, 512), wide(4, 8, 512),
            low(4, 4, 256, 128), low(4, 4, 576, 128), *sums,
            dma((4, Gather.SEMS)), dma((3, Scatter.SEMS)), dma((12,)), dma((4, 2, 2)), dma((2,)), dma((7, 2)),
            dma((2, 2, 3, 2)), dma((4, 2, 2)), dma((2,)), dma((2,)),
        ],
        compiler_params=pltpu.CompilerParams(collective_id=0, has_side_effects=True, vmem_limit_bytes=LIMIT),
    )(features, out_grad, params, *shards)


def unit_shards(
    features, bounds, out_grad, norm1_gain, norm1_shift, conv1_weight, norm2_gain, norm2_shift, conv2_weight,
    norm3_gain, norm3_shift, query_weight, key_weight, value_weight, output_weight,
):
    norms = (norm1_gain, norm1_shift, norm2_gain, norm2_shift, norm3_gain, norm3_shift)
    act_back, grad_back, weights, norms = whole_call(
        features[0], out_grad[0], unit_inputs(bounds, norms), conv1_weight, conv2_weight,
        query_weight, key_weight, value_weight, output_weight,
    )
    norms = norms[:, :64]
    g1, g2, ga = weights[:576], weights[576:1152], weights[1152:].reshape(4, 64, 128)
    return (
        act_back.astype(F32)[None], grad_back.astype(F32)[None], norms[0], norms[1], g1, norms[2], norms[3], g2,
        norms[4], norms[5], ga[0], ga[1], ga[2], ga[3],
    )


def extended(shard, sides, width):
    for axis, dim in sides:
        devices, length = (lax.axis_size(axis), shard.shape[dim])
        up = [(i, (i + 1) % devices) for i in range(devices - 1)]
        down = [(j, i) for i, j in up]
        last = lax.slice_in_dim(shard, length - width, length, axis=dim)
        initial = lax.slice_in_dim(shard, 0, width, axis=dim)
        before = lax.ppermute(last, axis, up)
        after = lax.ppermute(initial, axis, down)
        shard = jnp.concatenate([before, shard, after], axis=dim)
    return shard


def canvas_index(global_rows, first_row, second_row):
    return (global_rows >= first_row).astype(jnp.int32) + (global_rows >= second_row).astype(
        jnp.int32
    )


def swish(argument):
    return argument * jax.nn.sigmoid(argument)


def swish_slope(argument):
    sigmoid_value = jax.nn.sigmoid(argument)
    return sigmoid_value * (1.0 + argument * (1.0 - sigmoid_value))


def group_sums(member, grouped):
    return jnp.einsum("rk,rwgc->kg", member, grouped, precision=HIGHEST)


def spread_rows(member, lookup):
    return jnp.dot(member, lookup, precision=HIGHEST)


def norm_forward(inputs, member, counts, norm_gain, norm_shift):
    row_count, width, channels = inputs.shape
    grouped = inputs.reshape(row_count, width, GROUPS, channels // GROUPS)
    totals, square = lax.psum(
        (group_sums(member, grouped), group_sums(member, grouped * grouped)), "blk"
    )
    average = totals / counts[:, None]
    inverse = lax.rsqrt(square / counts[:, None] - average * average + EPSILON)
    average_rows = spread_rows(member, average)
    scale_rows = spread_rows(member, inverse)
    normal = (grouped - average_rows[:, None, :, None]) * scale_rows[:, None, :, None]
    normal = normal.reshape(row_count, width, channels)
    return (normal * norm_gain + norm_shift, normal, scale_rows)


def norm_backward(incoming, normal, scale_rows, member, counts, norm_gain):
    row_count, width, channels = incoming.shape
    gain_grad = jnp.sum(incoming * normal, axis=(0, 1))
    shift_grad = jnp.sum(incoming, axis=(0, 1))
    scaled = (incoming * norm_gain).reshape(row_count, width, GROUPS, channels // GROUPS)
    grouped_normal = normal.reshape(row_count, width, GROUPS, channels // GROUPS)
    first_sum, second_sum = lax.psum(
        (group_sums(member, scaled), group_sums(member, scaled * grouped_normal)), "blk"
    )
    first_rows = spread_rows(member, first_sum / counts[:, None])
    second_rows = spread_rows(member, second_sum / counts[:, None])
    result = scale_rows[:, None, :, None] * (
        scaled - first_rows[:, None, :, None] - grouped_normal * second_rows[:, None, :, None]
    )
    return (result.reshape(row_count, width, channels), gain_grad, shift_grad)


def gather_taps(padded, seg_pad, seg_rows, direction):
    row_count = seg_rows.shape[0]
    width = padded.shape[1]
    widened = jnp.pad(padded, ((0, 0), (1, 1), (0, 0)))
    pieces = []
    for step_row in (-1, 0, 1):
        low_row = 1 + direction * step_row
        allowed = (seg_pad[low_row : low_row + row_count] == seg_rows).astype(padded.dtype)[
            :, None, None
        ]
        for step_col in (-1, 0, 1):
            low_col = 1 + direction * step_col
            pieces.append(
                widened[low_row : low_row + row_count, low_col : low_col + width, :] * allowed
            )
    return jnp.stack(pieces, axis=2)


def conv_apply(activation, seg_pad, seg_rows, weight_matrix):
    row_count, width, channels = activation.shape
    padded = extended(activation, (("blk", 0),), 1)
    stacked = gather_taps(padded, seg_pad, seg_rows, 1).reshape(row_count * width, 9 * channels)
    result = jnp.dot(stacked, weight_matrix, preferred_element_type=jnp.float32)
    return (result.reshape(row_count, width, channels), stacked)


def conv_reverse(gradient, stacked, seg_pad, seg_rows, weight_matrix):
    row_count, width, channels = gradient.shape
    flattened = gradient.reshape(row_count * width, channels)
    weight_grad = lax.dot_general(
        stacked, flattened, (((0,), (0,)), ((), ())), preferred_element_type=jnp.float32
    )
    padded = extended(gradient, (("blk", 0),), 1)
    mirrored = gather_taps(padded, seg_pad, seg_rows, -1).reshape(row_count * width, 9, channels)
    kernel = weight_matrix.reshape(9, channels, channels)
    result = lax.dot_general(
        mirrored, kernel, (((1, 2), (0, 2)), ((), ())), preferred_element_type=jnp.float32
    )
    return (result.reshape(row_count, width, channels), weight_grad)


def attention_forward(
    queries, keys_local, values_local, token_seg, first_row, second_row, width, scale
):
    token_count, channels = queries.shape

    def absorb(running, portion, offset):
        key_block, value_block = portion
        maximum, totals, accumulated = running
        key_seg = canvas_index(
            jnp.arange(key_block.shape[0], dtype=jnp.int32) // width, first_row, second_row
        )
        shared = token_seg[:, None] == key_seg[None, :]
        scores = (
            lax.dot_general(
                queries, key_block, (((1,), (1,)), ((), ())), preferred_element_type=jnp.float32
            )
            * scale
        )
        masked = jnp.where(shared, scores, NEGATIVE)
        new_maximum = jnp.maximum(maximum, jnp.max(masked, axis=1))
        weights = jnp.where(shared, jnp.exp(masked - new_maximum[:, None]), 0.0)
        totals = jnp.sum(weights, axis=1)
        accumulated = jnp.dot(
            weights.astype(jnp.bfloat16), value_block, preferred_element_type=jnp.float32
        )
        return (new_maximum, totals, accumulated)

    initial = (
        jnp.full((token_count,), NEGATIVE, jnp.float32),
        jnp.zeros((token_count,), jnp.float32),
        jnp.zeros((token_count, channels), jnp.float32),
    )
    maximum, totals, accumulated = absorb(
        initial,
        (
            lax.all_gather(keys_local, "blk", axis=0, tiled=True),
            lax.all_gather(values_local, "blk", axis=0, tiled=True),
        ),
        jnp.int32(0),
    )
    return (accumulated / totals[:, None], maximum + jnp.log(totals))


def attention_query_grad(
    queries,
    heads_grad,
    log_total,
    correction,
    keys_local,
    values_local,
    token_seg,
    first_row,
    second_row,
    width,
    scale,
):

    def absorb(running, portion, offset):
        key_block, value_block = portion
        key_seg = canvas_index(
            jnp.arange(key_block.shape[0], dtype=jnp.int32) // width, first_row, second_row
        )
        shared = token_seg[:, None] == key_seg[None, :]
        scores = (
            lax.dot_general(
                queries, key_block, (((1,), (1,)), ((), ())), preferred_element_type=jnp.float32
            )
            * scale
        )
        weights = jnp.where(
            shared, jnp.exp(jnp.where(shared, scores, NEGATIVE) - log_total[:, None]), 0.0
        )
        slopes = lax.dot_general(
            heads_grad, value_block, (((1,), (1,)), ((), ())), preferred_element_type=jnp.float32
        )
        score_grad = (weights * (slopes - correction[:, None])).astype(jnp.bfloat16)
        return jnp.dot(score_grad, key_block, preferred_element_type=jnp.float32) * scale

    return absorb(
        jnp.zeros(queries.shape, jnp.float32),
        (
            lax.all_gather(keys_local, "blk", axis=0, tiled=True),
            lax.all_gather(values_local, "blk", axis=0, tiled=True),
        ),
        jnp.int32(0),
    )


def attention_key_grad(
    queries,
    heads_grad,
    log_total,
    correction,
    keys_local,
    values_local,
    token_seg,
    first_row,
    second_row,
    width,
    scale,
):

    def absorb(running, portion, offset):
        query_part, upstream_part, total_part, correct_part = portion
        query_seg = canvas_index(
            jnp.arange(query_part.shape[0], dtype=jnp.int32) // width, first_row, second_row
        )
        query_low = query_part.astype(jnp.bfloat16)
        upstream_low = upstream_part.astype(jnp.bfloat16)
        shared = query_seg[:, None] == token_seg[None, :]
        scores = (
            lax.dot_general(
                query_low, keys_local, (((1,), (1,)), ((), ())), preferred_element_type=jnp.float32
            )
            * scale
        )
        weights = jnp.where(
            shared, jnp.exp(jnp.where(shared, scores, NEGATIVE) - total_part[:, None]), 0.0
        )
        value_acc = lax.dot_general(
            weights.astype(jnp.bfloat16),
            upstream_low,
            (((0,), (0,)), ((), ())),
            preferred_element_type=jnp.float32,
        )
        slopes = lax.dot_general(
            upstream_low, values_local, (((1,), (1,)), ((), ())), preferred_element_type=jnp.float32
        )
        score_grad = (weights * (slopes - correct_part[:, None])).astype(jnp.bfloat16)
        key_acc = (
            lax.dot_general(
                score_grad, query_low, (((0,), (0,)), ((), ())), preferred_element_type=jnp.float32
            )
            * scale
        )
        return (key_acc, value_acc)

    empty = jnp.zeros(keys_local.shape, jnp.float32)
    return absorb(
        (empty, empty),
        (
            lax.all_gather(queries.astype(jnp.float32), "blk", axis=0, tiled=True),
            lax.all_gather(heads_grad.astype(jnp.float32), "blk", axis=0, tiled=True),
            lax.all_gather(log_total, "blk", axis=0, tiled=True),
            lax.all_gather(correction, "blk", axis=0, tiled=True),
        ),
        jnp.int32(0),
    )


def collect(
    conv1_weight,
    conv2_weight,
    query_weight,
    key_weight,
    value_weight,
    output_weight,
    norm1_gain,
    norm1_shift,
    norm2_gain,
    norm2_shift,
    norm3_gain,
    norm3_shift,
):
    row_parts = (
        lax.all_gather(conv1_weight, "blk", axis=0, tiled=True),
        lax.all_gather(conv2_weight, "blk", axis=0, tiled=True),
        lax.all_gather(query_weight, "blk", axis=0, tiled=True),
        lax.all_gather(key_weight, "blk", axis=0, tiled=True),
        lax.all_gather(value_weight, "blk", axis=0, tiled=True),
        lax.all_gather(output_weight, "blk", axis=0, tiled=True),
        lax.all_gather(norm1_gain, "blk", axis=0, tiled=True),
        lax.all_gather(norm1_shift, "blk", axis=0, tiled=True),
        lax.all_gather(norm2_gain, "blk", axis=0, tiled=True),
        lax.all_gather(norm2_shift, "blk", axis=0, tiled=True),
        lax.all_gather(norm3_gain, "blk", axis=0, tiled=True),
        lax.all_gather(norm3_shift, "blk", axis=0, tiled=True),
    )
    full_parts = (
        lax.all_gather(row_parts[0], "dp", axis=1, tiled=True),
        lax.all_gather(row_parts[1], "dp", axis=1, tiled=True),
        lax.all_gather(row_parts[2], "dp", axis=1, tiled=True),
        lax.all_gather(row_parts[3], "dp", axis=1, tiled=True),
        lax.all_gather(row_parts[4], "dp", axis=1, tiled=True),
        lax.all_gather(row_parts[5], "dp", axis=1, tiled=True),
    )
    return (tuple(full_parts), tuple(row_parts[6:]))


def reduce_all(gradients):
    row_sums = (
        lax.psum_scatter(gradients[0], "blk", scatter_dimension=0, tiled=True),
        lax.psum_scatter(gradients[1], "blk", scatter_dimension=0, tiled=True),
        lax.psum_scatter(gradients[2], "blk", scatter_dimension=0, tiled=True),
        lax.psum_scatter(gradients[3], "blk", scatter_dimension=0, tiled=True),
        lax.psum_scatter(gradients[4], "blk", scatter_dimension=0, tiled=True),
        lax.psum_scatter(gradients[5], "blk", scatter_dimension=0, tiled=True),
        lax.psum_scatter(gradients[6], "blk", scatter_dimension=0, tiled=True),
        lax.psum_scatter(gradients[7], "blk", scatter_dimension=0, tiled=True),
        lax.psum_scatter(gradients[8], "blk", scatter_dimension=0, tiled=True),
        lax.psum_scatter(gradients[9], "blk", scatter_dimension=0, tiled=True),
        lax.psum_scatter(gradients[10], "blk", scatter_dimension=0, tiled=True),
        lax.psum_scatter(gradients[11], "blk", scatter_dimension=0, tiled=True),
    )
    matrix_sums = (
        lax.psum_scatter(row_sums[0], "dp", scatter_dimension=1, tiled=True),
        lax.psum_scatter(row_sums[1], "dp", scatter_dimension=1, tiled=True),
        lax.psum_scatter(row_sums[2], "dp", scatter_dimension=1, tiled=True),
        lax.psum_scatter(row_sums[3], "dp", scatter_dimension=1, tiled=True),
        lax.psum_scatter(row_sums[4], "dp", scatter_dimension=1, tiled=True),
        lax.psum_scatter(row_sums[5], "dp", scatter_dimension=1, tiled=True),
    )
    norm_sums = lax.psum(
        (row_sums[6], row_sums[7], row_sums[8], row_sums[9], row_sums[10], row_sums[11]), "dp"
    )
    return tuple(matrix_sums) + tuple(norm_sums)


def one_batch(inputs_low, bound_pair, upstream_low, matrices, norm_params, position, blocks):
    row_count, width, channels = inputs_low.shape
    token_count = row_count * width
    total_rows = row_count * blocks
    scale = channels ** (-0.5)
    first_row = bound_pair[0]
    second_row = bound_pair[1]
    local_rows = position * row_count + jnp.arange(row_count, dtype=jnp.int32)
    padded_rows = position * row_count - 1 + jnp.arange(row_count + 2, dtype=jnp.int32)
    seg_rows = canvas_index(local_rows, first_row, second_row)
    seg_pad = canvas_index(padded_rows, first_row, second_row)
    member = (seg_rows[:, None] == jnp.arange(CANVASES, dtype=jnp.int32)[None, :]).astype(
        jnp.float32
    )
    counts = jnp.stack([first_row, second_row - first_row, total_rows - second_row]).astype(
        jnp.float32
    ) * float(width * (channels // GROUPS))
    gains = [item.astype(jnp.float32) for item in norm_params]
    inputs = inputs_low.astype(jnp.float32)
    norm_one, normal_one, scale_one = norm_forward(inputs, member, counts, gains[0], gains[1])
    act_one = swish(norm_one).astype(jnp.bfloat16)
    hidden_one, stacked_one = conv_apply(act_one, seg_pad, seg_rows, matrices[0])
    norm_two, normal_two, scale_two = norm_forward(hidden_one, member, counts, gains[2], gains[3])
    act_two = swish(norm_two).astype(jnp.bfloat16)
    hidden_two, stacked_two = conv_apply(act_two, seg_pad, seg_rows, matrices[1])
    residual = inputs + hidden_two
    norm_three, normal_three, scale_three = norm_forward(
        residual, member, counts, gains[4], gains[5]
    )
    normed = norm_three.astype(jnp.bfloat16).reshape(token_count, channels)
    queries = jnp.dot(normed, matrices[2], preferred_element_type=jnp.float32).astype(jnp.bfloat16)
    keys_local = jnp.dot(normed, matrices[3], preferred_element_type=jnp.float32).astype(
        jnp.bfloat16
    )
    values_local = jnp.dot(normed, matrices[4], preferred_element_type=jnp.float32).astype(
        jnp.bfloat16
    )
    token_seg = jnp.repeat(seg_rows, width)
    attended, log_total = attention_forward(
        queries, keys_local, values_local, token_seg, first_row, second_row, width, scale
    )
    heads = attended.astype(jnp.bfloat16)
    activation = residual + jnp.dot(heads, matrices[5], preferred_element_type=jnp.float32).reshape(
        row_count, width, channels
    )
    upstream = upstream_low.reshape(token_count, channels)
    output_weight_grad = lax.dot_general(
        heads, upstream, (((0,), (0,)), ((), ())), preferred_element_type=jnp.float32
    )
    heads_grad = lax.dot_general(
        upstream, matrices[5], (((1,), (1,)), ((), ())), preferred_element_type=jnp.float32
    ).astype(jnp.bfloat16)
    correction = jnp.sum(heads_grad.astype(jnp.float32) * attended, axis=1)
    query_sum = attention_query_grad(
        queries,
        heads_grad,
        log_total,
        correction,
        keys_local,
        values_local,
        token_seg,
        first_row,
        second_row,
        width,
        scale,
    )
    key_sum, value_sum = attention_key_grad(
        queries,
        heads_grad,
        log_total,
        correction,
        keys_local,
        values_local,
        token_seg,
        first_row,
        second_row,
        width,
        scale,
    )
    query_low = query_sum.astype(jnp.bfloat16)
    key_low = key_sum.astype(jnp.bfloat16)
    value_low = value_sum.astype(jnp.bfloat16)
    contract_rows = (((0,), (0,)), ((), ()))
    contract_cols = (((1,), (1,)), ((), ()))
    query_weight_grad = lax.dot_general(
        normed, query_low, contract_rows, preferred_element_type=jnp.float32
    )
    key_weight_grad = lax.dot_general(
        normed, key_low, contract_rows, preferred_element_type=jnp.float32
    )
    value_weight_grad = lax.dot_general(
        normed, value_low, contract_rows, preferred_element_type=jnp.float32
    )
    normed_grad = (
        lax.dot_general(query_low, matrices[2], contract_cols, preferred_element_type=jnp.float32)
        + lax.dot_general(key_low, matrices[3], contract_cols, preferred_element_type=jnp.float32)
        + lax.dot_general(value_low, matrices[4], contract_cols, preferred_element_type=jnp.float32)
    )
    back_three, gain_three_grad, shift_three_grad = norm_backward(
        normed_grad.reshape(row_count, width, channels),
        normal_three,
        scale_three,
        member,
        counts,
        gains[4],
    )
    residual_grad = upstream_low.astype(jnp.float32) + back_three
    act_two_grad, conv_two_grad = conv_reverse(
        residual_grad.astype(jnp.bfloat16), stacked_two, seg_pad, seg_rows, matrices[1]
    )
    back_two, gain_two_grad, shift_two_grad = norm_backward(
        act_two_grad * swish_slope(norm_two), normal_two, scale_two, member, counts, gains[2]
    )
    act_one_grad, conv_one_grad = conv_reverse(
        back_two.astype(jnp.bfloat16), stacked_one, seg_pad, seg_rows, matrices[0]
    )
    back_one, gain_one_grad, shift_one_grad = norm_backward(
        act_one_grad * swish_slope(norm_one), normal_one, scale_one, member, counts, gains[0]
    )
    input_grad = residual_grad + back_one
    local_grads = (
        conv_one_grad,
        conv_two_grad,
        query_weight_grad,
        key_weight_grad,
        value_weight_grad,
        output_weight_grad,
        gain_one_grad,
        shift_one_grad,
        gain_two_grad,
        shift_two_grad,
        gain_three_grad,
        shift_three_grad,
    )
    return (activation, input_grad, local_grads)


def shards(
    features,
    bounds,
    out_grad,
    norm1_gain,
    norm1_shift,
    conv1_weight,
    norm2_gain,
    norm2_shift,
    conv2_weight,
    norm3_gain,
    norm3_shift,
    query_weight,
    key_weight,
    value_weight,
    output_weight,
):
    blocks = lax.axis_size("blk")
    position = lax.axis_index("blk")
    micro_count = features.shape[1]
    shard_sums = None
    outputs = []
    input_grads = []
    for micro_index in range(micro_count):
        matrices, norm_params = collect(
            conv1_weight,
            conv2_weight,
            query_weight,
            key_weight,
            value_weight,
            output_weight,
            norm1_gain,
            norm1_shift,
            norm2_gain,
            norm2_shift,
            norm3_gain,
            norm3_shift,
        )
        activation, input_grad, local_grads = one_batch(
            features[0, micro_index],
            bounds[0, micro_index],
            out_grad[0, micro_index],
            matrices,
            norm_params,
            position,
            blocks,
        )
        outputs.append(activation)
        input_grads.append(input_grad)
        reduced = reduce_all(local_grads)
        shard_sums = (
            reduced
            if shard_sums is None
            else tuple((acc + new for acc, new in zip(shard_sums, reduced)))
        )
    activations = jnp.stack(outputs)[None]
    input_grad_all = jnp.stack(input_grads)[None]
    return (
        activations,
        input_grad_all,
        shard_sums[6],
        shard_sums[7],
        shard_sums[0],
        shard_sums[8],
        shard_sums[9],
        shard_sums[1],
        shard_sums[10],
        shard_sums[11],
        shard_sums[2],
        shard_sums[3],
        shard_sums[4],
        shard_sums[5],
    )


def solution(mesh):
    in_specs = (
        P("dp", None, "blk", None, None),
        P("dp", None, None),
        P("dp", None, "blk", None, None),
        P("blk"),
        P("blk"),
        P("blk", "dp"),
        P("blk"),
        P("blk"),
        P("blk", "dp"),
        P("blk"),
        P("blk"),
        P("blk", "dp"),
        P("blk", "dp"),
        P("blk", "dp"),
        P("blk", "dp"),
    )
    out_specs = (
        P("dp", None, "blk", None, None),
        P("dp", None, "blk", None, None),
        P("blk"),
        P("blk"),
        P("blk", "dp"),
        P("blk"),
        P("blk"),
        P("blk", "dp"),
        P("blk"),
        P("blk"),
        P("blk", "dp"),
        P("blk", "dp"),
        P("blk", "dp"),
        P("blk", "dp"),
    )
    near = mesh.shape["dp"] == 4 and mesh.shape["blk"] == 8
    return jax.shard_map(unit_shards if near else shards, mesh=mesh, in_specs=in_specs, out_specs=out_specs, check_vma=False)
```

```python
import functools
import types

import jax
import jax.numpy as jnp
from jax import lax
from jax.experimental import pallas as pl
from jax.experimental.pallas import tpu as pltpu
from jax.sharding import PartitionSpec as P

GROUPS = 32
CANVASES = 3


EPSILON = 1e-06
HIGHEST = lax.Precision.HIGHEST
NEGATIVE = -1e30
MESH = pl.DeviceIdType.MESH
def in_order(s):
    s.ow(), s.gpl0(), s.g1l0(), s.g1o0(), s.g2o0(), s.gpo0(), s.g2l0(), s.gpl1()
    s.gao0(), s.g1l1(), s.g2y0(), s.gpl2(), s.g1y0(), s.gpo2(), s.g1x0(), s.gpo1()
    s.g2l1(), s.gpl3(), s.g1o1(), s.gpo3(), s.g1l2(), s.gal0(), s.g2o1(), s.g1o2()
    s.gpx2(), s.g1l3(), s.gpy3(), s.gpx1(), s.gpy0(), s.g1o3(), s.gpx0(), s.xs()
    s.g2x0(), s.gal1(), s.gpy1(), s.gpx3(), s.g2l2(), s.g1x1(), s.gpy2(), s.g1x2()
    s.g1y3(), s.g1x3(), s.g1y2(), s.bw(), s.gal2(), s.g2l3(), s.gpd3(), s.gpd1()
    s.g2o3(), s.gal3(), s.os(), s.gpd0(), s.n1a(), s.gpd2(), s.g1y1(), s.gax0()
    s.g1d0(), s.g1d3(), s.g2o2(), s.n1b(), s.n1c(), s.gao2(), s.gao3(), s.g1d1()
    s.g1d2(), s.n1d(), s.gao1(), s.g2y3(), s.g1a(), s.n1e(), s.c10(), s.c11()
    s.n2a(), s.gay3(), s.gay0(), s.g2x3(), s.g2d0(), s.g2x2(), s.g2x1(), s.g2y2()
    s.gax1(), s.g2y1(), s.gay2(), s.gay1(), s.n2b(), s.n2c(), s.ob(), s.gax3()
    s.n2d(), s.n2e(), s.g2d3(), s.g2d2(), s.g2d1(), s.g2a(), s.c20(), s.c21()
    s.gax2(), s.gad1(), s.n3a(), s.t1(), s.or0(), s.gad3(), s.gad2(), s.gad0()
    s.or1(), s.n3b(), s.n3c(), s.t2(), s.gaa(), s.po0(), s.pj1(), s.nr0()
    s.po1(), s.po2(), s.pj0(), s.po3(), s.nr1(), s.pj2(), s.pj3(), s.qf()
    s.qb(), s.hw(), s.gz(), s.hd(), s.ks(), s.an(), s.b3a(), s.aw()
    s.rab0(), s.rab2(), s.rab1(), s.rab3(), s.b3b(), s.b3c(), s.rac1(), s.rac3()
    s.rac2(), s.rac0(), s.b3d(), s.w20(), s.d20(), s.d21(), s.b2a(), s.w21()
    s.rae2(), s.r2b0(), s.w22(), s.r2b3(), s.r2b1(), s.rae1(), s.b2b(), s.r2b2()
    s.r2c3(), s.r2c2(), s.r2c1(), s.b2c(), s.rae0(), s.raf2(), s.b2d(), s.d10()
    s.d11(), s.b1a(), s.raf1(), s.r2e3(), s.r2e2(), s.w10(), s.b1m(), s.rae3()
    s.ps(), s.b1b(), s.r2c0(), s.r1b0(), s.w11(), s.r1b1(), s.w12(), s.r2f2()
    s.py(), s.r1b3(), s.r1b2(), s.r2f3(), s.r1c3(), s.r2e1(), s.raf0(), s.r1e3()
    s.r1c2(), s.raf3(), s.r1f3(), s.r1c1(), s.r2f1(), s.r1e2(), s.r1e1(), s.r1c0()
    s.pz(), s.r2e0(), s.r1f2(), s.r1f1(), s.rat(), s.r1e0(), s.r2f0(), s.r2t()
    s.r1f0(), s.r1t()


DIRECT = (False, False, False, False)
LIMIT = 60 << 20
SPLIT, SPLIT_A = 432, 192
CUT, CUT_A = 112, 48


class Place:
    def __init__(self):
        self.d = lax.axis_index("dp")
        self.b = lax.axis_index("blk")
        self.y, self.c = self.d // 2, self.d % 2
        self.z, self.x = self.b // 2, self.b % 2
        self.up = {"dp": self.d, "blk": self.b + 2}
        self.down = {"dp": self.d, "blk": self.b - 2}
        self.xn = {"dp": self.d, "blk": self.z * 2 + 1 - self.x}
        self.yn = {"dp": (1 - self.y) * 2 + self.c, "blk": self.b}
        self.cn = {"dp": self.y * 2 + 1 - self.c, "blk": self.b}


def remote(src, dst, send, recv, device):
    return pltpu.make_async_remote_copy(
        src_ref=src, dst_ref=dst, send_sem=send, recv_sem=recv, device_id=device, device_id_type=MESH
    )


def steps_of(z, nz):
    visits = [(z, None)]
    for k in range(1, nz):
        visits.append((z - k, z >= k))
        visits.append((z + k, z + k < nz))
    return visits


def guarded(valid, body):
    if valid is None:
        body()
    else:
        pl.when(valid)(body)


class Gather:
    SEMS = 27

    def __init__(self, here, nz, at, block, sems, direct):
        self.here, self.nz, self.at, self.block, self.sems, self.direct = here, nz, at, block, sems, direct
        self.visits = steps_of(here.z, nz)

    def ends(self, kind, z):
        if kind[0] == "c":
            return self.sems.at[26], self.sems.at[16]
        send = {"z": 17 + z, "zd": 21 + z}.get(kind, 25)
        recv = {"z": 0, "zd": 0, "x": 4, "y": 8, "da": 12, "db": 12}[kind] + z
        return self.sems.at[send], self.sems.at[recv]

    def cp(self, kind, z, src, device):
        return remote(src, src, *self.ends(kind, z), device)

    def own(self, z):
        return self.at(z, self.here.x, self.here.d, None)

    def colx(self, z, half=None):
        return self.at(z, 1 - self.here.x, self.here.d, half)

    def coly(self, z, half=None):
        return self.at(z, self.here.x, (1 - self.here.y) * 2 + self.here.c, half)

    def cold(self, z, half=None):
        return self.at(z, 1 - self.here.x, (1 - self.here.y) * 2 + self.here.c, half)

    def line_cp(self, k):
        here = self.here
        z = (here.z + k) % self.nz
        device = {"dp": here.d, "blk": z * 2 + here.x}
        return remote(self.own(here.z), self.own(here.z), self.sems.at[17 + z], self.sems.at[here.z], device)

    def line(self, j):
        z, valid = self.visits[j]
        here = self.here
        if j == 0 and self.direct:
            for k in range(1, self.nz):
                self.line_cp(k).start()
            return

        def body():
            src = self.own(z)
            if j > 0:
                self.cp("z", z, src, here.up).wait_recv()
            if self.direct:
                return
            if j == 0 or j % 2 == 1:

                @pl.when(here.z < self.nz - 1)
                def _():
                    self.cp("z", z, src, here.up).start()

            if j == 0 or j % 2 == 0:

                @pl.when(here.z > 0)
                def _():
                    self.cp("zd", z, src, here.down).start()

        guarded(valid, body)

    def out(self, j):
        z, valid = self.visits[j]
        here = self.here

        def body():
            src = self.own(z)
            self.cp("x", z, src, here.xn).start()
            self.cp("y", z, src, here.yn).start()
            self.cp("co", z, src, here.cn).start()

        guarded(valid, body)

    def have(self, j):
        self.line(j)
        self.out(j)

    def from_x(self, j):
        z, valid = self.visits[j]

        def body():
            self.cp("x", z, self.colx(z), self.here.xn).wait_recv()
            self.cp("da", z, self.colx(z, 0), self.here.yn).start()
            self.cp("cx", z, self.colx(z), self.here.cn).start()

        guarded(valid, body)

    def from_y(self, j):
        z, valid = self.visits[j]

        def body():
            self.cp("y", z, self.coly(z), self.here.yn).wait_recv()
            self.cp("db", z, self.coly(z, 1), self.here.xn).start()
            self.cp("cy", z, self.coly(z), self.here.cn).start()

        guarded(valid, body)

    def cross(self, j):
        self.from_x(j)
        self.from_y(j)

    def diagonal(self, j):
        z, valid = self.visits[j]
        here = self.here

        def body():
            self.cp("da", z, self.cold(z), here.yn).wait_recv()
            self.cp("cd", z, self.cold(z), here.cn).start()

        guarded(valid, body)

    def arrive(self):
        self.cp("co", 0, self.block(4 * self.nz), self.here.cn).wait_recv()

    def finish(self):
        here = self.here
        if self.direct:
            for k in range(1, self.nz):
                self.line_cp(k).wait_send()
        else:
            for j, (z, valid) in enumerate(self.visits):
                valid = True if valid is None else valid
                if j == 0 or j % 2 == 1:
                    going = jnp.logical_and(valid, here.z < self.nz - 1)
                    pl.when(going)(lambda: self.cp("z", z, self.own(z), here.up).wait_send())
                if j == 0 or j % 2 == 0:
                    going = jnp.logical_and(valid, here.z > 0)
                    pl.when(going)(lambda: self.cp("zd", z, self.own(z), here.down).wait_send())
        self.cp("x", 0, self.block(3 * self.nz), here.xn).wait_send()
        self.cp("co", 0, self.block(4 * self.nz), here.cn).wait_send()

    def table(self, name):
        kinds = {"l": self.line, "o": self.out, "x": self.from_x, "y": self.from_y, "d": self.diagonal}
        found = {name + "a": self.arrive}
        for kind, step in kinds.items():
            for k in range(self.nz):
                js = (0,) if k == 0 else (2 * k - 1, 2 * k)
                found["%s%s%d" % (name, kind, k)] = lambda js=js, step=step: [step(j) for j in js]
        return found


class Scatter:
    SEMS = 20

    def __init__(self, here, nz, at, core_at, part, block, sems, bufs):
        self.here, self.nz, self.at, self.core_at, self.part = here, nz, at, core_at, part
        self.block, self.sems = block, sems
        self.half, self.side, self.last = bufs
        self.visits = steps_of(here.z, nz)[::-1]

    def cp(self, send, recv, src, dst, device):
        return remote(src, dst, self.sems.at[17 + send], self.sems.at[recv], device)

    def places(self, z, c):
        here = self.here
        y, x = here.y, here.x
        return [(z, x, y * 2 + c), (z, 1 - x, y * 2 + c), (z, x, (1 - y) * 2 + c), (z, 1 - x, (1 - y) * 2 + c)]

    def mine(self, z, k):
        return self.at(*self.places(z, self.here.c)[k])

    def core_cp(self, z, k):
        place = self.places(z, 1 - self.here.c)[k]
        return self.cp(0, z, self.at(*place), self.core_at(k, *place), self.here.cn)

    def core_in(self, z, k):
        return self.core_at(k, *self.places(z, self.here.c)[k])[...]

    def begin(self, z):
        for k in (3, 1, 2, 0):
            self.core_cp(z, k).start()

    def half_cp(self, z, h):
        return self.cp(1, 4 + 4 * h + z, self.part(self.mine(z, 3), h), self.half[h].at[z], (self.here.xn, self.here.yn)[h])

    def side_cp(self, z, side, h):
        return self.cp(
            1, 12 + z, self.part(self.mine(z, 1 + side), h), self.part(self.side.at[side, z], h),
            (self.here.xn, self.here.yn)[side],
        )

    def corner(self, j):
        z, valid = self.visits[j]

        def body():
            self.cp(0, z, self.block(4), self.block(4), self.here.cn).wait_recv()
            for k in (3, 1, 2):
                place = self.mine(z, k)
                place[...] = place[...] + self.core_in(z, k)
                if k == 3:
                    self.half_cp(z, 0).start()
                    self.half_cp(z, 1).start()
                else:
                    self.side_cp(z, k - 1, k - 1).start()

        guarded(valid, body)

    def edges(self, j):
        z, valid = self.visits[j]

        def body():
            for side, h in ((0, 1), (1, 0)):
                self.half_cp(z, h).wait_recv()
                place = self.part(self.mine(z, 1 + side), h)
                place[...] = place[...] + self.half[h][z]
                self.side_cp(z, side, h).start()

        guarded(valid, body)

    def column(self, j, out):
        z, valid = self.visits[j]
        here = self.here

        def body():
            place = self.mine(z, 0)
            total = place[...].astype(jnp.float32) + self.core_in(z, 0).astype(jnp.float32)
            self.cp(1, 12 + z, self.side.at[:, z], self.side.at[:, z], here.xn).wait_recv()
            for side in (0, 1):
                total = total + self.side[side, z].astype(jnp.float32)
            if j == len(self.visits) - 1:
                out[...] = total
            else:
                place[...] = total.astype(jnp.bfloat16)
                self.last_cp(z).start()

        guarded(valid, body)

    def last_cp(self, z):
        here = self.here
        device = {"dp": here.d, "blk": z * 2 + here.x}
        return self.cp(2, 16, self.mine(z, 0), self.last.at[here.z], device)

    def others(self):
        others = self.last.at[pl.ds(0, self.nz - 1)]
        return self.cp(2, 16, others, others, self.here.up)

    def total(self, out):
        here = self.here
        self.others().wait_recv()
        for k in range(1, self.nz):
            out[...] += self.last[(here.z + k) % self.nz].astype(jnp.float32)

    def finish(self):
        here = self.here
        self.cp(0, 0, self.block(4 * self.nz), self.block(4 * self.nz), here.cn).wait_send()
        self.cp(1, 0, self.block(3 * self.nz), self.block(3 * self.nz), here.xn).wait_send()
        self.others().wait_send()

    def table(self, name, out):
        kinds = {"c": self.corner, "e": self.edges, "f": lambda j: self.column(j, out)}
        top = 2 * (self.nz - 1)
        found = {name + "t": lambda: self.total(out)}
        for z in range(self.nz):
            found["%sb%d" % (name, z)] = functools.partial(self.begin, z)
        for kind, step in kinds.items():
            for k in range(self.nz):
                js = (top,) if k == 0 else (top - 2 * k, top - 2 * k + 1)
                found["%s%s%d" % (name, kind, k)] = lambda js=js, step=step: [step(j) for j in js]
        return found


def part_of(ref, half, split, rows):
    return ref.at[pl.ds(0, split)] if half == 0 else ref.at[pl.ds(split, rows - split)]


def weight_block(ref):
    return lambda n: ref.at[pl.ds(0, n * 288), pl.ds(0, 256)]


def stacked_block(ref):
    return lambda n: ref.at[pl.ds(0, n // 2), :, pl.ds(0, 256)]


def weight_places(ref, rows, split=0):
    def at(z, x, d, half=None):
        base, count = (z * 2 + x) * rows, rows
        if half is not None:
            base, count = base + half * split, rows - split if half else split
        return ref.at[pl.ds(pl.multiple_of(base, 16), count), pl.ds(pl.multiple_of(d * 128, 128), 128)]

    return at


BF = jnp.bfloat16
F32 = jnp.float32
ROW = 8
PARAMS = 16


def both(a, b):
    return jnp.logical_and(a, b)


def cols(a, b):
    return lax.dot_general(a, b, (((1,), (1,)), ((), ())), preferred_element_type=F32)


def mm(a, b):
    return jnp.dot(a, b, preferred_element_type=F32)


class Unit(Place):
    def __init__(self):
        super().__init__()
        self.q = jnp.where(self.c == 0, self.x, 3 - self.x)
        self.mu = self.z % 2
        self.alone = self.z == self.q

    def member(self, q, z):
        return {"dp": self.y * 2 + q // 2, "blk": z * 2 + jnp.where(q < 2, q, 3 - q)}

    def peer(self, q):
        return self.member(q, self.z)

    def worker(self, m):
        return self.member(self.z, 2 * self.c + m)

    def keeper(self, h):
        return {"dp": self.y * 2 + self.z // 2, "blk": self.q * 2 + h}

    def column_worker(self, m):
        return {"dp": self.y * 2 + self.z // 2, "blk": (2 * self.c + m) * 2 + self.x}

    def column_keeper(self, k):
        return {"dp": self.y * 2 + self.z // 2, "blk": (2 * self.c + k) * 2 + self.x}

    def line(self, k):
        return {"dp": self.d, "blk": ((self.z + k) % 4) * 2 + self.x}

    def greet(self, shares, lines):
        barrier = pltpu.get_barrier_semaphore()

        def greet(device):
            pl.semaphore_signal(barrier, inc=1, device_id=device, device_id_type=MESH)

        for k in (1, 2, 3):
            greet(self.peer((self.q + k) % 4))
        count = 3
        if lines:
            greet(self.yn)
            for k in (1, 2, 3):
                greet(self.line(k))
            count += 4
        if shares:
            for m in (0, 1):
                pl.when(jnp.logical_not(both(self.alone, self.mu == m)))(lambda m=m: greet(self.worker(m)))
            for h in (0, 1):
                pl.when(jnp.logical_not(both(self.alone, self.x == h)))(lambda h=h: greet(self.keeper(h)))
            near = self.c == self.z // 2
            for k in (0, 1):
                pl.when(jnp.logical_not(both(near, self.mu == k)))(lambda k=k: greet(self.column_worker(k)))
            count = count + 6 - 2 * self.alone.astype(jnp.int32) - near.astype(jnp.int32)
        return count

    def enter(self, count):
        pl.semaphore_wait(pltpu.get_barrier_semaphore(), count)


class Share:
    def __init__(self, u, sems, local):
        self.u, self.sems, self.local = u, sems, local

    def send(self, src, dst):
        u = self.u
        for m in (0, 1):
            mine = both(u.alone, u.mu == m)
            place = dst.at[pl.ds(4 * u.x, 4)]
            pl.when(mine)(lambda: pltpu.make_async_copy(src.at[m], place, self.local).start())
            pl.when(jnp.logical_not(mine))(
                lambda: remote(src.at[m], place, self.sems.at[0, m], self.sems.at[1, u.x], u.worker(m)).start()
            )

    def wait(self, src, dst):
        u = self.u
        for h in (0, 1):
            mine = both(u.alone, u.x == h)
            place = dst.at[pl.ds(4 * h, 4)]
            pl.when(mine)(lambda: pltpu.make_async_copy(src.at[0], place, self.local).wait())
            pl.when(jnp.logical_not(mine))(
                lambda: remote(place, place, self.sems.at[0, 0], self.sems.at[1, h], u.keeper(h)).wait_recv()
            )

    def sent(self, src, dst):
        u = self.u
        for m in (0, 1):
            place = dst.at[pl.ds(4 * u.x, 4)]
            pl.when(jnp.logical_not(both(u.alone, u.mu == m)))(
                lambda: remote(src.at[m], place, self.sems.at[0, m], self.sems.at[1, u.x], u.worker(m)).wait_send()
            )

    def back(self, src, dst):
        u = self.u
        for h in (0, 1):
            mine = both(u.alone, u.x == h)
            piece = src.at[pl.ds(4 * h, 4)]
            pl.when(mine)(lambda: pltpu.make_async_copy(piece, dst.at[u.mu], self.local).start())
            pl.when(jnp.logical_not(mine))(
                lambda: remote(piece, dst.at[u.mu], self.sems.at[0, h], self.sems.at[1, u.mu], u.keeper(h)).start()
            )

    def back_wait(self, src, dst):
        u = self.u
        for m in (0, 1):
            mine = both(u.alone, u.mu == m)
            pl.when(mine)(lambda: pltpu.make_async_copy(src.at[pl.ds(0, 4)], dst.at[m], self.local).wait())
            pl.when(jnp.logical_not(mine))(
                lambda: remote(dst.at[m], dst.at[m], self.sems.at[0, 0], self.sems.at[1, m], u.worker(m)).wait_recv()
            )
        for h in (0, 1):
            pl.when(jnp.logical_not(both(u.alone, u.x == h)))(
                lambda: remote(
                    src.at[pl.ds(4 * h, 4)], dst.at[u.mu], self.sems.at[0, h], self.sems.at[1, u.mu], u.keeper(h)
                ).wait_send()
            )


class ColumnShare:
    def __init__(self, u, buf, sems, local):
        self.u, self.buf, self.sems, self.local = u, buf, sems, local
        self.alone = u.c == u.z // 2

    def place(self, z):
        return self.buf.at[z, pl.ds(4 * self.u.x, 4)]

    def cp(self, src, m):
        u = self.u
        return remote(src.at[m], self.place(u.z), self.sems.at[0, m], self.sems.at[1, u.mu], u.column_worker(m))

    def send(self, src):
        u = self.u
        for m in (0, 1):
            mine = both(self.alone, u.mu == m)
            pl.when(mine)(lambda: pltpu.make_async_copy(src.at[m], self.place(u.z), self.local).start())
            pl.when(jnp.logical_not(mine))(lambda: self.cp(src, m).start())

    def wait(self, src):
        u = self.u
        for k in (0, 1):
            mine = both(self.alone, u.mu == k)
            place = self.place(2 * u.c + k)
            pl.when(mine)(lambda: pltpu.make_async_copy(src.at[0], place, self.local).wait())
            pl.when(jnp.logical_not(mine))(
                lambda: remote(place, place, self.sems.at[0, 0], self.sems.at[1, k], u.column_keeper(k)).wait_recv()
            )

    def sent(self, src):
        u = self.u
        for m in (0, 1):
            pl.when(jnp.logical_not(both(self.alone, u.mu == m)))(lambda: self.cp(src, m).wait_send())


class Swap:
    def __init__(self, u, buf, sems):
        self.u, self.buf, self.sems = u, buf, sems

    def send(self):
        u = self.u
        block = self.buf.at[u.q]
        for k in (1, 2, 3):
            remote(block, block, self.sems.at[0], self.sems.at[1], u.peer((u.q + k) % 4)).start()

    def three(self):
        block = self.buf.at[pl.ds(0, 3)]
        return remote(block, block, self.sems.at[0], self.sems.at[1], self.u.cn)

    def wait(self):
        self.three().wait_recv()

    def sent(self):
        self.three().wait_send()

    def total(self):
        return self.buf[0] + self.buf[1] + self.buf[2] + self.buf[3]


class Spread:
    def __init__(self, u, buf, sems, parts):
        self.u, self.buf, self.sems, self.parts = u, buf, sems, parts

    def cp(self, kind, p, part):
        u = self.u
        ref = self.buf.at[p, part]
        device = u.xn if kind == 1 else u.cn
        return remote(ref, ref, self.sems.at[0, kind, part], self.sems.at[1, kind, part], device)

    def send(self, part):
        self.cp(1, self.u.q, part).start()
        self.cp(0, self.u.q, part).start()

    def across(self):
        q = self.u.q
        return q + 1 - 2 * (q % 2)

    def relay(self, part):
        copy = self.cp(1, self.across(), part)
        copy.wait_recv()
        self.cp(2, self.across(), part).start()

    def near(self, part):
        self.cp(0, 3 - self.u.q, part).wait_recv()

    def far(self, part):
        self.cp(2, 3 - self.across(), part).wait_recv()

    def sent(self, part):
        self.cp(1, self.u.q, part).wait_send()
        self.cp(0, self.u.q, part).wait_send()
        self.cp(2, self.across(), part).wait_send()


class Halo:
    def __init__(self, u, buf, sems):
        self.u, self.buf, self.sems = u, buf, sems

    def cp(self, downward):
        u, buf = self.u, self.buf
        if downward:
            return remote(buf.at[1], buf.at[ROW + 1], self.sems.at[0, 0], self.sems.at[1, 0], u.peer(jnp.maximum(u.q - 1, 0)))
        return remote(buf.at[ROW], buf.at[0], self.sems.at[0, 1], self.sems.at[1, 1], u.peer(jnp.minimum(u.q + 1, 3)))

    def send(self):
        u, buf = self.u, self.buf
        pl.when(u.q > 0)(lambda: self.cp(True).start())
        pl.when(u.q < 3)(lambda: self.cp(False).start())

        @pl.when(u.q == 0)
        def _():
            buf[0] = jnp.zeros(buf.shape[1:], buf.dtype)

        @pl.when(u.q == 3)
        def _():
            buf[ROW + 1] = jnp.zeros(buf.shape[1:], buf.dtype)

    def wait(self):
        u = self.u
        pl.when(u.q > 0)(lambda: self.cp(False).wait_recv())
        pl.when(u.q < 3)(lambda: self.cp(True).wait_recv())

    def sent(self):
        u = self.u
        pl.when(u.q > 0)(lambda: self.cp(True).wait_send())
        pl.when(u.q < 3)(lambda: self.cp(False).wait_send())


def canvas_of(rows, limits):
    return (rows >= limits[0:1]).astype(F32) + (rows >= limits[1:2]).astype(F32)


def row_numbers(u, offset, shape):
    return (ROW * u.q + offset + lax.broadcasted_iota(jnp.int32, shape, 0)).astype(F32)


def counts_of(limits, total_rows):
    each = 64.0 * 16.0
    return (limits[0:1] * each, (limits[1:2] - limits[0:1]) * each, (total_rows - limits[1:2]) * each)


def group_total(sums):
    width = sums.shape[1]
    lane = lax.broadcasted_iota(jnp.int32, sums.shape, 1)
    for step in (1, 2, 4, 8):
        after = pltpu.roll(sums, width - step, 1)
        before = pltpu.roll(sums, step, 1)
        sums = sums + jnp.where((lane // step) % 2 == 0, after, before)
    return sums


def canvas_sums(first, second, seg):
    out = []
    for rows in (first, second):
        for k in range(CANVASES):
            out.append(jnp.sum(jnp.where(seg == float(k), rows, 0.0), axis=0, keepdims=True))
    out.append(jnp.zeros((2, first.shape[1]), F32))
    return jnp.concatenate(out, axis=0)


def by_row(values, seg):
    return jnp.where(seg == 0.0, values[0], jnp.where(seg == 1.0, values[1], values[2]))


def moments(total, counts, seg):
    grouped = group_total(total)
    averages, inverses = [], []
    for k in range(CANVASES):
        average = grouped[k : k + 1] / counts[k]
        averages.append(average)
        inverses.append(lax.rsqrt(grouped[3 + k : 4 + k] / counts[k] - average * average + EPSILON))
    return by_row(averages, seg), by_row(inverses, seg)


def sigmoid(argument):
    return 0.5 * jnp.tanh(0.5 * argument) + 0.5


def each_row(body):
    lax.fori_loop(0, ROW, lambda r, carry: (body(r), carry)[1], 0)


def row_of(ref, r):
    return ref[pl.ds(r, 1), :]


def tap_masks(u, limits, masks):
    shape = (ROW, limits.shape[1])
    rows = row_numbers(u, 0, shape)
    seg = canvas_of(rows, limits)
    masks[0] = both(canvas_of(rows - 1.0, limits) == seg, rows >= 1.0).astype(F32)
    masks[1] = both(canvas_of(rows + 1.0, limits) == seg, rows < 4.0 * ROW - 1.0).astype(F32)
    return seg


def shifted(line):
    position = lax.broadcasted_iota(jnp.int32, line.shape, 0)
    width = line.shape[0]
    before = jnp.where(position == 0, 0.0, pltpu.roll(line, 1, 0))
    after = jnp.where(position == width - 1, 0.0, pltpu.roll(line, width - 1, 0))
    return before, line, after


def taps_inner(buf, masks, taps):
    def body(s):
        lines = shifted(buf[s + 1].astype(F32))
        for k in range(3):
            taps[3 + k, s] = lines[k].astype(BF)

        @pl.when(s < ROW - 1)
        def _():
            mask = masks[0, pl.ds(s + 1, 1), :]
            for k in range(3):
                taps[k, s + 1] = (lines[k] * mask).astype(BF)

        @pl.when(s > 0)
        def _():
            mask = masks[1, pl.ds(s - 1, 1), :]
            for k in range(3):
                taps[6 + k, s - 1] = (lines[k] * mask).astype(BF)

    each_row(body)


def taps_outer(buf, masks, taps):
    for k, line in enumerate(shifted(buf[0].astype(F32))):
        taps[k, 0] = (line * masks[0, 0:1, :]).astype(BF)
    for k, line in enumerate(shifted(buf[ROW + 1].astype(F32))):
        taps[6 + k, ROW - 1] = (line * masks[1, ROW - 1 : ROW, :]).astype(BF)


def conv_tile(taps, weight, m, flip):
    total = None
    for tap in range(9):
        left = taps[8 - tap if flip else tap, pl.ds(pl.multiple_of(m * 4, 4), 4)].reshape(256, -1)
        right = weight[tap * 512 : (tap + 1) * 512, :]
        term = cols(left, right) if flip else mm(left, right)
        total = term if total is None else total + term
    return total.reshape(4, 64, -1)


def conv_weight_grad(act_t, taps, out, first, last):
    def body(tap, carry):
        piece = mm(act_t[...], taps[8 - tap].reshape(512, -1))
        out[pl.ds(pl.multiple_of(tap * 512, 512), 512), :] = piece.astype(BF)
        return carry

    lax.fori_loop(first, last, body, 0)


def attn_places(ref, split=0):
    def at(z, x, d, half=None):
        place = ref.at[z * 2 + x]
        lanes = pl.ds(pl.multiple_of(d * 128, 128), 128)
        if half is None:
            return place.at[:, lanes]
        return place.at[pl.ds(half * split, 256 - split if half else split), lanes]

    return at


def param_places(ref):
    def at(z, x, d, half=None):
        place = ref.at[z * 2 + x]
        lanes = pl.ds(pl.multiple_of(d * 128, 128), 128)
        if half is None:
            return place.at[:, lanes]
        return place.at[pl.ds(half * 8, 8), lanes]

    return at


class Halves:
    def __init__(self, ref):
        self.ref = ref

    @property
    def at(self):
        return self

    def __getitem__(self, index):
        member, part = index
        return self.ref.at[member, pl.ds(part * (ROW // 2), ROW // 2)]


ANY = pl.BlockSpec(memory_space=pl.ANY)
VM = pl.BlockSpec(memory_space=pltpu.VMEM)


class Blocks:
    def __init__(self, ref):
        self.ref = ref

    @property
    def at(self):
        return self

    def __getitem__(self, index):
        member, part = index
        x = jnp.where(member < 2, member, 3 - member)
        return self.ref.at[2 * (member // 2) + part, pl.ds(4 * x, 4)]


def unit_inputs(bounds, norms):
    d, b = lax.axis_index("dp"), lax.axis_index("blk")
    rows = jnp.stack([item.astype(F32) for item in norms])
    lane = jnp.arange(128)[None] // 64
    params = jnp.where((d == b // 2) & (lane == b % 2), jnp.concatenate([rows, rows], axis=1), 0.0)
    limits = jnp.broadcast_to(bounds.reshape(-1).astype(F32)[:, None], (4, 128))
    blank = jnp.zeros((2, 128), F32)
    return jnp.concatenate([params, blank, limits, blank, blank])


def whole_kernel(
    feat, grad, par, s1, s2, sq, sk, sv, so,
    act_back, grad_back, weights_out, norm_out,
    w1, w2, wa, pb, bb, xin, oall, nall, taps, a1, a2, masks, hidden, resid, small, rows_a, rows_b, swaps, lds,
    wg1, wg2, scores, gk, gv, lcol, dcol, big, gres, low, act, act_t1, act_t2, ga, mine, psum_y, psum_z,
    core_a, core_2, half_a, rest_a, side_a, last_a, half_2, rest_2, side_2, last_2, half_1, rest_1, side_1, last_1,
    gsems, ssems, local, share_sems, bound_sems, swap_sems, spread_sems, halo_sems, py_sems, pz_sems,
):
    u = Unit()
    greeters = u.greet(True, True)
    mine[...] = jnp.zeros_like(mine)
    table = {}
    ats = (weight_places(w1, 576, SPLIT), weight_places(w2, 576, SPLIT), attn_places(wa, SPLIT_A), param_places(pb))
    blocks = (weight_block(w1), weight_block(w2), stacked_block(wa), stacked_block(pb))
    groups = [Gather(u, 4, ats[k], blocks[k], gsems.at[k], DIRECT[k]) for k in range(4)]
    for name, group in zip(("g1", "g2", "ga", "gp"), groups):
        table.update(group.table(name))
    own = [pltpu.make_async_copy(src, groups[k].own(u.z), local.at[k]) for k, src in ((0, s1), (1, s2), (3, par))]
    for k, src in enumerate((sq, sk, sv, so)):
        own.append(pltpu.make_async_copy(src, groups[2].own(u.z).at[pl.ds(64 * k, 64)], local.at[8 + k]))
    keep = pltpu.make_async_copy(par, bb.at[u.c], local.at[4])
    for copy in own + [keep]:
        copy.start()
    g1_out, g2_out = weights_out.at[pl.ds(0, 576)], weights_out.at[pl.ds(576, 576)]
    ga_out = weights_out.at[pl.ds(1152, 256)]
    share_x, share_a, share_g = [Share(u, share_sems.at[k], local.at[5 + k]) for k in range(3)]
    share_o = ColumnShare(u, oall, share_sems.at[3], local.at[2])
    swap = [Swap(u, swaps.at[k], swap_sems.at[k]) for k in range(6)] + [Swap(u, lds, swap_sems.at[6])]
    halo = [Halo(u, (a1, a2)[k % 2], halo_sems.at[k]) for k in range(4)]
    spread_o = Spread(u, Blocks(oall), spread_sems.at[0], 2)
    spread_n = Spread(u, Halves(nall), spread_sems.at[1], 2)

    w2_at = weight_places(w2, 576)
    part_a = lambda ref, h: part_of(ref, h, CUT_A, 256)
    part_w = lambda ref, h: part_of(ref, h, CUT, 576)
    sum_a = Scatter(
        u, 4, attn_places(ga), lambda k, z, x, d: core_a.at[k, z], part_a, stacked_block(ga), ssems.at[0], ((half_a, rest_a), side_a, last_a)
    )
    sum_2 = Scatter(
        u, 4, weight_places(wg2, 576), lambda k, z, x, d: core_2.at[k, z], part_w, weight_block(wg2), ssems.at[1], ((half_2, rest_2), side_2, last_2)
    )
    sum_1 = Scatter(
        u, 4, weight_places(wg1, 576), lambda k, z, x, d: w2_at(z, x, d), part_w, weight_block(wg1), ssems.at[2], ((half_1, rest_1), side_1, last_1)
    )
    for name, total, out in (("ra", sum_a, ga_out), ("r2", sum_2, g2_out), ("r1", sum_1, g1_out)):
        table.update(total.table(name, out))
    bound_cp = remote(par, bb.at[u.c], bound_sems.at[0], bound_sems.at[1], u.cn)
    state = {}

    def step(function):
        table[function.__name__] = function
        return function


    @step
    def xs():
        share_x.send(feat, xin)
        bound_cp.start()

    @step
    def os():
        share_o.send(grad)

    @step
    def ow():
        for copy in own:
            copy.wait()
        u.enter(greeters)

    @step
    def bw():
        keep.wait()
        remote(par, bb.at[1 - u.c], bound_sems.at[0], bound_sems.at[1], u.cn).wait_recv()
        limits = jnp.where(u.mu == 0, bb[u.z // 2, 8:10, :], bb[u.z // 2, 10:12, :])
        limits = jnp.concatenate([limits] * 4, axis=1)
        small[7] = jnp.concatenate([limits, jnp.zeros((6, limits.shape[1]), F32)], axis=0)
        state["seg"] = tap_masks(u, limits, masks)
        state["counts"] = counts_of(limits, 4.0 * ROW)

    def first(r):
        return xin[r].astype(F32)

    def second(r):
        return hidden[r]

    def third(r):
        return resid[r]

    values = (first, second, third)

    def norm_sums(k):
        def body(r):
            line = values[k](r)
            rows_a[pl.ds(r, 1), :] = jnp.sum(line, axis=0, keepdims=True)
            rows_b[pl.ds(r, 1), :] = jnp.sum(line * line, axis=0, keepdims=True)

        each_row(body)
        swap[k].buf[u.q] = canvas_sums(rows_a[...], rows_b[...], state["seg"])
        swap[k].send()

    def norm_stats(k):
        swap[k].wait()
        average, inverse = moments(swap[k].total(), state["counts"], state["seg"])
        small[2 * k] = average
        small[2 * k + 1] = inverse

    def param(j):
        return small[6, j : j + 1, :]

    def xhat(k, r):
        return (values[k](r) - small[2 * k, pl.ds(r, 1), :]) * small[2 * k + 1, pl.ds(r, 1), :]

    def normal(k, r):
        return xhat(k, r) * param(2 * k) + param(2 * k + 1)

    def activate(k, buf):
        def body(r):
            line = normal(k, r)
            buf[r + 1] = (line * sigmoid(line)).astype(BF)

        each_row(body)

    @step
    def n1a():
        share_x.wait(feat, xin)
        norm_sums(0)

    @step
    def n1b():
        groups[3].arrive()
        total = pb[0, 0:8, :]
        for b in range(1, 8):
            total = total + pb[b, 0:8, :]
        small[6] = total
        norm_stats(0)

    def conv_steps(name, k, buf):
        def c():
            activate(k, buf)
            halo[k].send()

        def d():
            taps_inner(buf, masks, taps)

        def e():
            halo[k].wait()
            taps_outer(buf, masks, taps)
            halo[k].sent()

        table[name + "c"], table[name + "d"], table[name + "e"] = c, d, e

    conv_steps("n1", 0, a1)
    conv_steps("n2", 1, a2)

    @step
    def t1():
        act_t1[...] = a1[1 : ROW + 1].reshape(512, 512).T

    @step
    def t2():
        act_t2[...] = a2[1 : ROW + 1].reshape(512, 512).T

    def first_conv(m):
        hidden[4 * m : 4 * m + 4] = conv_tile(taps, w1, m, False)

    def second_conv(m):
        resid[4 * m : 4 * m + 4] = conv_tile(taps, w2, m, False) + xin[4 * m : 4 * m + 4].astype(F32)

    for m in (0, 1):
        table["c1%d" % m] = functools.partial(first_conv, m)
        table["c2%d" % m] = functools.partial(second_conv, m)
    table["n2a"], table["n2b"] = functools.partial(norm_sums, 1), functools.partial(norm_stats, 1)
    table["n3a"], table["n3b"] = functools.partial(norm_sums, 2), functools.partial(norm_stats, 2)

    @step
    def n3c():
        def row(r):
            nall[u.q, r] = normal(2, r).astype(BF)

        for part in range(2):
            lax.fori_loop(4 * part, 4 * part + 4, lambda r, carry: (row(r), carry)[1], 0)
            spread_n.send(part)

    @step
    def ob():
        share_o.wait(grad)
        for part in range(2):
            spread_o.send(part)

    for part in (0, 1):
        table["or%d" % part] = functools.partial(spread_o.relay, part)
        table["nr%d" % part] = functools.partial(spread_n.relay, part)

    scale = 512.0 ** (-0.5)
    steep = scale * 1.4426950408889634

    def slot(ref, i):
        return ref.at[pl.ds(pl.multiple_of(i * 512, 512), 512)]

    def query_of(i):
        return slot(wg1, i)

    def key_of(i):
        return slot(wg1, 4 + i)

    def value_of(i):
        return slot(wg2, i)

    def upstream_of(i):
        return slot(wg2, 4 + i)

    heads, gq = slot(wg1, 8), slot(wg2, 8)

    def matrix(k):
        return wa[:, pl.ds(k * 64, 64), :].reshape(512, 512)

    across = u.q + 1 - 2 * (u.q % 2)
    members = (u.q, 3 - u.q, across, 3 - across)

    def project(k):
        if k in (1, 3):
            for part in range(2):
                (spread_n.near if k == 1 else spread_n.far)(part)
        tokens = nall[members[k]].reshape(512, 512)
        query_of(members[k])[...] = mm(tokens, matrix(0)).astype(BF)
        key_of(members[k])[...] = mm(tokens, matrix(1)).astype(BF)
        value_of(members[k])[...] = mm(tokens, matrix(2)).astype(BF)

    def project_up(k):
        if k == 1:
            for part in range(2):
                spread_o.near(part)
                spread_o.far(part)
        upstream = oall[members[k]].reshape(512, 512)
        upstream_of(members[k])[...] = cols(upstream, matrix(3)).astype(BF)

    for k in range(4):
        table["pj%d" % k] = functools.partial(project, k)
        table["po%d" % k] = functools.partial(project_up, k)

    def canvas(rows):
        return (rows >= small[7, 0:1, 0:1]).astype(F32) + (rows >= small[7, 1:2, 0:1]).astype(F32)

    def seg_col(q, offset, count):
        token = offset + lax.broadcasted_iota(jnp.int32, (count, 1), 0)
        return canvas((ROW * q + token // 64).astype(F32))

    def seg_row(q):
        token = lax.broadcasted_iota(jnp.int32, (1, 512), 1)
        return canvas((ROW * q + token // 64).astype(F32))

    def kept(j, i):
        return taps.at[i, pl.ds(pl.multiple_of(j * 4, 4), 4)]

    def queries(j, carry):
        block = pl.ds(pl.multiple_of(j * 256, 256), 256)
        query = query_of(u.q)[block]
        seg = seg_col(u.q, j * 256, 256)
        most = jnp.full((256, 1), NEGATIVE, F32)
        for i in range(4):
            part = jnp.where(seg == seg_row(i), cols(query, key_of(i)[...]) * steep, NEGATIVE)
            scores[i] = part
            most = jnp.maximum(most, jnp.max(part, axis=1, keepdims=True))
        total = jnp.zeros((256, 1), F32)
        for i in range(4):
            part = jnp.exp2(scores[i] - most)
            total = total + jnp.sum(part, axis=1, keepdims=True)
            scores[i] = part
        inverse = 1.0 / total
        found = jnp.zeros((256, 512), F32)
        for i in range(4):
            part = (scores[i] * inverse).astype(BF)
            kept(j, i)[...] = part.reshape(4, 64, 512)
            found = found + mm(part, value_of(i)[...])
        heads[block, :] = found.astype(BF)
        lcol[block, :] = jnp.broadcast_to(most + jnp.log2(total), (256, 128))
        return carry

    @step
    def qf():
        lax.fori_loop(0, 2, queries, 0)

    def queries_back(j, carry):
        block = pl.ds(pl.multiple_of(j * 256, 256), 256)
        upstream = upstream_of(u.q)[block]
        correction = jnp.zeros((256, 1), F32)
        for i in range(4):
            slope = cols(upstream, value_of(i)[...])
            scores[i] = slope
            part = kept(j, i)[...].reshape(256, 512).astype(F32)
            correction = correction + jnp.sum(part * slope, axis=1, keepdims=True)
        back = jnp.zeros((256, 512), F32)
        for i in range(4):
            part = kept(j, i)[...].reshape(256, 512).astype(F32)
            back = back + mm((part * (scores[i] - correction)).astype(BF), key_of(i)[...])
        gq[block, :] = (back * scale).astype(BF)
        dcol[block, :] = jnp.broadcast_to(correction, (256, 128))
        return carry

    @step
    def qb():
        lax.fori_loop(0, 2, queries_back, 0)
        lds[u.q] = jnp.concatenate([lcol[...].T[0:1], dcol[...].T[0:1], jnp.zeros((6, 512), F32)], axis=0)
        swap[6].send()

    @step
    def gz():
        for group in groups:
            group.finish()

    @step
    def hd():
        act[...] = (resid[...] + mm(heads[...], matrix(3)).reshape(ROW, 64, 512)).astype(BF)
        share_a.back(act, act_back)

    @step
    def hw():
        ga[:, 192:256, :] = mm(heads[...].T, oall[u.q].reshape(512, 512)).astype(BF).reshape(8, 64, 512)

    def keys(i, carry):
        query, upstream = query_of(i)[...], upstream_of(i)[...]
        for j in (0, 1):
            key, value = key_of(u.q)[256 * j : 256 * j + 256], value_of(u.q)[256 * j : 256 * j + 256]
            shared = seg_col(u.q, j * 256, 256) == seg_row(i)
            part = jnp.exp2(jnp.where(shared, cols(key, query) * steep, NEGATIVE) - lds[i, 0:1, :])
            slope = cols(value, upstream) - lds[i, 1:2, :]
            rows = pl.ds(4 * j, 4)
            gres[rows] += mm(part.astype(BF), upstream).reshape(4, 64, 512)
            big[rows] += mm((part * slope).astype(BF), query).reshape(4, 64, 512)
        return carry

    @step
    def ks():
        big[...] = jnp.zeros_like(big)
        gres[...] = jnp.zeros_like(gres)
        swap[6].wait()
        lax.fori_loop(0, 4, keys, 0)
        gk[...] = (big[...] * scale).astype(BF).reshape(512, 512)
        gv[...] = gres[...].astype(BF).reshape(512, 512)

    @step
    def aw():
        tokens = nall[u.q].reshape(512, 512).T
        for k, part in enumerate((gq, gk, gv)):
            ga[:, k * 64 : (k + 1) * 64, :] = mm(tokens, part[...]).astype(BF).reshape(8, 64, 512)

    @step
    def an():
        total = None
        for k, part in enumerate((gq, gk, gv)):
            term = cols(part[...], matrix(k))
            total = term if total is None else total + term
        big[...] = total.reshape(ROW, 64, 512)


    def back_sums(k, slope):
        def body(r):
            line = big[r]
            if slope:
                value = normal(k, r)
                part = sigmoid(value)
                line = line * (part * (1.0 + value * (1.0 - part)))
                big[r] = line
            rows_a[pl.ds(r, 1), :] = jnp.sum(line, axis=0, keepdims=True)
            rows_b[pl.ds(r, 1), :] = jnp.sum(line * xhat(k, r), axis=0, keepdims=True)

        each_row(body)
        swap[3 + k].buf[u.q] = canvas_sums(rows_a[...], rows_b[...], state["seg"])
        swap[3 + k].send()

    def back_means(k):
        swap[3 + k].wait()
        total = swap[3 + k].total()
        mine[2 * k : 2 * k + 1, :] = jnp.sum(total[3:6], axis=0, keepdims=True)
        mine[2 * k + 1 : 2 * k + 2, :] = jnp.sum(total[0:3], axis=0, keepdims=True)
        grouped = group_total(total * param(2 * k))
        counts, seg = state["counts"], state["seg"]
        rows_a[...] = by_row([grouped[j : j + 1] / counts[j] for j in range(3)], seg)
        rows_b[...] = by_row([grouped[3 + j : 4 + j] / counts[j] for j in range(3)], seg)

    def back(k, r):
        line = big[r] * param(2 * k) - row_of(rows_a, r) - xhat(k, r) * row_of(rows_b, r)
        return line * small[2 * k + 1, pl.ds(r, 1), :]

    @step
    def b3a():
        back_sums(2, False)

    @step
    def b3b():
        back_means(2)

        def row(r):
            line = oall[u.q, r].astype(F32) + back(2, r)
            gres[r] = line
            a2[r + 1] = line.astype(BF)

        each_row(row)
        halo[3].send()

    @step
    def b2a():
        back_sums(1, True)

    @step
    def b2b():
        back_means(1)

        def row(r):
            a1[r + 1] = back(1, r).astype(BF)

        each_row(row)
        halo[2].send()

    @step
    def b1a():
        back_sums(0, True)

    @step
    def b1m():
        back_means(0)

    @step
    def b1b():
        def row(r):
            low[r] = (gres[r] + back(0, r)).astype(BF)

        each_row(row)
        share_g.back(low, grad_back)

    @step
    def ps():
        remote(mine, psum_y, py_sems.at[0], py_sems.at[1], u.yn).start()

    def back_taps(name, k, buf):
        def c():
            taps_inner(buf, masks, taps)

        def d():
            halo[k].wait()
            taps_outer(buf, masks, taps)
            halo[k].sent()

        table[name + "c"], table[name + "d"] = c, d

    back_taps("b3", 3, a2)
    back_taps("b2", 2, a1)

    def tile_back(weight, m):
        big[4 * m : 4 * m + 4] = conv_tile(taps, weight, m, True)

    for m in (0, 1):
        table["d2%d" % m] = functools.partial(tile_back, w2, m)
        table["d1%d" % m] = functools.partial(tile_back, w1, m)
    for k in range(3):
        table["w2%d" % k] = functools.partial(conv_weight_grad, act_t2, taps, wg2, 3 * k, 3 * k + 3)
        table["w1%d" % k] = functools.partial(conv_weight_grad, act_t1, taps, wg1, 3 * k, 3 * k + 3)

    def line_cp(block, k):
        return remote(block, block, pz_sems.at[0], pz_sems.at[1], u.line(k))

    @step
    def py():
        remote(mine, psum_y, py_sems.at[0], py_sems.at[1], u.yn).wait()
        psum_z[u.z] = mine[...] + psum_y[...]
        for k in (1, 2, 3):
            line_cp(psum_z.at[u.z], k).start()

    @step
    def pz():
        line_cp(psum_z.at[pl.ds(0, 3)], 1).wait_recv()
        total = psum_z[0] + psum_z[1] + psum_z[2] + psum_z[3]
        norm_out[...] = pltpu.roll(total, lax.rem(512 - 64 * u.b, 512), 1)[:, 0:128]

    in_order(types.SimpleNamespace(**table))

    share_a.back_wait(act, act_back)
    share_g.back_wait(low, grad_back)
    for total in (sum_a, sum_2, sum_1):
        total.finish()
    bound_cp.wait_send()
    share_x.sent(feat, xin)
    share_o.sent(grad)
    for item in swap:
        item.sent()
    for item in (spread_o, spread_n):
        for part in range(2):
            item.sent(part)
    line_cp(psum_z.at[pl.ds(0, 3)], 1).wait_send()


def whole_call(features, out_grad, params, *shards):
    full = lambda shape, kind: jax.ShapeDtypeStruct(shape, kind)
    dma = pltpu.SemaphoreType.DMA
    rows, padded, square, weight = (ROW, 64, 512), (ROW + 2, 64, 512), (512, 512), (4608, 512)
    low = lambda *shape: pltpu.VMEM(shape, BF)
    wide = lambda *shape: pltpu.VMEM(shape, F32)
    sums = []
    for r, cut in ((256, CUT_A), (576, CUT), (576, CUT)):
        sums += [low(4, cut, 128), low(4, r - cut, 128), low(2, 4, r, 128), low(4, r, 128)]
    return pl.pallas_call(
        whole_kernel,
        out_shape=[
            full((2, 4, 64, 512), BF), full((2, 4, 64, 512), BF), full((1408, 128), F32),
            full((8, 128), F32),
        ],
        in_specs=[ANY] * 9,
        out_specs=[ANY, ANY, VM, VM],
        scratch_shapes=[
            low(*weight), low(*weight), low(8, 256, 512), wide(8, PARAMS, 512), wide(2, PARAMS, 128), low(*rows),
            low(4, *rows), low(4, *rows), low(9, *rows), low(*padded), low(*padded), wide(2, ROW, 512),
            wide(*rows), wide(*rows), wide(8, 8, 512), wide(ROW, 512), wide(ROW, 512), wide(6, 4, 8, 512), wide(4, 8, 512),
            low(*weight), low(*weight), wide(4, 256, 512), low(*square), low(*square),
            wide(512, 128), wide(512, 128), wide(*rows), wide(*rows), low(*rows), low(*rows), low(*square), low(*square),
            low(8, 256, 512), wide(8, 512), wide(8, 512), wide(4, 8, 512),
            low(4, 4, 256, 128), low(4, 4, 576, 128), *sums,
            dma((4, Gather.SEMS)), dma((3, Scatter.SEMS)), dma((12,)), dma((4, 2, 2)), dma((2,)), dma((7, 2)),
            dma((2, 2, 3, 2)), dma((4, 2, 2)), dma((2,)), dma((2,)),
        ],
        compiler_params=pltpu.CompilerParams(collective_id=0, has_side_effects=True, vmem_limit_bytes=LIMIT),
    )(features, out_grad, params, *shards)


def unit_shards(
    features, bounds, out_grad, norm1_gain, norm1_shift, conv1_weight, norm2_gain, norm2_shift, conv2_weight,
    norm3_gain, norm3_shift, query_weight, key_weight, value_weight, output_weight,
):
    norms = (norm1_gain, norm1_shift, norm2_gain, norm2_shift, norm3_gain, norm3_shift)
    act_back, grad_back, weights, norms = whole_call(
        features[0], out_grad[0], unit_inputs(bounds, norms), conv1_weight, conv2_weight,
        query_weight, key_weight, value_weight, output_weight,
    )
    norms = norms[:, :64]
    g1, g2, ga = weights[:576], weights[576:1152], weights[1152:].reshape(4, 64, 128)
    return (
        act_back.astype(F32)[None], grad_back.astype(F32)[None], norms[0], norms[1], g1, norms[2], norms[3], g2,
        norms[4], norms[5], ga[0], ga[1], ga[2], ga[3],
    )


def extended(shard, sides, width):
    for axis, dim in sides:
        devices, length = (lax.axis_size(axis), shard.shape[dim])
        up = [(i, (i + 1) % devices) for i in range(devices - 1)]
        down = [(j, i) for i, j in up]
        last = lax.slice_in_dim(shard, length - width, length, axis=dim)
        initial = lax.slice_in_dim(shard, 0, width, axis=dim)
        before = lax.ppermute(last, axis, up)
        after = lax.ppermute(initial, axis, down)
        shard = jnp.concatenate([before, shard, after], axis=dim)
    return shard


def canvas_index(global_rows, first_row, second_row):
    return (global_rows >= first_row).astype(jnp.int32) + (global_rows >= second_row).astype(
        jnp.int32
    )


def swish(argument):
    return argument * jax.nn.sigmoid(argument)


def swish_slope(argument):
    sigmoid_value = jax.nn.sigmoid(argument)
    return sigmoid_value * (1.0 + argument * (1.0 - sigmoid_value))


def group_sums(member, grouped):
    return jnp.einsum("rk,rwgc->kg", member, grouped, precision=HIGHEST)


def spread_rows(member, lookup):
    return jnp.dot(member, lookup, precision=HIGHEST)


def norm_forward(inputs, member, counts, norm_gain, norm_shift):
    row_count, width, channels = inputs.shape
    grouped = inputs.reshape(row_count, width, GROUPS, channels // GROUPS)
    totals, square = lax.psum(
        (group_sums(member, grouped), group_sums(member, grouped * grouped)), "blk"
    )
    average = totals / counts[:, None]
    inverse = lax.rsqrt(square / counts[:, None] - average * average + EPSILON)
    average_rows = spread_rows(member, average)
    scale_rows = spread_rows(member, inverse)
    normal = (grouped - average_rows[:, None, :, None]) * scale_rows[:, None, :, None]
    normal = normal.reshape(row_count, width, channels)
    return (normal * norm_gain + norm_shift, normal, scale_rows)


def norm_backward(incoming, normal, scale_rows, member, counts, norm_gain):
    row_count, width, channels = incoming.shape
    gain_grad = jnp.sum(incoming * normal, axis=(0, 1))
    shift_grad = jnp.sum(incoming, axis=(0, 1))
    scaled = (incoming * norm_gain).reshape(row_count, width, GROUPS, channels // GROUPS)
    grouped_normal = normal.reshape(row_count, width, GROUPS, channels // GROUPS)
    first_sum, second_sum = lax.psum(
        (group_sums(member, scaled), group_sums(member, scaled * grouped_normal)), "blk"
    )
    first_rows = spread_rows(member, first_sum / counts[:, None])
    second_rows = spread_rows(member, second_sum / counts[:, None])
    result = scale_rows[:, None, :, None] * (
        scaled - first_rows[:, None, :, None] - grouped_normal * second_rows[:, None, :, None]
    )
    return (result.reshape(row_count, width, channels), gain_grad, shift_grad)


def gather_taps(padded, seg_pad, seg_rows, direction):
    row_count = seg_rows.shape[0]
    width = padded.shape[1]
    widened = jnp.pad(padded, ((0, 0), (1, 1), (0, 0)))
    pieces = []
    for step_row in (-1, 0, 1):
        low_row = 1 + direction * step_row
        allowed = (seg_pad[low_row : low_row + row_count] == seg_rows).astype(padded.dtype)[
            :, None, None
        ]
        for step_col in (-1, 0, 1):
            low_col = 1 + direction * step_col
            pieces.append(
                widened[low_row : low_row + row_count, low_col : low_col + width, :] * allowed
            )
    return jnp.stack(pieces, axis=2)


def conv_apply(activation, seg_pad, seg_rows, weight_matrix):
    row_count, width, channels = activation.shape
    padded = extended(activation, (("blk", 0),), 1)
    stacked = gather_taps(padded, seg_pad, seg_rows, 1).reshape(row_count * width, 9 * channels)
    result = jnp.dot(stacked, weight_matrix, preferred_element_type=jnp.float32)
    return (result.reshape(row_count, width, channels), stacked)


def conv_reverse(gradient, stacked, seg_pad, seg_rows, weight_matrix):
    row_count, width, channels = gradient.shape
    flattened = gradient.reshape(row_count * width, channels)
    weight_grad = lax.dot_general(
        stacked, flattened, (((0,), (0,)), ((), ())), preferred_element_type=jnp.float32
    )
    padded = extended(gradient, (("blk", 0),), 1)
    mirrored = gather_taps(padded, seg_pad, seg_rows, -1).reshape(row_count * width, 9, channels)
    kernel = weight_matrix.reshape(9, channels, channels)
    result = lax.dot_general(
        mirrored, kernel, (((1, 2), (0, 2)), ((), ())), preferred_element_type=jnp.float32
    )
    return (result.reshape(row_count, width, channels), weight_grad)


def attention_forward(
    queries, keys_local, values_local, token_seg, first_row, second_row, width, scale
):
    token_count, channels = queries.shape

    def absorb(running, portion, offset):
        key_block, value_block = portion
        maximum, totals, accumulated = running
        key_seg = canvas_index(
            jnp.arange(key_block.shape[0], dtype=jnp.int32) // width, first_row, second_row
        )
        shared = token_seg[:, None] == key_seg[None, :]
        scores = (
            lax.dot_general(
                queries, key_block, (((1,), (1,)), ((), ())), preferred_element_type=jnp.float32
            )
            * scale
        )
        masked = jnp.where(shared, scores, NEGATIVE)
        new_maximum = jnp.maximum(maximum, jnp.max(masked, axis=1))
        weights = jnp.where(shared, jnp.exp(masked - new_maximum[:, None]), 0.0)
        totals = jnp.sum(weights, axis=1)
        accumulated = jnp.dot(
            weights.astype(jnp.bfloat16), value_block, preferred_element_type=jnp.float32
        )
        return (new_maximum, totals, accumulated)

    initial = (
        jnp.full((token_count,), NEGATIVE, jnp.float32),
        jnp.zeros((token_count,), jnp.float32),
        jnp.zeros((token_count, channels), jnp.float32),
    )
    maximum, totals, accumulated = absorb(
        initial,
        (
            lax.all_gather(keys_local, "blk", axis=0, tiled=True),
            lax.all_gather(values_local, "blk", axis=0, tiled=True),
        ),
        jnp.int32(0),
    )
    return (accumulated / totals[:, None], maximum + jnp.log(totals))


def attention_query_grad(
    queries,
    heads_grad,
    log_total,
    correction,
    keys_local,
    values_local,
    token_seg,
    first_row,
    second_row,
    width,
    scale,
):

    def absorb(running, portion, offset):
        key_block, value_block = portion
        key_seg = canvas_index(
            jnp.arange(key_block.shape[0], dtype=jnp.int32) // width, first_row, second_row
        )
        shared = token_seg[:, None] == key_seg[None, :]
        scores = (
            lax.dot_general(
                queries, key_block, (((1,), (1,)), ((), ())), preferred_element_type=jnp.float32
            )
            * scale
        )
        weights = jnp.where(
            shared, jnp.exp(jnp.where(shared, scores, NEGATIVE) - log_total[:, None]), 0.0
        )
        slopes = lax.dot_general(
            heads_grad, value_block, (((1,), (1,)), ((), ())), preferred_element_type=jnp.float32
        )
        score_grad = (weights * (slopes - correction[:, None])).astype(jnp.bfloat16)
        return jnp.dot(score_grad, key_block, preferred_element_type=jnp.float32) * scale

    return absorb(
        jnp.zeros(queries.shape, jnp.float32),
        (
            lax.all_gather(keys_local, "blk", axis=0, tiled=True),
            lax.all_gather(values_local, "blk", axis=0, tiled=True),
        ),
        jnp.int32(0),
    )


def attention_key_grad(
    queries,
    heads_grad,
    log_total,
    correction,
    keys_local,
    values_local,
    token_seg,
    first_row,
    second_row,
    width,
    scale,
):

    def absorb(running, portion, offset):
        query_part, upstream_part, total_part, correct_part = portion
        query_seg = canvas_index(
            jnp.arange(query_part.shape[0], dtype=jnp.int32) // width, first_row, second_row
        )
        query_low = query_part.astype(jnp.bfloat16)
        upstream_low = upstream_part.astype(jnp.bfloat16)
        shared = query_seg[:, None] == token_seg[None, :]
        scores = (
            lax.dot_general(
                query_low, keys_local, (((1,), (1,)), ((), ())), preferred_element_type=jnp.float32
            )
            * scale
        )
        weights = jnp.where(
            shared, jnp.exp(jnp.where(shared, scores, NEGATIVE) - total_part[:, None]), 0.0
        )
        value_acc = lax.dot_general(
            weights.astype(jnp.bfloat16),
            upstream_low,
            (((0,), (0,)), ((), ())),
            preferred_element_type=jnp.float32,
        )
        slopes = lax.dot_general(
            upstream_low, values_local, (((1,), (1,)), ((), ())), preferred_element_type=jnp.float32
        )
        score_grad = (weights * (slopes - correct_part[:, None])).astype(jnp.bfloat16)
        key_acc = (
            lax.dot_general(
                score_grad, query_low, (((0,), (0,)), ((), ())), preferred_element_type=jnp.float32
            )
            * scale
        )
        return (key_acc, value_acc)

    empty = jnp.zeros(keys_local.shape, jnp.float32)
    return absorb(
        (empty, empty),
        (
            lax.all_gather(queries.astype(jnp.float32), "blk", axis=0, tiled=True),
            lax.all_gather(heads_grad.astype(jnp.float32), "blk", axis=0, tiled=True),
            lax.all_gather(log_total, "blk", axis=0, tiled=True),
            lax.all_gather(correction, "blk", axis=0, tiled=True),
        ),
        jnp.int32(0),
    )


def collect(
    conv1_weight,
    conv2_weight,
    query_weight,
    key_weight,
    value_weight,
    output_weight,
    norm1_gain,
    norm1_shift,
    norm2_gain,
    norm2_shift,
    norm3_gain,
    norm3_shift,
):
    row_parts = (
        lax.all_gather(conv1_weight, "blk", axis=0, tiled=True),
        lax.all_gather(conv2_weight, "blk", axis=0, tiled=True),
        lax.all_gather(query_weight, "blk", axis=0, tiled=True),
        lax.all_gather(key_weight, "blk", axis=0, tiled=True),
        lax.all_gather(value_weight, "blk", axis=0, tiled=True),
        lax.all_gather(output_weight, "blk", axis=0, tiled=True),
        lax.all_gather(norm1_gain, "blk", axis=0, tiled=True),
        lax.all_gather(norm1_shift, "blk", axis=0, tiled=True),
        lax.all_gather(norm2_gain, "blk", axis=0, tiled=True),
        lax.all_gather(norm2_shift, "blk", axis=0, tiled=True),
        lax.all_gather(norm3_gain, "blk", axis=0, tiled=True),
        lax.all_gather(norm3_shift, "blk", axis=0, tiled=True),
    )
    full_parts = (
        lax.all_gather(row_parts[0], "dp", axis=1, tiled=True),
        lax.all_gather(row_parts[1], "dp", axis=1, tiled=True),
        lax.all_gather(row_parts[2], "dp", axis=1, tiled=True),
        lax.all_gather(row_parts[3], "dp", axis=1, tiled=True),
        lax.all_gather(row_parts[4], "dp", axis=1, tiled=True),
        lax.all_gather(row_parts[5], "dp", axis=1, tiled=True),
    )
    return (tuple(full_parts), tuple(row_parts[6:]))


def reduce_all(gradients):
    row_sums = (
        lax.psum_scatter(gradients[0], "blk", scatter_dimension=0, tiled=True),
        lax.psum_scatter(gradients[1], "blk", scatter_dimension=0, tiled=True),
        lax.psum_scatter(gradients[2], "blk", scatter_dimension=0, tiled=True),
        lax.psum_scatter(gradients[3], "blk", scatter_dimension=0, tiled=True),
        lax.psum_scatter(gradients[4], "blk", scatter_dimension=0, tiled=True),
        lax.psum_scatter(gradients[5], "blk", scatter_dimension=0, tiled=True),
        lax.psum_scatter(gradients[6], "blk", scatter_dimension=0, tiled=True),
        lax.psum_scatter(gradients[7], "blk", scatter_dimension=0, tiled=True),
        lax.psum_scatter(gradients[8], "blk", scatter_dimension=0, tiled=True),
        lax.psum_scatter(gradients[9], "blk", scatter_dimension=0, tiled=True),
        lax.psum_scatter(gradients[10], "blk", scatter_dimension=0, tiled=True),
        lax.psum_scatter(gradients[11], "blk", scatter_dimension=0, tiled=True),
    )
    matrix_sums = (
        lax.psum_scatter(row_sums[0], "dp", scatter_dimension=1, tiled=True),
        lax.psum_scatter(row_sums[1], "dp", scatter_dimension=1, tiled=True),
        lax.psum_scatter(row_sums[2], "dp", scatter_dimension=1, tiled=True),
        lax.psum_scatter(row_sums[3], "dp", scatter_dimension=1, tiled=True),
        lax.psum_scatter(row_sums[4], "dp", scatter_dimension=1, tiled=True),
        lax.psum_scatter(row_sums[5], "dp", scatter_dimension=1, tiled=True),
    )
    norm_sums = lax.psum(
        (row_sums[6], row_sums[7], row_sums[8], row_sums[9], row_sums[10], row_sums[11]), "dp"
    )
    return tuple(matrix_sums) + tuple(norm_sums)


def one_batch(inputs_low, bound_pair, upstream_low, matrices, norm_params, position, blocks):
    row_count, width, channels = inputs_low.shape
    token_count = row_count * width
    total_rows = row_count * blocks
    scale = channels ** (-0.5)
    first_row = bound_pair[0]
    second_row = bound_pair[1]
    local_rows = position * row_count + jnp.arange(row_count, dtype=jnp.int32)
    padded_rows = position * row_count - 1 + jnp.arange(row_count + 2, dtype=jnp.int32)
    seg_rows = canvas_index(local_rows, first_row, second_row)
    seg_pad = canvas_index(padded_rows, first_row, second_row)
    member = (seg_rows[:, None] == jnp.arange(CANVASES, dtype=jnp.int32)[None, :]).astype(
        jnp.float32
    )
    counts = jnp.stack([first_row, second_row - first_row, total_rows - second_row]).astype(
        jnp.float32
    ) * float(width * (channels // GROUPS))
    gains = [item.astype(jnp.float32) for item in norm_params]
    inputs = inputs_low.astype(jnp.float32)
    norm_one, normal_one, scale_one = norm_forward(inputs, member, counts, gains[0], gains[1])
    act_one = swish(norm_one).astype(jnp.bfloat16)
    hidden_one, stacked_one = conv_apply(act_one, seg_pad, seg_rows, matrices[0])
    norm_two, normal_two, scale_two = norm_forward(hidden_one, member, counts, gains[2], gains[3])
    act_two = swish(norm_two).astype(jnp.bfloat16)
    hidden_two, stacked_two = conv_apply(act_two, seg_pad, seg_rows, matrices[1])
    residual = inputs + hidden_two
    norm_three, normal_three, scale_three = norm_forward(
        residual, member, counts, gains[4], gains[5]
    )
    normed = norm_three.astype(jnp.bfloat16).reshape(token_count, channels)
    queries = jnp.dot(normed, matrices[2], preferred_element_type=jnp.float32).astype(jnp.bfloat16)
    keys_local = jnp.dot(normed, matrices[3], preferred_element_type=jnp.float32).astype(
        jnp.bfloat16
    )
    values_local = jnp.dot(normed, matrices[4], preferred_element_type=jnp.float32).astype(
        jnp.bfloat16
    )
    token_seg = jnp.repeat(seg_rows, width)
    attended, log_total = attention_forward(
        queries, keys_local, values_local, token_seg, first_row, second_row, width, scale
    )
    heads = attended.astype(jnp.bfloat16)
    activation = residual + jnp.dot(heads, matrices[5], preferred_element_type=jnp.float32).reshape(
        row_count, width, channels
    )
    upstream = upstream_low.reshape(token_count, channels)
    output_weight_grad = lax.dot_general(
        heads, upstream, (((0,), (0,)), ((), ())), preferred_element_type=jnp.float32
    )
    heads_grad = lax.dot_general(
        upstream, matrices[5], (((1,), (1,)), ((), ())), preferred_element_type=jnp.float32
    ).astype(jnp.bfloat16)
    correction = jnp.sum(heads_grad.astype(jnp.float32) * attended, axis=1)
    query_sum = attention_query_grad(
        queries,
        heads_grad,
        log_total,
        correction,
        keys_local,
        values_local,
        token_seg,
        first_row,
        second_row,
        width,
        scale,
    )
    key_sum, value_sum = attention_key_grad(
        queries,
        heads_grad,
        log_total,
        correction,
        keys_local,
        values_local,
        token_seg,
        first_row,
        second_row,
        width,
        scale,
    )
    query_low = query_sum.astype(jnp.bfloat16)
    key_low = key_sum.astype(jnp.bfloat16)
    value_low = value_sum.astype(jnp.bfloat16)
    contract_rows = (((0,), (0,)), ((), ()))
    contract_cols = (((1,), (1,)), ((), ()))
    query_weight_grad = lax.dot_general(
        normed, query_low, contract_rows, preferred_element_type=jnp.float32
    )
    key_weight_grad = lax.dot_general(
        normed, key_low, contract_rows, preferred_element_type=jnp.float32
    )
    value_weight_grad = lax.dot_general(
        normed, value_low, contract_rows, preferred_element_type=jnp.float32
    )
    normed_grad = (
        lax.dot_general(query_low, matrices[2], contract_cols, preferred_element_type=jnp.float32)
        + lax.dot_general(key_low, matrices[3], contract_cols, preferred_element_type=jnp.float32)
        + lax.dot_general(value_low, matrices[4], contract_cols, preferred_element_type=jnp.float32)
    )
    back_three, gain_three_grad, shift_three_grad = norm_backward(
        normed_grad.reshape(row_count, width, channels),
        normal_three,
        scale_three,
        member,
        counts,
        gains[4],
    )
    residual_grad = upstream_low.astype(jnp.float32) + back_three
    act_two_grad, conv_two_grad = conv_reverse(
        residual_grad.astype(jnp.bfloat16), stacked_two, seg_pad, seg_rows, matrices[1]
    )
    back_two, gain_two_grad, shift_two_grad = norm_backward(
        act_two_grad * swish_slope(norm_two), normal_two, scale_two, member, counts, gains[2]
    )
    act_one_grad, conv_one_grad = conv_reverse(
        back_two.astype(jnp.bfloat16), stacked_one, seg_pad, seg_rows, matrices[0]
    )
    back_one, gain_one_grad, shift_one_grad = norm_backward(
        act_one_grad * swish_slope(norm_one), normal_one, scale_one, member, counts, gains[0]
    )
    input_grad = residual_grad + back_one
    local_grads = (
        conv_one_grad,
        conv_two_grad,
        query_weight_grad,
        key_weight_grad,
        value_weight_grad,
        output_weight_grad,
        gain_one_grad,
        shift_one_grad,
        gain_two_grad,
        shift_two_grad,
        gain_three_grad,
        shift_three_grad,
    )
    return (activation, input_grad, local_grads)


def shards(
    features,
    bounds,
    out_grad,
    norm1_gain,
    norm1_shift,
    conv1_weight,
    norm2_gain,
    norm2_shift,
    conv2_weight,
    norm3_gain,
    norm3_shift,
    query_weight,
    key_weight,
    value_weight,
    output_weight,
):
    blocks = lax.axis_size("blk")
    position = lax.axis_index("blk")
    micro_count = features.shape[1]
    shard_sums = None
    outputs = []
    input_grads = []
    for micro_index in range(micro_count):
        matrices, norm_params = collect(
            conv1_weight,
            conv2_weight,
            query_weight,
            key_weight,
            value_weight,
            output_weight,
            norm1_gain,
            norm1_shift,
            norm2_gain,
            norm2_shift,
            norm3_gain,
            norm3_shift,
        )
        activation, input_grad, local_grads = one_batch(
            features[0, micro_index],
            bounds[0, micro_index],
            out_grad[0, micro_index],
            matrices,
            norm_params,
            position,
            blocks,
        )
        outputs.append(activation)
        input_grads.append(input_grad)
        reduced = reduce_all(local_grads)
        shard_sums = (
            reduced
            if shard_sums is None
            else tuple((acc + new for acc, new in zip(shard_sums, reduced)))
        )
    activations = jnp.stack(outputs)[None]
    input_grad_all = jnp.stack(input_grads)[None]
    return (
        activations,
        input_grad_all,
        shard_sums[6],
        shard_sums[7],
        shard_sums[0],
        shard_sums[8],
        shard_sums[9],
        shard_sums[1],
        shard_sums[10],
        shard_sums[11],
        shard_sums[2],
        shard_sums[3],
        shard_sums[4],
        shard_sums[5],
    )


def solution(mesh):
    in_specs = (
        P("dp", None, "blk", None, None),
        P("dp", None, None),
        P("dp", None, "blk", None, None),
        P("blk"),
        P("blk"),
        P("blk", "dp"),
        P("blk"),
        P("blk"),
        P("blk", "dp"),
        P("blk"),
        P("blk"),
        P("blk", "dp"),
        P("blk", "dp"),
        P("blk", "dp"),
        P("blk", "dp"),
    )
    out_specs = (
        P("dp", None, "blk", None, None),
        P("dp", None, "blk", None, None),
        P("blk"),
        P("blk"),
        P("blk", "dp"),
        P("blk"),
        P("blk"),
        P("blk", "dp"),
        P("blk"),
        P("blk"),
        P("blk", "dp"),
        P("blk", "dp"),
        P("blk", "dp"),
        P("blk", "dp"),
    )
    near = mesh.shape["dp"] == 4 and mesh.shape["blk"] == 8
    return jax.shard_map(unit_shards if near else shards, mesh=mesh, in_specs=in_specs, out_specs=out_specs, check_vma=False)
```

```python
import functools
import types

import jax
import jax.numpy as jnp
from jax import lax
from jax.experimental import pallas as pl
from jax.experimental.pallas import tpu as pltpu
from jax.sharding import PartitionSpec as P

GROUPS = 32
CANVASES = 3


EPSILON = 1e-06
HIGHEST = lax.Precision.HIGHEST
NEGATIVE = -1e30
MESH = pl.DeviceIdType.MESH
def in_order(s):
    s.ow(), s.gpl0(), s.g1l0(), s.g1o0(), s.g2o0(), s.gpo0(), s.g2l0(), s.gpl1()
    s.gao0(), s.g1l1(), s.g2y0(), s.gpl2(), s.g1y0(), s.gpo2(), s.g1x0(), s.gpo1()
    s.g2l1(), s.gpl3(), s.g1o1(), s.gpo3(), s.g1l2(), s.gal0(), s.g2o1(), s.g1o2()
    s.gpx2(), s.g1l3(), s.gpy3(), s.gpx1(), s.gpy0(), s.g1o3(), s.gpx0(), s.xs()
    s.g2x0(), s.gal1(), s.gpy1(), s.gpx3(), s.g2l2(), s.g1x1(), s.gpy2(), s.g1x2()
    s.g1y3(), s.g1x3(), s.g1y2(), s.bw(), s.gal2(), s.g2l3(), s.gpd3(), s.gpd1()
    s.g2o3(), s.gal3(), s.os(), s.gpd0(), s.n1a(), s.gpd2(), s.g1y1(), s.gax0()
    s.g1d0(), s.g1d3(), s.g2o2(), s.n1b(), s.n1c(), s.gao2(), s.gao3(), s.g1d1()
    s.g1d2(), s.n1d(), s.gao1(), s.g2y3(), s.g1a(), s.n1e(), s.c10(), s.c11()
    s.n2a(), s.gay3(), s.gay0(), s.g2x3(), s.g2d0(), s.g2x2(), s.g2x1(), s.g2y2()
    s.gax1(), s.g2y1(), s.gay2(), s.gay1(), s.n2b(), s.n2c(), s.ob(), s.gax3()
    s.n2d(), s.n2e(), s.g2d3(), s.g2d2(), s.g2d1(), s.g2a(), s.c20(), s.c21()
    s.gax2(), s.gad1(), s.n3a(), s.t1(), s.or0(), s.gad3(), s.gad2(), s.gad0()
    s.or1(), s.n3b(), s.n3c(), s.t2(), s.gaa(), s.po0(), s.pj1(), s.nr0()
    s.po1(), s.po2(), s.pj0(), s.po3(), s.nr1(), s.pj2(), s.pj3(), s.qf()
    s.qb(), s.hw(), s.gz(), s.hd(), s.ks(), s.an(), s.b3a(), s.aw()
    s.rab0(), s.rab2(), s.rab1(), s.rab3(), s.b3b(), s.b3c(), s.rac1(), s.rac3()
    s.rac2(), s.rac0(), s.b3d(), s.w20(), s.d20(), s.d21(), s.b2a(), s.w21()
    s.rae2(), s.r2b0(), s.w22(), s.r2b3(), s.r2b1(), s.rae1(), s.b2b(), s.r2b2()
    s.r2c3(), s.r2c2(), s.r2c1(), s.b2c(), s.rae0(), s.raf2(), s.b2d(), s.d10()
    s.d11(), s.b1a(), s.raf1(), s.r2e3(), s.r2e2(), s.w10(), s.b1m(), s.rae3()
    s.ps(), s.b1b(), s.r2c0(), s.r1b0(), s.w11(), s.r1b1(), s.w12(), s.r2f2()
    s.py(), s.r1b3(), s.r1b2(), s.r2f3(), s.r1c3(), s.r2e1(), s.raf0(), s.r1e3()
    s.r1c2(), s.raf3(), s.r1f3(), s.r1c1(), s.r2f1(), s.r1e2(), s.r1e1(), s.r1c0()
    s.pz(), s.r2e0(), s.r1f2(), s.r1f1(), s.rat(), s.r1e0(), s.r2f0(), s.r2t()
    s.r1f0(), s.r1t()


DIRECT = (False, False, False, False)
LIMIT = 60 << 20
SPLIT, SPLIT_A = 432, 192
CUT, CUT_A = 112, 48


class Place:
    def __init__(self):
        self.d = lax.axis_index("dp")
        self.b = lax.axis_index("blk")
        self.y, self.c = self.d // 2, self.d % 2
        self.z, self.x = self.b // 2, self.b % 2
        self.up = {"dp": self.d, "blk": self.b + 2}
        self.down = {"dp": self.d, "blk": self.b - 2}
        self.xn = {"dp": self.d, "blk": self.z * 2 + 1 - self.x}
        self.yn = {"dp": (1 - self.y) * 2 + self.c, "blk": self.b}
        self.cn = {"dp": self.y * 2 + 1 - self.c, "blk": self.b}


def remote(src, dst, send, recv, device):
    return pltpu.make_async_remote_copy(
        src_ref=src, dst_ref=dst, send_sem=send, recv_sem=recv, device_id=device, device_id_type=MESH
    )


def steps_of(z, nz):
    visits = [(z, None)]
    for k in range(1, nz):
        visits.append((z - k, z >= k))
        visits.append((z + k, z + k < nz))
    return visits


def guarded(valid, body):
    if valid is None:
        body()
    else:
        pl.when(valid)(body)


class Gather:
    SEMS = 27

    def __init__(self, here, nz, at, block, sems, direct):
        self.here, self.nz, self.at, self.block, self.sems, self.direct = here, nz, at, block, sems, direct
        self.visits = steps_of(here.z, nz)

    def ends(self, kind, z):
        if kind[0] == "c":
            return self.sems.at[26], self.sems.at[16]
        send = {"z": 17 + z, "zd": 21 + z}.get(kind, 25)
        recv = {"z": 0, "zd": 0, "x": 4, "y": 8, "da": 12, "db": 12}[kind] + z
        return self.sems.at[send], self.sems.at[recv]

    def cp(self, kind, z, src, device):
        return remote(src, src, *self.ends(kind, z), device)

    def own(self, z):
        return self.at(z, self.here.x, self.here.d, None)

    def colx(self, z, half=None):
        return self.at(z, 1 - self.here.x, self.here.d, half)

    def coly(self, z, half=None):
        return self.at(z, self.here.x, (1 - self.here.y) * 2 + self.here.c, half)

    def cold(self, z, half=None):
        return self.at(z, 1 - self.here.x, (1 - self.here.y) * 2 + self.here.c, half)

    def line_cp(self, k):
        here = self.here
        z = (here.z + k) % self.nz
        device = {"dp": here.d, "blk": z * 2 + here.x}
        return remote(self.own(here.z), self.own(here.z), self.sems.at[17 + z], self.sems.at[here.z], device)

    def line(self, j):
        z, valid = self.visits[j]
        here = self.here
        if j == 0 and self.direct:
            for k in range(1, self.nz):
                self.line_cp(k).start()
            return

        def body():
            src = self.own(z)
            if j > 0:
                self.cp("z", z, src, here.up).wait_recv()
            if self.direct:
                return
            if j == 0 or j % 2 == 1:

                @pl.when(here.z < self.nz - 1)
                def _():
                    self.cp("z", z, src, here.up).start()

            if j == 0 or j % 2 == 0:

                @pl.when(here.z > 0)
                def _():
                    self.cp("zd", z, src, here.down).start()

        guarded(valid, body)

    def out(self, j):
        z, valid = self.visits[j]
        here = self.here

        def body():
            src = self.own(z)
            self.cp("x", z, src, here.xn).start()
            self.cp("y", z, src, here.yn).start()
            self.cp("co", z, src, here.cn).start()

        guarded(valid, body)

    def have(self, j):
        self.line(j)
        self.out(j)

    def from_x(self, j):
        z, valid = self.visits[j]

        def body():
            self.cp("x", z, self.colx(z), self.here.xn).wait_recv()
            self.cp("da", z, self.colx(z, 0), self.here.yn).start()
            self.cp("cx", z, self.colx(z), self.here.cn).start()

        guarded(valid, body)

    def from_y(self, j):
        z, valid = self.visits[j]

        def body():
            self.cp("y", z, self.coly(z), self.here.yn).wait_recv()
            self.cp("db", z, self.coly(z, 1), self.here.xn).start()
            self.cp("cy", z, self.coly(z), self.here.cn).start()

        guarded(valid, body)

    def cross(self, j):
        self.from_x(j)
        self.from_y(j)

    def diagonal(self, j):
        z, valid = self.visits[j]
        here = self.here

        def body():
            self.cp("da", z, self.cold(z), here.yn).wait_recv()
            self.cp("cd", z, self.cold(z), here.cn).start()

        guarded(valid, body)

    def arrive(self):
        self.cp("co", 0, self.block(4 * self.nz), self.here.cn).wait_recv()

    def finish(self):
        here = self.here
        if self.direct:
            for k in range(1, self.nz):
                self.line_cp(k).wait_send()
        else:
            for j, (z, valid) in enumerate(self.visits):
                valid = True if valid is None else valid
                if j == 0 or j % 2 == 1:
                    going = jnp.logical_and(valid, here.z < self.nz - 1)
                    pl.when(going)(lambda: self.cp("z", z, self.own(z), here.up).wait_send())
                if j == 0 or j % 2 == 0:
                    going = jnp.logical_and(valid, here.z > 0)
                    pl.when(going)(lambda: self.cp("zd", z, self.own(z), here.down).wait_send())
        self.cp("x", 0, self.block(3 * self.nz), here.xn).wait_send()
        self.cp("co", 0, self.block(4 * self.nz), here.cn).wait_send()

    def table(self, name):
        kinds = {"l": self.line, "o": self.out, "x": self.from_x, "y": self.from_y, "d": self.diagonal}
        found = {name + "a": self.arrive}
        for kind, step in kinds.items():
            for k in range(self.nz):
                js = (0,) if k == 0 else (2 * k - 1, 2 * k)
                found["%s%s%d" % (name, kind, k)] = lambda js=js, step=step: [step(j) for j in js]
        return found


class Scatter:
    SEMS = 20

    def __init__(self, here, nz, at, core_at, part, block, sems, bufs):
        self.here, self.nz, self.at, self.core_at, self.part = here, nz, at, core_at, part
        self.block, self.sems = block, sems
        self.half, self.side, self.last = bufs
        self.visits = steps_of(here.z, nz)[::-1]

    def cp(self, send, recv, src, dst, device):
        return remote(src, dst, self.sems.at[17 + send], self.sems.at[recv], device)

    def places(self, z, c):
        here = self.here
        y, x = here.y, here.x
        return [(z, x, y * 2 + c), (z, 1 - x, y * 2 + c), (z, x, (1 - y) * 2 + c), (z, 1 - x, (1 - y) * 2 + c)]

    def mine(self, z, k):
        return self.at(*self.places(z, self.here.c)[k])

    def core_cp(self, z, k):
        place = self.places(z, 1 - self.here.c)[k]
        return self.cp(0, z, self.at(*place), self.core_at(k, *place), self.here.cn)

    def core_in(self, z, k):
        return self.core_at(k, *self.places(z, self.here.c)[k])[...]

    def begin(self, z):
        for k in (3, 1, 2, 0):
            self.core_cp(z, k).start()

    def half_cp(self, z, h):
        return self.cp(1, 4 + 4 * h + z, self.part(self.mine(z, 3), h), self.half[h].at[z], (self.here.xn, self.here.yn)[h])

    def side_cp(self, z, side, h):
        return self.cp(
            1, 12 + z, self.part(self.mine(z, 1 + side), h), self.part(self.side.at[side, z], h),
            (self.here.xn, self.here.yn)[side],
        )

    def corner(self, j):
        z, valid = self.visits[j]

        def body():
            self.cp(0, z, self.block(4), self.block(4), self.here.cn).wait_recv()
            for k in (3, 1, 2):
                place = self.mine(z, k)
                place[...] = place[...] + self.core_in(z, k)
                if k == 3:
                    self.half_cp(z, 0).start()
                    self.half_cp(z, 1).start()
                else:
                    self.side_cp(z, k - 1, k - 1).start()

        guarded(valid, body)

    def edges(self, j):
        z, valid = self.visits[j]

        def body():
            for side, h in ((0, 1), (1, 0)):
                self.half_cp(z, h).wait_recv()
                place = self.part(self.mine(z, 1 + side), h)
                place[...] = place[...] + self.half[h][z]
                self.side_cp(z, side, h).start()

        guarded(valid, body)

    def column(self, j, out):
        z, valid = self.visits[j]
        here = self.here

        def body():
            place = self.mine(z, 0)
            total = place[...].astype(jnp.float32) + self.core_in(z, 0).astype(jnp.float32)
            self.cp(1, 12 + z, self.side.at[:, z], self.side.at[:, z], here.xn).wait_recv()
            for side in (0, 1):
                total = total + self.side[side, z].astype(jnp.float32)
            if j == len(self.visits) - 1:
                out[...] = total
            else:
                place[...] = total.astype(jnp.bfloat16)
                self.last_cp(z).start()

        guarded(valid, body)

    def last_cp(self, z):
        here = self.here
        device = {"dp": here.d, "blk": z * 2 + here.x}
        return self.cp(2, 16, self.mine(z, 0), self.last.at[here.z], device)

    def others(self):
        others = self.last.at[pl.ds(0, self.nz - 1)]
        return self.cp(2, 16, others, others, self.here.up)

    def total(self, out):
        here = self.here
        self.others().wait_recv()
        for k in range(1, self.nz):
            out[...] += self.last[(here.z + k) % self.nz].astype(jnp.float32)

    def finish(self):
        here = self.here
        self.cp(0, 0, self.block(4 * self.nz), self.block(4 * self.nz), here.cn).wait_send()
        self.cp(1, 0, self.block(3 * self.nz), self.block(3 * self.nz), here.xn).wait_send()
        self.others().wait_send()

    def table(self, name, out):
        kinds = {"c": self.corner, "e": self.edges, "f": lambda j: self.column(j, out)}
        top = 2 * (self.nz - 1)
        found = {name + "t": lambda: self.total(out)}
        for z in range(self.nz):
            found["%sb%d" % (name, z)] = functools.partial(self.begin, z)
        for kind, step in kinds.items():
            for k in range(self.nz):
                js = (top,) if k == 0 else (top - 2 * k, top - 2 * k + 1)
                found["%s%s%d" % (name, kind, k)] = lambda js=js, step=step: [step(j) for j in js]
        return found


def part_of(ref, half, split, rows):
    return ref.at[pl.ds(0, split)] if half == 0 else ref.at[pl.ds(split, rows - split)]


def weight_block(ref):
    return lambda n: ref.at[pl.ds(0, n * 288), pl.ds(0, 256)]


def stacked_block(ref):
    return lambda n: ref.at[pl.ds(0, n // 2), :, pl.ds(0, 256)]


def weight_places(ref, rows, split=0):
    def at(z, x, d, half=None):
        base, count = (z * 2 + x) * rows, rows
        if half is not None:
            base, count = base + half * split, rows - split if half else split
        return ref.at[pl.ds(pl.multiple_of(base, 16), count), pl.ds(pl.multiple_of(d * 128, 128), 128)]

    return at


BF = jnp.bfloat16
F32 = jnp.float32
ROW = 8
PARAMS = 16


def both(a, b):
    return jnp.logical_and(a, b)


def cols(a, b):
    return lax.dot_general(a, b, (((1,), (1,)), ((), ())), preferred_element_type=F32)


def mm(a, b):
    return jnp.dot(a, b, preferred_element_type=F32)


class Unit(Place):
    def __init__(self):
        super().__init__()
        self.q = jnp.where(self.c == 0, self.x, 3 - self.x)
        self.mu = self.z % 2
        self.alone = self.z == self.q

    def member(self, q, z):
        return {"dp": self.y * 2 + q // 2, "blk": z * 2 + jnp.where(q < 2, q, 3 - q)}

    def peer(self, q):
        return self.member(q, self.z)

    def worker(self, m):
        return self.member(self.z, 2 * self.c + m)

    def keeper(self, h):
        return {"dp": self.y * 2 + self.z // 2, "blk": self.q * 2 + h}

    def column_worker(self, m):
        return {"dp": self.y * 2 + self.z // 2, "blk": (2 * self.c + m) * 2 + self.x}

    def column_keeper(self, k):
        return {"dp": self.y * 2 + self.z // 2, "blk": (2 * self.c + k) * 2 + self.x}

    def line(self, k):
        return {"dp": self.d, "blk": ((self.z + k) % 4) * 2 + self.x}

    def greet(self, shares, lines):
        barrier = pltpu.get_barrier_semaphore()

        def greet(device):
            pl.semaphore_signal(barrier, inc=1, device_id=device, device_id_type=MESH)

        for k in (1, 2, 3):
            greet(self.peer((self.q + k) % 4))
        count = 3
        if lines:
            greet(self.yn)
            for k in (1, 2, 3):
                greet(self.line(k))
            count += 4
        if shares:
            for m in (0, 1):
                pl.when(jnp.logical_not(both(self.alone, self.mu == m)))(lambda m=m: greet(self.worker(m)))
            for h in (0, 1):
                pl.when(jnp.logical_not(both(self.alone, self.x == h)))(lambda h=h: greet(self.keeper(h)))
            near = self.c == self.z // 2
            for k in (0, 1):
                pl.when(jnp.logical_not(both(near, self.mu == k)))(lambda k=k: greet(self.column_worker(k)))
            count = count + 6 - 2 * self.alone.astype(jnp.int32) - near.astype(jnp.int32)
        return count

    def enter(self, count):
        pl.semaphore_wait(pltpu.get_barrier_semaphore(), count)


class Share:
    def __init__(self, u, sems, local):
        self.u, self.sems, self.local = u, sems, local

    def send(self, src, dst):
        u = self.u
        for m in (0, 1):
            mine = both(u.alone, u.mu == m)
            place = dst.at[pl.ds(4 * u.x, 4)]
            pl.when(mine)(lambda: pltpu.make_async_copy(src.at[m], place, self.local).start())
            pl.when(jnp.logical_not(mine))(
                lambda: remote(src.at[m], place, self.sems.at[0, m], self.sems.at[1, u.x], u.worker(m)).start()
            )

    def wait(self, src, dst):
        u = self.u
        for h in (0, 1):
            mine = both(u.alone, u.x == h)
            place = dst.at[pl.ds(4 * h, 4)]
            pl.when(mine)(lambda: pltpu.make_async_copy(src.at[0], place, self.local).wait())
            pl.when(jnp.logical_not(mine))(
                lambda: remote(place, place, self.sems.at[0, 0], self.sems.at[1, h], u.keeper(h)).wait_recv()
            )

    def sent(self, src, dst):
        u = self.u
        for m in (0, 1):
            place = dst.at[pl.ds(4 * u.x, 4)]
            pl.when(jnp.logical_not(both(u.alone, u.mu == m)))(
                lambda: remote(src.at[m], place, self.sems.at[0, m], self.sems.at[1, u.x], u.worker(m)).wait_send()
            )

    def back(self, src, dst):
        u = self.u
        for h in (0, 1):
            mine = both(u.alone, u.x == h)
            piece = src.at[pl.ds(4 * h, 4)]
            pl.when(mine)(lambda: pltpu.make_async_copy(piece, dst.at[u.mu], self.local).start())
            pl.when(jnp.logical_not(mine))(
                lambda: remote(piece, dst.at[u.mu], self.sems.at[0, h], self.sems.at[1, u.mu], u.keeper(h)).start()
            )

    def back_wait(self, src, dst):
        u = self.u
        for m in (0, 1):
            mine = both(u.alone, u.mu == m)
            pl.when(mine)(lambda: pltpu.make_async_copy(src.at[pl.ds(0, 4)], dst.at[m], self.local).wait())
            pl.when(jnp.logical_not(mine))(
                lambda: remote(dst.at[m], dst.at[m], self.sems.at[0, 0], self.sems.at[1, m], u.worker(m)).wait_recv()
            )
        for h in (0, 1):
            pl.when(jnp.logical_not(both(u.alone, u.x == h)))(
                lambda: remote(
                    src.at[pl.ds(4 * h, 4)], dst.at[u.mu], self.sems.at[0, h], self.sems.at[1, u.mu], u.keeper(h)
                ).wait_send()
            )


class ColumnShare:
    def __init__(self, u, buf, sems, local):
        self.u, self.buf, self.sems, self.local = u, buf, sems, local
        self.alone = u.c == u.z // 2

    def place(self, z):
        return self.buf.at[z, pl.ds(4 * self.u.x, 4)]

    def cp(self, src, m):
        u = self.u
        return remote(src.at[m], self.place(u.z), self.sems.at[0, m], self.sems.at[1, u.mu], u.column_worker(m))

    def send(self, src):
        u = self.u
        for m in (0, 1):
            mine = both(self.alone, u.mu == m)
            pl.when(mine)(lambda: pltpu.make_async_copy(src.at[m], self.place(u.z), self.local).start())
            pl.when(jnp.logical_not(mine))(lambda: self.cp(src, m).start())

    def wait(self, src):
        u = self.u
        for k in (0, 1):
            mine = both(self.alone, u.mu == k)
            place = self.place(2 * u.c + k)
            pl.when(mine)(lambda: pltpu.make_async_copy(src.at[0], place, self.local).wait())
            pl.when(jnp.logical_not(mine))(
                lambda: remote(place, place, self.sems.at[0, 0], self.sems.at[1, k], u.column_keeper(k)).wait_recv()
            )

    def sent(self, src):
        u = self.u
        for m in (0, 1):
            pl.when(jnp.logical_not(both(self.alone, u.mu == m)))(lambda: self.cp(src, m).wait_send())


class Swap:
    def __init__(self, u, buf, sems):
        self.u, self.buf, self.sems = u, buf, sems

    def send(self):
        u = self.u
        block = self.buf.at[u.q]
        for k in (1, 2, 3):
            remote(block, block, self.sems.at[0], self.sems.at[1], u.peer((u.q + k) % 4)).start()

    def three(self):
        block = self.buf.at[pl.ds(0, 3)]
        return remote(block, block, self.sems.at[0], self.sems.at[1], self.u.cn)

    def wait(self):
        self.three().wait_recv()

    def sent(self):
        self.three().wait_send()

    def total(self):
        return self.buf[0] + self.buf[1] + self.buf[2] + self.buf[3]


class Spread:
    def __init__(self, u, buf, sems, parts):
        self.u, self.buf, self.sems, self.parts = u, buf, sems, parts

    def cp(self, kind, p, part):
        u = self.u
        ref = self.buf.at[p, part]
        device = u.xn if kind == 1 else u.cn
        return remote(ref, ref, self.sems.at[0, kind, part], self.sems.at[1, kind, part], device)

    def send(self, part):
        self.cp(1, self.u.q, part).start()
        self.cp(0, self.u.q, part).start()

    def across(self):
        q = self.u.q
        return q + 1 - 2 * (q % 2)

    def relay(self, part):
        copy = self.cp(1, self.across(), part)
        copy.wait_recv()
        self.cp(2, self.across(), part).start()

    def near(self, part):
        self.cp(0, 3 - self.u.q, part).wait_recv()

    def far(self, part):
        self.cp(2, 3 - self.across(), part).wait_recv()

    def sent(self, part):
        self.cp(1, self.u.q, part).wait_send()
        self.cp(0, self.u.q, part).wait_send()
        self.cp(2, self.across(), part).wait_send()


class Halo:
    def __init__(self, u, buf, sems):
        self.u, self.buf, self.sems = u, buf, sems

    def cp(self, downward):
        u, buf = self.u, self.buf
        if downward:
            return remote(buf.at[1], buf.at[ROW + 1], self.sems.at[0, 0], self.sems.at[1, 0], u.peer(jnp.maximum(u.q - 1, 0)))
        return remote(buf.at[ROW], buf.at[0], self.sems.at[0, 1], self.sems.at[1, 1], u.peer(jnp.minimum(u.q + 1, 3)))

    def send(self):
        u, buf = self.u, self.buf
        pl.when(u.q > 0)(lambda: self.cp(True).start())
        pl.when(u.q < 3)(lambda: self.cp(False).start())

        @pl.when(u.q == 0)
        def _():
            buf[0] = jnp.zeros(buf.shape[1:], buf.dtype)

        @pl.when(u.q == 3)
        def _():
            buf[ROW + 1] = jnp.zeros(buf.shape[1:], buf.dtype)

    def wait(self):
        u = self.u
        pl.when(u.q > 0)(lambda: self.cp(False).wait_recv())
        pl.when(u.q < 3)(lambda: self.cp(True).wait_recv())

    def sent(self):
        u = self.u
        pl.when(u.q > 0)(lambda: self.cp(True).wait_send())
        pl.when(u.q < 3)(lambda: self.cp(False).wait_send())


def canvas_of(rows, limits):
    return (rows >= limits[0:1]).astype(F32) + (rows >= limits[1:2]).astype(F32)


def row_numbers(u, offset, shape):
    return (ROW * u.q + offset + lax.broadcasted_iota(jnp.int32, shape, 0)).astype(F32)


def counts_of(limits, total_rows):
    each = 64.0 * 16.0
    return (limits[0:1] * each, (limits[1:2] - limits[0:1]) * each, (total_rows - limits[1:2]) * each)


def group_total(sums):
    width = sums.shape[1]
    lane = lax.broadcasted_iota(jnp.int32, sums.shape, 1)
    for step in (1, 2, 4, 8):
        after = pltpu.roll(sums, width - step, 1)
        before = pltpu.roll(sums, step, 1)
        sums = sums + jnp.where((lane // step) % 2 == 0, after, before)
    return sums


def canvas_sums(first, second, seg):
    out = []
    for rows in (first, second):
        for k in range(CANVASES):
            out.append(jnp.sum(jnp.where(seg == float(k), rows, 0.0), axis=0, keepdims=True))
    out.append(jnp.zeros((2, first.shape[1]), F32))
    return jnp.concatenate(out, axis=0)


def by_row(values, seg):
    return jnp.where(seg == 0.0, values[0], jnp.where(seg == 1.0, values[1], values[2]))


def moments(total, counts, seg):
    grouped = group_total(total)
    averages, inverses = [], []
    for k in range(CANVASES):
        average = grouped[k : k + 1] / counts[k]
        averages.append(average)
        inverses.append(lax.rsqrt(grouped[3 + k : 4 + k] / counts[k] - average * average + EPSILON))
    return by_row(averages, seg), by_row(inverses, seg)


def sigmoid(argument):
    return 0.5 * jnp.tanh(0.5 * argument) + 0.5


def each_row(body):
    lax.fori_loop(0, ROW, lambda r, carry: (body(r), carry)[1], 0)


def row_of(ref, r):
    return ref[pl.ds(r, 1), :]


def tap_masks(u, limits, masks):
    shape = (ROW, limits.shape[1])
    rows = row_numbers(u, 0, shape)
    seg = canvas_of(rows, limits)
    masks[0] = both(canvas_of(rows - 1.0, limits) == seg, rows >= 1.0).astype(F32)
    masks[1] = both(canvas_of(rows + 1.0, limits) == seg, rows < 4.0 * ROW - 1.0).astype(F32)
    return seg


def shifted(line):
    position = lax.broadcasted_iota(jnp.int32, line.shape, 0)
    width = line.shape[0]
    before = jnp.where(position == 0, 0.0, pltpu.roll(line, 1, 0))
    after = jnp.where(position == width - 1, 0.0, pltpu.roll(line, width - 1, 0))
    return before, line, after


def taps_inner(buf, masks, taps):
    def body(s):
        lines = shifted(buf[s + 1].astype(F32))
        for k in range(3):
            taps[3 + k, s] = lines[k].astype(BF)

        @pl.when(s < ROW - 1)
        def _():
            mask = masks[0, pl.ds(s + 1, 1), :]
            for k in range(3):
                taps[k, s + 1] = (lines[k] * mask).astype(BF)

        @pl.when(s > 0)
        def _():
            mask = masks[1, pl.ds(s - 1, 1), :]
            for k in range(3):
                taps[6 + k, s - 1] = (lines[k] * mask).astype(BF)

    each_row(body)


def taps_outer(buf, masks, taps):
    for k, line in enumerate(shifted(buf[0].astype(F32))):
        taps[k, 0] = (line * masks[0, 0:1, :]).astype(BF)
    for k, line in enumerate(shifted(buf[ROW + 1].astype(F32))):
        taps[6 + k, ROW - 1] = (line * masks[1, ROW - 1 : ROW, :]).astype(BF)


def conv_tile(taps, weight, m, flip):
    total = None
    for tap in range(9):
        left = taps[8 - tap if flip else tap, pl.ds(pl.multiple_of(m * 4, 4), 4)].reshape(256, -1)
        right = weight[tap * 512 : (tap + 1) * 512, :]
        term = cols(left, right) if flip else mm(left, right)
        total = term if total is None else total + term
    return total.reshape(4, 64, -1)


def conv_weight_grad(act_t, taps, out, first, last):
    def body(tap, carry):
        piece = mm(act_t[...], taps[8 - tap].reshape(512, -1))
        out[pl.ds(pl.multiple_of(tap * 512, 512), 512), :] = piece.astype(BF)
        return carry

    lax.fori_loop(first, last, body, 0)


def attn_places(ref, split=0):
    def at(z, x, d, half=None):
        place = ref.at[z * 2 + x]
        lanes = pl.ds(pl.multiple_of(d * 128, 128), 128)
        if half is None:
            return place.at[:, lanes]
        return place.at[pl.ds(half * split, 256 - split if half else split), lanes]

    return at


def param_places(ref):
    def at(z, x, d, half=None):
        place = ref.at[z * 2 + x]
        lanes = pl.ds(pl.multiple_of(d * 128, 128), 128)
        if half is None:
            return place.at[:, lanes]
        return place.at[pl.ds(half * 8, 8), lanes]

    return at


class Halves:
    def __init__(self, ref):
        self.ref = ref

    @property
    def at(self):
        return self

    def __getitem__(self, index):
        member, part = index
        return self.ref.at[member, pl.ds(part * (ROW // 2), ROW // 2)]


ANY = pl.BlockSpec(memory_space=pl.ANY)
VM = pl.BlockSpec(memory_space=pltpu.VMEM)


class Blocks:
    def __init__(self, ref):
        self.ref = ref

    @property
    def at(self):
        return self

    def __getitem__(self, index):
        member, part = index
        x = jnp.where(member < 2, member, 3 - member)
        return self.ref.at[2 * (member // 2) + part, pl.ds(4 * x, 4)]


def unit_inputs(bounds, norms):
    d, b = lax.axis_index("dp"), lax.axis_index("blk")
    rows = jnp.stack([item.astype(F32) for item in norms])
    lane = jnp.arange(128)[None] // 64
    params = jnp.where((d == b // 2) & (lane == b % 2), jnp.concatenate([rows, rows], axis=1), 0.0)
    limits = jnp.broadcast_to(bounds.reshape(-1).astype(F32)[:, None], (4, 128))
    blank = jnp.zeros((2, 128), F32)
    return jnp.concatenate([params, blank, limits, blank, blank])


def whole_kernel(
    feat, grad, par, s1, s2, sq, sk, sv, so,
    act_back, grad_back, weights_out, norm_out,
    w1, w2, wa, pb, bb, xin, oall, nall, taps, a1, a2, masks, hidden, resid, small, rows_a, rows_b, swaps, lds,
    wg1, wg2, scores, gk, gv, lcol, dcol, big, gres, low, act, act_t1, act_t2, ga, mine, psum_y, psum_z,
    core_a, core_2, half_a, rest_a, side_a, last_a, half_2, rest_2, side_2, last_2, half_1, rest_1, side_1, last_1,
    gsems, ssems, local, share_sems, bound_sems, swap_sems, spread_sems, halo_sems, py_sems, pz_sems,
):
    u = Unit()
    greeters = u.greet(True, True)
    mine[...] = jnp.zeros_like(mine)
    table = {}
    ats = (weight_places(w1, 576, SPLIT), weight_places(w2, 576, SPLIT), attn_places(wa, SPLIT_A), param_places(pb))
    blocks = (weight_block(w1), weight_block(w2), stacked_block(wa), stacked_block(pb))
    groups = [Gather(u, 4, ats[k], blocks[k], gsems.at[k], DIRECT[k]) for k in range(4)]
    for name, group in zip(("g1", "g2", "ga", "gp"), groups):
        table.update(group.table(name))
    own = [pltpu.make_async_copy(src, groups[k].own(u.z), local.at[k]) for k, src in ((0, s1), (1, s2), (3, par))]
    for k, src in enumerate((sq, sk, sv, so)):
        own.append(pltpu.make_async_copy(src, groups[2].own(u.z).at[pl.ds(64 * k, 64)], local.at[8 + k]))
    keep = pltpu.make_async_copy(par, bb.at[u.c], local.at[4])
    for copy in own + [keep]:
        copy.start()
    g1_out, g2_out = weights_out.at[pl.ds(0, 576)], weights_out.at[pl.ds(576, 576)]
    ga_out = weights_out.at[pl.ds(1152, 256)]
    share_x, share_a, share_g = [Share(u, share_sems.at[k], local.at[5 + k]) for k in range(3)]
    share_o = ColumnShare(u, oall, share_sems.at[3], local.at[2])
    swap = [Swap(u, swaps.at[k], swap_sems.at[k]) for k in range(6)] + [Swap(u, lds, swap_sems.at[6])]
    halo = [Halo(u, (a1, a2)[k % 2], halo_sems.at[k]) for k in range(4)]
    spread_o = Spread(u, Blocks(oall), spread_sems.at[0], 2)
    spread_n = Spread(u, Halves(nall), spread_sems.at[1], 2)

    w2_at = weight_places(w2, 576)
    part_a = lambda ref, h: part_of(ref, h, CUT_A, 256)
    part_w = lambda ref, h: part_of(ref, h, CUT, 576)
    sum_a = Scatter(
        u, 4, attn_places(ga), lambda k, z, x, d: core_a.at[k, z], part_a, stacked_block(ga), ssems.at[0], ((half_a, rest_a), side_a, last_a)
    )
    sum_2 = Scatter(
        u, 4, weight_places(wg2, 576), lambda k, z, x, d: core_2.at[k, z], part_w, weight_block(wg2), ssems.at[1], ((half_2, rest_2), side_2, last_2)
    )
    sum_1 = Scatter(
        u, 4, weight_places(wg1, 576), lambda k, z, x, d: w2_at(z, x, d), part_w, weight_block(wg1), ssems.at[2], ((half_1, rest_1), side_1, last_1)
    )
    for name, total, out in (("ra", sum_a, ga_out), ("r2", sum_2, g2_out), ("r1", sum_1, g1_out)):
        table.update(total.table(name, out))
    bound_cp = remote(par, bb.at[u.c], bound_sems.at[0], bound_sems.at[1], u.cn)
    state = {}

    def step(function):
        table[function.__name__] = function
        return function


    @step
    def xs():
        share_x.send(feat, xin)
        bound_cp.start()

    @step
    def os():
        share_o.send(grad)

    @step
    def ow():
        for copy in own:
            copy.wait()
        u.enter(greeters)

    @step
    def bw():
        keep.wait()
        remote(par, bb.at[1 - u.c], bound_sems.at[0], bound_sems.at[1], u.cn).wait_recv()
        limits = jnp.where(u.mu == 0, bb[u.z // 2, 8:10, :], bb[u.z // 2, 10:12, :])
        limits = jnp.concatenate([limits] * 4, axis=1)
        small[7] = jnp.concatenate([limits, jnp.zeros((6, limits.shape[1]), F32)], axis=0)
        state["seg"] = tap_masks(u, limits, masks)
        state["counts"] = counts_of(limits, 4.0 * ROW)

    def first(r):
        return xin[r].astype(F32)

    def second(r):
        return hidden[r]

    def third(r):
        return resid[r]

    values = (first, second, third)

    def norm_sums(k):
        def body(r):
            line = values[k](r)
            rows_a[pl.ds(r, 1), :] = jnp.sum(line, axis=0, keepdims=True)
            rows_b[pl.ds(r, 1), :] = jnp.sum(line * line, axis=0, keepdims=True)

        each_row(body)
        swap[k].buf[u.q] = canvas_sums(rows_a[...], rows_b[...], state["seg"])
        swap[k].send()

    def norm_stats(k):
        swap[k].wait()
        average, inverse = moments(swap[k].total(), state["counts"], state["seg"])
        small[2 * k] = average
        small[2 * k + 1] = inverse

    def param(j):
        return small[6, j : j + 1, :]

    def xhat(k, r):
        return (values[k](r) - small[2 * k, pl.ds(r, 1), :]) * small[2 * k + 1, pl.ds(r, 1), :]

    def normal(k, r):
        return xhat(k, r) * param(2 * k) + param(2 * k + 1)

    def activate(k, buf):
        def body(r):
            line = normal(k, r)
            buf[r + 1] = (line * sigmoid(line)).astype(BF)

        each_row(body)

    @step
    def n1a():
        share_x.wait(feat, xin)
        norm_sums(0)

    @step
    def n1b():
        groups[3].arrive()
        total = pb[0, 0:8, :]
        for b in range(1, 8):
            total = total + pb[b, 0:8, :]
        small[6] = total
        norm_stats(0)

    def conv_steps(name, k, buf):
        def c():
            activate(k, buf)
            halo[k].send()

        def d():
            taps_inner(buf, masks, taps)

        def e():
            halo[k].wait()
            taps_outer(buf, masks, taps)
            halo[k].sent()

        table[name + "c"], table[name + "d"], table[name + "e"] = c, d, e

    conv_steps("n1", 0, a1)
    conv_steps("n2", 1, a2)

    @step
    def t1():
        act_t1[...] = a1[1 : ROW + 1].reshape(512, 512).T

    @step
    def t2():
        act_t2[...] = a2[1 : ROW + 1].reshape(512, 512).T

    def first_conv(m):
        hidden[4 * m : 4 * m + 4] = conv_tile(taps, w1, m, False)

    def second_conv(m):
        resid[4 * m : 4 * m + 4] = conv_tile(taps, w2, m, False) + xin[4 * m : 4 * m + 4].astype(F32)

    for m in (0, 1):
        table["c1%d" % m] = functools.partial(first_conv, m)
        table["c2%d" % m] = functools.partial(second_conv, m)
    table["n2a"], table["n2b"] = functools.partial(norm_sums, 1), functools.partial(norm_stats, 1)
    table["n3a"], table["n3b"] = functools.partial(norm_sums, 2), functools.partial(norm_stats, 2)

    @step
    def n3c():
        def row(r):
            nall[u.q, r] = normal(2, r).astype(BF)

        for part in range(2):
            lax.fori_loop(4 * part, 4 * part + 4, lambda r, carry: (row(r), carry)[1], 0)
            spread_n.send(part)

    @step
    def ob():
        share_o.wait(grad)
        for part in range(2):
            spread_o.send(part)

    for part in (0, 1):
        table["or%d" % part] = functools.partial(spread_o.relay, part)
        table["nr%d" % part] = functools.partial(spread_n.relay, part)

    scale = 512.0 ** (-0.5)
    steep = scale * 1.4426950408889634

    def slot(ref, i):
        return ref.at[pl.ds(pl.multiple_of(i * 512, 512), 512)]

    def query_of(i):
        return slot(wg1, i)

    def key_of(i):
        return slot(wg1, 4 + i)

    def value_of(i):
        return slot(wg2, i)

    def upstream_of(i):
        return slot(wg2, 4 + i)

    heads, gq = slot(wg1, 8), slot(wg2, 8)

    def matrix(k):
        return wa[:, pl.ds(k * 64, 64), :].reshape(512, 512)

    across = u.q + 1 - 2 * (u.q % 2)
    members = (u.q, 3 - u.q, across, 3 - across)

    def project(k):
        if k in (1, 3):
            for part in range(2):
                (spread_n.near if k == 1 else spread_n.far)(part)
        tokens = nall[members[k]].reshape(512, 512)
        query_of(members[k])[...] = mm(tokens, matrix(0)).astype(BF)
        key_of(members[k])[...] = mm(tokens, matrix(1)).astype(BF)
        value_of(members[k])[...] = mm(tokens, matrix(2)).astype(BF)

    def project_up(k):
        if k == 1:
            for part in range(2):
                spread_o.near(part)
                spread_o.far(part)
        upstream = oall[members[k]].reshape(512, 512)
        upstream_of(members[k])[...] = cols(upstream, matrix(3)).astype(BF)

    for k in range(4):
        table["pj%d" % k] = functools.partial(project, k)
        table["po%d" % k] = functools.partial(project_up, k)

    def canvas(rows):
        return (rows >= small[7, 0:1, 0:1]).astype(F32) + (rows >= small[7, 1:2, 0:1]).astype(F32)

    def seg_col(q, offset, count):
        token = offset + lax.broadcasted_iota(jnp.int32, (count, 1), 0)
        return canvas((ROW * q + token // 64).astype(F32))

    def seg_row(q):
        token = lax.broadcasted_iota(jnp.int32, (1, 512), 1)
        return canvas((ROW * q + token // 64).astype(F32))

    def kept(j, i):
        return taps.at[i, pl.ds(pl.multiple_of(j * 4, 4), 4)]

    def queries(j):
        block = pl.ds(j * 256, 256)
        query = query_of(u.q)[block]
        seg = seg_col(u.q, j * 256, 256)
        most = jnp.full((256, 1), NEGATIVE, F32)
        for i in range(4):
            part = jnp.where(seg == seg_row(i), cols(query, key_of(i)[...]) * steep, NEGATIVE)
            scores[j, i] = part
            most = jnp.maximum(most, jnp.max(part, axis=1, keepdims=True))
        total = jnp.zeros((256, 1), F32)
        for i in range(4):
            part = jnp.exp2(scores[j, i] - most)
            total = total + jnp.sum(part, axis=1, keepdims=True)
            scores[j, i] = part
        inverse = 1.0 / total
        found = jnp.zeros((256, 512), F32)
        for i in range(4):
            part = (scores[j, i] * inverse).astype(BF)
            kept(j, i)[...] = part.reshape(4, 64, 512)
            found = found + mm(part, value_of(i)[...])
        heads[block, :] = found.astype(BF)
        lcol[block, :] = jnp.broadcast_to(most + jnp.log2(total), (256, 128))

    @step
    def qf():
        for j in (0, 1):
            queries(j)

    def queries_back(j):
        block = pl.ds(j * 256, 256)
        upstream = upstream_of(u.q)[block]
        correction = jnp.zeros((256, 1), F32)
        for i in range(4):
            slope = cols(upstream, value_of(i)[...])
            scores[j, i] = slope
            part = kept(j, i)[...].reshape(256, 512).astype(F32)
            correction = correction + jnp.sum(part * slope, axis=1, keepdims=True)
        back = jnp.zeros((256, 512), F32)
        for i in range(4):
            part = kept(j, i)[...].reshape(256, 512).astype(F32)
            back = back + mm((part * (scores[j, i] - correction)).astype(BF), key_of(i)[...])
        gq[block, :] = (back * scale).astype(BF)
        dcol[block, :] = jnp.broadcast_to(correction, (256, 128))

    @step
    def qb():
        for j in (0, 1):
            queries_back(j)
        lds[u.q] = jnp.concatenate([lcol[...].T[0:1], dcol[...].T[0:1], jnp.zeros((6, 512), F32)], axis=0)
        swap[6].send()

    @step
    def gz():
        for group in groups:
            group.finish()

    @step
    def hd():
        act[...] = (resid[...] + mm(heads[...], matrix(3)).reshape(ROW, 64, 512)).astype(BF)
        share_a.back(act, act_back)

    @step
    def hw():
        ga[:, 192:256, :] = mm(heads[...].T, oall[u.q].reshape(512, 512)).astype(BF).reshape(8, 64, 512)

    def keys(i, carry):
        query, upstream = query_of(i)[...], upstream_of(i)[...]
        for j in (0, 1):
            key, value = key_of(u.q)[256 * j : 256 * j + 256], value_of(u.q)[256 * j : 256 * j + 256]
            shared = seg_col(u.q, j * 256, 256) == seg_row(i)
            part = jnp.exp2(jnp.where(shared, cols(key, query) * steep, NEGATIVE) - lds[i, 0:1, :])
            slope = cols(value, upstream) - lds[i, 1:2, :]
            rows = pl.ds(4 * j, 4)
            gres[rows] += mm(part.astype(BF), upstream).reshape(4, 64, 512)
            big[rows] += mm((part * slope).astype(BF), query).reshape(4, 64, 512)
        return carry

    @step
    def ks():
        big[...] = jnp.zeros_like(big)
        gres[...] = jnp.zeros_like(gres)
        swap[6].wait()
        lax.fori_loop(0, 4, keys, 0)
        gk[...] = (big[...] * scale).astype(BF).reshape(512, 512)
        gv[...] = gres[...].astype(BF).reshape(512, 512)

    @step
    def aw():
        tokens = nall[u.q].reshape(512, 512).T
        for k, part in enumerate((gq, gk, gv)):
            ga[:, k * 64 : (k + 1) * 64, :] = mm(tokens, part[...]).astype(BF).reshape(8, 64, 512)

    @step
    def an():
        total = None
        for k, part in enumerate((gq, gk, gv)):
            term = cols(part[...], matrix(k))
            total = term if total is None else total + term
        big[...] = total.reshape(ROW, 64, 512)


    def back_sums(k, slope):
        def body(r):
            line = big[r]
            if slope:
                value = normal(k, r)
                part = sigmoid(value)
                line = line * (part * (1.0 + value * (1.0 - part)))
                big[r] = line
            rows_a[pl.ds(r, 1), :] = jnp.sum(line, axis=0, keepdims=True)
            rows_b[pl.ds(r, 1), :] = jnp.sum(line * xhat(k, r), axis=0, keepdims=True)

        each_row(body)
        swap[3 + k].buf[u.q] = canvas_sums(rows_a[...], rows_b[...], state["seg"])
        swap[3 + k].send()

    def back_means(k):
        swap[3 + k].wait()
        total = swap[3 + k].total()
        mine[2 * k : 2 * k + 1, :] = jnp.sum(total[3:6], axis=0, keepdims=True)
        mine[2 * k + 1 : 2 * k + 2, :] = jnp.sum(total[0:3], axis=0, keepdims=True)
        grouped = group_total(total * param(2 * k))
        counts, seg = state["counts"], state["seg"]
        rows_a[...] = by_row([grouped[j : j + 1] / counts[j] for j in range(3)], seg)
        rows_b[...] = by_row([grouped[3 + j : 4 + j] / counts[j] for j in range(3)], seg)

    def back(k, r):
        line = big[r] * param(2 * k) - row_of(rows_a, r) - xhat(k, r) * row_of(rows_b, r)
        return line * small[2 * k + 1, pl.ds(r, 1), :]

    @step
    def b3a():
        back_sums(2, False)

    @step
    def b3b():
        back_means(2)

        def row(r):
            line = oall[u.q, r].astype(F32) + back(2, r)
            gres[r] = line
            a2[r + 1] = line.astype(BF)

        each_row(row)
        halo[3].send()

    @step
    def b2a():
        back_sums(1, True)

    @step
    def b2b():
        back_means(1)

        def row(r):
            a1[r + 1] = back(1, r).astype(BF)

        each_row(row)
        halo[2].send()

    @step
    def b1a():
        back_sums(0, True)

    @step
    def b1m():
        back_means(0)

    @step
    def b1b():
        def row(r):
            low[r] = (gres[r] + back(0, r)).astype(BF)

        each_row(row)
        share_g.back(low, grad_back)

    @step
    def ps():
        remote(mine, psum_y, py_sems.at[0], py_sems.at[1], u.yn).start()

    def back_taps(name, k, buf):
        def c():
            taps_inner(buf, masks, taps)

        def d():
            halo[k].wait()
            taps_outer(buf, masks, taps)
            halo[k].sent()

        table[name + "c"], table[name + "d"] = c, d

    back_taps("b3", 3, a2)
    back_taps("b2", 2, a1)

    def tile_back(weight, m):
        big[4 * m : 4 * m + 4] = conv_tile(taps, weight, m, True)

    for m in (0, 1):
        table["d2%d" % m] = functools.partial(tile_back, w2, m)
        table["d1%d" % m] = functools.partial(tile_back, w1, m)
    for k in range(3):
        table["w2%d" % k] = functools.partial(conv_weight_grad, act_t2, taps, wg2, 3 * k, 3 * k + 3)
        table["w1%d" % k] = functools.partial(conv_weight_grad, act_t1, taps, wg1, 3 * k, 3 * k + 3)

    def line_cp(block, k):
        return remote(block, block, pz_sems.at[0], pz_sems.at[1], u.line(k))

    @step
    def py():
        remote(mine, psum_y, py_sems.at[0], py_sems.at[1], u.yn).wait()
        psum_z[u.z] = mine[...] + psum_y[...]
        for k in (1, 2, 3):
            line_cp(psum_z.at[u.z], k).start()

    @step
    def pz():
        line_cp(psum_z.at[pl.ds(0, 3)], 1).wait_recv()
        total = psum_z[0] + psum_z[1] + psum_z[2] + psum_z[3]
        norm_out[...] = pltpu.roll(total, lax.rem(512 - 64 * u.b, 512), 1)[:, 0:128]

    in_order(types.SimpleNamespace(**table))

    share_a.back_wait(act, act_back)
    share_g.back_wait(low, grad_back)
    for total in (sum_a, sum_2, sum_1):
        total.finish()
    bound_cp.wait_send()
    share_x.sent(feat, xin)
    share_o.sent(grad)
    for item in swap:
        item.sent()
    for item in (spread_o, spread_n):
        for part in range(2):
            item.sent(part)
    line_cp(psum_z.at[pl.ds(0, 3)], 1).wait_send()


def whole_call(features, out_grad, params, *shards):
    full = lambda shape, kind: jax.ShapeDtypeStruct(shape, kind)
    dma = pltpu.SemaphoreType.DMA
    rows, padded, square, weight = (ROW, 64, 512), (ROW + 2, 64, 512), (512, 512), (4608, 512)
    low = lambda *shape: pltpu.VMEM(shape, BF)
    wide = lambda *shape: pltpu.VMEM(shape, F32)
    sums = []
    for r, cut in ((256, CUT_A), (576, CUT), (576, CUT)):
        sums += [low(4, cut, 128), low(4, r - cut, 128), low(2, 4, r, 128), low(4, r, 128)]
    return pl.pallas_call(
        whole_kernel,
        out_shape=[
            full((2, 4, 64, 512), BF), full((2, 4, 64, 512), BF), full((1408, 128), F32),
            full((8, 128), F32),
        ],
        in_specs=[ANY] * 9,
        out_specs=[ANY, ANY, VM, VM],
        scratch_shapes=[
            low(*weight), low(*weight), low(8, 256, 512), wide(8, PARAMS, 512), wide(2, PARAMS, 128), low(*rows),
            low(4, *rows), low(4, *rows), low(9, *rows), low(*padded), low(*padded), wide(2, ROW, 512),
            wide(*rows), wide(*rows), wide(8, 8, 512), wide(ROW, 512), wide(ROW, 512), wide(6, 4, 8, 512), wide(4, 8, 512),
            low(*weight), low(*weight), wide(2, 4, 256, 512), low(*square), low(*square),
            wide(512, 128), wide(512, 128), wide(*rows), wide(*rows), low(*rows), low(*rows), low(*square), low(*square),
            low(8, 256, 512), wide(8, 512), wide(8, 512), wide(4, 8, 512),
            low(4, 4, 256, 128), low(4, 4, 576, 128), *sums,
            dma((4, Gather.SEMS)), dma((3, Scatter.SEMS)), dma((12,)), dma((4, 2, 2)), dma((2,)), dma((7, 2)),
            dma((2, 2, 3, 2)), dma((4, 2, 2)), dma((2,)), dma((2,)),
        ],
        compiler_params=pltpu.CompilerParams(collective_id=0, has_side_effects=True, vmem_limit_bytes=LIMIT),
    )(features, out_grad, params, *shards)


def unit_shards(
    features, bounds, out_grad, norm1_gain, norm1_shift, conv1_weight, norm2_gain, norm2_shift, conv2_weight,
    norm3_gain, norm3_shift, query_weight, key_weight, value_weight, output_weight,
):
    norms = (norm1_gain, norm1_shift, norm2_gain, norm2_shift, norm3_gain, norm3_shift)
    act_back, grad_back, weights, norms = whole_call(
        features[0], out_grad[0], unit_inputs(bounds, norms), conv1_weight, conv2_weight,
        query_weight, key_weight, value_weight, output_weight,
    )
    norms = norms[:, :64]
    g1, g2, ga = weights[:576], weights[576:1152], weights[1152:].reshape(4, 64, 128)
    return (
        act_back.astype(F32)[None], grad_back.astype(F32)[None], norms[0], norms[1], g1, norms[2], norms[3], g2,
        norms[4], norms[5], ga[0], ga[1], ga[2], ga[3],
    )


def extended(shard, sides, width):
    for axis, dim in sides:
        devices, length = (lax.axis_size(axis), shard.shape[dim])
        up = [(i, (i + 1) % devices) for i in range(devices - 1)]
        down = [(j, i) for i, j in up]
        last = lax.slice_in_dim(shard, length - width, length, axis=dim)
        initial = lax.slice_in_dim(shard, 0, width, axis=dim)
        before = lax.ppermute(last, axis, up)
        after = lax.ppermute(initial, axis, down)
        shard = jnp.concatenate([before, shard, after], axis=dim)
    return shard


def canvas_index(global_rows, first_row, second_row):
    return (global_rows >= first_row).astype(jnp.int32) + (global_rows >= second_row).astype(
        jnp.int32
    )


def swish(argument):
    return argument * jax.nn.sigmoid(argument)


def swish_slope(argument):
    sigmoid_value = jax.nn.sigmoid(argument)
    return sigmoid_value * (1.0 + argument * (1.0 - sigmoid_value))


def group_sums(member, grouped):
    return jnp.einsum("rk,rwgc->kg", member, grouped, precision=HIGHEST)


def spread_rows(member, lookup):
    return jnp.dot(member, lookup, precision=HIGHEST)


def norm_forward(inputs, member, counts, norm_gain, norm_shift):
    row_count, width, channels = inputs.shape
    grouped = inputs.reshape(row_count, width, GROUPS, channels // GROUPS)
    totals, square = lax.psum(
        (group_sums(member, grouped), group_sums(member, grouped * grouped)), "blk"
    )
    average = totals / counts[:, None]
    inverse = lax.rsqrt(square / counts[:, None] - average * average + EPSILON)
    average_rows = spread_rows(member, average)
    scale_rows = spread_rows(member, inverse)
    normal = (grouped - average_rows[:, None, :, None]) * scale_rows[:, None, :, None]
    normal = normal.reshape(row_count, width, channels)
    return (normal * norm_gain + norm_shift, normal, scale_rows)


def norm_backward(incoming, normal, scale_rows, member, counts, norm_gain):
    row_count, width, channels = incoming.shape
    gain_grad = jnp.sum(incoming * normal, axis=(0, 1))
    shift_grad = jnp.sum(incoming, axis=(0, 1))
    scaled = (incoming * norm_gain).reshape(row_count, width, GROUPS, channels // GROUPS)
    grouped_normal = normal.reshape(row_count, width, GROUPS, channels // GROUPS)
    first_sum, second_sum = lax.psum(
        (group_sums(member, scaled), group_sums(member, scaled * grouped_normal)), "blk"
    )
    first_rows = spread_rows(member, first_sum / counts[:, None])
    second_rows = spread_rows(member, second_sum / counts[:, None])
    result = scale_rows[:, None, :, None] * (
        scaled - first_rows[:, None, :, None] - grouped_normal * second_rows[:, None, :, None]
    )
    return (result.reshape(row_count, width, channels), gain_grad, shift_grad)


def gather_taps(padded, seg_pad, seg_rows, direction):
    row_count = seg_rows.shape[0]
    width = padded.shape[1]
    widened = jnp.pad(padded, ((0, 0), (1, 1), (0, 0)))
    pieces = []
    for step_row in (-1, 0, 1):
        low_row = 1 + direction * step_row
        allowed = (seg_pad[low_row : low_row + row_count] == seg_rows).astype(padded.dtype)[
            :, None, None
        ]
        for step_col in (-1, 0, 1):
            low_col = 1 + direction * step_col
            pieces.append(
                widened[low_row : low_row + row_count, low_col : low_col + width, :] * allowed
            )
    return jnp.stack(pieces, axis=2)


def conv_apply(activation, seg_pad, seg_rows, weight_matrix):
    row_count, width, channels = activation.shape
    padded = extended(activation, (("blk", 0),), 1)
    stacked = gather_taps(padded, seg_pad, seg_rows, 1).reshape(row_count * width, 9 * channels)
    result = jnp.dot(stacked, weight_matrix, preferred_element_type=jnp.float32)
    return (result.reshape(row_count, width, channels), stacked)


def conv_reverse(gradient, stacked, seg_pad, seg_rows, weight_matrix):
    row_count, width, channels = gradient.shape
    flattened = gradient.reshape(row_count * width, channels)
    weight_grad = lax.dot_general(
        stacked, flattened, (((0,), (0,)), ((), ())), preferred_element_type=jnp.float32
    )
    padded = extended(gradient, (("blk", 0),), 1)
    mirrored = gather_taps(padded, seg_pad, seg_rows, -1).reshape(row_count * width, 9, channels)
    kernel = weight_matrix.reshape(9, channels, channels)
    result = lax.dot_general(
        mirrored, kernel, (((1, 2), (0, 2)), ((), ())), preferred_element_type=jnp.float32
    )
    return (result.reshape(row_count, width, channels), weight_grad)


def attention_forward(
    queries, keys_local, values_local, token_seg, first_row, second_row, width, scale
):
    token_count, channels = queries.shape

    def absorb(running, portion, offset):
        key_block, value_block = portion
        maximum, totals, accumulated = running
        key_seg = canvas_index(
            jnp.arange(key_block.shape[0], dtype=jnp.int32) // width, first_row, second_row
        )
        shared = token_seg[:, None] == key_seg[None, :]
        scores = (
            lax.dot_general(
                queries, key_block, (((1,), (1,)), ((), ())), preferred_element_type=jnp.float32
            )
            * scale
        )
        masked = jnp.where(shared, scores, NEGATIVE)
        new_maximum = jnp.maximum(maximum, jnp.max(masked, axis=1))
        weights = jnp.where(shared, jnp.exp(masked - new_maximum[:, None]), 0.0)
        totals = jnp.sum(weights, axis=1)
        accumulated = jnp.dot(
            weights.astype(jnp.bfloat16), value_block, preferred_element_type=jnp.float32
        )
        return (new_maximum, totals, accumulated)

    initial = (
        jnp.full((token_count,), NEGATIVE, jnp.float32),
        jnp.zeros((token_count,), jnp.float32),
        jnp.zeros((token_count, channels), jnp.float32),
    )
    maximum, totals, accumulated = absorb(
        initial,
        (
            lax.all_gather(keys_local, "blk", axis=0, tiled=True),
            lax.all_gather(values_local, "blk", axis=0, tiled=True),
        ),
        jnp.int32(0),
    )
    return (accumulated / totals[:, None], maximum + jnp.log(totals))


def attention_query_grad(
    queries,
    heads_grad,
    log_total,
    correction,
    keys_local,
    values_local,
    token_seg,
    first_row,
    second_row,
    width,
    scale,
):

    def absorb(running, portion, offset):
        key_block, value_block = portion
        key_seg = canvas_index(
            jnp.arange(key_block.shape[0], dtype=jnp.int32) // width, first_row, second_row
        )
        shared = token_seg[:, None] == key_seg[None, :]
        scores = (
            lax.dot_general(
                queries, key_block, (((1,), (1,)), ((), ())), preferred_element_type=jnp.float32
            )
            * scale
        )
        weights = jnp.where(
            shared, jnp.exp(jnp.where(shared, scores, NEGATIVE) - log_total[:, None]), 0.0
        )
        slopes = lax.dot_general(
            heads_grad, value_block, (((1,), (1,)), ((), ())), preferred_element_type=jnp.float32
        )
        score_grad = (weights * (slopes - correction[:, None])).astype(jnp.bfloat16)
        return jnp.dot(score_grad, key_block, preferred_element_type=jnp.float32) * scale

    return absorb(
        jnp.zeros(queries.shape, jnp.float32),
        (
            lax.all_gather(keys_local, "blk", axis=0, tiled=True),
            lax.all_gather(values_local, "blk", axis=0, tiled=True),
        ),
        jnp.int32(0),
    )


def attention_key_grad(
    queries,
    heads_grad,
    log_total,
    correction,
    keys_local,
    values_local,
    token_seg,
    first_row,
    second_row,
    width,
    scale,
):

    def absorb(running, portion, offset):
        query_part, upstream_part, total_part, correct_part = portion
        query_seg = canvas_index(
            jnp.arange(query_part.shape[0], dtype=jnp.int32) // width, first_row, second_row
        )
        query_low = query_part.astype(jnp.bfloat16)
        upstream_low = upstream_part.astype(jnp.bfloat16)
        shared = query_seg[:, None] == token_seg[None, :]
        scores = (
            lax.dot_general(
                query_low, keys_local, (((1,), (1,)), ((), ())), preferred_element_type=jnp.float32
            )
            * scale
        )
        weights = jnp.where(
            shared, jnp.exp(jnp.where(shared, scores, NEGATIVE) - total_part[:, None]), 0.0
        )
        value_acc = lax.dot_general(
            weights.astype(jnp.bfloat16),
            upstream_low,
            (((0,), (0,)), ((), ())),
            preferred_element_type=jnp.float32,
        )
        slopes = lax.dot_general(
            upstream_low, values_local, (((1,), (1,)), ((), ())), preferred_element_type=jnp.float32
        )
        score_grad = (weights * (slopes - correct_part[:, None])).astype(jnp.bfloat16)
        key_acc = (
            lax.dot_general(
                score_grad, query_low, (((0,), (0,)), ((), ())), preferred_element_type=jnp.float32
            )
            * scale
        )
        return (key_acc, value_acc)

    empty = jnp.zeros(keys_local.shape, jnp.float32)
    return absorb(
        (empty, empty),
        (
            lax.all_gather(queries.astype(jnp.float32), "blk", axis=0, tiled=True),
            lax.all_gather(heads_grad.astype(jnp.float32), "blk", axis=0, tiled=True),
            lax.all_gather(log_total, "blk", axis=0, tiled=True),
            lax.all_gather(correction, "blk", axis=0, tiled=True),
        ),
        jnp.int32(0),
    )


def collect(
    conv1_weight,
    conv2_weight,
    query_weight,
    key_weight,
    value_weight,
    output_weight,
    norm1_gain,
    norm1_shift,
    norm2_gain,
    norm2_shift,
    norm3_gain,
    norm3_shift,
):
    row_parts = (
        lax.all_gather(conv1_weight, "blk", axis=0, tiled=True),
        lax.all_gather(conv2_weight, "blk", axis=0, tiled=True),
        lax.all_gather(query_weight, "blk", axis=0, tiled=True),
        lax.all_gather(key_weight, "blk", axis=0, tiled=True),
        lax.all_gather(value_weight, "blk", axis=0, tiled=True),
        lax.all_gather(output_weight, "blk", axis=0, tiled=True),
        lax.all_gather(norm1_gain, "blk", axis=0, tiled=True),
        lax.all_gather(norm1_shift, "blk", axis=0, tiled=True),
        lax.all_gather(norm2_gain, "blk", axis=0, tiled=True),
        lax.all_gather(norm2_shift, "blk", axis=0, tiled=True),
        lax.all_gather(norm3_gain, "blk", axis=0, tiled=True),
        lax.all_gather(norm3_shift, "blk", axis=0, tiled=True),
    )
    full_parts = (
        lax.all_gather(row_parts[0], "dp", axis=1, tiled=True),
        lax.all_gather(row_parts[1], "dp", axis=1, tiled=True),
        lax.all_gather(row_parts[2], "dp", axis=1, tiled=True),
        lax.all_gather(row_parts[3], "dp", axis=1, tiled=True),
        lax.all_gather(row_parts[4], "dp", axis=1, tiled=True),
        lax.all_gather(row_parts[5], "dp", axis=1, tiled=True),
    )
    return (tuple(full_parts), tuple(row_parts[6:]))


def reduce_all(gradients):
    row_sums = (
        lax.psum_scatter(gradients[0], "blk", scatter_dimension=0, tiled=True),
        lax.psum_scatter(gradients[1], "blk", scatter_dimension=0, tiled=True),
        lax.psum_scatter(gradients[2], "blk", scatter_dimension=0, tiled=True),
        lax.psum_scatter(gradients[3], "blk", scatter_dimension=0, tiled=True),
        lax.psum_scatter(gradients[4], "blk", scatter_dimension=0, tiled=True),
        lax.psum_scatter(gradients[5], "blk", scatter_dimension=0, tiled=True),
        lax.psum_scatter(gradients[6], "blk", scatter_dimension=0, tiled=True),
        lax.psum_scatter(gradients[7], "blk", scatter_dimension=0, tiled=True),
        lax.psum_scatter(gradients[8], "blk", scatter_dimension=0, tiled=True),
        lax.psum_scatter(gradients[9], "blk", scatter_dimension=0, tiled=True),
        lax.psum_scatter(gradients[10], "blk", scatter_dimension=0, tiled=True),
        lax.psum_scatter(gradients[11], "blk", scatter_dimension=0, tiled=True),
    )
    matrix_sums = (
        lax.psum_scatter(row_sums[0], "dp", scatter_dimension=1, tiled=True),
        lax.psum_scatter(row_sums[1], "dp", scatter_dimension=1, tiled=True),
        lax.psum_scatter(row_sums[2], "dp", scatter_dimension=1, tiled=True),
        lax.psum_scatter(row_sums[3], "dp", scatter_dimension=1, tiled=True),
        lax.psum_scatter(row_sums[4], "dp", scatter_dimension=1, tiled=True),
        lax.psum_scatter(row_sums[5], "dp", scatter_dimension=1, tiled=True),
    )
    norm_sums = lax.psum(
        (row_sums[6], row_sums[7], row_sums[8], row_sums[9], row_sums[10], row_sums[11]), "dp"
    )
    return tuple(matrix_sums) + tuple(norm_sums)


def one_batch(inputs_low, bound_pair, upstream_low, matrices, norm_params, position, blocks):
    row_count, width, channels = inputs_low.shape
    token_count = row_count * width
    total_rows = row_count * blocks
    scale = channels ** (-0.5)
    first_row = bound_pair[0]
    second_row = bound_pair[1]
    local_rows = position * row_count + jnp.arange(row_count, dtype=jnp.int32)
    padded_rows = position * row_count - 1 + jnp.arange(row_count + 2, dtype=jnp.int32)
    seg_rows = canvas_index(local_rows, first_row, second_row)
    seg_pad = canvas_index(padded_rows, first_row, second_row)
    member = (seg_rows[:, None] == jnp.arange(CANVASES, dtype=jnp.int32)[None, :]).astype(
        jnp.float32
    )
    counts = jnp.stack([first_row, second_row - first_row, total_rows - second_row]).astype(
        jnp.float32
    ) * float(width * (channels // GROUPS))
    gains = [item.astype(jnp.float32) for item in norm_params]
    inputs = inputs_low.astype(jnp.float32)
    norm_one, normal_one, scale_one = norm_forward(inputs, member, counts, gains[0], gains[1])
    act_one = swish(norm_one).astype(jnp.bfloat16)
    hidden_one, stacked_one = conv_apply(act_one, seg_pad, seg_rows, matrices[0])
    norm_two, normal_two, scale_two = norm_forward(hidden_one, member, counts, gains[2], gains[3])
    act_two = swish(norm_two).astype(jnp.bfloat16)
    hidden_two, stacked_two = conv_apply(act_two, seg_pad, seg_rows, matrices[1])
    residual = inputs + hidden_two
    norm_three, normal_three, scale_three = norm_forward(
        residual, member, counts, gains[4], gains[5]
    )
    normed = norm_three.astype(jnp.bfloat16).reshape(token_count, channels)
    queries = jnp.dot(normed, matrices[2], preferred_element_type=jnp.float32).astype(jnp.bfloat16)
    keys_local = jnp.dot(normed, matrices[3], preferred_element_type=jnp.float32).astype(
        jnp.bfloat16
    )
    values_local = jnp.dot(normed, matrices[4], preferred_element_type=jnp.float32).astype(
        jnp.bfloat16
    )
    token_seg = jnp.repeat(seg_rows, width)
    attended, log_total = attention_forward(
        queries, keys_local, values_local, token_seg, first_row, second_row, width, scale
    )
    heads = attended.astype(jnp.bfloat16)
    activation = residual + jnp.dot(heads, matrices[5], preferred_element_type=jnp.float32).reshape(
        row_count, width, channels
    )
    upstream = upstream_low.reshape(token_count, channels)
    output_weight_grad = lax.dot_general(
        heads, upstream, (((0,), (0,)), ((), ())), preferred_element_type=jnp.float32
    )
    heads_grad = lax.dot_general(
        upstream, matrices[5], (((1,), (1,)), ((), ())), preferred_element_type=jnp.float32
    ).astype(jnp.bfloat16)
    correction = jnp.sum(heads_grad.astype(jnp.float32) * attended, axis=1)
    query_sum = attention_query_grad(
        queries,
        heads_grad,
        log_total,
        correction,
        keys_local,
        values_local,
        token_seg,
        first_row,
        second_row,
        width,
        scale,
    )
    key_sum, value_sum = attention_key_grad(
        queries,
        heads_grad,
        log_total,
        correction,
        keys_local,
        values_local,
        token_seg,
        first_row,
        second_row,
        width,
        scale,
    )
    query_low = query_sum.astype(jnp.bfloat16)
    key_low = key_sum.astype(jnp.bfloat16)
    value_low = value_sum.astype(jnp.bfloat16)
    contract_rows = (((0,), (0,)), ((), ()))
    contract_cols = (((1,), (1,)), ((), ()))
    query_weight_grad = lax.dot_general(
        normed, query_low, contract_rows, preferred_element_type=jnp.float32
    )
    key_weight_grad = lax.dot_general(
        normed, key_low, contract_rows, preferred_element_type=jnp.float32
    )
    value_weight_grad = lax.dot_general(
        normed, value_low, contract_rows, preferred_element_type=jnp.float32
    )
    normed_grad = (
        lax.dot_general(query_low, matrices[2], contract_cols, preferred_element_type=jnp.float32)
        + lax.dot_general(key_low, matrices[3], contract_cols, preferred_element_type=jnp.float32)
        + lax.dot_general(value_low, matrices[4], contract_cols, preferred_element_type=jnp.float32)
    )
    back_three, gain_three_grad, shift_three_grad = norm_backward(
        normed_grad.reshape(row_count, width, channels),
        normal_three,
        scale_three,
        member,
        counts,
        gains[4],
    )
    residual_grad = upstream_low.astype(jnp.float32) + back_three
    act_two_grad, conv_two_grad = conv_reverse(
        residual_grad.astype(jnp.bfloat16), stacked_two, seg_pad, seg_rows, matrices[1]
    )
    back_two, gain_two_grad, shift_two_grad = norm_backward(
        act_two_grad * swish_slope(norm_two), normal_two, scale_two, member, counts, gains[2]
    )
    act_one_grad, conv_one_grad = conv_reverse(
        back_two.astype(jnp.bfloat16), stacked_one, seg_pad, seg_rows, matrices[0]
    )
    back_one, gain_one_grad, shift_one_grad = norm_backward(
        act_one_grad * swish_slope(norm_one), normal_one, scale_one, member, counts, gains[0]
    )
    input_grad = residual_grad + back_one
    local_grads = (
        conv_one_grad,
        conv_two_grad,
        query_weight_grad,
        key_weight_grad,
        value_weight_grad,
        output_weight_grad,
        gain_one_grad,
        shift_one_grad,
        gain_two_grad,
        shift_two_grad,
        gain_three_grad,
        shift_three_grad,
    )
    return (activation, input_grad, local_grads)


def shards(
    features,
    bounds,
    out_grad,
    norm1_gain,
    norm1_shift,
    conv1_weight,
    norm2_gain,
    norm2_shift,
    conv2_weight,
    norm3_gain,
    norm3_shift,
    query_weight,
    key_weight,
    value_weight,
    output_weight,
):
    blocks = lax.axis_size("blk")
    position = lax.axis_index("blk")
    micro_count = features.shape[1]
    shard_sums = None
    outputs = []
    input_grads = []
    for micro_index in range(micro_count):
        matrices, norm_params = collect(
            conv1_weight,
            conv2_weight,
            query_weight,
            key_weight,
            value_weight,
            output_weight,
            norm1_gain,
            norm1_shift,
            norm2_gain,
            norm2_shift,
            norm3_gain,
            norm3_shift,
        )
        activation, input_grad, local_grads = one_batch(
            features[0, micro_index],
            bounds[0, micro_index],
            out_grad[0, micro_index],
            matrices,
            norm_params,
            position,
            blocks,
        )
        outputs.append(activation)
        input_grads.append(input_grad)
        reduced = reduce_all(local_grads)
        shard_sums = (
            reduced
            if shard_sums is None
            else tuple((acc + new for acc, new in zip(shard_sums, reduced)))
        )
    activations = jnp.stack(outputs)[None]
    input_grad_all = jnp.stack(input_grads)[None]
    return (
        activations,
        input_grad_all,
        shard_sums[6],
        shard_sums[7],
        shard_sums[0],
        shard_sums[8],
        shard_sums[9],
        shard_sums[1],
        shard_sums[10],
        shard_sums[11],
        shard_sums[2],
        shard_sums[3],
        shard_sums[4],
        shard_sums[5],
    )


def solution(mesh):
    in_specs = (
        P("dp", None, "blk", None, None),
        P("dp", None, None),
        P("dp", None, "blk", None, None),
        P("blk"),
        P("blk"),
        P("blk", "dp"),
        P("blk"),
        P("blk"),
        P("blk", "dp"),
        P("blk"),
        P("blk"),
        P("blk", "dp"),
        P("blk", "dp"),
        P("blk", "dp"),
        P("blk", "dp"),
    )
    out_specs = (
        P("dp", None, "blk", None, None),
        P("dp", None, "blk", None, None),
        P("blk"),
        P("blk"),
        P("blk", "dp"),
        P("blk"),
        P("blk"),
        P("blk", "dp"),
        P("blk"),
        P("blk"),
        P("blk", "dp"),
        P("blk", "dp"),
        P("blk", "dp"),
        P("blk", "dp"),
    )
    near = mesh.shape["dp"] == 4 and mesh.shape["blk"] == 8
    return jax.shard_map(unit_shards if near else shards, mesh=mesh, in_specs=in_specs, out_specs=out_specs, check_vma=False)
```
